32 devices in a mesh: dp: 16 (over z, x, core), ctx: 2 (over y).
Axes of the slice: x: 2, y: 2, z: 4, core: 2. Of those that a mesh axis runs over, the one named last changes fastest.
Arguments:
- tokens: bfloat16 [2, 32, 1024, 768], P(None, 'dp', 'ctx'), may hold values from -6 to 6
- cotangent: bfloat16 [2, 32, 1024, 768], P(None, 'dp', 'ctx'), may hold values from -6 to 6
- placing: int32 [2, 32], replicated, may hold values from 0 to 31, as said below
- starts: int32 [2, 32], replicated, may hold values from 0 to 1, as said below
- memory_tokens: float32 [16, 768], replicated, may hold values from -6 to 6
- norm_one_gain: float32 [768], replicated, may hold values from 0.5 to 1.5
- norm_one_bias: float32 [768], replicated, may hold values from -1.8 to 1.8
- qkv_weight: bfloat16 [768, 2304], P('dp'), may hold values from -0.21875 to 0.21875
- qv_bias: float32 [2, 768], replicated, may hold values from -1.8 to 1.8
- out_weight: bfloat16 [768, 768], P('dp'), may hold values from -1.75 to 1.75
- out_bias: float32 [768], replicated, may hold values from -1.8 to 1.8
- norm_two_gain: float32 [768], replicated, may hold values from 0.5 to 1.5
- norm_two_bias: float32 [768], replicated, may hold values from -1.8 to 1.8
- expand_weight: bfloat16 [768, 3072], P('dp'), may hold values from -0.21875 to 0.21875
- expand_bias: float32 [3072], replicated, may hold values from -1.8 to 1.8
- contract_weight: bfloat16 [768, 3072], P('dp'), may hold values from -0.109375 to 0.109375
- contract_bias: float32 [768], replicated, may hold values from -1.8 to 1.8
- read_weight: bfloat16 [768, 384], P('dp'), may hold values from -0.21875 to 0.21875
- key_weight: bfloat16 [768, 384], P('dp'), may hold values from -0.21875 to 0.21875
- value_weight: bfloat16 [768, 768], P('dp'), may hold values from -0.21875 to 0.21875
Outputs:
- block_out: bfloat16 [2, 32, 1024, 768], P(None, 'dp', 'ctx')
- token_grad: bfloat16 [2, 32, 1024, 768], P(None, 'dp', 'ctx')
- memory_tokens_grad: float32 [16, 768], replicated
- norm_one_gain_grad: float32 [768], replicated
- norm_one_bias_grad: float32 [768], replicated
- qkv_weight_grad: float32 [768, 2304], P('dp')
- qv_bias_grad: float32 [2, 768], replicated
- out_weight_grad: float32 [768, 768], P('dp')
- out_bias_grad: float32 [768], replicated
- norm_two_gain_grad: float32 [768], replicated
- norm_two_bias_grad: float32 [768], replicated
- expand_weight_grad: float32 [768, 3072], P('dp')
- expand_bias_grad: float32 [3072], replicated
- contract_weight_grad: float32 [768, 3072], P('dp')
- contract_bias_grad: float32 [768], replicated
- read_weight_grad: float32 [768, 384], P('dp')
- key_weight_grad: float32 [768, 384], P('dp')
- value_weight_grad: float32 [768, 768], P('dp')
The draws below stay inside these ranges and needn't reach their ends.
Inputs may be any that keep to these rules, and one draw needn't show every extreme that they name: In each micro-batch placing is a permutation; slot p belongs to index p // 2 of dp. A sequence is a run of given positions from one with starts = 1 to the next; its segments lie on consecutive slots of one index, in their order, so every slot p with p % 2 == 0 begins a sequence. `starts`: given position 0 of each micro-batch is 1. A sequence has 1 to 2 segments, and in every micro-batch one has exactly 2.
All inputs are finite; a program needn't handle non-finite values.
Results may differ from the reference program's by a relative error of at most 0.024.
Values may be sent and summed in bfloat16 or wider, within the bound.
A program may use at most 640 MiB of HBM per device.

```python
import jax
import jax.numpy as jnp
from jax import lax

D = 768
H = 12
HD = 64
FF = 3072
M = 16
DK = 384
DPHI = 2304
SEG = 1024
SEG_MB = 2
MB = 2
NSEGM = 32


def plan(key):
    owners = NSEGM // SEG_MB
    key_break, key_long, key_rank = jax.random.split(jax.random.fold_in(key, 11), 3)
    breaks = jax.random.randint(key_break, (MB, owners, SEG_MB), 0, 2, dtype=jnp.int32)
    longest = jax.random.randint(key_long, (MB, 1, 1), 0, owners, dtype=jnp.int32)
    column = jnp.arange(SEG_MB, dtype=jnp.int32)[None, None, :]
    owner = jnp.arange(owners, dtype=jnp.int32)[None, :, None]
    breaks = jnp.where(column == 0, 1, jnp.where(owner == longest, 0, breaks)).reshape(MB, NSEGM)
    places = jnp.arange(NSEGM, dtype=jnp.int32)[None, :]
    heads_at = lax.cummax(jnp.where(breaks == 1, places, 0), axis=1)
    ranking = jax.random.permutation(key_rank, MB * NSEGM).reshape(MB, NSEGM).astype(jnp.int32)
    sortkey = jnp.take_along_axis(ranking, heads_at, axis=1) * NSEGM + places
    sorted_slots = jnp.argsort(sortkey, axis=1).astype(jnp.int32)
    placing = jnp.argsort(sorted_slots, axis=1).astype(jnp.int32)
    starts = jnp.take_along_axis(breaks, sorted_slots, axis=1).astype(jnp.int32)
    return (placing, starts)


def draw_placing(key, part):
    return plan(key)[0]


def draw_starts(key, part):
    return plan(key)[1]


def block_levels(stream_key, extent, cuts, low, top_value):
    def one(dim, parts):
        draws = jax.random.uniform(jax.random.fold_in(jax.random.fold_in(stream_key, 6), dim), (parts,), jnp.float32, low / len(cuts), top_value / len(cuts))
        return jnp.repeat(jnp.exp(draws), extent[dim] // parts).reshape((-1,) + (1,) * (len(extent) - dim - 1))

    gain = one(*cuts[0])
    for cut in cuts[1:]:
        gain = gain * one(*cut)
    return gain


def noise(key, extent, deviation, reach, pieces=(), kind=jnp.bfloat16):
    values = deviation * jax.random.normal(key, extent, jnp.float32)
    if pieces:
        values = values * block_levels(key, extent, pieces, -0.22, 0.18)
    return jnp.clip(values, -reach, reach).astype(kind)


def setup_inputs(seed: int = 0) -> dict:
    arg_keys = jax.random.split(jax.random.key(seed), 21)
    tokens = noise(arg_keys[0], (MB, NSEGM, SEG, D), 1.0, 6.0, ((1, 16), (2, 2)))
    cotangent = noise(arg_keys[1], (MB, NSEGM, SEG, D), 1.0, 6.0, ((1, 16), (2, 2)))
    placing = draw_placing(jax.random.fold_in(arg_keys[20], 71), 0)
    starts = draw_starts(jax.random.fold_in(arg_keys[20], 71), 0)
    memory_tokens = noise(arg_keys[4], (M, D), 1.0, 6.0, (), jnp.float32)
    norm_one_gain = jnp.clip(1.0 + 0.1 * jax.random.normal(arg_keys[5], (D,), jnp.float32), 0.5, 1.5)
    norm_one_bias = noise(arg_keys[6], (D,), 0.3, 1.8, (), jnp.float32)
    qkv_weight = noise(arg_keys[7], (D, 3 * D), D ** -0.5, 0.21875, ((0, 16),))
    qv_bias = noise(arg_keys[8], (2, D), 0.3, 1.8, (), jnp.float32)
    out_weight = noise(arg_keys[9], (D, D), (max(D // 64, 4)) ** -0.5, 1.75, ((0, 16),))
    out_bias = noise(arg_keys[10], (D,), 0.3, 1.8, (), jnp.float32)
    norm_two_gain = jnp.clip(1.0 + 0.1 * jax.random.normal(arg_keys[11], (D,), jnp.float32), 0.5, 1.5)
    norm_two_bias = noise(arg_keys[12], (D,), 0.3, 1.8, (), jnp.float32)
    expand_weight = noise(arg_keys[13], (D, FF), D ** -0.5, 0.21875, ((0, 16),))
    expand_bias = noise(arg_keys[14], (FF,), 0.3, 1.8, (), jnp.float32)
    contract_weight = noise(arg_keys[15], (D, FF), FF ** -0.5, 0.109375, ((0, 16),))
    contract_bias = noise(arg_keys[16], (D,), 0.3, 1.8, (), jnp.float32)
    read_weight = noise(arg_keys[17], (D, DK), D ** -0.5, 0.21875, ((0, 16),))
    key_weight = noise(arg_keys[18], (D, DK), D ** -0.5, 0.21875, ((0, 16),))
    value_weight = noise(arg_keys[19], (D, D), D ** -0.5, 0.21875, ((0, 16),))
    return {"tokens": tokens, "cotangent": cotangent, "placing": placing, "starts": starts, "memory_tokens": memory_tokens, "norm_one_gain": norm_one_gain, "norm_one_bias": norm_one_bias, "qkv_weight": qkv_weight, "qv_bias": qv_bias, "out_weight": out_weight, "out_bias": out_bias, "norm_two_gain": norm_two_gain, "norm_two_bias": norm_two_bias, "expand_weight": expand_weight, "expand_bias": expand_bias, "contract_weight": contract_weight, "contract_bias": contract_bias, "read_weight": read_weight, "key_weight": key_weight, "value_weight": value_weight}


@jax.custom_vjp
def low(v):
    return lax.optimization_barrier(v.astype(jnp.bfloat16)).astype(jnp.float32)

@jax.custom_vjp
def low_back(v):
    return v

def low_keep(v):
    return (low(v), None)

def low_pass(kept, grad):
    return (grad,)

def back_keep(v):
    return (v, None)

def back_low(kept, grad):
    return (low(grad),)
low.defvjp(low_keep, low_pass)
low_back.defvjp(back_keep, back_low)
norm_eps = 1e-05

def layer_norm(rows_in, gain_vec, bias_vec):
    centred = rows_in - lax.optimization_barrier(jnp.mean(rows_in, axis=-1, keepdims=True))
    spread = lax.optimization_barrier(jnp.mean(centred * centred, axis=-1, keepdims=True))
    return centred * lax.rsqrt(spread + norm_eps) * gain_vec + bias_vec

def feature_map(rows_in):
    halves = jnp.concatenate([jax.nn.softplus(rows_in), jax.nn.softplus(-rows_in)], axis=-1)
    return jnp.concatenate([halves * jnp.roll(halves, amount, axis=-1) for amount in (1, 2, 3)], axis=-1)

def exact_dot(left_side, right_side):
    return jnp.dot(left_side, right_side, precision=lax.Precision.HIGHEST)

def segment(weights, carried, inputs):
    memory_tokens, one_gain, one_bias, qkv_weight, qv_bias, out_weight, out_bias, two_gain, two_bias, expand_weight, expand_bias, contract_weight, contract_bias, read_weight, key_weight, value_weight = weights
    memory_state, normal = carried
    seg_rows, start_flag = inputs
    keep_factor = (start_flag == 0).astype(jnp.float32)
    memory_state = memory_state * keep_factor
    normal = normal * keep_factor
    read_query = feature_map(exact_dot(memory_tokens, read_weight))
    read_numer = exact_dot(read_query, memory_state)
    read_denom = 1.0 + exact_dot(read_query, normal[:, None])[:, 0]
    hidden = jnp.concatenate([memory_tokens + read_numer / read_denom[:, None], seg_rows], axis=0)
    row_total = hidden.shape[0]
    model_width = hidden.shape[1]
    normed_a = low(layer_norm(hidden, one_gain, one_bias))
    qkv_shift = jnp.concatenate([qv_bias[0], jnp.zeros((model_width,), jnp.float32), qv_bias[1]])
    qkv_low = low(low_back(exact_dot(normed_a, qkv_weight) + qkv_shift))
    head_split = qkv_low.reshape(row_total, 3, H, HD)
    scores = low_back(jnp.einsum('qhd,khd->hqk', head_split[:, 0], head_split[:, 1], precision=lax.Precision.HIGHEST)) * HD ** (-0.5)
    place = jnp.arange(row_total, dtype=jnp.int32)
    causal = place[None, :] <= place[:, None]
    raw_weights = jnp.where(causal[None], jnp.exp(scores), 0.0)
    normed_weights = raw_weights / lax.optimization_barrier(jnp.sum(raw_weights, axis=-1, keepdims=True))
    attended = jnp.einsum('hqk,khd->qhd', low(normed_weights), head_split[:, 2], precision=lax.Precision.HIGHEST)
    attended = low(low_back(attended.reshape(row_total, model_width)))
    after_attn = hidden + low_back(exact_dot(attended, out_weight) + out_bias)
    normed_b = low(layer_norm(after_attn, two_gain, two_bias))
    expanded = low_back(exact_dot(normed_b, expand_weight) + expand_bias)
    activation = low(jax.nn.gelu(expanded, approximate=True))
    contracted = lax.dot_general(activation, contract_weight, (((1,), (1,)), ((), ())), precision=lax.Precision.HIGHEST)
    result = after_attn + low_back(contracted + contract_bias)
    mem_out = result[:M]
    key_feat = feature_map(exact_dot(mem_out, key_weight))
    value_new = exact_dot(mem_out, value_weight)
    new_state = memory_state + lax.dot_general(key_feat, value_new, (((0,), (0,)), ((), ())), precision=lax.Precision.HIGHEST)
    new_normal = normal + lax.optimization_barrier(jnp.sum(key_feat, axis=0))
    return ((new_state, new_normal), result[M:])

def reference(tokens, cotangent, placing, starts, memory_tokens, norm_one_gain, norm_one_bias, qkv_weight, qv_bias, out_weight, out_bias, norm_two_gain, norm_two_bias, expand_weight, expand_bias, contract_weight, contract_bias, read_weight, key_weight, value_weight):
    seg_total = MB * NSEGM
    offsets = (jnp.arange(MB, dtype=jnp.int32) * NSEGM)[:, None]
    flat_route = (placing.astype(jnp.int32) + offsets).reshape(seg_total).astype(jnp.int32)
    seq_flags = jnp.take(starts.reshape(seg_total), flat_route)
    inverse = jnp.argsort(flat_route).astype(jnp.int32)
    weights = (memory_tokens.astype(jnp.float32), norm_one_gain.astype(jnp.float32), norm_one_bias.astype(jnp.float32), qkv_weight.astype(jnp.float32), qv_bias.astype(jnp.float32), out_weight.astype(jnp.float32), out_bias.astype(jnp.float32), norm_two_gain.astype(jnp.float32), norm_two_bias.astype(jnp.float32), expand_weight.astype(jnp.float32), expand_bias.astype(jnp.float32), contract_weight.astype(jnp.float32), contract_bias.astype(jnp.float32), read_weight.astype(jnp.float32), key_weight.astype(jnp.float32), value_weight.astype(jnp.float32))
    inputs_all = tokens.astype(jnp.float32).reshape(seg_total, SEG, D)
    checked = jax.checkpoint(segment)

    def forward(values_in, weight_list):

        def step_fn(carried, inputs):
            route_at, flag = inputs
            seg_rows = lax.dynamic_index_in_dim(values_in, route_at, 0, keepdims=False)
            return checked(weight_list, carried, (seg_rows, flag))
        initial = (jnp.zeros((DPHI, D), jnp.float32), jnp.zeros((DPHI,), jnp.float32))
        final_state, results = lax.scan(step_fn, initial, (flat_route, seq_flags))
        return jnp.take(results, inverse, axis=0)
    outputs, pull = jax.vjp(forward, inputs_all, weights)
    grad_inputs, grad_weights = pull(cotangent.astype(jnp.float32).reshape(seg_total, SEG, D))
    return (outputs.reshape(MB, NSEGM, SEG, D).astype(jnp.bfloat16), grad_inputs.reshape(MB, NSEGM, SEG, D).astype(jnp.bfloat16), grad_weights[0], grad_weights[1], grad_weights[2], grad_weights[3], grad_weights[4], grad_weights[5], grad_weights[6], grad_weights[7], grad_weights[8], grad_weights[9], grad_weights[10], grad_weights[11], grad_weights[12], grad_weights[13], grad_weights[14], grad_weights[15])
```

```python
import functools

import jax
import jax.numpy as jnp
from jax import lax
from jax.experimental import pallas as pl
from jax.experimental.pallas import tpu as pltpu
from jax.sharding import PartitionSpec as P

H = 12
HD = 64
EPS = 1e-05
CHUNK = 256
F32 = jnp.float32
BF16 = jnp.bfloat16


def norm_parts(rows):
    centred = rows - jnp.mean(rows, axis=-1, keepdims=True)
    spread = jnp.mean(centred * centred, axis=-1, keepdims=True)
    rstd = lax.rsqrt(spread + EPS)
    return centred * rstd, rstd


def norm_back(grad, unit, rstd, gain):
    scaled = grad * gain
    first = jnp.mean(scaled, axis=-1, keepdims=True)
    second = jnp.mean(scaled * unit, axis=-1, keepdims=True)
    grad_rows = rstd * (scaled - first - unit * second)
    return grad_rows, jnp.sum(grad * unit, axis=0), jnp.sum(grad, axis=0)


def feature_map(rows):
    halves = jnp.concatenate([jax.nn.softplus(rows), jax.nn.softplus(-rows)], axis=-1)
    return jnp.concatenate([halves * jnp.roll(halves, j, axis=-1) for j in (1, 2, 3)], axis=-1)


def gelu_tanh(rows):
    return jax.nn.gelu(rows, approximate=True)


def dot_dims(a, b, ca, cb, precision=None):
    return lax.dot_general(
        a, b, (((ca,), (cb,)), ((), ())), precision=precision, preferred_element_type=F32
    )


exact = functools.partial(dot_dims, precision=lax.Precision.HIGHEST)


def head_rows(scale):
    lane = lax.broadcasted_iota(jnp.int32, (1, 2 * HD), 1)
    low = jnp.where(lane < HD, scale, 0.0).astype(BF16)
    high = jnp.where(lane < HD, 0.0, scale).astype(BF16)
    return low, high


def causal_tail(scores, first):
    key = lax.broadcasted_iota(jnp.int32, scores.shape, 0)
    query = lax.broadcasted_iota(jnp.int32, scores.shape, 1)
    return jnp.where(key - first <= query, scores, 0.0)


def attn_fwd_kernel(q_ref, k_ref, v_ref, km_ref, vm_ref, o_ref, lse_ref, keys, vals_t, vmem_t):
    mem = km_ref.shape[1]
    rows = q_ref.shape[0]
    keys[0:mem, :] = km_ref[0]
    keys[mem:, :] = k_ref[...]
    vals_t[...] = v_ref[...].T
    vmem_t[...] = vm_ref[0].T
    picks = head_rows(HD**-0.5)
    for part in range(rows // CHUNK):
        lo, hi = part * CHUNK, (part + 1) * CHUNK
        query = q_ref[lo:hi, :]
        outs = []
        for head in range(2):
            band = slice(head * HD, (head + 1) * HD)
            scores = dot_dims(keys[0 : mem + hi, :], query * picks[head], 1, 1)
            raw = jnp.exp(scores)
            tail = causal_tail(raw[mem + lo :], 0)
            if lo:
                raw = jnp.concatenate([raw[: mem + lo], tail], axis=0)
            else:
                raw = jnp.concatenate([raw[:mem], tail], axis=0)
            total = jnp.sum(raw, axis=0, keepdims=True)
            lse_ref[0, 0, head : head + 1, lo:hi] = jnp.log(total)
            weights = (raw * (1.0 / total)).astype(BF16)
            outs.append(
                dot_dims(vals_t[band, 0:hi], weights[mem:], 1, 0)
                + dot_dims(vmem_t[band, :], weights[:mem], 1, 0)
            )
        o_ref[lo:hi, :] = jnp.concatenate(outs, axis=0).T.astype(BF16)


def attn_fwd(qkv, kv_mem, segs):
    rows, width = qkv.shape[0] // segs, qkv.shape[1] // 3
    mem = kv_mem.shape[1]
    pairs = H // 2
    wide = 2 * HD
    spec = lambda off: pl.BlockSpec((rows, wide), lambda s, p, off=off: (s, off * pairs + p))
    mspec = lambda off: pl.BlockSpec((1, mem, wide), lambda s, p, off=off: (s, 0, off * pairs + p))
    return pl.pallas_call(
        attn_fwd_kernel,
        grid=(segs, pairs),
        in_specs=[spec(0), spec(1), spec(2), mspec(0), mspec(1)],
        out_specs=[
            pl.BlockSpec((rows, wide), lambda s, p: (s, p)),
            pl.BlockSpec((1, 1, 2, rows), lambda s, p: (s, p, 0, 0)),
        ],
        out_shape=[
            jax.ShapeDtypeStruct((segs * rows, width), BF16),
            jax.ShapeDtypeStruct((segs, pairs, 2, rows), F32),
        ],
        scratch_shapes=[
            pltpu.VMEM((mem + rows, wide), BF16),
            pltpu.VMEM((wide, rows), BF16),
            pltpu.VMEM((wide, mem), BF16),
        ],
        compiler_params=pltpu.CompilerParams(vmem_limit_bytes=40 * 2**20),
        cost_estimate=pl.CostEstimate(
            flops=segs * H * rows * rows * 512,
            bytes_accessed=segs * rows * width * 8,
            transcendentals=segs * H * rows * rows // 2,
        ),
        name="attn_fwd",
    )(qkv, qkv, qkv, kv_mem, kv_mem)


def attn_bwd_kernel(
    q_ref, k_ref, v_ref, km_ref, vm_ref, o_ref, g_ref, lse_ref,
    out_ref, dkm_ref, dvm_ref,
    keys, vals, keys_t, kmem_t, dq, dk, dv,
):
    phase = pl.program_id(2)
    mem = km_ref.shape[1]
    rows = q_ref.shape[0]

    @pl.when(phase == 0)
    def _():
        keys[0:mem, :] = km_ref[0]
        keys[mem:, :] = k_ref[...]
        vals[0:mem, :] = vm_ref[0]
        vals[mem:, :] = v_ref[...]
        keys_t[...] = k_ref[...].T
        kmem_t[...] = km_ref[0].T
        dk[...] = jnp.zeros_like(dk)
        dv[...] = jnp.zeros_like(dv)
        scaled_picks = head_rows(HD**-0.5)
        picks = head_rows(1.0)
        for part in range(rows // CHUNK):
            lo, hi = part * CHUNK, (part + 1) * CHUNK
            end = mem + hi
            query = q_ref[lo:hi, :]
            grad = g_ref[lo:hi, :]
            inner = (grad.astype(F32) * o_ref[lo:hi, :].astype(F32)).T
            dqs = []
            for head in range(2):
                band = slice(head * HD, (head + 1) * HD)
                query_h = query * scaled_picks[head]
                grad_h = grad * picks[head]
                log_total = lse_ref[0, 0, head : head + 1, lo:hi]
                centre = jnp.sum(inner[band], axis=0, keepdims=True)
                prob = jnp.exp(dot_dims(keys[0:end, :], query_h, 1, 1) - log_total)
                prob = jnp.concatenate(
                    [prob[: mem + lo], causal_tail(prob[mem + lo :], 0)], axis=0
                )
                grad_p = dot_dims(vals[0:end, :], grad_h, 1, 1)
                grad_s = (prob * (grad_p - centre)).astype(BF16)
                dv[0:end, :] += dot_dims(prob.astype(BF16), grad_h, 1, 0)
                dk[0:end, :] += dot_dims(grad_s, query_h, 1, 0)
                dqs.append(
                    dot_dims(keys_t[band, 0:hi], grad_s[mem:], 1, 0)
                    + dot_dims(kmem_t[band, :], grad_s[:mem], 1, 0)
                )
            dq[lo:hi, :] = (jnp.concatenate(dqs, axis=0) * HD**-0.5).T.astype(BF16)
        out_ref[...] = dq[...]
        dkm_ref[0] = dk[0:mem, :]
        dvm_ref[0] = dv[0:mem, :]

    @pl.when(phase == 1)
    def _():
        out_ref[...] = dk[mem:, :].astype(BF16)

    @pl.when(phase == 2)
    def _():
        out_ref[...] = dv[mem:, :].astype(BF16)


def attn_bwd(qkv, kv_mem, attended, grad, lse, segs):
    rows, width = qkv.shape[0] // segs, qkv.shape[1] // 3
    mem = kv_mem.shape[1]
    pairs = H // 2
    wide = 2 * HD
    spec = lambda off: pl.BlockSpec((rows, wide), lambda s, p, f, off=off: (s, off * pairs + p))
    mspec = lambda off: pl.BlockSpec(
        (1, mem, wide), lambda s, p, f, off=off: (s, 0, off * pairs + p)
    )
    return pl.pallas_call(
        attn_bwd_kernel,
        grid=(segs, pairs, 3),
        in_specs=[
            spec(0), spec(1), spec(2), mspec(0), mspec(1), spec(0), spec(0),
            pl.BlockSpec((1, 1, 2, rows), lambda s, p, f: (s, p, 0, 0)),
        ],
        out_specs=[
            pl.BlockSpec((rows, wide), lambda s, p, f: (s, f * pairs + p)),
            mspec(0),
            mspec(0),
        ],
        out_shape=[
            jax.ShapeDtypeStruct(qkv.shape, BF16),
            jax.ShapeDtypeStruct((segs, mem, width), F32),
            jax.ShapeDtypeStruct((segs, mem, width), F32),
        ],
        scratch_shapes=[
            pltpu.VMEM((mem + rows, wide), BF16),
            pltpu.VMEM((mem + rows, wide), BF16),
            pltpu.VMEM((wide, rows), BF16),
            pltpu.VMEM((wide, mem), BF16),
            pltpu.VMEM((rows, wide), BF16),
            pltpu.VMEM((mem + rows, wide), F32),
            pltpu.VMEM((mem + rows, wide), F32),
        ],
        compiler_params=pltpu.CompilerParams(vmem_limit_bytes=48 * 2**20),
        cost_estimate=pl.CostEstimate(
            flops=segs * H * rows * rows * 1280,
            bytes_accessed=segs * rows * width * 18,
            transcendentals=segs * H * rows * rows // 2,
        ),
        name="attn_bwd",
    )(qkv, qkv, qkv, kv_mem, kv_mem, attended, grad, lse)


def assemble_kernel(widths, *refs):
    piece_refs = refs[:4]
    out_refs = refs[4 : 4 + len(widths)]
    sem = refs[-1]
    index = lax.axis_index("dp")
    deep, _, _ = index // 4, (index // 2) % 2, index % 2
    cross = (index // 2) % 2
    core = index % 2
    shard = piece_refs[0].shape[1]
    copies = []
    for which in range(4):
        flip_x, flip_c = which % 2, which // 2
        for dz in range(4):
            slot = ((deep ^ dz) * 2 + (cross ^ flip_x)) * 2 + (core ^ flip_c)
            start = 0
            for k, width in enumerate(widths):
                copies.append(
                    pltpu.make_async_copy(
                        piece_refs[which].at[dz, :, pl.ds(start, width)],
                        out_refs[k].at[pl.ds(pl.multiple_of(slot * shard, 16), shard), :],
                        sem.at[len(copies)],
                    )
                )
                start += width
    for copy in copies:
        copy.start()
    for copy in copies:
        copy.wait()


def dp_pairs(flip):
    return [(i, i ^ flip) for i in range(16)]


def gather_group(shards):
    widths = tuple(s.shape[1] for s in shards)
    mine = shards[0] if len(shards) == 1 else jnp.concatenate(shards, axis=1)
    deep = jnp.stack([mine] + [lax.ppermute(mine, "dp", dp_pairs(4 * k)) for k in (1, 2, 3)])
    cross = lax.ppermute(deep, "dp", dp_pairs(2))
    pieces = [deep, cross, lax.ppermute(deep, "dp", dp_pairs(1)), lax.ppermute(cross, "dp", dp_pairs(1))]
    rows = mine.shape[0] * 16
    return pl.pallas_call(
        functools.partial(assemble_kernel, widths),
        in_specs=[pl.BlockSpec(memory_space=pl.ANY)] * 4,
        out_specs=[pl.BlockSpec(memory_space=pl.ANY)] * len(widths),
        out_shape=[jax.ShapeDtypeStruct((rows, w), BF16) for w in widths],
        scratch_shapes=[pltpu.SemaphoreType.DMA((16 * len(widths),))],
        compiler_params=pltpu.CompilerParams(vmem_limit_bytes=4 * 2**20),
        cost_estimate=pl.CostEstimate(
            flops=0, bytes_accessed=4 * rows * sum(widths), transcendentals=0
        ),
        name="assemble",
    )(*pieces)


def pick(parts, at, axis):
    return lax.dynamic_index_in_dim(parts, at, axis, keepdims=False)


def add_low(a, b):
    return (a.astype(F32) + b.astype(F32)).astype(BF16)


def scatter_group(grad):
    index = lax.axis_index("dp")
    deep, cross, core = index // 4, (index // 2) % 2, index % 2
    shard = grad.shape[0] // 16
    parts = grad.reshape(4, 2, 2, shard, grad.shape[1])
    got = lax.ppermute(pick(parts, 1 - core, 2), "dp", dp_pairs(1))
    parts = add_low(pick(parts, core, 2), got)
    got = lax.ppermute(pick(parts, 1 - cross, 1), "dp", dp_pairs(2))
    parts = add_low(pick(parts, cross, 1), got)
    total = pick(parts, deep, 0).astype(F32)
    for k in (1, 2, 3):
        total = total + lax.ppermute(pick(parts, deep ^ k, 0), "dp", dp_pairs(4 * k)).astype(F32)
    low = total.astype(BF16)
    return low.astype(F32) + lax.ppermute(low, "ctx", [(0, 1), (1, 0)]).astype(F32)


def sum_everywhere(flat):
    flat = flat + lax.ppermute(flat, "dp", dp_pairs(1))
    flat = flat + lax.ppermute(flat, "dp", dp_pairs(2))
    far = [lax.ppermute(flat, "dp", dp_pairs(4 * k)) for k in (1, 2, 3)]
    flat = (flat + far[0]) + (far[1] + far[2])
    return flat + lax.ppermute(flat, "ctx", [(0, 1), (1, 0)])


def split_heads(rows):
    return rows.reshape(rows.shape[0], rows.shape[1], H, HD)


def plain_scores(query, key, allowed):
    scores = jnp.einsum("sqhd,skhd->shqk", query, key, preferred_element_type=F32) * HD**-0.5
    return scores, allowed[None, None]


def plain_fwd(qkv, kv_all, allowed):
    width = qkv.shape[2] // 3
    query = split_heads(qkv[:, :, :width])
    key, value = split_heads(kv_all[:, :, :width]), split_heads(kv_all[:, :, width:])
    scores, allowed = plain_scores(query, key, allowed)
    raw = jnp.where(allowed, jnp.exp(scores), 0.0)
    total = jnp.sum(raw, axis=-1)
    weights = (raw / total[..., None]).astype(BF16)
    mixed = jnp.einsum("shqk,skhd->sqhd", weights, value, preferred_element_type=F32)
    return mixed.reshape(qkv.shape[0], -1, width).astype(BF16), jnp.log(total)


def plain_bwd(qkv, kv_all, allowed, log_total, grad):
    segs, width = qkv.shape[0], qkv.shape[2] // 3
    query = split_heads(qkv[:, :, :width])
    key, value = split_heads(kv_all[:, :, :width]), split_heads(kv_all[:, :, width:])
    grad = split_heads(grad)
    scores, allowed = plain_scores(query, key, allowed)
    prob = jnp.where(allowed, jnp.exp(scores - log_total[..., None]), 0.0)
    grad_p = jnp.einsum("sqhd,skhd->shqk", grad, value, preferred_element_type=F32)
    inner = jnp.sum(prob * grad_p, axis=-1, keepdims=True)
    grad_s = (prob * (grad_p - inner) * HD**-0.5).astype(BF16)
    dq = jnp.einsum("shqk,skhd->sqhd", grad_s, key, preferred_element_type=F32)
    dk = jnp.einsum("shqk,sqhd->skhd", grad_s, query, preferred_element_type=F32)
    dv = jnp.einsum("shqk,sqhd->skhd", prob.astype(BF16), grad, preferred_element_type=F32)
    flat = lambda a: a.reshape(segs, -1, width)
    return flat(dq), jnp.concatenate([flat(dk), flat(dv)], axis=2)


def memory_forward(mt, p):
    mem = mt.shape[0]
    keep = {}
    width = mt.shape[1]
    unit, rstd = norm_parts(mt)
    normed = (unit * p["one_gain"] + p["one_bias"]).astype(BF16)
    qkv = (dot_dims(normed, p["qkv"], 1, 0) + p["shift"]).astype(BF16)
    at = jnp.arange(mem, dtype=jnp.int32)
    allowed = at[None, :] <= at[:, None]
    attended, log_total = plain_fwd(qkv[None], qkv[None, :, width:], allowed)
    attended = attended[0]
    after = mt + dot_dims(attended, p["out"], 1, 0) + p["out_bias"]
    unit_b, rstd_b = norm_parts(after)
    normed_b = (unit_b * p["two_gain"] + p["two_bias"]).astype(BF16)
    expanded = dot_dims(normed_b, p["expand"], 1, 0) + p["expand_bias"]
    activ = gelu_tanh(expanded).astype(BF16)
    result = after + dot_dims(activ, p["contract"], 1, 1) + p["contract_bias"]
    key_pre = exact(result, p["key"].astype(F32), 1, 0)
    value_new = exact(result, p["value"].astype(F32), 1, 0)
    read_pre = exact(mt, p["read"].astype(F32), 1, 0)
    key_feat, key_pull = jax.vjp(feature_map, key_pre)
    read_feat, read_pull = jax.vjp(feature_map, read_pre)
    mix = exact(read_feat, key_feat, 1, 1)
    numer = exact(mix, value_new, 1, 0)
    denom = 1.0 + jnp.sum(mix, axis=1, keepdims=True)
    follow = mt + numer / denom
    unit_f, rstd_f = norm_parts(follow)
    normed_f = (unit_f * p["one_gain"] + p["one_bias"]).astype(BF16)
    kv_follow = (dot_dims(normed_f, p["qkv"][:, width:], 1, 0) + p["shift"][width:]).astype(BF16)
    keep = dict(
        unit=unit, rstd=rstd, normed=normed, qkv=qkv, allowed=allowed, attended=attended,
        log_total=log_total, unit_b=unit_b, rstd_b=rstd_b, normed_b=normed_b, expanded=expanded,
        activ=activ, result=result, key_feat=key_feat, read_feat=read_feat, key_pull=key_pull,
        read_pull=read_pull, value_new=value_new, mix=mix, numer=numer, denom=denom, unit_f=unit_f,
        rstd_f=rstd_f, normed_f=normed_f,
    )
    return qkv[:, width:], kv_follow, keep


def memory_backward(mt, p, m, grad_kv_first, grad_kv_follow, mine):
    width = mt.shape[1]
    low = lambda a: a.astype(BF16)
    grad_f = low(grad_kv_follow)
    grad_follow, gain_f, bias_f = norm_back(
        dot_dims(grad_f, p["qkv"][:, width:], 1, 1), m["unit_f"], m["rstd_f"], p["one_gain"]
    )
    grad_mt = grad_follow
    grad_numer = grad_follow / m["denom"]
    grad_denom = -jnp.sum(grad_follow * m["numer"], axis=1, keepdims=True) / (m["denom"] * m["denom"])
    grad_mix = exact(grad_numer, m["value_new"], 1, 1) + grad_denom
    grad_value = exact(m["mix"], grad_numer, 0, 0)
    [grad_read_pre] = m["read_pull"](exact(grad_mix, m["key_feat"], 1, 0))
    [grad_key_pre] = m["key_pull"](exact(grad_mix, m["read_feat"], 0, 0))
    grad_mt = grad_mt + exact(grad_read_pre, p["read"].astype(F32), 1, 1)
    grad_result = exact(grad_key_pre, p["key"].astype(F32), 1, 1) + exact(
        grad_value, p["value"].astype(F32), 1, 1
    )
    grad_contract = low(grad_result)
    _, gelu_pull = jax.vjp(gelu_tanh, m["expanded"])
    grad_expanded = low(gelu_pull(dot_dims(grad_contract, p["contract"], 1, 0))[0])
    grad_after, two_gain, two_bias = norm_back(
        dot_dims(grad_expanded, p["expand"], 1, 1), m["unit_b"], m["rstd_b"], p["two_gain"]
    )
    grad_after = grad_after + grad_result
    grad_attn_out = low(grad_after)
    grad_attended = low(dot_dims(grad_attn_out, p["out"], 1, 1))
    dq, dkv = plain_bwd(
        m["qkv"][None], m["qkv"][None, :, width:], m["allowed"], m["log_total"], grad_attended[None]
    )
    grad_qkv = low(jnp.concatenate([dq[0], dkv[0] + grad_kv_first], axis=1))
    grad_first, gain_a, bias_a = norm_back(
        dot_dims(grad_qkv, p["qkv"], 1, 1), m["unit"], m["rstd"], p["one_gain"]
    )
    grad_mt = grad_mt + grad_first + grad_after
    wide = grad_qkv.astype(F32)
    kv_rows = grad_f.astype(F32)
    sums = jnp.sum(wide, axis=0)
    follow_sums = jnp.sum(kv_rows, axis=0)
    matrices = (
        dot_dims(mine(m["normed"]), grad_qkv, 0, 0)
        + jnp.concatenate(
            [
                jnp.zeros((mine(mt).shape[1], width), F32),
                dot_dims(mine(m["normed_f"]), grad_f, 0, 0),
            ],
            axis=1,
        ),
        dot_dims(mine(m["attended"]), grad_attn_out, 0, 0),
        dot_dims(mine(m["normed_b"]), grad_expanded, 0, 0),
        dot_dims(mine(grad_contract), m["activ"], 0, 0),
        exact(mine(mt), grad_read_pre, 0, 0),
        exact(mine(m["result"]), grad_key_pre, 0, 0),
        exact(mine(m["result"]), grad_value, 0, 0),
    )
    column_sum = lambda a: jnp.sum(a.astype(F32), axis=0)
    vectors = (
        gain_f + gain_a,
        bias_f + bias_a,
        jnp.stack([sums[:width], sums[2 * width :] + follow_sums[width:]]),
        column_sum(grad_attn_out),
        two_gain,
        two_bias,
        column_sum(grad_expanded),
        column_sum(grad_contract),
    )
    return grad_mt, matrices, vectors


def local(
    tokens,
    cotangent,
    placing,
    starts,
    memory_tokens,
    norm_one_gain,
    norm_one_bias,
    qkv_weight,
    qv_bias,
    out_weight,
    out_bias,
    norm_two_gain,
    norm_two_bias,
    expand_weight,
    expand_bias,
    contract_weight,
    contract_bias,
    read_weight,
    key_weight,
    value_weight,
):
    del placing
    groups, ranks = lax.axis_size("dp"), lax.axis_size("ctx")
    group, rank = lax.axis_index("dp"), lax.axis_index("ctx")
    micros, segs_local, tok_rows, width = tokens.shape
    mem = memory_tokens.shape[0]
    shard = qkv_weight.shape[0]
    quick = groups == 16 and ranks == 2 and micros == 2 and (tok_rows * ranks) % CHUNK == 0
    names = ("qkv", "out", "expand", "contract", "read", "key", "value")
    shards = (qkv_weight, out_weight, expand_weight, contract_weight, read_weight, key_weight, value_weight)
    if quick:
        whole = (
            *gather_group(shards[:1]),
            *gather_group(shards[1:3]),
            *gather_group(shards[3:]),
        )
    else:
        whole = tuple(lax.all_gather(s, "dp", axis=0, tiled=True) for s in shards)
    p = dict(zip(names, whole))
    p.update(
        one_gain=norm_one_gain, one_bias=norm_one_bias, out_bias=out_bias, two_gain=norm_two_gain,
        two_bias=norm_two_bias, expand_bias=expand_bias, contract_bias=contract_bias,
        shift=jnp.concatenate([qv_bias[0], jnp.zeros((width,), F32), qv_bias[1]]),
    )
    flags = lax.dynamic_slice_in_dim(starts, group * segs_local, segs_local, 1)

    swap = [(0, 1), (1, 0)]

    def to_segments(held):
        keep, give = pick(held, rank, 0), pick(held, 1 - rank, 0)
        got = lax.ppermute(give, "ctx", swap)
        first = jnp.where(rank == 0, keep, got)
        last = jnp.where(rank == 0, got, keep)
        return jnp.concatenate([first, last], axis=1).reshape(-1, width)

    def from_segments(rows):
        rows = rows.reshape(segs_local, ranks, tok_rows, width)
        keep, give = pick(rows, rank, 1), pick(rows, 1 - rank, 1)
        got = lax.ppermute(give, "ctx", swap)
        return jnp.stack([jnp.where(rank == 0, keep, got), jnp.where(rank == 0, got, keep)])

    if quick:
        rows_in, rows_grad = to_segments(tokens), to_segments(cotangent)
        flags = pick(flags, rank, 0)
        segs = segs_local
    else:
        rows_in, rows_grad = tokens.reshape(-1, width), cotangent.reshape(-1, width)
        flags = flags.reshape(-1)
        segs = micros * segs_local
    seg_rows = rows_in.shape[0] // segs

    kv_first, kv_follow, m = memory_forward(memory_tokens, p)
    kv_mem = jnp.where((flags == 0)[:, None, None], kv_follow[None], kv_first[None])
    hidden = rows_in.astype(F32)
    unit_a, rstd_a = norm_parts(hidden)
    normed_a = (unit_a * norm_one_gain + norm_one_bias).astype(BF16)
    qkv = (dot_dims(normed_a, p["qkv"], 1, 0) + p["shift"]).astype(BF16)
    if quick:
        attended, lse = attn_fwd(qkv, kv_mem, segs)
    else:
        seg_qkv = qkv.reshape(segs, seg_rows, 3 * width)
        kv_all = lax.all_gather(seg_qkv[:, :, width:], "ctx", axis=1, tiled=True)
        kv_all = jnp.concatenate([kv_mem, kv_all], axis=1)
        query_at = mem + rank * seg_rows + jnp.arange(seg_rows, dtype=jnp.int32)
        key_at = jnp.arange(mem + ranks * seg_rows, dtype=jnp.int32)
        allowed = key_at[None, :] <= query_at[:, None]
        attended, lse = plain_fwd(seg_qkv, kv_all, allowed)
        attended = attended.reshape(-1, width)
    after = hidden + dot_dims(attended, p["out"], 1, 0) + out_bias
    unit_b, rstd_b = norm_parts(after)
    normed_b = (unit_b * norm_two_gain + norm_two_bias).astype(BF16)
    expanded = (dot_dims(normed_b, p["expand"], 1, 0) + expand_bias).astype(BF16)
    activ = gelu_tanh(expanded.astype(F32)).astype(BF16)
    result = (after + dot_dims(activ, p["contract"], 1, 1) + contract_bias).astype(BF16)

    grad_activ = dot_dims(rows_grad, p["contract"], 1, 0)
    _, gelu_pull = jax.vjp(gelu_tanh, expanded.astype(F32))
    grad_expanded = gelu_pull(grad_activ)[0].astype(BF16)
    unit_b, rstd_b = norm_parts(after)
    grad_after, two_gain, two_bias = norm_back(
        dot_dims(grad_expanded, p["expand"], 1, 1), unit_b, rstd_b, norm_two_gain
    )
    grad_after = grad_after + rows_grad.astype(F32)
    grad_attn_out = grad_after.astype(BF16)
    grad_attended = dot_dims(grad_attn_out, p["out"], 1, 1).astype(BF16)
    if quick:
        grad_qkv, dk_mem, dv_mem = attn_bwd(qkv, kv_mem, attended, grad_attended, lse, segs)
        dkv_mem = jnp.concatenate([dk_mem, dv_mem], axis=2)
    else:
        dq, dkv = plain_bwd(
            seg_qkv, kv_all, allowed, lse, grad_attended.reshape(segs, seg_rows, width)
        )
        dkv_mem = dkv[:, :mem]
        dkv = lax.psum_scatter(
            dkv[:, mem:].astype(BF16), "ctx", scatter_dimension=1, tiled=True
        )
        grad_qkv = jnp.concatenate([dq.astype(BF16), dkv], axis=2).reshape(-1, 3 * width)
    follows = (flags == 0).astype(F32)[:, None, None]
    pooled = jnp.stack([jnp.sum(dkv_mem * (1.0 - follows), axis=0), jnp.sum(dkv_mem * follows, axis=0)])
    unit_a, rstd_a = norm_parts(hidden)
    grad_hidden, one_gain, one_bias = norm_back(
        dot_dims(grad_qkv, p["qkv"], 1, 1), unit_a, rstd_a, norm_one_gain
    )
    grad_rows = (grad_hidden + grad_after).astype(BF16)

    terms = (
        dot_dims(normed_a, grad_qkv, 0, 0).astype(BF16),
        dot_dims(attended, grad_attn_out, 0, 0).astype(BF16),
        dot_dims(normed_b, grad_expanded, 0, 0).astype(BF16),
        dot_dims(rows_grad, activ, 0, 0).astype(BF16),
    )
    column_sum = lambda a: jnp.sum(a.astype(F32), axis=0)
    qkv_sums = column_sum(grad_qkv)
    vectors = (
        one_gain,
        one_bias,
        jnp.stack([qkv_sums[:width], qkv_sums[2 * width :]]),
        column_sum(grad_attn_out),
        two_gain,
        two_bias,
        column_sum(grad_expanded),
        column_sum(rows_grad),
    )
    if quick:
        summed = tuple(scatter_group(t) for t in terms)
        pooled = sum_everywhere(pooled)
        lengths = [v.size for v in vectors]
        flat = sum_everywhere(jnp.concatenate([v.reshape(-1) for v in vectors]).reshape(-1, 128))
        flat = flat.reshape(-1)
        split, at = [], 0
        for v in vectors:
            split.append(flat[at : at + v.size].reshape(v.shape))
            at += v.size
        vectors = tuple(split)
        del lengths
    else:
        summed = tuple(
            lax.psum(
                lax.psum_scatter(t, "dp", scatter_dimension=0, tiled=True).astype(F32), "ctx"
            )
            for t in terms
        )
        pooled, vectors = lax.psum((pooled, vectors), ("dp", "ctx"))

    mine = lambda a: lax.dynamic_slice_in_dim(a, group * shard, shard, 1)
    grad_mt, mem_matrices, mem_vectors = memory_backward(
        memory_tokens, p, m, pooled[0], pooled[1], mine
    )
    matrices = tuple(a + b for a, b in zip(summed, mem_matrices)) + mem_matrices[4:]
    vectors = tuple(a + b for a, b in zip(vectors, mem_vectors))
    if quick:
        block_out, token_grad = from_segments(result), from_segments(grad_rows)
    else:
        block_out, token_grad = result.reshape(tokens.shape), grad_rows.reshape(tokens.shape)
    return (
        block_out,
        token_grad,
        grad_mt,
        vectors[0],
        vectors[1],
        matrices[0],
        vectors[2],
        matrices[1],
        vectors[3],
        vectors[4],
        vectors[5],
        matrices[2],
        vectors[6],
        matrices[3],
        vectors[7],
        matrices[4],
        matrices[5],
        matrices[6],
    )


def solution(mesh):
    rows = P(None, "dp", "ctx", None)
    matrix = P("dp", None)
    full = P()
    return jax.shard_map(
        local,
        mesh=mesh,
        in_specs=(
            rows, rows, full, full, full, full, full, matrix, full, matrix, full, full, full,
            matrix, full, matrix, full, matrix, matrix, matrix,
        ),
        out_specs=(
            rows, rows, full, full, full, matrix, full, matrix, full, full, full, matrix, full,
            matrix, full, matrix, matrix, matrix,
        ),
        check_vma=False,
    )
```

```python
import functools

import jax
import jax.numpy as jnp
from jax import lax
from jax.experimental import pallas as pl
from jax.experimental.pallas import tpu as pltpu
from jax.sharding import PartitionSpec as P

H = 12
HD = 64
EPS = 1e-05
CHUNK = 256
F32 = jnp.float32
BF16 = jnp.bfloat16


def norm_parts(rows):
    centred = rows - jnp.mean(rows, axis=-1, keepdims=True)
    spread = jnp.mean(centred * centred, axis=-1, keepdims=True)
    rstd = lax.rsqrt(spread + EPS)
    return centred * rstd, rstd


def norm_back(grad, unit, rstd, gain):
    scaled = grad * gain
    first = jnp.mean(scaled, axis=-1, keepdims=True)
    second = jnp.mean(scaled * unit, axis=-1, keepdims=True)
    grad_rows = rstd * (scaled - first - unit * second)
    return grad_rows, jnp.sum(grad * unit, axis=0), jnp.sum(grad, axis=0)


def feature_map(rows):
    halves = jnp.concatenate([jax.nn.softplus(rows), jax.nn.softplus(-rows)], axis=-1)
    return jnp.concatenate([halves * jnp.roll(halves, j, axis=-1) for j in (1, 2, 3)], axis=-1)


def gelu_tanh(rows):
    return jax.nn.gelu(rows, approximate=True)


def dot_dims(a, b, ca, cb, precision=None):
    return lax.dot_general(
        a, b, (((ca,), (cb,)), ((), ())), precision=precision, preferred_element_type=F32
    )


exact = functools.partial(dot_dims, precision=lax.Precision.HIGHEST)


def head_rows(scale):
    lane = lax.broadcasted_iota(jnp.int32, (1, 2 * HD), 1)
    low = jnp.where(lane < HD, scale, 0.0).astype(BF16)
    high = jnp.where(lane < HD, 0.0, scale).astype(BF16)
    return low, high


def causal_tail(scores, first):
    key = lax.broadcasted_iota(jnp.int32, scores.shape, 0)
    query = lax.broadcasted_iota(jnp.int32, scores.shape, 1)
    return jnp.where(key - first <= query, scores, 0.0)


def attn_fwd_kernel(q_ref, k_ref, v_ref, km_ref, vm_ref, o_ref, lse_ref, keys, vals_t, vmem_t):
    mem = km_ref.shape[0]
    rows = q_ref.shape[0]
    keys[0:mem, :] = km_ref[...]
    keys[mem:, :] = k_ref[...]
    vals_t[...] = v_ref[...].T
    vmem_t[...] = vm_ref[...].T
    picks = head_rows(HD**-0.5)
    for part in range(rows // CHUNK):
        lo, hi = part * CHUNK, (part + 1) * CHUNK
        query = q_ref[lo:hi, :]
        outs = []
        for head in range(2):
            band = slice(head * HD, (head + 1) * HD)
            scores = dot_dims(keys[0 : mem + hi, :], query * picks[head], 1, 1)
            raw = jnp.exp(scores)
            tail = causal_tail(raw[mem + lo :], 0)
            if lo:
                raw = jnp.concatenate([raw[: mem + lo], tail], axis=0)
            else:
                raw = jnp.concatenate([raw[:mem], tail], axis=0)
            total = jnp.sum(raw, axis=0, keepdims=True)
            lse_ref[0, head : head + 1, lo:hi] = jnp.log(total)
            weights = (raw * (1.0 / total)).astype(BF16)
            outs.append(
                dot_dims(vals_t[band, 0:hi], weights[mem:], 1, 0)
                + dot_dims(vmem_t[band, :], weights[:mem], 1, 0)
            )
        o_ref[lo:hi, :] = jnp.concatenate(outs, axis=0).T.astype(BF16)


def attn_fwd_after_kernel(q_ref, k_ref, v_ref, km_ref, vm_ref, held_ref, *rest):
    del held_ref
    attn_fwd_kernel(q_ref, k_ref, v_ref, km_ref, vm_ref, *rest)


def attn_fwd(qkv, kv_mem, seg, rows, held):
    width = qkv.shape[1] // 3
    mem = kv_mem.shape[0]
    pairs = H // 2
    wide = 2 * HD
    spec = lambda off: pl.BlockSpec((rows, wide), lambda p, off=off: (seg, off * pairs + p))
    mspec = lambda off: pl.BlockSpec((mem, wide), lambda p, off=off: (0, off * pairs + p))
    more = [] if held is None else [held]
    return pl.pallas_call(
        attn_fwd_kernel if held is None else attn_fwd_after_kernel,
        grid=(pairs,),
        in_specs=[spec(0), spec(1), spec(2), mspec(0), mspec(1)]
        + [pl.BlockSpec(memory_space=pl.ANY)] * len(more),
        out_specs=[
            pl.BlockSpec((rows, wide), lambda p: (seg, p)),
            pl.BlockSpec((1, 2, rows), lambda p: (p, 0, 0)),
        ],
        out_shape=[
            jax.ShapeDtypeStruct((qkv.shape[0], width), BF16),
            jax.ShapeDtypeStruct((pairs, 2, rows), F32),
        ],
        scratch_shapes=[
            pltpu.VMEM((mem + rows, wide), BF16),
            pltpu.VMEM((wide, rows), BF16),
            pltpu.VMEM((wide, mem), BF16),
        ],
        input_output_aliases={5: 0} if more else {},
        compiler_params=pltpu.CompilerParams(vmem_limit_bytes=40 * 2**20),
        cost_estimate=pl.CostEstimate(
            flops=pairs * rows * rows * 4000,
            bytes_accessed=rows * width * 8,
            transcendentals=0,
        ),
        name="attn_fwd",
    )(qkv, qkv, qkv, kv_mem, kv_mem, *more)


def attn_mem_kernel(q_ref, km_ref, vm_ref, o_ref, g_ref, lse_ref, dkm_ref, dvm_ref, mid_ref):
    scaled_picks, picks = head_rows(HD**-0.5), head_rows(1.0)
    grad, query = g_ref[...], q_ref[...]
    inner = (grad.astype(F32) * o_ref[...].astype(F32)).T
    dk, dv = 0.0, 0.0
    for head in range(2):
        band = slice(head * HD, (head + 1) * HD)
        query_h, grad_h = query * scaled_picks[head], grad * picks[head]
        centre = jnp.sum(inner[band], axis=0, keepdims=True)
        mid_ref[0, head : head + 1, :] = centre
        prob = jnp.exp(dot_dims(km_ref[0], query_h, 1, 1) - lse_ref[0, head : head + 1, :])
        grad_s = (prob * (dot_dims(vm_ref[0], grad_h, 1, 1) - centre)).astype(BF16)
        dv = dv + dot_dims(prob.astype(BF16), grad_h, 1, 0)
        dk = dk + dot_dims(grad_s, query_h, 1, 0)
    dkm_ref[0] = dk
    dvm_ref[0] = dv


def attn_mem(qkv, kv_mem, attended, grad, lse):
    segs, pairs, mem, wide = kv_mem.shape[0], H // 2, kv_mem.shape[1], 2 * HD
    rows, width = lse.shape[2], qkv.shape[1] // 3
    spec = pl.BlockSpec((rows, wide), lambda s, p: (s, p))
    mspec = lambda off: pl.BlockSpec((1, mem, wide), lambda s, p, off=off: (s, 0, off * pairs + p))
    lspec = pl.BlockSpec((1, 2, rows), lambda s, p: (s * pairs + p, 0, 0))
    return pl.pallas_call(
        attn_mem_kernel,
        grid=(segs, pairs),
        in_specs=[spec, mspec(0), mspec(1), spec, spec, lspec],
        out_specs=[mspec(0), mspec(0), lspec],
        out_shape=[
            jax.ShapeDtypeStruct((segs, mem, width), F32),
            jax.ShapeDtypeStruct((segs, mem, width), F32),
            jax.ShapeDtypeStruct((segs * pairs, 2, rows), F32),
        ],
        compiler_params=pltpu.CompilerParams(vmem_limit_bytes=40 * 2**20),
        cost_estimate=pl.CostEstimate(
            flops=segs * rows * width * 4000, bytes_accessed=segs * rows * width * 6, transcendentals=0
        ),
        name="attn_mem",
    )(qkv, kv_mem, kv_mem, attended, grad, lse)


def attn_bwd_kernel(
    q_ref, k_ref, v_ref, km_ref, vm_ref, g_ref, lse_ref, mid_ref,
    out_ref,
    keys, vals, keys_t, kmem_t, dq, dk, dv,
):
    phase = pl.program_id(1)
    mem = km_ref.shape[0]
    rows = q_ref.shape[0]

    @pl.when(phase == 0)
    def _():
        keys[0:mem, :] = km_ref[...]
        keys[mem:, :] = k_ref[...]
        vals[0:mem, :] = vm_ref[...]
        vals[mem:, :] = v_ref[...]
        keys_t[...] = k_ref[...].T
        kmem_t[...] = km_ref[...].T
        dk[...] = jnp.zeros_like(dk)
        dv[...] = jnp.zeros_like(dv)
        scaled_picks = head_rows(HD**-0.5)
        picks = head_rows(1.0)
        for part in range(rows // CHUNK):
            lo, hi = part * CHUNK, (part + 1) * CHUNK
            end = mem + hi
            query = q_ref[lo:hi, :]
            grad = g_ref[lo:hi, :]
            dqs = []
            for head in range(2):
                band = slice(head * HD, (head + 1) * HD)
                query_h = query * scaled_picks[head]
                grad_h = grad * picks[head]
                log_total = lse_ref[0, head : head + 1, lo:hi]
                centre = mid_ref[0, head : head + 1, lo:hi]
                prob = jnp.exp(dot_dims(keys[0:end, :], query_h, 1, 1) - log_total)
                prob = jnp.concatenate(
                    [prob[: mem + lo], causal_tail(prob[mem + lo :], 0)], axis=0
                )
                grad_p = dot_dims(vals[0:end, :], grad_h, 1, 1)
                grad_s = (prob * (grad_p - centre)).astype(BF16)
                dv[0:end, :] += dot_dims(prob.astype(BF16), grad_h, 1, 0)
                dk[0:end, :] += dot_dims(grad_s, query_h, 1, 0)
                dqs.append(
                    dot_dims(keys_t[band, 0:hi], grad_s[mem:], 1, 0)
                    + dot_dims(kmem_t[band, :], grad_s[:mem], 1, 0)
                )
            dq[lo:hi, :] = (jnp.concatenate(dqs, axis=0) * HD**-0.5).T.astype(BF16)
        out_ref[...] = dq[...]

    @pl.when(phase == 1)
    def _():
        out_ref[...] = dk[mem:, :].astype(BF16)

    @pl.when(phase == 2)
    def _():
        out_ref[...] = dv[mem:, :].astype(BF16)


def attn_bwd(qkv, kv_mem, grad, lse, middle, seg, first, count):
    pairs = H // 2
    rows, width = lse.shape[2], qkv.shape[1] // 3
    mem = kv_mem.shape[0]
    wide = 2 * HD
    spec = lambda off: pl.BlockSpec((rows, wide), lambda p, f, off=off: (seg, off * pairs + first + p))
    mspec = lambda off: pl.BlockSpec((mem, wide), lambda p, f, off=off: (0, off * pairs + first + p))
    lspec = pl.BlockSpec((1, 2, rows), lambda p, f: (seg * pairs + first + p, 0, 0))
    return pl.pallas_call(
        attn_bwd_kernel,
        grid=(count, 3),
        in_specs=[
            spec(0), spec(1), spec(2), mspec(0), mspec(1), spec(0), lspec, lspec,
        ],
        out_specs=pl.BlockSpec((rows, wide), lambda p, f: (0, f * count + p)),
        out_shape=jax.ShapeDtypeStruct((rows, 3 * count * wide), BF16),
        scratch_shapes=[
            pltpu.VMEM((mem + rows, wide), BF16),
            pltpu.VMEM((mem + rows, wide), BF16),
            pltpu.VMEM((wide, rows), BF16),
            pltpu.VMEM((wide, mem), BF16),
            pltpu.VMEM((rows, wide), BF16),
            pltpu.VMEM((mem + rows, wide), F32),
            pltpu.VMEM((mem + rows, wide), F32),
        ],
        compiler_params=pltpu.CompilerParams(vmem_limit_bytes=48 * 2**20),
        cost_estimate=pl.CostEstimate(
            flops=count * rows * rows * 6500,
            bytes_accessed=rows * count * wide * 18,
            transcendentals=0,
        ),
        name="attn_bwd",
    )(qkv, qkv, qkv, kv_mem, kv_mem, grad, lse, middle)


def choose(told, kept, got, out):
    own = pl.program_id(0) % 2 == told[1]

    @pl.when(own)
    def _():
        out[...] = kept[0]

    @pl.when(jnp.logical_not(own))
    def _():
        out[...] = got[0]


def half_specs(rows, width):
    return [pl.BlockSpec((1, rows, width), lambda i, told: ((i // 2) ^ told[0], 0, 0))] * 2


def enter_kernel(told, kept, got, gain, bias, weight, shift, rows_ref, normed_ref, qkv_ref):
    choose(told, kept, got, rows_ref)
    unit, _ = norm_parts(rows_ref[...].astype(F32))
    normed = (unit * gain[...] + bias[...]).astype(BF16)
    normed_ref[...] = normed
    wide = weight.shape[1] // 3
    for k in range(3):
        at = slice(k * wide, (k + 1) * wide)
        qkv_ref[:, at] = (dot_dims(normed, weight[:, at], 1, 0) + shift[:, at]).astype(BF16)


def enter(told, kept, got, gain, bias, weight, shift):
    segs, rows, width = kept.shape
    whole = lambda r, c: pl.BlockSpec((r, c), lambda i, told: (0, 0), pipeline_mode=pl.Buffered(1))
    block = lambda c: pl.BlockSpec((rows, c), lambda i, told: (i, 0))
    sizes = (width, width, 3 * width)
    return pl.pallas_call(
        enter_kernel,
        grid_spec=pltpu.PrefetchScalarGridSpec(
            num_scalar_prefetch=1,
            grid=(2 * segs,),
            in_specs=[*half_specs(rows, width), whole(1, width), whole(1, width), whole(width, 3 * width), whole(1, 3 * width)],
            out_specs=[block(c) for c in sizes],
        ),
        out_shape=[jax.ShapeDtypeStruct((2 * segs * rows, c), BF16) for c in sizes],
        compiler_params=pltpu.CompilerParams(vmem_limit_bytes=48 * 2**20),
        cost_estimate=pl.CostEstimate(
            flops=8 * segs * rows * width * width * 3, bytes_accessed=segs * rows * width * 28, transcendentals=0
        ),
        name="enter",
    )(told, kept, got, gain[None], bias[None], weight, shift[None])


def middle_kernel(
    told, kept, got, rows_ref, attended, out_w, expand_w, contract_w, out_b, gain, bias, expand_b, contract_b,
    result_ref, cot_ref, normed_ref, activ_ref, grad_exp_ref, grad_out_ref, grad_att_ref,
    sums_ref, exp_sums_ref,
):
    choose(told, kept, got, cot_ref)
    cot = cot_ref[...]
    after = rows_ref[...].astype(F32) + dot_dims(attended[...], out_w[...], 1, 0) + out_b[...]
    unit, rstd = norm_parts(after)
    normed = (unit * gain[...] + bias[...]).astype(BF16)
    normed_ref[...] = normed
    total = after + contract_b[...]
    back = 0.0

    @pl.when(pl.program_id(0) == 0)
    def _():
        sums_ref[...] = jnp.zeros_like(sums_ref)
        exp_sums_ref[...] = jnp.zeros_like(exp_sums_ref)

    parts = 6
    wide = expand_w.shape[1] // parts
    bend, cube = 0.7978845608028654, 0.044715
    for part in range(parts):
        at = slice(part * wide, (part + 1) * wide)
        value = dot_dims(normed, expand_w[:, at], 1, 0) + expand_b[:, at]
        square = value * value
        curve = jnp.tanh(bend * value * (1.0 + cube * square))
        half = 0.5 * (1.0 + curve)
        activ = (value * half).astype(BF16)
        activ_ref[:, at] = activ
        slope = half + 0.5 * bend * value * (1.0 - curve * curve) * (1.0 + 3.0 * cube * square)
        grad = (dot_dims(cot, contract_w[:, at], 1, 0) * slope).astype(BF16)
        grad_exp_ref[:, at] = grad
        exp_sums_ref[:, at] += jnp.sum(grad.astype(F32), axis=0, keepdims=True)
        total = total + dot_dims(activ, contract_w[:, at], 1, 1)
        back = back + dot_dims(grad, expand_w[:, at], 1, 1)
    result_ref[...] = total.astype(BF16)
    wide_cot = cot.astype(F32)
    grad_rows, gain_sum, bias_sum = norm_back(back, unit, rstd, gain[...])
    grad_out = (grad_rows + wide_cot).astype(BF16)
    grad_out_ref[...] = grad_out
    grad_att_ref[...] = dot_dims(grad_out, out_w[...], 1, 1).astype(BF16)
    sums = (
        jnp.sum(grad_out.astype(F32), axis=0, keepdims=True),
        gain_sum[None],
        bias_sum[None],
        jnp.sum(wide_cot, axis=0, keepdims=True),
    )
    for k, value in enumerate(sums):
        sums_ref[k : k + 1, :] += value


def middle(told, kept, got, rows_in, attended, out_w, expand_w, contract_w, out_b, gain, bias, expand_b, contract_b):
    segs, rows, width = kept.shape
    wide = expand_w.shape[1]
    whole = lambda r, c: pl.BlockSpec((r, c), lambda i, told: (0, 0), pipeline_mode=pl.Buffered(1))
    block = lambda c: pl.BlockSpec((rows, c), lambda i, told: (i, 0))
    sizes = (width, width, width, wide, wide, width, width)
    count = 2 * segs * rows
    fixed = lambda r, c: pl.BlockSpec((r, c), lambda i, told: (0, 0))
    return pl.pallas_call(
        middle_kernel,
        grid_spec=pltpu.PrefetchScalarGridSpec(
            num_scalar_prefetch=1,
            grid=(2 * segs,),
            in_specs=[
                *half_specs(rows, width), block(width), block(width), whole(width, width), whole(width, wide),
                whole(width, wide), whole(1, width), whole(1, width), whole(1, width), whole(1, wide), whole(1, width),
            ],
            out_specs=[*[block(c) for c in sizes], fixed(8, width), fixed(1, wide)],
        ),
        out_shape=[
            *[jax.ShapeDtypeStruct((count, c), BF16) for c in sizes],
            jax.ShapeDtypeStruct((8, width), F32),
            jax.ShapeDtypeStruct((1, wide), F32),
        ],
        compiler_params=pltpu.CompilerParams(vmem_limit_bytes=60 * 2**20),
        cost_estimate=pl.CostEstimate(
            flops=count * width * (8 * wide + 4 * width) * 2, bytes_accessed=count * (14 * width + 4 * wide), transcendentals=0
        ),
        name="middle",
    )(
        told, kept, got, rows_in, attended, out_w, expand_w, contract_w, out_b[None], gain[None], bias[None],
        expand_b[None], contract_b[None],
    )


def gather_kernel(halved, count, kinds, *refs):
    shards, outs = refs[:count], refs[count : 2 * count]
    send_sem, recv_sem, local_sem = refs[2 * count :]
    index, plane = lax.axis_index("dp"), lax.axis_index("ctx")
    deep, cross, core = index // 4, (index // 2) % 2, index % 2
    place = lambda z, x, c: (z * 2 + x) * 2 + c
    up, down = {"dp": place(deep + 1, cross, core)}, {"dp": place(deep - 1, cross, core)}
    beside, sibling = {"dp": place(deep, 1 - cross, core)}, {"dp": place(deep, cross, 1 - core)}
    other = {"ctx": 1 - plane}
    rows = shards[0].shape[0]
    numbers, sends = {}, []

    def valid(kind):
        way, far = kind
        return deep >= 0 if way == "own" else deep >= far if way == "below" else deep + far <= 3

    def level(kind):
        way, far = kind
        return deep if way == "own" else deep - far if way == "below" else deep + far

    def view(k, z, x, c, part):
        at = pl.ds(pl.multiple_of(place(z, x, c) * rows, 16), rows)
        return outs[k].at[at, :] if part is None else outs[k].at[at, half(k, part)]

    def half(k, part):
        wide = outs[k].shape[1] // 2
        return pl.ds(pl.multiple_of(part * wide, 128), wide)

    def copy(key, source, landing, device):
        number = numbers.setdefault(key, len(numbers))
        return pltpu.make_async_remote_copy(
            source, landing, send_sem.at[number], recv_sem.at[number],
            device_id=device, device_id_type=pl.DeviceIdType.MESH,
        )

    def send(when, key, source, landing, device):
        def begin():
            copy(key, source, landing, device).start()

        def end():
            copy(key, source, landing, device).wait_send()

        sends.append((when, end))
        if when is None:
            begin()
        else:
            pl.when(when)(begin)

    def arrived(key, landing):
        copy(key, landing, landing, sibling).wait_recv()

    barrier = pltpu.get_barrier_semaphore()
    for device in (beside, sibling, other):
        pl.semaphore_signal(barrier, inc=1, device_id=device, device_id_type=pl.DeviceIdType.MESH)
    for when, device in ((deep < 3, up), (deep > 0, down)):

        @pl.when(when)
        def _(device=device):
            pl.semaphore_signal(barrier, inc=1, device_id=device, device_id_type=pl.DeviceIdType.MESH)

    inner = (deep > 0) & (deep < 3)
    for when, peers in ((inner, 5), (jnp.logical_not(inner), 4)):

        @pl.when(when)
        def _(peers=peers):
            pl.semaphore_wait(barrier, peers)

    own = ("own", 0)
    locals_ = []
    for k in range(count):
        part = plane if k in halved else None
        mine = view(k, deep, cross, core, None)
        locals_.append(pltpu.make_async_copy(shards[k], mine, local_sem.at[k]))
        locals_[-1].start()
        source = shards[k] if part is None else shards[k].at[:, half(k, part)]
        landing = view(k, deep, cross, core, part)
        send(deep < 3, ("z", ("below", 1), k), source, landing, up)
        send(deep > 0, ("z", ("above", 1), k), source, landing, down)
        send(None, ("x", own, k), source, landing, beside)
        send(None, ("core", "z", own, k), shards[k], mine, sibling)

    def onward(k, flow, kind, x):
        part = plane if k in halved else None
        block = view(k, level(kind), x, core, part)
        ok = valid(kind)
        if flow == "z":
            way, far = kind
            if far < 3:
                if way == "below":
                    send(ok & (deep < 3), ("z", (way, far + 1), k), block, block, up)
                else:
                    send(ok & (deep > 0), ("z", (way, far + 1), k), block, block, down)
            send(ok, ("x", kind, k), block, block, beside)
        send(ok, ("core", flow, kind, k), block, block, sibling)
        if k in halved:
            send(ok, ("y", flow, kind, k), block, block, other)

    def take(flow, kind):
        x = cross if flow == "z" else 1 - cross
        for k in range(count):
            part = plane if k in halved else None

            @pl.when(valid(kind))
            def _():
                arrived((flow, kind, k), view(k, level(kind), x, core, part))

            onward(k, flow, kind, x)

    for far in range(1, 4):
        take("z", ("below", far))
        take("z", ("above", far))
        for kind in kinds:
            if kind[1] == far - 1:
                take("x", kind)
    for kind in kinds:
        if kind[1] == 3:
            take("x", kind)
    crossing = [(flow, kind, k) for flow in ("z", "x") for kind in kinds for k in halved]
    crossing = [c for c in crossing if c[:2] != ("z", own)]
    for flow, kind, k in crossing:
        x = cross if flow == "z" else 1 - cross
        block = lambda c: view(k, level(kind), x, c, 1 - plane)

        @pl.when(valid(kind))
        def _():
            arrived(("y", flow, kind, k), block(core))

        send(valid(kind), ("core", "y", flow, kind, k), block(core), block(core), sibling)
    for flow in ("z", "x"):
        x = cross if flow == "z" else 1 - cross
        for kind in kinds:
            for k in range(count):
                part = plane if k in halved and (flow, kind) != ("z", own) else None

                @pl.when(valid(kind))
                def _():
                    arrived(("core", flow, kind, k), view(k, level(kind), x, 1 - core, part))

    for flow, kind, k in crossing:
        x = cross if flow == "z" else 1 - cross

        @pl.when(valid(kind))
        def _():
            arrived(("core", "y", flow, kind, k), view(k, level(kind), x, 1 - core, 1 - plane))

    for when, end in sends:
        if when is None:
            end()
        else:
            pl.when(when)(end)
    for held in locals_:
        held.wait()


def gather_weights(shards, halved):
    kinds = [("own", 0)] + [(way, far) for far in (1, 2, 3) for way in ("below", "above")]
    count = len(shards)
    rows = shards[0].shape[0] * 16
    copies = 6 * count + 7 * count + 13 * len(halved) + 14 * count + 13 * len(halved)
    any_space = pl.BlockSpec(memory_space=pl.ANY)
    return pl.pallas_call(
        functools.partial(gather_kernel, halved, count, kinds),
        in_specs=[any_space] * count,
        out_specs=[any_space] * count,
        out_shape=[jax.ShapeDtypeStruct((rows, s.shape[1]), BF16) for s in shards],
        scratch_shapes=[
            pltpu.SemaphoreType.DMA((copies,)),
            pltpu.SemaphoreType.DMA((copies,)),
            pltpu.SemaphoreType.DMA((count,)),
        ],
        compiler_params=pltpu.CompilerParams(
            collective_id=0, has_side_effects=True, vmem_limit_bytes=4 * 2**20
        ),
        cost_estimate=pl.CostEstimate(
            flops=8 * 10**10, bytes_accessed=4 * rows * sum(s.shape[1] for s in shards), transcendentals=0
        ),
        name="gather_weights",
    )(*shards)


def dp_pairs(flip):
    return [(i, i ^ flip) for i in range(16)]


def behind(value, *earlier):
    return lax.optimization_barrier((value, earlier))[0]


def pick(parts, at, axis):
    return lax.dynamic_index_in_dim(parts, at, axis, keepdims=False)


def add_low(a, b):
    return (a.astype(F32) + b.astype(F32)).astype(BF16)


class Scatter:
    def __init__(self, grad):
        index = lax.axis_index("dp")
        self.deep, self.cross, self.core = index // 4, (index // 2) % 2, index % 2
        parts = grad.reshape(4, 2, 2, grad.shape[0] // 16, grad.shape[1])
        self.keep, self.give = pick(parts, self.core, 2), pick(parts, 1 - self.core, 2)

    def over_core(self, *beside):
        got = behind(lax.ppermute(self.give, "dp", dp_pairs(1)), *beside)
        parts = add_low(self.keep, got)
        self.keep, self.give = pick(parts, self.cross, 1), pick(parts, 1 - self.cross, 1)
        return self

    def over_x(self, *beside):
        got = behind(lax.ppermute(self.give, "dp", dp_pairs(2)), *beside)
        parts = add_low(self.keep, got)
        self.keep = pick(parts, self.deep, 0)
        self.give = tuple(pick(parts, self.deep ^ k, 0) for k in (1, 2, 3))
        return self

    def over_z(self, *beside):
        far = [lax.ppermute(self.give[k - 1], "dp", dp_pairs(4 * k)) for k in (1, 2, 3)]
        total = self.keep.astype(F32)
        for part in behind(far, *beside):
            total = total + part.astype(F32)
        self.keep = self.give = total.astype(BF16)
        return self

    def over_y(self, *beside):
        got = behind(lax.ppermute(self.give, "ctx", [(0, 1), (1, 0)]), *beside)
        return self.keep.astype(F32) + got.astype(F32)


def sum_over(flat, step, *beside):
    if step == 0:
        return flat + behind(lax.ppermute(flat, "ctx", [(0, 1), (1, 0)]), *beside)
    if step < 3:
        return flat + behind(lax.ppermute(flat, "dp", dp_pairs(step)), *beside)
    far = behind([lax.ppermute(flat, "dp", dp_pairs(4 * k)) for k in (1, 2, 3)], *beside)
    return (flat + far[0]) + (far[1] + far[2])


def split_heads(rows):
    return rows.reshape(rows.shape[0], rows.shape[1], H, HD)


def plain_scores(query, key, allowed):
    scores = jnp.einsum("sqhd,skhd->shqk", query, key, preferred_element_type=F32) * HD**-0.5
    return scores, allowed[None, None]


def plain_fwd(qkv, kv_all, allowed):
    width = qkv.shape[2] // 3
    query = split_heads(qkv[:, :, :width])
    key, value = split_heads(kv_all[:, :, :width]), split_heads(kv_all[:, :, width:])
    scores, allowed = plain_scores(query, key, allowed)
    raw = jnp.where(allowed, jnp.exp(scores), 0.0)
    total = jnp.sum(raw, axis=-1)
    weights = (raw / total[..., None]).astype(BF16)
    mixed = jnp.einsum("shqk,skhd->sqhd", weights, value, preferred_element_type=F32)
    return mixed.reshape(qkv.shape[0], -1, width).astype(BF16), jnp.log(total)


def plain_bwd(qkv, kv_all, allowed, log_total, grad):
    segs, width = qkv.shape[0], qkv.shape[2] // 3
    query = split_heads(qkv[:, :, :width])
    key, value = split_heads(kv_all[:, :, :width]), split_heads(kv_all[:, :, width:])
    grad = split_heads(grad)
    scores, allowed = plain_scores(query, key, allowed)
    prob = jnp.where(allowed, jnp.exp(scores - log_total[..., None]), 0.0)
    grad_p = jnp.einsum("sqhd,skhd->shqk", grad, value, preferred_element_type=F32)
    inner = jnp.sum(prob * grad_p, axis=-1, keepdims=True)
    grad_s = (prob * (grad_p - inner) * HD**-0.5).astype(BF16)
    dq = jnp.einsum("shqk,skhd->sqhd", grad_s, key, preferred_element_type=F32)
    dk = jnp.einsum("shqk,sqhd->skhd", grad_s, query, preferred_element_type=F32)
    dv = jnp.einsum("shqk,sqhd->skhd", prob.astype(BF16), grad, preferred_element_type=F32)
    flat = lambda a: a.reshape(segs, -1, width)
    return flat(dq), jnp.concatenate([flat(dk), flat(dv)], axis=2)


def memory_forward(mt, p):
    mem = mt.shape[0]
    keep = {}
    width = mt.shape[1]
    unit, rstd = norm_parts(mt)
    normed = (unit * p["one_gain"] + p["one_bias"]).astype(BF16)
    qkv = (dot_dims(normed, p["qkv"], 1, 0) + p["shift"]).astype(BF16)
    at = jnp.arange(mem, dtype=jnp.int32)
    allowed = at[None, :] <= at[:, None]
    attended, log_total = plain_fwd(qkv[None], qkv[None, :, width:], allowed)
    attended = attended[0]
    after = mt + dot_dims(attended, p["out"], 1, 0) + p["out_bias"]
    unit_b, rstd_b = norm_parts(after)
    normed_b = (unit_b * p["two_gain"] + p["two_bias"]).astype(BF16)
    expanded = dot_dims(normed_b, p["expand"], 1, 0) + p["expand_bias"]
    activ = gelu_tanh(expanded).astype(BF16)
    result = after + dot_dims(activ, p["contract"], 1, 1) + p["contract_bias"]
    key_pre = exact(result, p["key"].astype(F32), 1, 0)
    value_new = exact(result, p["value"].astype(F32), 1, 0)
    read_pre = exact(mt, p["read"].astype(F32), 1, 0)
    key_feat, key_pull = jax.vjp(feature_map, key_pre)
    read_feat, read_pull = jax.vjp(feature_map, read_pre)
    mix = exact(read_feat, key_feat, 1, 1)
    numer = exact(mix, value_new, 1, 0)
    denom = 1.0 + jnp.sum(mix, axis=1, keepdims=True)
    follow = mt + numer / denom
    unit_f, rstd_f = norm_parts(follow)
    normed_f = (unit_f * p["one_gain"] + p["one_bias"]).astype(BF16)
    kv_follow = (dot_dims(normed_f, p["qkv"][:, width:], 1, 0) + p["shift"][width:]).astype(BF16)
    keep = dict(
        unit=unit, rstd=rstd, normed=normed, qkv=qkv, allowed=allowed, attended=attended,
        log_total=log_total, unit_b=unit_b, rstd_b=rstd_b, normed_b=normed_b, expanded=expanded,
        activ=activ, result=result, key_feat=key_feat, read_feat=read_feat, key_pull=key_pull,
        read_pull=read_pull, value_new=value_new, mix=mix, numer=numer, denom=denom, unit_f=unit_f,
        rstd_f=rstd_f, normed_f=normed_f,
    )
    return qkv[:, width:], kv_follow, keep


def memory_backward(mt, p, m, grad_kv_first, grad_kv_follow, mine, turn):
    width = mt.shape[1]
    low = lambda a: a.astype(BF16)
    grad_f = low(turn(0, grad_kv_follow))
    grad_follow, gain_f, bias_f = norm_back(
        dot_dims(grad_f, p["qkv"][:, width:], 1, 1), m["unit_f"], m["rstd_f"], p["one_gain"]
    )
    grad_mt = grad_follow
    grad_numer = grad_follow / m["denom"]
    grad_denom = -jnp.sum(grad_follow * m["numer"], axis=1, keepdims=True) / (m["denom"] * m["denom"])
    grad_mix = exact(grad_numer, m["value_new"], 1, 1) + grad_denom
    grad_value = exact(m["mix"], grad_numer, 0, 0)
    [grad_read_pre] = m["read_pull"](exact(grad_mix, m["key_feat"], 1, 0))
    [grad_key_pre] = m["key_pull"](exact(grad_mix, m["read_feat"], 0, 0))
    grad_mt = grad_mt + exact(grad_read_pre, p["read"].astype(F32), 1, 1)
    grad_result = exact(grad_key_pre, p["key"].astype(F32), 1, 1) + exact(
        grad_value, p["value"].astype(F32), 1, 1
    )
    grad_result = turn(1, grad_result)
    grad_contract = low(grad_result)
    _, gelu_pull = jax.vjp(gelu_tanh, m["expanded"])
    grad_expanded = low(gelu_pull(dot_dims(grad_contract, p["contract"], 1, 0))[0])
    grad_after, two_gain, two_bias = norm_back(
        dot_dims(grad_expanded, p["expand"], 1, 1), m["unit_b"], m["rstd_b"], p["two_gain"]
    )
    grad_after = grad_after + grad_result
    grad_attn_out = low(grad_after)
    grad_attended = low(dot_dims(grad_attn_out, p["out"], 1, 1))
    dq, dkv = plain_bwd(
        m["qkv"][None], m["qkv"][None, :, width:], m["allowed"], m["log_total"], grad_attended[None]
    )
    grad_qkv = low(turn(2, jnp.concatenate([dq[0], dkv[0] + grad_kv_first], axis=1)))
    grad_first, gain_a, bias_a = norm_back(
        dot_dims(grad_qkv, p["qkv"], 1, 1), m["unit"], m["rstd"], p["one_gain"]
    )
    grad_mt = grad_mt + grad_first + grad_after
    wide = grad_qkv.astype(F32)
    kv_rows = grad_f.astype(F32)
    sums = jnp.sum(wide, axis=0)
    follow_sums = jnp.sum(kv_rows, axis=0)
    matrices = (
        dot_dims(mine(m["normed"]), grad_qkv, 0, 0)
        + jnp.concatenate(
            [
                jnp.zeros((mine(mt).shape[1], width), F32),
                dot_dims(mine(m["normed_f"]), grad_f, 0, 0),
            ],
            axis=1,
        ),
        dot_dims(mine(m["attended"]), grad_attn_out, 0, 0),
        dot_dims(mine(m["normed_b"]), grad_expanded, 0, 0),
        dot_dims(mine(grad_contract), m["activ"], 0, 0),
        exact(mine(mt), grad_read_pre, 0, 0),
        exact(mine(m["result"]), grad_key_pre, 0, 0),
        exact(mine(m["result"]), grad_value, 0, 0),
    )
    column_sum = lambda a: jnp.sum(a.astype(F32), axis=0)
    vectors = (
        gain_f + gain_a,
        bias_f + bias_a,
        jnp.stack([sums[:width], sums[2 * width :] + follow_sums[width:]]),
        column_sum(grad_attn_out),
        two_gain,
        two_bias,
        column_sum(grad_expanded),
        column_sum(grad_contract),
    )
    return grad_mt, matrices, vectors


def local(
    tokens,
    cotangent,
    placing,
    starts,
    memory_tokens,
    norm_one_gain,
    norm_one_bias,
    qkv_weight,
    qv_bias,
    out_weight,
    out_bias,
    norm_two_gain,
    norm_two_bias,
    expand_weight,
    expand_bias,
    contract_weight,
    contract_bias,
    read_weight,
    key_weight,
    value_weight,
):
    del placing
    groups, ranks = lax.axis_size("dp"), lax.axis_size("ctx")
    group, rank = lax.axis_index("dp"), lax.axis_index("ctx")
    micros, segs_local, tok_rows, width = tokens.shape
    mem = memory_tokens.shape[0]
    shard = qkv_weight.shape[0]
    quick = groups == 16 and ranks == 2 and micros == 2 and segs_local == 2 and (tok_rows * ranks) % CHUNK == 0
    names = ("qkv", "out", "expand", "contract", "read", "key", "value")
    shards = (qkv_weight, out_weight, expand_weight, contract_weight, read_weight, key_weight, value_weight)
    if quick:
        give = pick(tokens, 1 - rank, 0)
        joined = (
            jnp.concatenate([qkv_weight, read_weight, key_weight], axis=1),
            expand_weight,
            contract_weight,
            jnp.concatenate([out_weight, value_weight], axis=1),
        )
        qkv_read_key, expand_full, contract_full, out_value = gather_weights(
            behind(joined, give), (2, 3)
        )
        feat = read_weight.shape[1]
        whole = (
            qkv_read_key[:, : 3 * width],
            out_value[:, :width],
            expand_full,
            contract_full,
            qkv_read_key[:, 3 * width : 3 * width + feat],
            qkv_read_key[:, 3 * width + feat :],
            out_value[:, width:],
        )
    else:
        whole = tuple(lax.all_gather(s, "dp", axis=0, tiled=True) for s in shards)
    p = dict(zip(names, whole))
    p.update(
        one_gain=norm_one_gain, one_bias=norm_one_bias, out_bias=out_bias, two_gain=norm_two_gain,
        two_bias=norm_two_bias, expand_bias=expand_bias, contract_bias=contract_bias,
        shift=jnp.concatenate([qv_bias[0], jnp.zeros((width,), F32), qv_bias[1]]),
    )
    flags = lax.dynamic_slice_in_dim(starts, group * segs_local, segs_local, 1)

    swap = [(0, 1), (1, 0)]

    def own_and_other(rows):
        halves = rows.reshape(ranks, tok_rows, width)
        return pick(halves, rank, 0), pick(halves, 1 - rank, 0)

    def swapped(given):
        return lax.ppermute(given, "ctx", swap)

    def settle(halves, flips):
        micro_rows = []
        for micro in range(2):
            pair = [jnp.where(rank == micro, kept, got) for kept, got in halves]
            flip = flips[micro]
            micro_rows.append(
                jnp.stack([jnp.where(flip, pair[1], pair[0]), jnp.where(flip, pair[0], pair[1])])
            )
        return jnp.stack(micro_rows)

    if quick:
        flips = flags[:, 1] == 1
        flip = pick(flips, rank, 0)
        told = jnp.stack([flip.astype(jnp.int32), rank.astype(jnp.int32)])
        got = swapped(give)
        give_grad = behind(pick(cotangent, 1 - rank, 0), got, expand_full)
        flags = pick(flags, rank, 0)
        flags = jnp.where(flip, flags[::-1], flags)
        segs = segs_local
        seg_rows = ranks * tok_rows
    else:
        rows_in, rows_grad = tokens.reshape(-1, width), cotangent.reshape(-1, width)
        flags = flags.reshape(-1)
        segs = micros * segs_local
        seg_rows = tok_rows

    kv_first, kv_follow, m = memory_forward(memory_tokens, p)
    kv_mem = jnp.where((flags == 0)[:, None, None], kv_follow[None], kv_first[None])
    if quick:
        rows_in, normed_a, qkv = enter(
            told, pick(tokens, rank, 0), got, norm_one_gain, norm_one_bias, qkv_read_key, p["shift"]
        )
        attended, lse_first = attn_fwd(behind(qkv, give_grad), kv_first, 0, seg_rows, None)
        got_grad = swapped(give_grad)
        attended, lse_second = attn_fwd(qkv, kv_mem[1], 1, seg_rows, attended)
        attended, got_grad = lax.optimization_barrier((attended, got_grad))
        (
            result, rows_grad, normed_b, activ, grad_expanded, grad_attn_out, grad_attended, mid_sums, expand_sums,
        ) = middle(
            told, pick(cotangent, rank, 0), got_grad, rows_in, attended, p["out"], p["expand"], p["contract"], out_bias,
            norm_two_gain, norm_two_bias, expand_bias, contract_bias,
        )
        grad_after = grad_attn_out
    else:
        hidden = rows_in.astype(F32)
        unit_a, rstd_a = norm_parts(hidden)
        normed_a = (unit_a * norm_one_gain + norm_one_bias).astype(BF16)
        qkv = (dot_dims(normed_a, p["qkv"], 1, 0) + p["shift"]).astype(BF16)
        seg_qkv = qkv.reshape(segs, seg_rows, 3 * width)
        kv_all = lax.all_gather(seg_qkv[:, :, width:], "ctx", axis=1, tiled=True)
        kv_all = jnp.concatenate([kv_mem, kv_all], axis=1)
        query_at = mem + rank * seg_rows + jnp.arange(seg_rows, dtype=jnp.int32)
        key_at = jnp.arange(mem + ranks * seg_rows, dtype=jnp.int32)
        allowed = key_at[None, :] <= query_at[:, None]
        attended, lse = plain_fwd(seg_qkv, kv_all, allowed)
        attended = attended.reshape(-1, width)
        after = hidden + dot_dims(attended, p["out"], 1, 0) + out_bias
        unit_b, rstd_b = norm_parts(after)
        normed_b = (unit_b * norm_two_gain + norm_two_bias).astype(BF16)
        expanded = dot_dims(normed_b, p["expand"], 1, 0) + expand_bias
        activ = gelu_tanh(expanded).astype(BF16)
        result = (after + dot_dims(activ, p["contract"], 1, 1) + contract_bias).astype(BF16)

    def input_back(at, grads, weights):
        grad = dot_dims(grads[0], weights[0], 1, 1)
        for g, w in zip(grads[1:], weights[1:]):
            grad = grad + dot_dims(g, w, 1, 1)
        unit, rstd = norm_parts(rows_in[at].astype(F32))
        grad_hidden, gain, bias = norm_back(grad, unit, rstd, norm_one_gain)
        return (grad_hidden + grad_after[at].astype(F32)).astype(BF16), gain, bias

    def pool(dkv_mem):
        follows = (flags == 0).astype(F32)[:, None, None]
        kinds = [jnp.sum(dkv_mem * (1.0 - follows), axis=0), jnp.sum(dkv_mem * follows, axis=0)]
        return jnp.stack(kinds)

    if quick:
        pairs, most = H // 2, H // 3
        cut = most * 2 * HD
        columns = lambda a, lo, hi: jnp.concatenate(
            [a[..., k * width + lo : k * width + hi] for k in range(3)], axis=-1
        )
        weights = [columns(p["qkv"], 0, cut), columns(p["qkv"], cut, width)]
        lse = jnp.concatenate([lse_first, lse_second], axis=0)
        mems = (kv_first, kv_mem[1])
        spans = [slice(0, seg_rows), slice(seg_rows, 2 * seg_rows)]

        block_halves = [own_and_other(result[a]) for a in spans]
        on_contract = Scatter(dot_dims(rows_grad, activ, 0, 0).astype(BF16))
        grad_expanded = behind(grad_expanded, on_contract.give)
        term_expand = dot_dims(normed_b, grad_expanded, 0, 0).astype(BF16)
        on_expand = Scatter(term_expand)
        on_contract.over_core(term_expand)
        grad_attn_out = behind(grad_attn_out, on_contract.give, on_expand.give)
        on_out = Scatter(dot_dims(attended, grad_attn_out, 0, 0).astype(BF16))
        dk_mem, dv_mem, middle_sums = attn_mem(
            qkv, kv_mem, attended, behind(grad_attended, on_out.give), lse
        )
        on_expand.over_core(middle_sums)
        pooled = pool(jnp.concatenate([dk_mem, dv_mem], axis=2))
        others = behind([other for _, other in block_halves], middle_sums)

        def back(seg, first, count, *earlier):
            grad = behind(grad_attended, *earlier)
            return attn_bwd(qkv, mems[seg], grad, lse, middle_sums, seg, first, count)

        normed = [normed_a[a] for a in spans]
        term = lambda grads: sum(dot_dims(normed[k], grads[k], 0, 0) for k in range(2)).astype(BF16)
        turn_a = back(0, 0, most, pooled, others, on_expand.give)
        pooled = sum_over(pooled, 0, turn_a)
        on_out.over_core(turn_a)
        on_contract.over_x(turn_a)
        turn_b = back(1, 0, most, turn_a, pooled, on_contract.give, on_out.give)
        pooled = sum_over(pooled, 1, turn_b)
        others = behind([swapped(other) for other in others], turn_b)
        block_halves = [(own, other) for (own, _), other in zip(block_halves, others)]
        on_expand.over_x(turn_b)
        on_contract.over_z(turn_b)
        most_grads = [turn_a, turn_b]
        on_most = Scatter(term(most_grads))
        turn_c = back(
            0, most, pairs - most, on_most.give, on_expand.give, on_contract.give, pooled
        )
        pooled = sum_over(pooled, 2, turn_c)
        on_most.over_core(turn_c)
        on_out.over_x(turn_c)
        got_contract = on_contract.over_y(turn_c)
        first_end = input_back(
            spans[0],
            [behind(most_grads[0], on_most.give, on_out.give, pooled), turn_c],
            weights,
        )
        kept_first, given_first = own_and_other(first_end[0])
        turn_d = back(1, most, pairs - most, given_first, got_contract)
        pooled = sum_over(pooled, 3, turn_d)
        on_expand.over_z(turn_d)
        on_most.over_x(turn_d)
        got_first = behind(swapped(given_first), turn_d)
        rest_grads = [turn_c, behind(turn_d, on_expand.give, on_most.give)]
        second_end = input_back(spans[1], [most_grads[1], rest_grads[1]], weights)
        kept_second, given_second = own_and_other(second_end[0])
        on_rest = Scatter(term(rest_grads))
        one_gain, one_bias = first_end[1] + second_end[1], first_end[2] + second_end[2]
        qkv_sums = [
            sum(jnp.sum(g[k].astype(F32), axis=0) for k in range(2)).reshape(3, -1)
            for g in (most_grads, rest_grads)
        ]
        qkv_sums = jnp.concatenate(qkv_sums, axis=1)
    else:
        _, gelu_pull = jax.vjp(gelu_tanh, expanded)
        grad_expanded = gelu_pull(dot_dims(rows_grad, p["contract"], 1, 0))[0].astype(BF16)
        grad_after, two_gain, two_bias = norm_back(
            dot_dims(grad_expanded, p["expand"], 1, 1), unit_b, rstd_b, norm_two_gain
        )
        grad_after = grad_after + rows_grad.astype(F32)
        grad_attn_out = grad_after.astype(BF16)
        grad_attended = dot_dims(grad_attn_out, p["out"], 1, 1).astype(BF16)
        dq, dkv = plain_bwd(
            seg_qkv, kv_all, allowed, lse, grad_attended.reshape(segs, seg_rows, width)
        )
        pooled = pool(dkv[:, :mem])
        dkv = lax.psum_scatter(
            dkv[:, mem:].astype(BF16), "ctx", scatter_dimension=1, tiled=True
        )
        grad_qkv = jnp.concatenate([dq.astype(BF16), dkv], axis=2).reshape(-1, 3 * width)
        grad_rows, one_gain, one_bias = input_back(slice(None), [grad_qkv], [p["qkv"]])
        terms = (
            dot_dims(normed_a, grad_qkv, 0, 0).astype(BF16),
            dot_dims(attended, grad_attn_out, 0, 0).astype(BF16),
            dot_dims(normed_b, grad_expanded, 0, 0).astype(BF16),
            dot_dims(rows_grad, activ, 0, 0).astype(BF16),
        )
        qkv_sums = jnp.sum(grad_qkv.astype(F32), axis=0).reshape(3, width)
    column_sum = lambda a: jnp.sum(a.astype(F32), axis=0)
    if quick:
        mid = (mid_sums[0], mid_sums[1], mid_sums[2], expand_sums[0], mid_sums[3])
    else:
        mid = (
            column_sum(grad_attn_out), two_gain, two_bias, column_sum(grad_expanded), column_sum(rows_grad),
        )
    vectors = (one_gain, one_bias, jnp.stack([qkv_sums[0], qkv_sums[2]]), *mid)
    flat = jnp.concatenate([v.reshape(-1) for v in vectors]).reshape(-1, 128)
    got = {}

    def turn(step, value):
        if not quick:
            return value
        if step == 0:
            return behind(value, flat, on_rest.give, on_most.give, given_second)
        if step == 1:
            got["second"] = behind(swapped(given_second), value)
            on_rest.over_core(value)
            on_most.over_z(value)
            on_out.over_z(value)
            got["flat"] = sum_over(flat, 0, value)
            return behind(value, on_rest.give, on_most.give, on_out.give, got["flat"])
        if step == 2:
            on_rest.over_x(value)
            got["most"], got["out"], got["expand"] = (
                on_most.over_y(value), on_out.over_y(value), on_expand.over_y(value)
            )
            got["flat"] = sum_over(sum_over(got["flat"], 1), 2, value)
            return behind(value, on_rest.give, got["flat"], got["most"], got["out"], got["expand"])
        return value

    if not quick:
        summed = tuple(
            lax.psum(
                lax.psum_scatter(t, "dp", scatter_dimension=0, tiled=True).astype(F32), "ctx"
            )
            for t in terms
        )
        pooled, vectors = lax.psum((pooled, vectors), ("dp", "ctx"))

    mine = lambda a: lax.dynamic_slice_in_dim(a, group * shard, shard, 1)
    grad_mt, mem_matrices, mem_vectors = memory_backward(
        memory_tokens, p, m, pooled[0], pooled[1], mine, turn
    )
    if quick:
        most_part = got["most"].reshape(shard, 3, cut)
        rest_part = on_rest.over_z().over_y().reshape(shard, 3, width - cut)
        summed = (
            jnp.concatenate([most_part, rest_part], axis=2).reshape(shard, 3 * width),
            got["out"],
            got["expand"],
            got_contract,
        )
        flat = sum_over(got["flat"], 3).reshape(-1)
        split, place = [], 0
        for v in vectors:
            split.append(flat[place : place + v.size].reshape(v.shape))
            place += v.size
        vectors = tuple(split)
    matrices = tuple(a + b for a, b in zip(summed, mem_matrices)) + mem_matrices[4:]
    vectors = tuple(a + b for a, b in zip(vectors, mem_vectors))
    if quick:
        block_out = settle(block_halves, flips)
        token_grad = settle([(kept_first, got_first), (kept_second, got["second"])], flips)
    else:
        block_out, token_grad = result.reshape(tokens.shape), grad_rows.reshape(tokens.shape)
    return (
        block_out,
        token_grad,
        grad_mt,
        vectors[0],
        vectors[1],
        matrices[0],
        vectors[2],
        matrices[1],
        vectors[3],
        vectors[4],
        vectors[5],
        matrices[2],
        vectors[6],
        matrices[3],
        vectors[7],
        matrices[4],
        matrices[5],
        matrices[6],
    )


def solution(mesh):
    rows = P(None, "dp", "ctx", None)
    matrix = P("dp", None)
    full = P()
    return jax.shard_map(
        local,
        mesh=mesh,
        in_specs=(
            rows, rows, full, full, full, full, full, matrix, full, matrix, full, full, full,
            matrix, full, matrix, full, matrix, matrix, matrix,
        ),
        out_specs=(
            rows, rows, full, full, full, matrix, full, matrix, full, full, full, matrix, full,
            matrix, full, matrix, matrix, matrix,
        ),
        check_vma=False,
    )
```

```python
import functools

import jax
import jax.numpy as jnp
from jax import lax
from jax.experimental import pallas as pl
from jax.experimental.pallas import tpu as pltpu
from jax.sharding import PartitionSpec as P

H = 12
HD = 64
EPS = 1e-05
CHUNK = 256
F32 = jnp.float32
BF16 = jnp.bfloat16


def norm_parts(rows):
    centred = rows - jnp.mean(rows, axis=-1, keepdims=True)
    spread = jnp.mean(centred * centred, axis=-1, keepdims=True)
    rstd = lax.rsqrt(spread + EPS)
    return centred * rstd, rstd


def norm_back(grad, unit, rstd, gain):
    scaled = grad * gain
    first = jnp.mean(scaled, axis=-1, keepdims=True)
    second = jnp.mean(scaled * unit, axis=-1, keepdims=True)
    grad_rows = rstd * (scaled - first - unit * second)
    return grad_rows, jnp.sum(grad * unit, axis=0), jnp.sum(grad, axis=0)


def feature_map(rows):
    halves = jnp.concatenate([jax.nn.softplus(rows), jax.nn.softplus(-rows)], axis=-1)
    return jnp.concatenate([halves * jnp.roll(halves, j, axis=-1) for j in (1, 2, 3)], axis=-1)


def gelu_tanh(rows):
    return jax.nn.gelu(rows, approximate=True)


def dot_dims(a, b, ca, cb, precision=None):
    return lax.dot_general(
        a, b, (((ca,), (cb,)), ((), ())), precision=precision, preferred_element_type=F32
    )


exact = functools.partial(dot_dims, precision=lax.Precision.HIGHEST)


def head_rows(scale):
    lane = lax.broadcasted_iota(jnp.int32, (1, 2 * HD), 1)
    low = jnp.where(lane < HD, scale, 0.0).astype(BF16)
    high = jnp.where(lane < HD, 0.0, scale).astype(BF16)
    return low, high


def causal_tail(scores, first):
    key = lax.broadcasted_iota(jnp.int32, scores.shape, 0)
    query = lax.broadcasted_iota(jnp.int32, scores.shape, 1)
    return jnp.where(key - first <= query, scores, 0.0)


def attn_fwd_kernel(q_ref, k_ref, v_ref, km_ref, vm_ref, o_ref, lse_ref, keys, vals_t, vmem_t):
    mem = km_ref.shape[0]
    rows = q_ref.shape[0]
    keys[0:mem, :] = km_ref[...]
    keys[mem:, :] = k_ref[...]
    vals_t[...] = v_ref[...].T
    vmem_t[...] = vm_ref[...].T
    picks = head_rows(HD**-0.5)
    for part in range(rows // CHUNK):
        lo, hi = part * CHUNK, (part + 1) * CHUNK
        query = q_ref[lo:hi, :]
        outs = []
        for head in range(2):
            band = slice(head * HD, (head + 1) * HD)
            scores = dot_dims(keys[0 : mem + hi, :], query * picks[head], 1, 1)
            raw = jnp.exp(scores)
            tail = causal_tail(raw[mem + lo :], 0)
            if lo:
                raw = jnp.concatenate([raw[: mem + lo], tail], axis=0)
            else:
                raw = jnp.concatenate([raw[:mem], tail], axis=0)
            total = jnp.sum(raw, axis=0, keepdims=True)
            lse_ref[0, head : head + 1, lo:hi] = jnp.log(total)
            weights = (raw * (1.0 / total)).astype(BF16)
            outs.append(
                dot_dims(vals_t[band, 0:hi], weights[mem:], 1, 0)
                + dot_dims(vmem_t[band, :], weights[:mem], 1, 0)
            )
        o_ref[lo:hi, :] = jnp.concatenate(outs, axis=0).T.astype(BF16)


def attn_fwd_after_kernel(q_ref, k_ref, v_ref, km_ref, vm_ref, held_ref, *rest):
    del held_ref
    attn_fwd_kernel(q_ref, k_ref, v_ref, km_ref, vm_ref, *rest)


def attn_fwd(qkv, kv_mem, seg, rows, held):
    width = qkv.shape[1] // 3
    mem = kv_mem.shape[0]
    pairs = H // 2
    wide = 2 * HD
    spec = lambda off: pl.BlockSpec((rows, wide), lambda p, off=off: (seg, off * pairs + p))
    mspec = lambda off: pl.BlockSpec((mem, wide), lambda p, off=off: (0, off * pairs + p))
    more = [] if held is None else [held]
    return pl.pallas_call(
        attn_fwd_kernel if held is None else attn_fwd_after_kernel,
        grid=(pairs,),
        in_specs=[spec(0), spec(1), spec(2), mspec(0), mspec(1)]
        + [pl.BlockSpec(memory_space=pl.ANY)] * len(more),
        out_specs=[
            pl.BlockSpec((rows, wide), lambda p: (seg, p)),
            pl.BlockSpec((1, 2, rows), lambda p: (p, 0, 0)),
        ],
        out_shape=[
            jax.ShapeDtypeStruct((qkv.shape[0], width), BF16),
            jax.ShapeDtypeStruct((pairs, 2, rows), F32),
        ],
        scratch_shapes=[
            pltpu.VMEM((mem + rows, wide), BF16),
            pltpu.VMEM((wide, rows), BF16),
            pltpu.VMEM((wide, mem), BF16),
        ],
        input_output_aliases={5: 0} if more else {},
        compiler_params=pltpu.CompilerParams(vmem_limit_bytes=40 * 2**20),
        cost_estimate=pl.CostEstimate(
            flops=pairs * rows * rows * 4000,
            bytes_accessed=rows * width * 8,
            transcendentals=0,
        ),
        name="attn_fwd",
    )(qkv, qkv, qkv, kv_mem, kv_mem, *more)


def attn_mem_kernel(q_ref, km_ref, vm_ref, o_ref, g_ref, lse_ref, dkm_ref, dvm_ref, mid_ref):
    scaled_picks, picks = head_rows(HD**-0.5), head_rows(1.0)
    grad, query = g_ref[...], q_ref[...]
    inner = (grad.astype(F32) * o_ref[...].astype(F32)).T
    dk, dv = 0.0, 0.0
    for head in range(2):
        band = slice(head * HD, (head + 1) * HD)
        query_h, grad_h = query * scaled_picks[head], grad * picks[head]
        centre = jnp.sum(inner[band], axis=0, keepdims=True)
        mid_ref[0, head : head + 1, :] = centre
        prob = jnp.exp(dot_dims(km_ref[0], query_h, 1, 1) - lse_ref[0, head : head + 1, :])
        grad_s = (prob * (dot_dims(vm_ref[0], grad_h, 1, 1) - centre)).astype(BF16)
        dv = dv + dot_dims(prob.astype(BF16), grad_h, 1, 0)
        dk = dk + dot_dims(grad_s, query_h, 1, 0)
    dkm_ref[0] = dk
    dvm_ref[0] = dv


def attn_mem(qkv, kv_mem, attended, grad, lse):
    segs, pairs, mem, wide = kv_mem.shape[0], H // 2, kv_mem.shape[1], 2 * HD
    rows, width = lse.shape[2], qkv.shape[1] // 3
    spec = pl.BlockSpec((rows, wide), lambda s, p: (s, p))
    mspec = lambda off: pl.BlockSpec((1, mem, wide), lambda s, p, off=off: (s, 0, off * pairs + p))
    lspec = pl.BlockSpec((1, 2, rows), lambda s, p: (s * pairs + p, 0, 0))
    return pl.pallas_call(
        attn_mem_kernel,
        grid=(segs, pairs),
        in_specs=[spec, mspec(0), mspec(1), spec, spec, lspec],
        out_specs=[mspec(0), mspec(0), lspec],
        out_shape=[
            jax.ShapeDtypeStruct((segs, mem, width), F32),
            jax.ShapeDtypeStruct((segs, mem, width), F32),
            jax.ShapeDtypeStruct((segs * pairs, 2, rows), F32),
        ],
        compiler_params=pltpu.CompilerParams(vmem_limit_bytes=40 * 2**20),
        cost_estimate=pl.CostEstimate(
            flops=segs * rows * width * 4000, bytes_accessed=segs * rows * width * 6, transcendentals=0
        ),
        name="attn_mem",
    )(qkv, kv_mem, kv_mem, attended, grad, lse)


def attn_bwd_kernel(
    q_ref, k_ref, v_ref, km_ref, vm_ref, g_ref, lse_ref, mid_ref,
    out_ref,
    keys, vals, keys_t, kmem_t, dq, dk, dv,
):
    phase = pl.program_id(1)
    mem = km_ref.shape[0]
    rows = q_ref.shape[0]

    @pl.when(phase == 0)
    def _():
        keys[0:mem, :] = km_ref[...]
        keys[mem:, :] = k_ref[...]
        vals[0:mem, :] = vm_ref[...]
        vals[mem:, :] = v_ref[...]
        keys_t[...] = k_ref[...].T
        kmem_t[...] = km_ref[...].T
        dk[...] = jnp.zeros_like(dk)
        dv[...] = jnp.zeros_like(dv)
        scaled_picks = head_rows(HD**-0.5)
        picks = head_rows(1.0)
        for part in range(rows // CHUNK):
            lo, hi = part * CHUNK, (part + 1) * CHUNK
            end = mem + hi
            query = q_ref[lo:hi, :]
            grad = g_ref[lo:hi, :]
            dqs = []
            for head in range(2):
                band = slice(head * HD, (head + 1) * HD)
                query_h = query * scaled_picks[head]
                grad_h = grad * picks[head]
                log_total = lse_ref[0, head : head + 1, lo:hi]
                centre = mid_ref[0, head : head + 1, lo:hi]
                prob = jnp.exp(dot_dims(keys[0:end, :], query_h, 1, 1) - log_total)
                prob = jnp.concatenate(
                    [prob[: mem + lo], causal_tail(prob[mem + lo :], 0)], axis=0
                )
                grad_p = dot_dims(vals[0:end, :], grad_h, 1, 1)
                grad_s = (prob * (grad_p - centre)).astype(BF16)
                dv[0:end, :] += dot_dims(prob.astype(BF16), grad_h, 1, 0)
                dk[0:end, :] += dot_dims(grad_s, query_h, 1, 0)
                dqs.append(
                    dot_dims(keys_t[band, 0:hi], grad_s[mem:], 1, 0)
                    + dot_dims(kmem_t[band, :], grad_s[:mem], 1, 0)
                )
            dq[lo:hi, :] = (jnp.concatenate(dqs, axis=0) * HD**-0.5).T.astype(BF16)
        out_ref[...] = dq[...]

    @pl.when(phase == 1)
    def _():
        out_ref[...] = dk[mem:, :].astype(BF16)

    @pl.when(phase == 2)
    def _():
        out_ref[...] = dv[mem:, :].astype(BF16)


def attn_bwd(qkv, kv_mem, grad, lse, middle, seg, first, count):
    pairs = H // 2
    rows, width = lse.shape[2], qkv.shape[1] // 3
    mem = kv_mem.shape[0]
    wide = 2 * HD
    spec = lambda off: pl.BlockSpec((rows, wide), lambda p, f, off=off: (seg, off * pairs + first + p))
    mspec = lambda off: pl.BlockSpec((mem, wide), lambda p, f, off=off: (0, off * pairs + first + p))
    lspec = pl.BlockSpec((1, 2, rows), lambda p, f: (seg * pairs + first + p, 0, 0))
    return pl.pallas_call(
        attn_bwd_kernel,
        grid=(count, 3),
        in_specs=[
            spec(0), spec(1), spec(2), mspec(0), mspec(1), spec(0), lspec, lspec,
        ],
        out_specs=pl.BlockSpec((rows, wide), lambda p, f: (0, f * count + p)),
        out_shape=jax.ShapeDtypeStruct((rows, 3 * count * wide), BF16),
        scratch_shapes=[
            pltpu.VMEM((mem + rows, wide), BF16),
            pltpu.VMEM((mem + rows, wide), BF16),
            pltpu.VMEM((wide, rows), BF16),
            pltpu.VMEM((wide, mem), BF16),
            pltpu.VMEM((rows, wide), BF16),
            pltpu.VMEM((mem + rows, wide), F32),
            pltpu.VMEM((mem + rows, wide), F32),
        ],
        compiler_params=pltpu.CompilerParams(vmem_limit_bytes=48 * 2**20),
        cost_estimate=pl.CostEstimate(
            flops=count * rows * rows * 6500,
            bytes_accessed=rows * count * wide * 18,
            transcendentals=0,
        ),
        name="attn_bwd",
    )(qkv, qkv, qkv, kv_mem, kv_mem, grad, lse, middle)


def choose(told, kept, got, out):
    own = pl.program_id(0) % 2 == told[1]

    @pl.when(own)
    def _():
        out[...] = kept[0]

    @pl.when(jnp.logical_not(own))
    def _():
        out[...] = got[0]


def half_specs(rows, width):
    return [pl.BlockSpec((1, rows, width), lambda i, told: ((i // 2) ^ told[0], 0, 0))] * 2


def enter_kernel(told, kept, got, gain, bias, weight, shift, rows_ref, normed_ref, qkv_ref):
    choose(told, kept, got, rows_ref)
    unit, _ = norm_parts(rows_ref[...].astype(F32))
    normed = (unit * gain[...] + bias[...]).astype(BF16)
    normed_ref[...] = normed
    wide = weight.shape[1] // 3
    for k in range(3):
        at = slice(k * wide, (k + 1) * wide)
        qkv_ref[:, at] = (dot_dims(normed, weight[:, at], 1, 0) + shift[:, at]).astype(BF16)


def enter(told, kept, got, gain, bias, weight, shift):
    segs, rows, width = kept.shape
    whole = lambda r, c: pl.BlockSpec((r, c), lambda i, told: (0, 0), pipeline_mode=pl.Buffered(1))
    block = lambda c: pl.BlockSpec((rows, c), lambda i, told: (i, 0))
    sizes = (width, width, 3 * width)
    return pl.pallas_call(
        enter_kernel,
        grid_spec=pltpu.PrefetchScalarGridSpec(
            num_scalar_prefetch=1,
            grid=(2 * segs,),
            in_specs=[*half_specs(rows, width), whole(1, width), whole(1, width), whole(width, 3 * width), whole(1, 3 * width)],
            out_specs=[block(c) for c in sizes],
        ),
        out_shape=[jax.ShapeDtypeStruct((2 * segs * rows, c), BF16) for c in sizes],
        compiler_params=pltpu.CompilerParams(vmem_limit_bytes=48 * 2**20),
        cost_estimate=pl.CostEstimate(
            flops=8 * segs * rows * width * width * 3, bytes_accessed=segs * rows * width * 28, transcendentals=0
        ),
        name="enter",
    )(told, kept, got, gain[None], bias[None], weight, shift[None])


def middle_kernel(
    told, kept, got, rows_ref, attended, out_w, expand_w, contract_w, out_b, gain, bias, expand_b, contract_b,
    result_ref, cot_ref, normed_ref, activ_ref, grad_exp_ref, grad_out_ref, grad_att_ref,
    sums_ref, exp_sums_ref,
):
    choose(told, kept, got, cot_ref)
    cot = cot_ref[...]
    after = rows_ref[...].astype(F32) + dot_dims(attended[...], out_w[...], 1, 0) + out_b[...]
    unit, rstd = norm_parts(after)
    normed = (unit * gain[...] + bias[...]).astype(BF16)
    normed_ref[...] = normed
    total = after + contract_b[...]
    back = 0.0

    @pl.when(pl.program_id(0) == 0)
    def _():
        sums_ref[...] = jnp.zeros_like(sums_ref)
        exp_sums_ref[...] = jnp.zeros_like(exp_sums_ref)

    parts = 6
    wide = expand_w.shape[1] // parts
    bend, cube = 0.7978845608028654, 0.044715
    for part in range(parts):
        at = slice(part * wide, (part + 1) * wide)
        value = dot_dims(normed, expand_w[:, at], 1, 0) + expand_b[:, at]
        square = value * value
        curve = jnp.tanh(bend * value * (1.0 + cube * square))
        half = 0.5 * (1.0 + curve)
        activ = (value * half).astype(BF16)
        activ_ref[:, at] = activ
        slope = half + 0.5 * bend * value * (1.0 - curve * curve) * (1.0 + 3.0 * cube * square)
        grad = (dot_dims(cot, contract_w[:, at], 1, 0) * slope).astype(BF16)
        grad_exp_ref[:, at] = grad
        exp_sums_ref[:, at] += jnp.sum(grad.astype(F32), axis=0, keepdims=True)
        total = total + dot_dims(activ, contract_w[:, at], 1, 1)
        back = back + dot_dims(grad, expand_w[:, at], 1, 1)
    result_ref[...] = total.astype(BF16)
    wide_cot = cot.astype(F32)
    grad_rows, gain_sum, bias_sum = norm_back(back, unit, rstd, gain[...])
    grad_out = (grad_rows + wide_cot).astype(BF16)
    grad_out_ref[...] = grad_out
    grad_att_ref[...] = dot_dims(grad_out, out_w[...], 1, 1).astype(BF16)
    sums = (
        jnp.sum(grad_out.astype(F32), axis=0, keepdims=True),
        gain_sum[None],
        bias_sum[None],
        jnp.sum(wide_cot, axis=0, keepdims=True),
    )
    for k, value in enumerate(sums):
        sums_ref[k : k + 1, :] += value


def middle(told, kept, got, rows_in, attended, out_w, expand_w, contract_w, out_b, gain, bias, expand_b, contract_b):
    segs, rows, width = kept.shape
    wide = expand_w.shape[1]
    whole = lambda r, c: pl.BlockSpec((r, c), lambda i, told: (0, 0), pipeline_mode=pl.Buffered(1))
    block = lambda c: pl.BlockSpec((rows, c), lambda i, told: (i, 0))
    sizes = (width, width, width, wide, wide, width, width)
    count = 2 * segs * rows
    fixed = lambda r, c: pl.BlockSpec((r, c), lambda i, told: (0, 0))
    return pl.pallas_call(
        middle_kernel,
        grid_spec=pltpu.PrefetchScalarGridSpec(
            num_scalar_prefetch=1,
            grid=(2 * segs,),
            in_specs=[
                *half_specs(rows, width), block(width), block(width), whole(width, width), whole(width, wide),
                whole(width, wide), whole(1, width), whole(1, width), whole(1, width), whole(1, wide), whole(1, width),
            ],
            out_specs=[*[block(c) for c in sizes], fixed(8, width), fixed(1, wide)],
        ),
        out_shape=[
            *[jax.ShapeDtypeStruct((count, c), BF16) for c in sizes],
            jax.ShapeDtypeStruct((8, width), F32),
            jax.ShapeDtypeStruct((1, wide), F32),
        ],
        compiler_params=pltpu.CompilerParams(vmem_limit_bytes=60 * 2**20),
        cost_estimate=pl.CostEstimate(
            flops=count * width * (8 * wide + 4 * width) * 2, bytes_accessed=count * (14 * width + 4 * wide), transcendentals=0
        ),
        name="middle",
    )(
        told, kept, got, rows_in, attended, out_w, expand_w, contract_w, out_b[None], gain[None], bias[None],
        expand_b[None], contract_b[None],
    )


def thirds(rows):
    parts = []
    for _ in range(3):
        parts.append(rows.astype(BF16))
        rows = rows - parts[-1].astype(F32)
    return jnp.concatenate(parts, axis=0)


def exact_low(rows, weight, side):
    count = rows.shape[0]
    out = dot_dims(thirds(rows), weight, 1, side)
    return out[:count] + out[count : 2 * count] + out[2 * count :]


def softplus(rows):
    return jnp.maximum(rows, 0.0) + jnp.log1p(jnp.exp(-jnp.abs(rows)))


def feature_parts(rows):
    halves = jnp.concatenate([softplus(rows), softplus(-rows)], axis=1)
    turned = [pltpu.roll(halves, j, 1) for j in (1, 2, 3)]
    return halves, turned, jnp.concatenate([halves * t for t in turned], axis=1)


def feature_back(rows, grad):
    halves, turned, _ = feature_parts(rows)
    wide = halves.shape[1]
    total = 0.0
    for j in (1, 2, 3):
        part = grad[:, (j - 1) * wide : j * wide]
        total = total + part * turned[j - 1] + pltpu.roll(part * halves, wide - j, 1)
    first, last = total[:, : wide // 2], total[:, wide // 2 :]
    return first * jax.nn.sigmoid(rows) - last * jax.nn.sigmoid(-rows)


def per_head(rows):
    tall = jnp.concatenate([rows] * H, axis=0)
    return tall * head_mask(tall.shape, rows.shape[0]).astype(rows.dtype)


def head_mask(shape, count):
    head = lax.broadcasted_iota(jnp.int32, shape, 0) // count
    return (lax.broadcasted_iota(jnp.int32, shape, 1) // HD == head).astype(F32)


def from_heads(tall, count):
    tall = tall * head_mask(tall.shape, count)
    total = tall[:count]
    for head in range(1, H):
        total = total + tall[head * count : (head + 1) * count]
    return total


def mem_weights(query, key):
    count = key.shape[0]
    tall = per_head(query)
    scores = dot_dims(tall, key, 1, 1) * HD**-0.5
    at = lax.rem(lax.broadcasted_iota(jnp.int32, scores.shape, 0), count)
    raw = jnp.where(lax.broadcasted_iota(jnp.int32, scores.shape, 1) <= at, jnp.exp(scores), 0.0)
    return tall, raw / jnp.sum(raw, axis=1, keepdims=True)


def read_parts(read_feat, key_feat, value_new):
    mix = exact(read_feat, key_feat, 1, 1)
    return mix, exact(mix, value_new, 1, 0), 1.0 + jnp.sum(mix, axis=1, keepdims=True)


def bring(sources, targets, sem):
    copies = [pltpu.make_async_copy(a, b, sem.at[k]) for k, (a, b) in enumerate(zip(sources, targets))]
    for copy in copies:
        copy.start()
    return copies


def mem_fwd_kernel(
    mt_ref, one_gain, one_bias, two_gain, two_bias, shift, out_b, expand_b, contract_b,
    qrk_hbm, ov_hbm, expand_hbm, contract_hbm,
    qkv_ref, attended_ref, after_ref, expanded_ref, result_ref, pre_ref, value_ref, follow_ref, kv_ref,
    qrk, ov, expand_w, contract_w, sem,
):
    copies = bring((qrk_hbm, ov_hbm, expand_hbm, contract_hbm), (qrk, ov, expand_w, contract_w), sem)
    mt = mt_ref[...]
    width = mt.shape[1]
    feat = pre_ref.shape[1] // 2
    unit, _ = norm_parts(mt)
    normed = (unit * one_gain[...] + one_bias[...]).astype(BF16)
    copies[0].wait()
    qkv = (dot_dims(normed, qrk[:, : 3 * width], 1, 0) + shift[...]).astype(BF16)
    qkv_ref[...] = qkv
    read_pre = exact_low(mt, qrk[:, 3 * width : 3 * width + feat], 0)
    _, weights = mem_weights(qkv[:, :width], qkv[:, width : 2 * width])
    mixed = dot_dims(weights.astype(BF16), qkv[:, 2 * width :], 1, 0)
    attended = from_heads(mixed, mt.shape[0]).astype(BF16)
    attended_ref[...] = attended
    copies[1].wait()
    after = mt + dot_dims(attended, ov[:, :width], 1, 0) + out_b[...]
    after_ref[...] = after
    unit, _ = norm_parts(after)
    normed = (unit * two_gain[...] + two_bias[...]).astype(BF16)
    copies[2].wait()
    expanded = dot_dims(normed, expand_w[...], 1, 0) + expand_b[...]
    expanded_ref[...] = expanded
    activ = gelu_tanh(expanded).astype(BF16)
    copies[3].wait()
    result = after + dot_dims(activ, contract_w[...], 1, 1) + contract_b[...]
    result_ref[...] = result
    key_pre = exact_low(result, qrk[:, 3 * width + feat :], 0)
    value_new = exact_low(result, ov[:, width:], 0)
    value_ref[...] = value_new
    pre_ref[:, :feat] = read_pre
    pre_ref[:, feat:] = key_pre
    _, numer, denom = read_parts(feature_parts(read_pre)[2], feature_parts(key_pre)[2], value_new)
    follow = mt + numer / denom
    follow_ref[...] = follow
    unit, _ = norm_parts(follow)
    normed = (unit * one_gain[...] + one_bias[...]).astype(BF16)
    kv_ref[...] = (dot_dims(normed, qrk[:, width : 3 * width], 1, 0) + shift[:, width:]).astype(BF16)


def mem_call(kernel, name, given, weights, outs, cycles):
    vmem = pl.BlockSpec(memory_space=pltpu.VMEM)
    return pl.pallas_call(
        kernel,
        in_specs=[vmem] * len(given) + [pl.BlockSpec(memory_space=pl.ANY)] * len(weights),
        out_specs=[vmem] * len(outs),
        out_shape=outs,
        scratch_shapes=[
            *[pltpu.VMEM(w.shape, w.dtype) for w in weights],
            pltpu.SemaphoreType.DMA((len(weights),)),
        ],
        compiler_params=pltpu.CompilerParams(vmem_limit_bytes=48 * 2**20),
        cost_estimate=pl.CostEstimate(flops=cycles * 10**9, bytes_accessed=17 * 10**6, transcendentals=0),
        name=name,
    )(*given, *weights)


def mem_forward(mt, given, weights):
    mem, width = mt.shape
    wide, feat = weights[2].shape[1], (weights[0].shape[1] - 3 * width) // 2
    shape = jax.ShapeDtypeStruct
    outs = [
        shape((mem, 3 * width), BF16), shape((mem, width), BF16), shape((mem, width), F32), shape((mem, wide), F32),
        shape((mem, width), F32), shape((mem, 2 * feat), F32), shape((mem, width), F32), shape((mem, width), F32),
        shape((mem, 2 * width), BF16),
    ]
    return mem_call(mem_fwd_kernel, "mem_fwd", (mt, *given), weights, outs, 15)


def mem_bwd_kernel(
    mt_ref, one_gain, one_bias, two_gain, two_bias, pooled, chosen,
    qkv_ref, attended_ref, after_ref, expanded_ref, result_ref, pre_ref, value_ref, follow_ref,
    qrk_hbm, ov_hbm, expand_hbm, contract_hbm,
    grad_mt_ref, qkv_grad, out_grad, expand_grad, contract_grad, read_grad, key_grad, value_grad, sums_ref, exp_sums_ref,
    qrk, ov, expand_w, contract_w, sem,
):
    copies = bring((qrk_hbm, ov_hbm, expand_hbm, contract_hbm), (qrk, ov, expand_w, contract_w), sem)
    mt = mt_ref[...]
    mem, width = mt.shape
    feat = pre_ref.shape[1] // 2
    sums_ref[...] = jnp.zeros_like(sums_ref)

    def add_row(k, value):
        sums_ref[k : k + 1, :] += value[None]

    def column(value):
        return jnp.sum(value.astype(F32), axis=0)

    unit_f, rstd_f = norm_parts(follow_ref[...])
    normed_f = (unit_f * one_gain[...] + one_bias[...]).astype(BF16)
    grad_f = pooled[1].astype(BF16)
    copies[0].wait()
    grad_follow, gain, bias = norm_back(
        dot_dims(grad_f, qrk[:, width : 3 * width], 1, 1), unit_f, rstd_f, one_gain[...]
    )
    add_row(0, gain)
    add_row(1, bias)
    add_row(3, column(grad_f[:, width:]))
    read_pre, key_pre, value_new = pre_ref[:, :feat], pre_ref[:, feat:], value_ref[...]
    read_feat, key_feat = feature_parts(read_pre)[2], feature_parts(key_pre)[2]
    mix, numer, denom = read_parts(read_feat, key_feat, value_new)
    grad_numer = grad_follow / denom
    grad_denom = -jnp.sum(grad_follow * numer, axis=1, keepdims=True) / (denom * denom)
    grad_mix = exact(grad_numer, value_new, 1, 1) + grad_denom
    grad_value = exact(mix, grad_numer, 0, 0)
    grad_read_pre = feature_back(read_pre, exact(grad_mix, key_feat, 1, 0))
    grad_key_pre = feature_back(key_pre, exact(grad_mix, read_feat, 0, 0))
    grad_mt = grad_follow + exact_low(grad_read_pre, qrk[:, 3 * width : 3 * width + feat], 1)
    copies[1].wait()
    grad_result = exact_low(grad_key_pre, qrk[:, 3 * width + feat :], 1) + exact_low(
        grad_value, ov[:, width:], 1
    )
    grad_contract = grad_result.astype(BF16)
    add_row(7, column(grad_contract))
    expanded = expanded_ref[...]
    bend, cube = 0.7978845608028654, 0.044715
    square = expanded * expanded
    curve = jnp.tanh(bend * expanded * (1.0 + cube * square))
    half = 0.5 * (1.0 + curve)
    activ = (expanded * half).astype(BF16)
    slope = half + 0.5 * bend * expanded * (1.0 - curve * curve) * (1.0 + 3.0 * cube * square)
    copies[3].wait()
    grad_expanded = (dot_dims(grad_contract, contract_w[...], 1, 0) * slope).astype(BF16)
    exp_sums_ref[...] = column(grad_expanded)[None]
    unit_b, rstd_b = norm_parts(after_ref[...])
    normed_b = (unit_b * two_gain[...] + two_bias[...]).astype(BF16)
    copies[2].wait()
    grad_after, gain, bias = norm_back(
        dot_dims(grad_expanded, expand_w[...], 1, 1), unit_b, rstd_b, two_gain[...]
    )
    add_row(5, gain)
    add_row(6, bias)
    grad_after = grad_after + grad_result
    grad_attn_out = grad_after.astype(BF16)
    add_row(4, column(grad_attn_out))
    grad_attended = dot_dims(grad_attn_out, ov[:, :width], 1, 1).astype(BF16)
    query, key, value = (qkv_ref[:, k * width : (k + 1) * width] for k in range(3))
    tall, weights = mem_weights(query, key)
    grad_tall = per_head(grad_attended)
    grad_weights = dot_dims(grad_tall, value, 1, 1)
    centre = jnp.sum(weights * grad_weights, axis=1, keepdims=True)
    grad_s = (weights * (grad_weights - centre) * HD**-0.5).astype(BF16)
    grad_qkv = jnp.concatenate(
        [
            from_heads(dot_dims(grad_s, key, 1, 0), mem),
            dot_dims(grad_s, tall, 0, 0) + pooled[0, :, :width],
            dot_dims(weights.astype(BF16), grad_tall, 0, 0) + pooled[0, :, width:],
        ],
        axis=1,
    ).astype(BF16)
    add_row(2, column(grad_qkv[:, :width]))
    add_row(3, column(grad_qkv[:, 2 * width :]))
    unit, rstd = norm_parts(mt)
    normed = (unit * one_gain[...] + one_bias[...]).astype(BF16)
    grad_first, gain, bias = norm_back(
        dot_dims(grad_qkv, qrk[:, : 3 * width], 1, 1), unit, rstd, one_gain[...]
    )
    add_row(0, gain)
    add_row(1, bias)
    grad_mt_ref[...] = grad_mt + grad_first + grad_after

    pick_low = lambda a: dot_dims(a, chosen[...], 1, 0).astype(BF16)
    pick_exact = lambda a: exact_low(a, chosen[...], 0)
    qkv_grad[...] = dot_dims(pick_low(normed), grad_qkv, 0, 0)
    qkv_grad[:, width:] += dot_dims(pick_low(normed_f), grad_f, 0, 0)
    out_grad[...] = dot_dims(pick_low(attended_ref[...]), grad_attn_out, 0, 0)
    expand_grad[...] = dot_dims(pick_low(normed_b), grad_expanded, 0, 0)
    contract_grad[...] = dot_dims(pick_low(grad_contract), activ, 0, 0)
    my_result = pick_exact(result_ref[...])
    read_grad[...] = exact(pick_exact(mt), grad_read_pre, 0, 0)
    key_grad[...] = exact(my_result, grad_key_pre, 0, 0)
    value_grad[...] = exact(my_result, grad_value, 0, 0)


def mem_backward(mt, norms, pooled, shard, group, kept, weights):
    mem, width = mt.shape
    wide, feat = weights[2].shape[1], (weights[0].shape[1] - 3 * width) // 2
    at = lax.broadcasted_iota(jnp.int32, (width, shard), 0) - group * shard
    chosen = (at == lax.broadcasted_iota(jnp.int32, (width, shard), 1)).astype(BF16)
    sizes = (3 * width, width, wide, wide, feat, feat, width)
    shape = jax.ShapeDtypeStruct
    outs = [
        shape((mem, width), F32), *[shape((shard, c), F32) for c in sizes], shape((8, width), F32), shape((1, wide), F32),
    ]
    grad_mt, *rest = mem_call(
        mem_bwd_kernel, "mem_bwd", (mt, *norms, pooled, chosen, *kept), weights, outs, 25
    )
    sums, expand_sums = rest[7:]
    vectors = (sums[0], sums[1], sums[2:4], sums[4], sums[5], sums[6], expand_sums[0], sums[7])
    return grad_mt, tuple(rest[:7]), vectors


def gather_kernel(halved, count, kinds, *refs):
    shards, outs = refs[:count], refs[count : 2 * count]
    send_sem, recv_sem, local_sem = refs[2 * count :]
    index, plane = lax.axis_index("dp"), lax.axis_index("ctx")
    deep, cross, core = index // 4, (index // 2) % 2, index % 2
    place = lambda z, x, c: (z * 2 + x) * 2 + c
    up, down = {"dp": place(deep + 1, cross, core)}, {"dp": place(deep - 1, cross, core)}
    beside, sibling = {"dp": place(deep, 1 - cross, core)}, {"dp": place(deep, cross, 1 - core)}
    other = {"ctx": 1 - plane}
    rows = shards[0].shape[0]
    numbers, sends = {}, []

    def valid(kind):
        way, far = kind
        return deep >= 0 if way == "own" else deep >= far if way == "below" else deep + far <= 3

    def level(kind):
        way, far = kind
        return deep if way == "own" else deep - far if way == "below" else deep + far

    def view(k, z, x, c, part):
        at = pl.ds(pl.multiple_of(place(z, x, c) * rows, 16), rows)
        return outs[k].at[at, :] if part is None else outs[k].at[at, half(k, part)]

    def half(k, part):
        wide = outs[k].shape[1] // 2
        return pl.ds(pl.multiple_of(part * wide, 128), wide)

    def copy(key, source, landing, device):
        number = numbers.setdefault(key, len(numbers))
        return pltpu.make_async_remote_copy(
            source, landing, send_sem.at[number], recv_sem.at[number],
            device_id=device, device_id_type=pl.DeviceIdType.MESH,
        )

    def send(when, key, source, landing, device):
        def begin():
            copy(key, source, landing, device).start()

        def end():
            copy(key, source, landing, device).wait_send()

        sends.append((when, end))
        if when is None:
            begin()
        else:
            pl.when(when)(begin)

    def arrived(key, landing):
        copy(key, landing, landing, sibling).wait_recv()

    barrier = pltpu.get_barrier_semaphore()
    for device in (beside, sibling, other):
        pl.semaphore_signal(barrier, inc=1, device_id=device, device_id_type=pl.DeviceIdType.MESH)
    for when, device in ((deep < 3, up), (deep > 0, down)):

        @pl.when(when)
        def _(device=device):
            pl.semaphore_signal(barrier, inc=1, device_id=device, device_id_type=pl.DeviceIdType.MESH)

    inner = (deep > 0) & (deep < 3)
    for when, peers in ((inner, 5), (jnp.logical_not(inner), 4)):

        @pl.when(when)
        def _(peers=peers):
            pl.semaphore_wait(barrier, peers)

    own = ("own", 0)
    locals_ = []
    for k in range(count):
        part = plane if k in halved else None
        mine = view(k, deep, cross, core, None)
        locals_.append(pltpu.make_async_copy(shards[k], mine, local_sem.at[k]))
        locals_[-1].start()
        source = shards[k] if part is None else shards[k].at[:, half(k, part)]
        landing = view(k, deep, cross, core, part)
        send(deep < 3, ("z", ("below", 1), k), source, landing, up)
        send(deep > 0, ("z", ("above", 1), k), source, landing, down)
        send(None, ("x", own, k), source, landing, beside)
        send(None, ("core", "z", own, k), shards[k], mine, sibling)

    def onward(k, flow, kind, x):
        part = plane if k in halved else None
        block = view(k, level(kind), x, core, part)
        ok = valid(kind)
        if flow == "z":
            way, far = kind
            if far < 3:
                if way == "below":
                    send(ok & (deep < 3), ("z", (way, far + 1), k), block, block, up)
                else:
                    send(ok & (deep > 0), ("z", (way, far + 1), k), block, block, down)
            send(ok, ("x", kind, k), block, block, beside)
        send(ok, ("core", flow, kind, k), block, block, sibling)
        if k in halved:
            send(ok, ("y", flow, kind, k), block, block, other)

    def take(flow, kind):
        x = cross if flow == "z" else 1 - cross
        for k in range(count):
            part = plane if k in halved else None

            @pl.when(valid(kind))
            def _():
                arrived((flow, kind, k), view(k, level(kind), x, core, part))

            onward(k, flow, kind, x)

    for far in range(1, 4):
        take("z", ("below", far))
        take("z", ("above", far))
        for kind in kinds:
            if kind[1] == far - 1:
                take("x", kind)
    for kind in kinds:
        if kind[1] == 3:
            take("x", kind)
    crossing = [(flow, kind, k) for flow in ("z", "x") for kind in kinds for k in halved]
    crossing = [c for c in crossing if c[:2] != ("z", own)]
    for flow, kind, k in crossing:
        x = cross if flow == "z" else 1 - cross
        block = lambda c: view(k, level(kind), x, c, 1 - plane)

        @pl.when(valid(kind))
        def _():
            arrived(("y", flow, kind, k), block(core))

        send(valid(kind), ("core", "y", flow, kind, k), block(core), block(core), sibling)
    for flow in ("z", "x"):
        x = cross if flow == "z" else 1 - cross
        for kind in kinds:
            for k in range(count):
                part = plane if k in halved and (flow, kind) != ("z", own) else None

                @pl.when(valid(kind))
                def _():
                    arrived(("core", flow, kind, k), view(k, level(kind), x, 1 - core, part))

    for flow, kind, k in crossing:
        x = cross if flow == "z" else 1 - cross

        @pl.when(valid(kind))
        def _():
            arrived(("core", "y", flow, kind, k), view(k, level(kind), x, 1 - core, 1 - plane))

    for when, end in sends:
        if when is None:
            end()
        else:
            pl.when(when)(end)
    for held in locals_:
        held.wait()


def gather_weights(shards, halved):
    kinds = [("own", 0)] + [(way, far) for far in (1, 2, 3) for way in ("below", "above")]
    count = len(shards)
    rows = shards[0].shape[0] * 16
    copies = 6 * count + 7 * count + 13 * len(halved) + 14 * count + 13 * len(halved)
    any_space = pl.BlockSpec(memory_space=pl.ANY)
    return pl.pallas_call(
        functools.partial(gather_kernel, halved, count, kinds),
        in_specs=[any_space] * count,
        out_specs=[any_space] * count,
        out_shape=[jax.ShapeDtypeStruct((rows, s.shape[1]), BF16) for s in shards],
        scratch_shapes=[
            pltpu.SemaphoreType.DMA((copies,)),
            pltpu.SemaphoreType.DMA((copies,)),
            pltpu.SemaphoreType.DMA((count,)),
        ],
        compiler_params=pltpu.CompilerParams(
            collective_id=0, has_side_effects=True, vmem_limit_bytes=4 * 2**20
        ),
        cost_estimate=pl.CostEstimate(
            flops=8 * 10**10, bytes_accessed=4 * rows * sum(s.shape[1] for s in shards), transcendentals=0
        ),
        name="gather_weights",
    )(*shards)


def dp_pairs(flip):
    return [(i, i ^ flip) for i in range(16)]


def behind(value, *earlier):
    return lax.optimization_barrier((value, earlier))[0]


def pick(parts, at, axis):
    return lax.dynamic_index_in_dim(parts, at, axis, keepdims=False)


def add_low(a, b):
    return (a.astype(F32) + b.astype(F32)).astype(BF16)


class Scatter:
    def __init__(self, grad):
        index = lax.axis_index("dp")
        self.deep, self.cross, self.core = index // 4, (index // 2) % 2, index % 2
        parts = grad.reshape(4, 2, 2, grad.shape[0] // 16, grad.shape[1])
        self.keep, self.give = pick(parts, self.core, 2), pick(parts, 1 - self.core, 2)

    def over_core(self, *beside):
        got = behind(lax.ppermute(self.give, "dp", dp_pairs(1)), *beside)
        parts = add_low(self.keep, got)
        self.keep, self.give = pick(parts, self.cross, 1), pick(parts, 1 - self.cross, 1)
        return self

    def over_x(self, *beside):
        got = behind(lax.ppermute(self.give, "dp", dp_pairs(2)), *beside)
        parts = add_low(self.keep, got)
        self.keep = pick(parts, self.deep, 0)
        self.give = tuple(pick(parts, self.deep ^ k, 0) for k in (1, 2, 3))
        return self

    def over_z(self, *beside):
        far = [lax.ppermute(self.give[k - 1], "dp", dp_pairs(4 * k)) for k in (1, 2, 3)]
        total = self.keep.astype(F32)
        for part in behind(far, *beside):
            total = total + part.astype(F32)
        self.keep = self.give = total.astype(BF16)
        return self

    def over_y(self, *beside):
        got = behind(lax.ppermute(self.give, "ctx", [(0, 1), (1, 0)]), *beside)
        return self.keep.astype(F32) + got.astype(F32)


def sum_over(flat, step, *beside):
    if step == 0:
        return flat + behind(lax.ppermute(flat, "ctx", [(0, 1), (1, 0)]), *beside)
    if step < 3:
        return flat + behind(lax.ppermute(flat, "dp", dp_pairs(step)), *beside)
    far = behind([lax.ppermute(flat, "dp", dp_pairs(4 * k)) for k in (1, 2, 3)], *beside)
    return (flat + far[0]) + (far[1] + far[2])


def split_heads(rows):
    return rows.reshape(rows.shape[0], rows.shape[1], H, HD)


def plain_scores(query, key, allowed):
    scores = jnp.einsum("sqhd,skhd->shqk", query, key, preferred_element_type=F32) * HD**-0.5
    return scores, allowed[None, None]


def plain_fwd(qkv, kv_all, allowed):
    width = qkv.shape[2] // 3
    query = split_heads(qkv[:, :, :width])
    key, value = split_heads(kv_all[:, :, :width]), split_heads(kv_all[:, :, width:])
    scores, allowed = plain_scores(query, key, allowed)
    raw = jnp.where(allowed, jnp.exp(scores), 0.0)
    total = jnp.sum(raw, axis=-1)
    weights = (raw / total[..., None]).astype(BF16)
    mixed = jnp.einsum("shqk,skhd->sqhd", weights, value, preferred_element_type=F32)
    return mixed.reshape(qkv.shape[0], -1, width).astype(BF16), jnp.log(total)


def plain_bwd(qkv, kv_all, allowed, log_total, grad):
    segs, width = qkv.shape[0], qkv.shape[2] // 3
    query = split_heads(qkv[:, :, :width])
    key, value = split_heads(kv_all[:, :, :width]), split_heads(kv_all[:, :, width:])
    grad = split_heads(grad)
    scores, allowed = plain_scores(query, key, allowed)
    prob = jnp.where(allowed, jnp.exp(scores - log_total[..., None]), 0.0)
    grad_p = jnp.einsum("sqhd,skhd->shqk", grad, value, preferred_element_type=F32)
    inner = jnp.sum(prob * grad_p, axis=-1, keepdims=True)
    grad_s = (prob * (grad_p - inner) * HD**-0.5).astype(BF16)
    dq = jnp.einsum("shqk,skhd->sqhd", grad_s, key, preferred_element_type=F32)
    dk = jnp.einsum("shqk,sqhd->skhd", grad_s, query, preferred_element_type=F32)
    dv = jnp.einsum("shqk,sqhd->skhd", prob.astype(BF16), grad, preferred_element_type=F32)
    flat = lambda a: a.reshape(segs, -1, width)
    return flat(dq), jnp.concatenate([flat(dk), flat(dv)], axis=2)


def memory_forward(mt, p):
    mem = mt.shape[0]
    keep = {}
    width = mt.shape[1]
    unit, rstd = norm_parts(mt)
    normed = (unit * p["one_gain"] + p["one_bias"]).astype(BF16)
    qkv = (dot_dims(normed, p["qkv"], 1, 0) + p["shift"]).astype(BF16)
    at = jnp.arange(mem, dtype=jnp.int32)
    allowed = at[None, :] <= at[:, None]
    attended, log_total = plain_fwd(qkv[None], qkv[None, :, width:], allowed)
    attended = attended[0]
    after = mt + dot_dims(attended, p["out"], 1, 0) + p["out_bias"]
    unit_b, rstd_b = norm_parts(after)
    normed_b = (unit_b * p["two_gain"] + p["two_bias"]).astype(BF16)
    expanded = dot_dims(normed_b, p["expand"], 1, 0) + p["expand_bias"]
    activ = gelu_tanh(expanded).astype(BF16)
    result = after + dot_dims(activ, p["contract"], 1, 1) + p["contract_bias"]
    key_pre = exact(result, p["key"].astype(F32), 1, 0)
    value_new = exact(result, p["value"].astype(F32), 1, 0)
    read_pre = exact(mt, p["read"].astype(F32), 1, 0)
    key_feat, key_pull = jax.vjp(feature_map, key_pre)
    read_feat, read_pull = jax.vjp(feature_map, read_pre)
    mix = exact(read_feat, key_feat, 1, 1)
    numer = exact(mix, value_new, 1, 0)
    denom = 1.0 + jnp.sum(mix, axis=1, keepdims=True)
    follow = mt + numer / denom
    unit_f, rstd_f = norm_parts(follow)
    normed_f = (unit_f * p["one_gain"] + p["one_bias"]).astype(BF16)
    kv_follow = (dot_dims(normed_f, p["qkv"][:, width:], 1, 0) + p["shift"][width:]).astype(BF16)
    keep = dict(
        unit=unit, rstd=rstd, normed=normed, qkv=qkv, allowed=allowed, attended=attended,
        log_total=log_total, unit_b=unit_b, rstd_b=rstd_b, normed_b=normed_b, expanded=expanded,
        activ=activ, result=result, key_feat=key_feat, read_feat=read_feat, key_pull=key_pull,
        read_pull=read_pull, value_new=value_new, mix=mix, numer=numer, denom=denom, unit_f=unit_f,
        rstd_f=rstd_f, normed_f=normed_f,
    )
    return qkv[:, width:], kv_follow, keep


def memory_backward(mt, p, m, grad_kv_first, grad_kv_follow, mine):
    width = mt.shape[1]
    low = lambda a: a.astype(BF16)
    grad_f = low(grad_kv_follow)
    grad_follow, gain_f, bias_f = norm_back(
        dot_dims(grad_f, p["qkv"][:, width:], 1, 1), m["unit_f"], m["rstd_f"], p["one_gain"]
    )
    grad_mt = grad_follow
    grad_numer = grad_follow / m["denom"]
    grad_denom = -jnp.sum(grad_follow * m["numer"], axis=1, keepdims=True) / (m["denom"] * m["denom"])
    grad_mix = exact(grad_numer, m["value_new"], 1, 1) + grad_denom
    grad_value = exact(m["mix"], grad_numer, 0, 0)
    [grad_read_pre] = m["read_pull"](exact(grad_mix, m["key_feat"], 1, 0))
    [grad_key_pre] = m["key_pull"](exact(grad_mix, m["read_feat"], 0, 0))
    grad_mt = grad_mt + exact(grad_read_pre, p["read"].astype(F32), 1, 1)
    grad_result = exact(grad_key_pre, p["key"].astype(F32), 1, 1) + exact(
        grad_value, p["value"].astype(F32), 1, 1
    )
    grad_contract = low(grad_result)
    _, gelu_pull = jax.vjp(gelu_tanh, m["expanded"])
    grad_expanded = low(gelu_pull(dot_dims(grad_contract, p["contract"], 1, 0))[0])
    grad_after, two_gain, two_bias = norm_back(
        dot_dims(grad_expanded, p["expand"], 1, 1), m["unit_b"], m["rstd_b"], p["two_gain"]
    )
    grad_after = grad_after + grad_result
    grad_attn_out = low(grad_after)
    grad_attended = low(dot_dims(grad_attn_out, p["out"], 1, 1))
    dq, dkv = plain_bwd(
        m["qkv"][None], m["qkv"][None, :, width:], m["allowed"], m["log_total"], grad_attended[None]
    )
    grad_qkv = low(jnp.concatenate([dq[0], dkv[0] + grad_kv_first], axis=1))
    grad_first, gain_a, bias_a = norm_back(
        dot_dims(grad_qkv, p["qkv"], 1, 1), m["unit"], m["rstd"], p["one_gain"]
    )
    grad_mt = grad_mt + grad_first + grad_after
    wide = grad_qkv.astype(F32)
    kv_rows = grad_f.astype(F32)
    sums = jnp.sum(wide, axis=0)
    follow_sums = jnp.sum(kv_rows, axis=0)
    matrices = (
        dot_dims(mine(m["normed"]), grad_qkv, 0, 0)
        + jnp.concatenate(
            [
                jnp.zeros((mine(mt).shape[1], width), F32),
                dot_dims(mine(m["normed_f"]), grad_f, 0, 0),
            ],
            axis=1,
        ),
        dot_dims(mine(m["attended"]), grad_attn_out, 0, 0),
        dot_dims(mine(m["normed_b"]), grad_expanded, 0, 0),
        dot_dims(mine(grad_contract), m["activ"], 0, 0),
        exact(mine(mt), grad_read_pre, 0, 0),
        exact(mine(m["result"]), grad_key_pre, 0, 0),
        exact(mine(m["result"]), grad_value, 0, 0),
    )
    column_sum = lambda a: jnp.sum(a.astype(F32), axis=0)
    vectors = (
        gain_f + gain_a,
        bias_f + bias_a,
        jnp.stack([sums[:width], sums[2 * width :] + follow_sums[width:]]),
        column_sum(grad_attn_out),
        two_gain,
        two_bias,
        column_sum(grad_expanded),
        column_sum(grad_contract),
    )
    return grad_mt, matrices, vectors


def local(
    tokens,
    cotangent,
    placing,
    starts,
    memory_tokens,
    norm_one_gain,
    norm_one_bias,
    qkv_weight,
    qv_bias,
    out_weight,
    out_bias,
    norm_two_gain,
    norm_two_bias,
    expand_weight,
    expand_bias,
    contract_weight,
    contract_bias,
    read_weight,
    key_weight,
    value_weight,
):
    del placing
    groups, ranks = lax.axis_size("dp"), lax.axis_size("ctx")
    group, rank = lax.axis_index("dp"), lax.axis_index("ctx")
    micros, segs_local, tok_rows, width = tokens.shape
    mem = memory_tokens.shape[0]
    shard = qkv_weight.shape[0]
    quick = groups == 16 and ranks == 2 and micros == 2 and segs_local == 2 and (tok_rows * ranks) % CHUNK == 0
    names = ("qkv", "out", "expand", "contract", "read", "key", "value")
    shards = (qkv_weight, out_weight, expand_weight, contract_weight, read_weight, key_weight, value_weight)
    if quick:
        give = pick(tokens, 1 - rank, 0)
        joined = (
            jnp.concatenate([qkv_weight, read_weight, key_weight], axis=1),
            expand_weight,
            contract_weight,
            jnp.concatenate([out_weight, value_weight], axis=1),
        )
        qkv_read_key, expand_full, contract_full, out_value = gather_weights(
            behind(joined, give), (2, 3)
        )
        feat = read_weight.shape[1]
        whole = (
            qkv_read_key[:, : 3 * width],
            out_value[:, :width],
            expand_full,
            contract_full,
            qkv_read_key[:, 3 * width : 3 * width + feat],
            qkv_read_key[:, 3 * width + feat :],
            out_value[:, width:],
        )
    else:
        whole = tuple(lax.all_gather(s, "dp", axis=0, tiled=True) for s in shards)
    p = dict(zip(names, whole))
    p.update(
        one_gain=norm_one_gain, one_bias=norm_one_bias, out_bias=out_bias, two_gain=norm_two_gain,
        two_bias=norm_two_bias, expand_bias=expand_bias, contract_bias=contract_bias,
        shift=jnp.concatenate([qv_bias[0], jnp.zeros((width,), F32), qv_bias[1]]),
    )
    flags = lax.dynamic_slice_in_dim(starts, group * segs_local, segs_local, 1)

    swap = [(0, 1), (1, 0)]

    def own_and_other(rows):
        halves = rows.reshape(ranks, tok_rows, width)
        return pick(halves, rank, 0), pick(halves, 1 - rank, 0)

    def swapped(given):
        return lax.ppermute(given, "ctx", swap)

    def settle(halves, flips):
        micro_rows = []
        for micro in range(2):
            pair = [jnp.where(rank == micro, kept, got) for kept, got in halves]
            flip = flips[micro]
            micro_rows.append(
                jnp.stack([jnp.where(flip, pair[1], pair[0]), jnp.where(flip, pair[0], pair[1])])
            )
        return jnp.stack(micro_rows)

    if quick:
        flips = flags[:, 1] == 1
        flip = pick(flips, rank, 0)
        told = jnp.stack([flip.astype(jnp.int32), rank.astype(jnp.int32)])
        got = swapped(give)
        give_grad = behind(pick(cotangent, 1 - rank, 0), got, expand_full)
        flags = pick(flags, rank, 0)
        flags = jnp.where(flip, flags[::-1], flags)
        segs = segs_local
        seg_rows = ranks * tok_rows
    else:
        rows_in, rows_grad = tokens.reshape(-1, width), cotangent.reshape(-1, width)
        flags = flags.reshape(-1)
        segs = micros * segs_local
        seg_rows = tok_rows

    if quick:
        norms = tuple(v[None] for v in (norm_one_gain, norm_one_bias, norm_two_gain, norm_two_bias))
        fixed = tuple(v[None] for v in (p["shift"], out_bias, expand_bias, contract_bias))
        mem_weights_in = (qkv_read_key, out_value, expand_full, contract_full)
        *kept, kv_follow = mem_forward(memory_tokens, (*norms, *fixed), mem_weights_in)
        kv_first = kept[0][:, width:]
    else:
        kv_first, kv_follow, m = memory_forward(memory_tokens, p)
    kv_mem = jnp.where((flags == 0)[:, None, None], kv_follow[None], kv_first[None])
    if quick:
        rows_in, normed_a, qkv = enter(
            told, pick(tokens, rank, 0), got, norm_one_gain, norm_one_bias, qkv_read_key, p["shift"]
        )
        attended, lse_first = attn_fwd(behind(qkv, give_grad), kv_first, 0, seg_rows, None)
        got_grad = swapped(give_grad)
        attended, lse_second = attn_fwd(qkv, kv_mem[1], 1, seg_rows, attended)
        attended, got_grad = lax.optimization_barrier((attended, got_grad))
        (
            result, rows_grad, normed_b, activ, grad_expanded, grad_attn_out, grad_attended, mid_sums, expand_sums,
        ) = middle(
            told, pick(cotangent, rank, 0), got_grad, rows_in, attended, p["out"], p["expand"], p["contract"], out_bias,
            norm_two_gain, norm_two_bias, expand_bias, contract_bias,
        )
        grad_after = grad_attn_out
    else:
        hidden = rows_in.astype(F32)
        unit_a, rstd_a = norm_parts(hidden)
        normed_a = (unit_a * norm_one_gain + norm_one_bias).astype(BF16)
        qkv = (dot_dims(normed_a, p["qkv"], 1, 0) + p["shift"]).astype(BF16)
        seg_qkv = qkv.reshape(segs, seg_rows, 3 * width)
        kv_all = lax.all_gather(seg_qkv[:, :, width:], "ctx", axis=1, tiled=True)
        kv_all = jnp.concatenate([kv_mem, kv_all], axis=1)
        query_at = mem + rank * seg_rows + jnp.arange(seg_rows, dtype=jnp.int32)
        key_at = jnp.arange(mem + ranks * seg_rows, dtype=jnp.int32)
        allowed = key_at[None, :] <= query_at[:, None]
        attended, lse = plain_fwd(seg_qkv, kv_all, allowed)
        attended = attended.reshape(-1, width)
        after = hidden + dot_dims(attended, p["out"], 1, 0) + out_bias
        unit_b, rstd_b = norm_parts(after)
        normed_b = (unit_b * norm_two_gain + norm_two_bias).astype(BF16)
        expanded = dot_dims(normed_b, p["expand"], 1, 0) + expand_bias
        activ = gelu_tanh(expanded).astype(BF16)
        result = (after + dot_dims(activ, p["contract"], 1, 1) + contract_bias).astype(BF16)

    def input_back(at, grads, weights):
        grad = dot_dims(grads[0], weights[0], 1, 1)
        for g, w in zip(grads[1:], weights[1:]):
            grad = grad + dot_dims(g, w, 1, 1)
        unit, rstd = norm_parts(rows_in[at].astype(F32))
        grad_hidden, gain, bias = norm_back(grad, unit, rstd, norm_one_gain)
        return (grad_hidden + grad_after[at].astype(F32)).astype(BF16), gain, bias

    def pool(dkv_mem):
        follows = (flags == 0).astype(F32)[:, None, None]
        kinds = [jnp.sum(dkv_mem * (1.0 - follows), axis=0), jnp.sum(dkv_mem * follows, axis=0)]
        return jnp.stack(kinds)

    if quick:
        pairs, most = H // 2, H // 3
        cut = most * 2 * HD
        columns = lambda a, lo, hi: jnp.concatenate(
            [a[..., k * width + lo : k * width + hi] for k in range(3)], axis=-1
        )
        weights = [columns(p["qkv"], 0, cut), columns(p["qkv"], cut, width)]
        lse = jnp.concatenate([lse_first, lse_second], axis=0)
        mems = (kv_first, kv_mem[1])
        spans = [slice(0, seg_rows), slice(seg_rows, 2 * seg_rows)]

        block_halves = [own_and_other(result[a]) for a in spans]
        on_contract = Scatter(dot_dims(rows_grad, activ, 0, 0).astype(BF16))
        grad_expanded = behind(grad_expanded, on_contract.give)
        term_expand = dot_dims(normed_b, grad_expanded, 0, 0).astype(BF16)
        on_expand = Scatter(term_expand)
        on_contract.over_core(term_expand)
        grad_attn_out = behind(grad_attn_out, on_contract.give, on_expand.give)
        term_out = dot_dims(attended, grad_attn_out, 0, 0).astype(BF16)
        dk_mem, dv_mem, middle_sums = attn_mem(
            qkv, kv_mem, attended, behind(grad_attended, term_out), lse
        )
        on_expand.over_core(middle_sums)
        pooled = pool(jnp.concatenate([dk_mem, dv_mem], axis=2))
        others = behind([other for _, other in block_halves], middle_sums)

        def back(seg, first, count, *earlier):
            grad = behind(grad_attended, *earlier)
            return attn_bwd(qkv, mems[seg], grad, lse, middle_sums, seg, first, count)

        normed = [normed_a[a] for a in spans]
        term = lambda grads: sum(dot_dims(normed[k], grads[k], 0, 0) for k in range(2)).astype(BF16)
        turn_a = back(0, 0, most, pooled, others, on_expand.give)
        pooled = sum_over(pooled, 0, turn_a)
        on_contract.over_x(turn_a)
        turn_b = back(1, 0, most, turn_a, pooled, on_contract.give)
        pooled = sum_over(pooled, 1, turn_b)
        others = behind([swapped(other) for other in others], turn_b)
        block_halves = [(own, other) for (own, _), other in zip(block_halves, others)]
        on_expand.over_x(turn_b)
        on_contract.over_z(turn_b)
        most_grads = [turn_a, turn_b]
        on_most = Scatter(jnp.concatenate([term(most_grads), term_out], axis=1))
        turn_c = back(
            0, most, pairs - most, on_most.give, on_expand.give, on_contract.give, pooled
        )
        pooled = sum_over(pooled, 2, turn_c)
        on_most.over_core(turn_c)
        got_contract = on_contract.over_y(turn_c)
        first_end = input_back(
            spans[0],
            [behind(most_grads[0], on_most.give, pooled), turn_c],
            weights,
        )
        kept_first, given_first = own_and_other(first_end[0])
        turn_d = back(1, most, pairs - most, given_first, got_contract)
        pooled = sum_over(pooled, 3, turn_d)
        on_expand.over_z(turn_d)
        on_most.over_x(turn_d)
        got_first = behind(swapped(given_first), turn_d)
        rest_grads = [turn_c, turn_d]
        on_rest = Scatter(term(rest_grads))
        last = behind(turn_d, on_expand.give, on_most.give, on_rest.give, pooled)
        second_end = input_back(spans[1], [most_grads[1], last], weights)
        on_rest.over_core(second_end[0])
        kept_second, given_second = own_and_other(second_end[0])
        one_gain, one_bias = first_end[1] + second_end[1], first_end[2] + second_end[2]
        qkv_sums = [
            sum(jnp.sum(g[k].astype(F32), axis=0) for k in range(2)).reshape(3, -1)
            for g in (most_grads, rest_grads)
        ]
        qkv_sums = jnp.concatenate(qkv_sums, axis=1)
    else:
        _, gelu_pull = jax.vjp(gelu_tanh, expanded)
        grad_expanded = gelu_pull(dot_dims(rows_grad, p["contract"], 1, 0))[0].astype(BF16)
        grad_after, two_gain, two_bias = norm_back(
            dot_dims(grad_expanded, p["expand"], 1, 1), unit_b, rstd_b, norm_two_gain
        )
        grad_after = grad_after + rows_grad.astype(F32)
        grad_attn_out = grad_after.astype(BF16)
        grad_attended = dot_dims(grad_attn_out, p["out"], 1, 1).astype(BF16)
        dq, dkv = plain_bwd(
            seg_qkv, kv_all, allowed, lse, grad_attended.reshape(segs, seg_rows, width)
        )
        pooled = pool(dkv[:, :mem])
        dkv = lax.psum_scatter(
            dkv[:, mem:].astype(BF16), "ctx", scatter_dimension=1, tiled=True
        )
        grad_qkv = jnp.concatenate([dq.astype(BF16), dkv], axis=2).reshape(-1, 3 * width)
        grad_rows, one_gain, one_bias = input_back(slice(None), [grad_qkv], [p["qkv"]])
        terms = (
            dot_dims(normed_a, grad_qkv, 0, 0).astype(BF16),
            dot_dims(attended, grad_attn_out, 0, 0).astype(BF16),
            dot_dims(normed_b, grad_expanded, 0, 0).astype(BF16),
            dot_dims(rows_grad, activ, 0, 0).astype(BF16),
        )
        qkv_sums = jnp.sum(grad_qkv.astype(F32), axis=0).reshape(3, width)
    column_sum = lambda a: jnp.sum(a.astype(F32), axis=0)
    if quick:
        mid = (mid_sums[0], mid_sums[1], mid_sums[2], expand_sums[0], mid_sums[3])
    else:
        mid = (
            column_sum(grad_attn_out), two_gain, two_bias, column_sum(grad_expanded), column_sum(rows_grad),
        )
    vectors = (one_gain, one_bias, jnp.stack([qkv_sums[0], qkv_sums[2]]), *mid)
    flat = jnp.concatenate([v.reshape(-1) for v in vectors]).reshape(-1, 128)
    got = {}

    def turn(step, value):
        if step == 0:
            return behind(value, flat, on_rest.give, on_most.give, given_second)
        got["second"] = behind(swapped(given_second), value)
        on_rest.over_x(value)
        on_most.over_z(value)
        got["flat"] = sum_over(flat, 0, value)
        got["expand"] = on_expand.over_y(value)
        got["flat"] = sum_over(sum_over(got["flat"], 1), 2)
        got["most"] = on_most.over_y()

    if not quick:
        summed = tuple(
            lax.psum(
                lax.psum_scatter(t, "dp", scatter_dimension=0, tiled=True).astype(F32), "ctx"
            )
            for t in terms
        )
        pooled, vectors = lax.psum((pooled, vectors), ("dp", "ctx"))

    if quick:
        pooled = turn(0, pooled)
        grad_mt, mem_matrices, mem_vectors = mem_backward(
            memory_tokens, norms, pooled, shard, group, kept, mem_weights_in
        )
        turn(1, grad_mt)
    else:
        mine = lambda a: lax.dynamic_slice_in_dim(a, group * shard, shard, 1)
        grad_mt, mem_matrices, mem_vectors = memory_backward(
            memory_tokens, p, m, pooled[0], pooled[1], mine
        )
    if quick:
        most_part = got["most"][:, : 3 * cut].reshape(shard, 3, cut)
        rest_part = on_rest.over_z().over_y().reshape(shard, 3, width - cut)
        summed = (
            jnp.concatenate([most_part, rest_part], axis=2).reshape(shard, 3 * width),
            got["most"][:, 3 * cut :],
            got["expand"],
            got_contract,
        )
        flat = sum_over(got["flat"], 3).reshape(-1)
        split, place = [], 0
        for v in vectors:
            split.append(flat[place : place + v.size].reshape(v.shape))
            place += v.size
        vectors = tuple(split)
    matrices = tuple(a + b for a, b in zip(summed, mem_matrices)) + mem_matrices[4:]
    vectors = tuple(a + b for a, b in zip(vectors, mem_vectors))
    if quick:
        block_out = settle(block_halves, flips)
        token_grad = settle([(kept_first, got_first), (kept_second, got["second"])], flips)
    else:
        block_out, token_grad = result.reshape(tokens.shape), grad_rows.reshape(tokens.shape)
    return (
        block_out,
        token_grad,
        grad_mt,
        vectors[0],
        vectors[1],
        matrices[0],
        vectors[2],
        matrices[1],
        vectors[3],
        vectors[4],
        vectors[5],
        matrices[2],
        vectors[6],
        matrices[3],
        vectors[7],
        matrices[4],
        matrices[5],
        matrices[6],
    )


def solution(mesh):
    rows = P(None, "dp", "ctx", None)
    matrix = P("dp", None)
    full = P()
    return jax.shard_map(
        local,
        mesh=mesh,
        in_specs=(
            rows, rows, full, full, full, full, full, matrix, full, matrix, full, full, full,
            matrix, full, matrix, full, matrix, matrix, matrix,
        ),
        out_specs=(
            rows, rows, full, full, full, matrix, full, matrix, full, full, full, matrix, full,
            matrix, full, matrix, matrix, matrix,
        ),
        check_vma=False,
    )
```

```python
import functools

import jax
import jax.numpy as jnp
from jax import lax
from jax.experimental import pallas as pl
from jax.experimental.pallas import tpu as pltpu
from jax.sharding import PartitionSpec as P

H = 12
HD = 64
EPS = 1e-05
CHUNK = 256
WIDE = 512
F32 = jnp.float32
BF16 = jnp.bfloat16


def norm_parts(rows):
    centred = rows - jnp.mean(rows, axis=-1, keepdims=True)
    spread = jnp.mean(centred * centred, axis=-1, keepdims=True)
    rstd = lax.rsqrt(spread + EPS)
    return centred * rstd, rstd


def norm_back(grad, unit, rstd, gain):
    scaled = grad * gain
    first = jnp.mean(scaled, axis=-1, keepdims=True)
    second = jnp.mean(scaled * unit, axis=-1, keepdims=True)
    grad_rows = rstd * (scaled - first - unit * second)
    return grad_rows, jnp.sum(grad * unit, axis=0), jnp.sum(grad, axis=0)


def feature_map(rows):
    halves = jnp.concatenate([jax.nn.softplus(rows), jax.nn.softplus(-rows)], axis=-1)
    return jnp.concatenate([halves * jnp.roll(halves, j, axis=-1) for j in (1, 2, 3)], axis=-1)


def gelu_tanh(rows):
    return jax.nn.gelu(rows, approximate=True)


def dot_dims(a, b, ca, cb, precision=None):
    return lax.dot_general(
        a, b, (((ca,), (cb,)), ((), ())), precision=precision, preferred_element_type=F32
    )


exact = functools.partial(dot_dims, precision=lax.Precision.HIGHEST)


def head_rows(scale):
    lane = lax.broadcasted_iota(jnp.int32, (1, 2 * HD), 1)
    low = jnp.where(lane < HD, scale, 0.0).astype(BF16)
    high = jnp.where(lane < HD, 0.0, scale).astype(BF16)
    return low, high


def causal_tail(scores):
    key = lax.broadcasted_iota(jnp.int32, scores.shape, 0)
    return jnp.where(key <= lax.broadcasted_iota(jnp.int32, scores.shape, 1), scores, 0.0)


def attn_fwd_kernel(q_ref, k_ref, v_ref, km_ref, vm_ref, o_ref, lse_ref, keys, vals_t, vmem_t):
    mem = km_ref.shape[0]
    keys[0:mem, :] = km_ref[...]
    keys[mem:, :] = k_ref[...]
    vals_t[...] = v_ref[...].T
    vmem_t[...] = vm_ref[...].T
    picks = head_rows(HD**-0.5)
    steps = [(part, head) for part in range(q_ref.shape[0] // WIDE) for head in range(2)]

    def begin(part, head):
        lo, hi = part * WIDE, (part + 1) * WIDE
        return dot_dims(keys[0 : mem + hi, :], q_ref[lo:hi, :] * picks[head], 1, 1)

    ahead = begin(*steps[0])
    outs = []
    for n, (part, head) in enumerate(steps):
        lo, hi = part * WIDE, (part + 1) * WIDE
        band = slice(head * HD, (head + 1) * HD)
        raw = jnp.exp(ahead)
        if n + 1 < len(steps):
            ahead = begin(*steps[n + 1])
        raw = jnp.concatenate([raw[: mem + lo], causal_tail(raw[mem + lo :])], axis=0)
        total = jnp.sum(raw, axis=0, keepdims=True)
        lse_ref[0, head : head + 1, lo:hi] = jnp.log(total)
        weights = (raw * (1.0 / total)).astype(BF16)
        outs.append(
            dot_dims(vals_t[band, 0:hi], weights[mem:], 1, 0)
            + dot_dims(vmem_t[band, :], weights[:mem], 1, 0)
        )
        if head == 1:
            o_ref[lo:hi, :] = jnp.concatenate(outs, axis=0).T.astype(BF16)
            outs = []


def attn_fwd_after_kernel(q_ref, k_ref, v_ref, km_ref, vm_ref, held_ref, *rest):
    del held_ref
    attn_fwd_kernel(q_ref, k_ref, v_ref, km_ref, vm_ref, *rest)


def attn_fwd(qkv, kv_mem, seg, rows, held):
    width = qkv.shape[1] // 3
    mem = kv_mem.shape[0]
    pairs = H // 2
    wide = 2 * HD
    spec = lambda off: pl.BlockSpec((rows, wide), lambda p, off=off: (seg, off * pairs + p))
    mspec = lambda off: pl.BlockSpec((mem, wide), lambda p, off=off: (0, off * pairs + p))
    more = [] if held is None else [held]
    return pl.pallas_call(
        attn_fwd_kernel if held is None else attn_fwd_after_kernel,
        grid=(pairs,),
        in_specs=[spec(0), spec(1), spec(2), mspec(0), mspec(1)]
        + [pl.BlockSpec(memory_space=pl.ANY)] * len(more),
        out_specs=[
            pl.BlockSpec((rows, wide), lambda p: (seg, p)),
            pl.BlockSpec((1, 2, rows), lambda p: (p, 0, 0)),
        ],
        out_shape=[
            jax.ShapeDtypeStruct((qkv.shape[0], width), BF16),
            jax.ShapeDtypeStruct((pairs, 2, rows), F32),
        ],
        scratch_shapes=[
            pltpu.VMEM((mem + rows, wide), BF16),
            pltpu.VMEM((wide, rows), BF16),
            pltpu.VMEM((wide, mem), BF16),
        ],
        input_output_aliases={5: 0} if more else {},
        compiler_params=pltpu.CompilerParams(vmem_limit_bytes=60 * 2**20),
        cost_estimate=pl.CostEstimate(
            flops=pairs * rows * rows * 4000,
            bytes_accessed=rows * width * 8,
            transcendentals=0,
        ),
        name="attn_fwd",
    )(qkv, qkv, qkv, kv_mem, kv_mem, *more)


def attn_mem_kernel(q_ref, km_ref, vm_ref, o_ref, g_ref, lse_ref, dkm_ref, dvm_ref, mid_ref):
    scaled_picks, picks = head_rows(HD**-0.5), head_rows(1.0)
    grad, query = g_ref[...], q_ref[...]
    inner = (grad.astype(F32) * o_ref[...].astype(F32)).T
    dk, dv = 0.0, 0.0
    for head in range(2):
        band = slice(head * HD, (head + 1) * HD)
        query_h, grad_h = query * scaled_picks[head], grad * picks[head]
        centre = jnp.sum(inner[band], axis=0, keepdims=True)
        mid_ref[0, head : head + 1, :] = centre
        prob = jnp.exp(dot_dims(km_ref[0], query_h, 1, 1) - lse_ref[0, head : head + 1, :])
        grad_s = (prob * (dot_dims(vm_ref[0], grad_h, 1, 1) - centre)).astype(BF16)
        dv = dv + dot_dims(prob.astype(BF16), grad_h, 1, 0)
        dk = dk + dot_dims(grad_s, query_h, 1, 0)
    dkm_ref[0] = dk
    dvm_ref[0] = dv


def attn_mem(qkv, kv_mem, attended, grad, lse):
    segs, pairs, mem, wide = kv_mem.shape[0], H // 2, kv_mem.shape[1], 2 * HD
    rows, width = lse.shape[2], qkv.shape[1] // 3
    spec = pl.BlockSpec((rows, wide), lambda s, p: (s, p))
    mspec = lambda off: pl.BlockSpec((1, mem, wide), lambda s, p, off=off: (s, 0, off * pairs + p))
    lspec = pl.BlockSpec((1, 2, rows), lambda s, p: (s * pairs + p, 0, 0))
    return pl.pallas_call(
        attn_mem_kernel,
        grid=(segs, pairs),
        in_specs=[spec, mspec(0), mspec(1), spec, spec, lspec],
        out_specs=[mspec(0), mspec(0), lspec],
        out_shape=[
            jax.ShapeDtypeStruct((segs, mem, width), F32),
            jax.ShapeDtypeStruct((segs, mem, width), F32),
            jax.ShapeDtypeStruct((segs * pairs, 2, rows), F32),
        ],
        compiler_params=pltpu.CompilerParams(vmem_limit_bytes=60 * 2**20),
        cost_estimate=pl.CostEstimate(
            flops=segs * rows * width * 4000, bytes_accessed=segs * rows * width * 6, transcendentals=0
        ),
        name="attn_mem",
    )(qkv, kv_mem, kv_mem, attended, grad, lse)


def attn_bwd_kernel(
    q_ref, k_ref, v_ref, km_ref, vm_ref, g_ref, lse_ref, mid_ref,
    out_ref,
    keys, vals, keys_t, kmem_t, dq, dk, dv,
):
    phase = pl.program_id(1)
    mem = km_ref.shape[0]
    rows = q_ref.shape[0]

    @pl.when((phase == 2) & (pl.program_id(0) < pl.num_programs(0) - 1))
    def _():
        keys[0:mem, :] = km_ref[...]
        keys[mem:, :] = k_ref[...]
        vals[0:mem, :] = vm_ref[...]
        vals[mem:, :] = v_ref[...]
        keys_t[...] = k_ref[...].T
        kmem_t[...] = km_ref[...].T
        dk[...] = jnp.zeros_like(dk)
        dv[...] = jnp.zeros_like(dv)
        scaled_picks = head_rows(HD**-0.5)
        picks = head_rows(1.0)
        for part in range(rows // CHUNK):
            lo, hi = part * CHUNK, (part + 1) * CHUNK
            end = mem + hi
            query = q_ref[lo:hi, :]
            grad = g_ref[lo:hi, :]
            dqs = []
            for head in range(2):
                band = slice(head * HD, (head + 1) * HD)
                query_h = query * scaled_picks[head]
                grad_h = grad * picks[head]
                log_total = lse_ref[0, head : head + 1, lo:hi]
                centre = mid_ref[0, head : head + 1, lo:hi]
                prob = jnp.exp(dot_dims(keys[0:end, :], query_h, 1, 1) - log_total)
                prob = jnp.concatenate(
                    [prob[: mem + lo], causal_tail(prob[mem + lo :])], axis=0
                )
                grad_p = dot_dims(vals[0:end, :], grad_h, 1, 1)
                grad_s = (prob * (grad_p - centre)).astype(BF16)
                dv[0:end, :] += dot_dims(prob.astype(BF16), grad_h, 1, 0)
                dk[0:end, :] += dot_dims(grad_s, query_h, 1, 0)
                dqs.append(
                    dot_dims(keys_t[band, 0:hi], grad_s[mem:], 1, 0)
                    + dot_dims(kmem_t[band, :], grad_s[:mem], 1, 0)
                )
            dq[lo:hi, :] = (jnp.concatenate(dqs, axis=0) * HD**-0.5).T.astype(BF16)
        out_ref[...] = dq[...]

    @pl.when((phase == 0) & (pl.program_id(0) > 0))
    def _():
        out_ref[...] = dk[mem:, :].astype(BF16)

    @pl.when((phase == 1) & (pl.program_id(0) > 0))
    def _():
        out_ref[...] = dv[mem:, :].astype(BF16)


def attn_bwd(qkv, kv_mem, grad, lse, middle, seg, first, count):
    pairs = H // 2
    rows, width = lse.shape[2], qkv.shape[1] // 3
    mem = kv_mem.shape[0]
    wide = 2 * HD
    at = lambda p: first + jnp.minimum(p, count - 1)
    spec = lambda off: pl.BlockSpec((rows, wide), lambda p, f, off=off: (seg, off * pairs + at(p)))
    mspec = lambda off: pl.BlockSpec((mem, wide), lambda p, f, off=off: (0, off * pairs + at(p)))
    lspec = pl.BlockSpec((1, 2, rows), lambda p, f: (seg * pairs + at(p), 0, 0))

    def place(p, f):
        late = jnp.where(f == 0, count, 2 * count) + p - 1
        now = jnp.where(p == count, 3 * count - 1, p)
        return (0, jnp.where((f == 2) | (p == 0), now, late))

    return pl.pallas_call(
        attn_bwd_kernel,
        grid=(count + 1, 3),
        in_specs=[
            spec(0), spec(1), spec(2), mspec(0), mspec(1), spec(0), lspec, lspec,
        ],
        out_specs=pl.BlockSpec((rows, wide), place),
        out_shape=jax.ShapeDtypeStruct((rows, 3 * count * wide), BF16),
        scratch_shapes=[
            pltpu.VMEM((mem + rows, wide), BF16),
            pltpu.VMEM((mem + rows, wide), BF16),
            pltpu.VMEM((wide, rows), BF16),
            pltpu.VMEM((wide, mem), BF16),
            pltpu.VMEM((rows, wide), BF16),
            pltpu.VMEM((mem + rows, wide), F32),
            pltpu.VMEM((mem + rows, wide), F32),
        ],
        compiler_params=pltpu.CompilerParams(vmem_limit_bytes=60 * 2**20),
        cost_estimate=pl.CostEstimate(
            flops=count * rows * rows * 6500,
            bytes_accessed=rows * count * wide * 18,
            transcendentals=0,
        ),
        name="attn_bwd",
    )(qkv, qkv, qkv, kv_mem, kv_mem, grad, lse, middle)


def choose(told, kept, got, out):
    own = pl.program_id(0) % 2 == told[1]

    @pl.when(own)
    def _():
        out[...] = kept[0, 0]

    @pl.when(jnp.logical_not(own))
    def _():
        out[...] = got[0]


def half_specs(rows, width):
    return [
        pl.BlockSpec((1, 1, rows, width), lambda i, told: (told[1], (i // 2) ^ told[0], 0, 0)),
        pl.BlockSpec((1, rows, width), lambda i, told: ((i // 2) ^ told[0], 0, 0)),
    ]


def enter_kernel(told, kept, got, gain, bias, weight, shift, rows_ref, normed_ref, qkv_ref):
    choose(told, kept, got, rows_ref)
    unit, _ = norm_parts(rows_ref[...].astype(F32))
    normed = (unit * gain[...] + bias[...]).astype(BF16)
    normed_ref[...] = normed
    wide = weight.shape[1] // 3
    for k in range(3):
        at = slice(k * wide, (k + 1) * wide)
        qkv_ref[:, at] = (dot_dims(normed, weight[:, at], 1, 0) + shift[:, at]).astype(BF16)


def enter(told, kept, got, gain, bias, weight, shift):
    _, segs, rows, width = kept.shape
    whole = lambda r, c: pl.BlockSpec((r, c), lambda i, told: (0, 0), pipeline_mode=pl.Buffered(1))
    block = lambda c: pl.BlockSpec((rows, c), lambda i, told: (i, 0))
    sizes = (width, width, 3 * width)
    return pl.pallas_call(
        enter_kernel,
        grid_spec=pltpu.PrefetchScalarGridSpec(
            num_scalar_prefetch=1,
            grid=(2 * segs,),
            in_specs=[*half_specs(rows, width), whole(1, width), whole(1, width), whole(width, 3 * width), whole(1, 3 * width)],
            out_specs=[block(c) for c in sizes],
        ),
        out_shape=[jax.ShapeDtypeStruct((2 * segs * rows, c), BF16) for c in sizes],
        compiler_params=pltpu.CompilerParams(vmem_limit_bytes=60 * 2**20),
        cost_estimate=pl.CostEstimate(
            flops=8 * segs * rows * width * width * 3, bytes_accessed=segs * rows * width * 28, transcendentals=0
        ),
        name="enter",
    )(told, kept, got, gain[None], bias[None], weight, shift[None])


def middle_kernel(
    told, kept, got, rows_ref, attended, out_w, expand_w, contract_w, out_b, gain, bias, expand_b, contract_b,
    result_ref, cot_ref, normed_ref, activ_ref, grad_exp_ref, grad_out_ref, grad_att_ref,
    sums_ref, exp_sums_ref,
):
    choose(told, kept, got, cot_ref)
    cot = cot_ref[...]
    after = rows_ref[...].astype(F32) + dot_dims(attended[...], out_w[...], 1, 0) + out_b[...]
    unit, rstd = norm_parts(after)
    normed = (unit * gain[...] + bias[...]).astype(BF16)
    normed_ref[...] = normed
    total = after + contract_b[...]
    back = 0.0

    @pl.when(pl.program_id(0) == 0)
    def _():
        sums_ref[...] = jnp.zeros_like(sums_ref)
        exp_sums_ref[...] = jnp.zeros_like(exp_sums_ref)

    parts = 4
    wide = expand_w.shape[1] // parts
    bend, cube = 0.7978845608028654, 0.044715
    for part in range(parts):
        at = slice(part * wide, (part + 1) * wide)
        value = dot_dims(normed, expand_w[:, at], 1, 0) + expand_b[:, at]
        square = value * value
        half = 0.5 + 0.5 * jnp.tanh(value * (bend + bend * cube * square))
        activ = (value * half).astype(BF16)
        activ_ref[:, at] = activ
        slope = half + (half - half * half) * (value * (2.0 * bend + 6.0 * bend * cube * square))
        grad = (dot_dims(cot, contract_w[:, at], 1, 0) * slope).astype(BF16)
        grad_exp_ref[:, at] = grad
        exp_sums_ref[:, at] += jnp.sum(grad.astype(F32), axis=0, keepdims=True)
        total = total + dot_dims(activ, contract_w[:, at], 1, 1)
        back = back + dot_dims(grad, expand_w[:, at], 1, 1)
    result_ref[...] = total.astype(BF16)
    wide_cot = cot.astype(F32)
    grad_rows, gain_sum, bias_sum = norm_back(back, unit, rstd, gain[...])
    grad_out = (grad_rows + wide_cot).astype(BF16)
    grad_out_ref[...] = grad_out
    grad_att_ref[...] = dot_dims(grad_out, out_w[...], 1, 1).astype(BF16)
    sums = (
        jnp.sum(grad_out.astype(F32), axis=0, keepdims=True),
        gain_sum[None],
        bias_sum[None],
        jnp.sum(wide_cot, axis=0, keepdims=True),
    )
    for k, value in enumerate(sums):
        sums_ref[k : k + 1, :] += value


def middle(told, kept, got, rows_in, attended, out_w, expand_w, contract_w, out_b, gain, bias, expand_b, contract_b):
    _, segs, rows, width = kept.shape
    wide = expand_w.shape[1]
    whole = lambda r, c: pl.BlockSpec((r, c), lambda i, told: (0, 0), pipeline_mode=pl.Buffered(1))
    block = lambda c: pl.BlockSpec((rows, c), lambda i, told: (i, 0))
    sizes = (width, width, width, wide, wide, width, width)
    count = 2 * segs * rows
    fixed = lambda r, c: pl.BlockSpec((r, c), lambda i, told: (0, 0))
    return pl.pallas_call(
        middle_kernel,
        grid_spec=pltpu.PrefetchScalarGridSpec(
            num_scalar_prefetch=1,
            grid=(2 * segs,),
            in_specs=[
                *half_specs(rows, width), block(width), block(width), whole(width, width), whole(width, wide),
                whole(width, wide), whole(1, width), whole(1, width), whole(1, width), whole(1, wide), whole(1, width),
            ],
            out_specs=[*[block(c) for c in sizes], fixed(8, width), fixed(1, wide)],
        ),
        out_shape=[
            *[jax.ShapeDtypeStruct((count, c), BF16) for c in sizes],
            jax.ShapeDtypeStruct((8, width), F32),
            jax.ShapeDtypeStruct((1, wide), F32),
        ],
        compiler_params=pltpu.CompilerParams(vmem_limit_bytes=60 * 2**20),
        cost_estimate=pl.CostEstimate(
            flops=count * width * (8 * wide + 4 * width) * 2, bytes_accessed=count * (14 * width + 4 * wide), transcendentals=0
        ),
        name="middle",
    )(
        told, kept, got, rows_in, attended, out_w, expand_w, contract_w, out_b[None], gain[None], bias[None],
        expand_b[None], contract_b[None],
    )


def thirds(rows):
    parts = []
    for _ in range(3):
        parts.append(rows.astype(BF16))
        rows = rows - parts[-1].astype(F32)
    return jnp.concatenate(parts, axis=0)


def exact_low(rows, weight, side):
    count = rows.shape[0]
    out = dot_dims(thirds(rows), weight, 1, side)
    return out[:count] + out[count : 2 * count] + out[2 * count :]


def softplus(rows):
    return jnp.maximum(rows, 0.0) + jnp.log1p(jnp.exp(-jnp.abs(rows)))


def feature_parts(rows):
    halves = jnp.concatenate([softplus(rows), softplus(-rows)], axis=1)
    turned = [pltpu.roll(halves, j, 1) for j in (1, 2, 3)]
    return halves, turned, jnp.concatenate([halves * t for t in turned], axis=1)


def feature_back(rows, grad):
    halves, turned, _ = feature_parts(rows)
    wide = halves.shape[1]
    total = 0.0
    for j in (1, 2, 3):
        part = grad[:, (j - 1) * wide : j * wide]
        total = total + part * turned[j - 1] + pltpu.roll(part * halves, wide - j, 1)
    first, last = total[:, : wide // 2], total[:, wide // 2 :]
    return first * jax.nn.sigmoid(rows) - last * jax.nn.sigmoid(-rows)


def per_head(rows):
    tall = jnp.concatenate([rows] * H, axis=0)
    return tall * head_mask(tall.shape, rows.shape[0]).astype(rows.dtype)


def head_mask(shape, count):
    head = lax.broadcasted_iota(jnp.int32, shape, 0) // count
    return (lax.broadcasted_iota(jnp.int32, shape, 1) // HD == head).astype(F32)


def from_heads(tall, count):
    tall = tall * head_mask(tall.shape, count)
    total = tall[:count]
    for head in range(1, H):
        total = total + tall[head * count : (head + 1) * count]
    return total


def mem_weights(query, key):
    count = key.shape[0]
    tall = per_head(query)
    scores = dot_dims(tall, key, 1, 1) * HD**-0.5
    at = lax.rem(lax.broadcasted_iota(jnp.int32, scores.shape, 0), count)
    raw = jnp.where(lax.broadcasted_iota(jnp.int32, scores.shape, 1) <= at, jnp.exp(scores), 0.0)
    return tall, raw / jnp.sum(raw, axis=1, keepdims=True)


def read_parts(read_feat, key_feat, value_new):
    mix = exact(read_feat, key_feat, 1, 1)
    return mix, exact(mix, value_new, 1, 0), 1.0 + jnp.sum(mix, axis=1, keepdims=True)


def bring(sources, targets, sem):
    copies = [pltpu.make_async_copy(a, b, sem.at[k]) for k, (a, b) in enumerate(zip(sources, targets))]
    for copy in copies:
        copy.start()
    return copies


def mem_fwd_kernel(
    mt_ref, one_gain, one_bias, two_gain, two_bias, shift, out_b, expand_b, contract_b,
    qrk_hbm, ov_hbm, expand_hbm, contract_hbm,
    qkv_ref, attended_ref, after_ref, expanded_ref, result_ref, pre_ref, value_ref, follow_ref, kv_ref,
    qrk, ov, expand_w, contract_w, sem,
):
    copies = bring((qrk_hbm, ov_hbm, expand_hbm, contract_hbm), (qrk, ov, expand_w, contract_w), sem)
    mt = mt_ref[...]
    width = mt.shape[1]
    feat = pre_ref.shape[1] // 2
    unit, _ = norm_parts(mt)
    normed = (unit * one_gain[...] + one_bias[...]).astype(BF16)
    copies[0].wait()
    qkv = (dot_dims(normed, qrk[:, : 3 * width], 1, 0) + shift[...]).astype(BF16)
    qkv_ref[...] = qkv
    read_pre = exact_low(mt, qrk[:, 3 * width : 3 * width + feat], 0)
    _, weights = mem_weights(qkv[:, :width], qkv[:, width : 2 * width])
    mixed = dot_dims(weights.astype(BF16), qkv[:, 2 * width :], 1, 0)
    attended = from_heads(mixed, mt.shape[0]).astype(BF16)
    attended_ref[...] = attended
    copies[1].wait()
    after = mt + dot_dims(attended, ov[:, :width], 1, 0) + out_b[...]
    after_ref[...] = after
    unit, _ = norm_parts(after)
    normed = (unit * two_gain[...] + two_bias[...]).astype(BF16)
    copies[2].wait()
    expanded = dot_dims(normed, expand_w[...], 1, 0) + expand_b[...]
    expanded_ref[...] = expanded
    activ = gelu_tanh(expanded).astype(BF16)
    copies[3].wait()
    result = after + dot_dims(activ, contract_w[...], 1, 1) + contract_b[...]
    result_ref[...] = result
    key_pre = exact_low(result, qrk[:, 3 * width + feat :], 0)
    value_new = exact_low(result, ov[:, width:], 0)
    value_ref[...] = value_new
    pre_ref[:, :feat] = read_pre
    pre_ref[:, feat:] = key_pre
    _, numer, denom = read_parts(feature_parts(read_pre)[2], feature_parts(key_pre)[2], value_new)
    follow = mt + numer / denom
    follow_ref[...] = follow
    unit, _ = norm_parts(follow)
    normed = (unit * one_gain[...] + one_bias[...]).astype(BF16)
    kv_ref[...] = (dot_dims(normed, qrk[:, width : 3 * width], 1, 0) + shift[:, width:]).astype(BF16)


def mem_call(kernel, name, given, weights, outs, cycles):
    vmem = pl.BlockSpec(memory_space=pltpu.VMEM)
    return pl.pallas_call(
        kernel,
        in_specs=[vmem] * len(given) + [pl.BlockSpec(memory_space=pl.ANY)] * len(weights),
        out_specs=[vmem] * len(outs),
        out_shape=outs,
        scratch_shapes=[
            *[pltpu.VMEM(w.shape, w.dtype) for w in weights],
            pltpu.SemaphoreType.DMA((len(weights),)),
        ],
        compiler_params=pltpu.CompilerParams(vmem_limit_bytes=60 * 2**20),
        cost_estimate=pl.CostEstimate(flops=cycles * 10**9, bytes_accessed=17 * 10**6, transcendentals=0),
        name=name,
    )(*given, *weights)


def mem_forward(mt, given, weights):
    mem, width = mt.shape
    wide, feat = weights[2].shape[1], (weights[0].shape[1] - 3 * width) // 2
    shape = jax.ShapeDtypeStruct
    outs = [
        shape((mem, 3 * width), BF16), shape((mem, width), BF16), shape((mem, width), F32), shape((mem, wide), F32),
        shape((mem, width), F32), shape((mem, 2 * feat), F32), shape((mem, width), F32), shape((mem, width), F32),
        shape((mem, 2 * width), BF16),
    ]
    return mem_call(mem_fwd_kernel, "mem_fwd", (mt, *given), weights, outs, 15)


def mem_bwd_kernel(
    mt_ref, one_gain, one_bias, two_gain, two_bias, pooled, chosen,
    qkv_ref, attended_ref, after_ref, expanded_ref, result_ref, pre_ref, value_ref, follow_ref,
    qrk_hbm, ov_hbm, expand_hbm, contract_hbm,
    grad_mt_ref, qkv_grad, out_grad, expand_grad, contract_grad, read_grad, key_grad, value_grad, sums_ref, exp_sums_ref,
    qrk, ov, expand_w, contract_w, sem,
):
    copies = bring((qrk_hbm, ov_hbm, expand_hbm, contract_hbm), (qrk, ov, expand_w, contract_w), sem)
    mt = mt_ref[...]
    mem, width = mt.shape
    feat = pre_ref.shape[1] // 2
    sums_ref[...] = jnp.zeros_like(sums_ref)

    def add_row(k, value):
        sums_ref[k : k + 1, :] += value[None]

    def column(value):
        return jnp.sum(value.astype(F32), axis=0)

    unit_f, rstd_f = norm_parts(follow_ref[...])
    normed_f = (unit_f * one_gain[...] + one_bias[...]).astype(BF16)
    grad_f = pooled[1].astype(BF16)
    copies[0].wait()
    grad_follow, gain, bias = norm_back(
        dot_dims(grad_f, qrk[:, width : 3 * width], 1, 1), unit_f, rstd_f, one_gain[...]
    )
    add_row(0, gain)
    add_row(1, bias)
    add_row(3, column(grad_f[:, width:]))
    read_pre, key_pre, value_new = pre_ref[:, :feat], pre_ref[:, feat:], value_ref[...]
    read_feat, key_feat = feature_parts(read_pre)[2], feature_parts(key_pre)[2]
    mix, numer, denom = read_parts(read_feat, key_feat, value_new)
    grad_numer = grad_follow / denom
    grad_denom = -jnp.sum(grad_follow * numer, axis=1, keepdims=True) / (denom * denom)
    grad_mix = exact(grad_numer, value_new, 1, 1) + grad_denom
    grad_value = exact(mix, grad_numer, 0, 0)
    grad_read_pre = feature_back(read_pre, exact(grad_mix, key_feat, 1, 0))
    grad_key_pre = feature_back(key_pre, exact(grad_mix, read_feat, 0, 0))
    grad_mt = grad_follow + exact_low(grad_read_pre, qrk[:, 3 * width : 3 * width + feat], 1)
    copies[1].wait()
    grad_result = exact_low(grad_key_pre, qrk[:, 3 * width + feat :], 1) + exact_low(
        grad_value, ov[:, width:], 1
    )
    grad_contract = grad_result.astype(BF16)
    add_row(7, column(grad_contract))
    expanded = expanded_ref[...]
    bend, cube = 0.7978845608028654, 0.044715
    square = expanded * expanded
    curve = jnp.tanh(bend * expanded * (1.0 + cube * square))
    half = 0.5 * (1.0 + curve)
    activ = (expanded * half).astype(BF16)
    slope = half + 0.5 * bend * expanded * (1.0 - curve * curve) * (1.0 + 3.0 * cube * square)
    copies[3].wait()
    grad_expanded = (dot_dims(grad_contract, contract_w[...], 1, 0) * slope).astype(BF16)
    exp_sums_ref[...] = column(grad_expanded)[None]
    unit_b, rstd_b = norm_parts(after_ref[...])
    normed_b = (unit_b * two_gain[...] + two_bias[...]).astype(BF16)
    copies[2].wait()
    grad_after, gain, bias = norm_back(
        dot_dims(grad_expanded, expand_w[...], 1, 1), unit_b, rstd_b, two_gain[...]
    )
    add_row(5, gain)
    add_row(6, bias)
    grad_after = grad_after + grad_result
    grad_attn_out = grad_after.astype(BF16)
    add_row(4, column(grad_attn_out))
    grad_attended = dot_dims(grad_attn_out, ov[:, :width], 1, 1).astype(BF16)
    query, key, value = (qkv_ref[:, k * width : (k + 1) * width] for k in range(3))
    tall, weights = mem_weights(query, key)
    grad_tall = per_head(grad_attended)
    grad_weights = dot_dims(grad_tall, value, 1, 1)
    centre = jnp.sum(weights * grad_weights, axis=1, keepdims=True)
    grad_s = (weights * (grad_weights - centre) * HD**-0.5).astype(BF16)
    grad_qkv = jnp.concatenate(
        [
            from_heads(dot_dims(grad_s, key, 1, 0), mem),
            dot_dims(grad_s, tall, 0, 0) + pooled[0, :, :width],
            dot_dims(weights.astype(BF16), grad_tall, 0, 0) + pooled[0, :, width:],
        ],
        axis=1,
    ).astype(BF16)
    add_row(2, column(grad_qkv[:, :width]))
    add_row(3, column(grad_qkv[:, 2 * width :]))
    unit, rstd = norm_parts(mt)
    normed = (unit * one_gain[...] + one_bias[...]).astype(BF16)
    grad_first, gain, bias = norm_back(
        dot_dims(grad_qkv, qrk[:, : 3 * width], 1, 1), unit, rstd, one_gain[...]
    )
    add_row(0, gain)
    add_row(1, bias)
    grad_mt_ref[...] = grad_mt + grad_first + grad_after

    pick_low = lambda a: dot_dims(a, chosen[...], 1, 0).astype(BF16)
    pick_exact = lambda a: exact_low(a, chosen[...], 0)
    qkv_grad[...] = dot_dims(pick_low(normed), grad_qkv, 0, 0)
    qkv_grad[:, width:] += dot_dims(pick_low(normed_f), grad_f, 0, 0)
    out_grad[...] = dot_dims(pick_low(attended_ref[...]), grad_attn_out, 0, 0)
    expand_grad[...] = dot_dims(pick_low(normed_b), grad_expanded, 0, 0)
    contract_grad[...] = dot_dims(pick_low(grad_contract), activ, 0, 0)
    my_result = pick_exact(result_ref[...])
    read_grad[...] = exact(pick_exact(mt), grad_read_pre, 0, 0)
    key_grad[...] = exact(my_result, grad_key_pre, 0, 0)
    value_grad[...] = exact(my_result, grad_value, 0, 0)


def mem_backward(mt, norms, pooled, shard, group, kept, weights):
    mem, width = mt.shape
    wide, feat = weights[2].shape[1], (weights[0].shape[1] - 3 * width) // 2
    at = lax.broadcasted_iota(jnp.int32, (width, shard), 0) - group * shard
    chosen = (at == lax.broadcasted_iota(jnp.int32, (width, shard), 1)).astype(BF16)
    sizes = (3 * width, width, wide, wide, feat, feat, width)
    shape = jax.ShapeDtypeStruct
    outs = [
        shape((mem, width), F32), *[shape((shard, c), F32) for c in sizes], shape((8, width), F32), shape((1, wide), F32),
    ]
    grad_mt, *rest = mem_call(
        mem_bwd_kernel, "mem_bwd", (mt, *norms, pooled, chosen, *kept), weights, outs, 25
    )
    sums, expand_sums = rest[7:]
    vectors = (sums[0], sums[1], sums[2:4], sums[4], sums[5], sums[6], expand_sums[0], sums[7])
    return grad_mt, tuple(rest[:7]), vectors


def gather_kernel(halved, count, kinds, *refs):
    shards, outs = refs[:count], refs[count : 2 * count]
    send_sem, recv_sem, local_sem = refs[2 * count :]
    index, plane = lax.axis_index("dp"), lax.axis_index("ctx")
    deep, cross, core = index // 4, (index // 2) % 2, index % 2
    place = lambda z, x, c: (z * 2 + x) * 2 + c
    up, down = {"dp": place(deep + 1, cross, core)}, {"dp": place(deep - 1, cross, core)}
    beside, sibling = {"dp": place(deep, 1 - cross, core)}, {"dp": place(deep, cross, 1 - core)}
    other = {"ctx": 1 - plane}
    rows = shards[0].shape[0]
    numbers, sends = {}, []

    def valid(kind):
        way, far = kind
        return deep >= 0 if way == "own" else deep >= far if way == "below" else deep + far <= 3

    def level(kind):
        way, far = kind
        return deep if way == "own" else deep - far if way == "below" else deep + far

    def view(k, z, x, c, part):
        at = pl.ds(pl.multiple_of(place(z, x, c) * rows, 16), rows)
        return outs[k].at[at, :] if part is None else outs[k].at[at, half(k, part)]

    def half(k, part):
        wide = outs[k].shape[1] // 2
        return pl.ds(pl.multiple_of(part * wide, 128), wide)

    def copy(key, source, landing, device):
        number = numbers.setdefault(key, len(numbers))
        return pltpu.make_async_remote_copy(
            source, landing, send_sem.at[number], recv_sem.at[number],
            device_id=device, device_id_type=pl.DeviceIdType.MESH,
        )

    def send(when, key, source, landing, device):
        def begin():
            copy(key, source, landing, device).start()

        def end():
            copy(key, source, landing, device).wait_send()

        sends.append((when, end))
        if when is None:
            begin()
        else:
            pl.when(when)(begin)

    def arrived(key, landing):
        copy(key, landing, landing, sibling).wait_recv()

    barrier = pltpu.get_barrier_semaphore()
    for device in (beside, sibling, other):
        pl.semaphore_signal(barrier, inc=1, device_id=device, device_id_type=pl.DeviceIdType.MESH)
    for when, device in ((deep < 3, up), (deep > 0, down)):

        @pl.when(when)
        def _(device=device):
            pl.semaphore_signal(barrier, inc=1, device_id=device, device_id_type=pl.DeviceIdType.MESH)

    inner = (deep > 0) & (deep < 3)
    for when, peers in ((inner, 5), (jnp.logical_not(inner), 4)):

        @pl.when(when)
        def _(peers=peers):
            pl.semaphore_wait(barrier, peers)

    own = ("own", 0)
    locals_ = []
    for k in range(count):
        part = plane if k in halved else None
        mine = view(k, deep, cross, core, None)
        locals_.append(pltpu.make_async_copy(shards[k], mine, local_sem.at[k]))
        locals_[-1].start()
        source = shards[k] if part is None else shards[k].at[:, half(k, part)]
        landing = view(k, deep, cross, core, part)
        send(deep < 3, ("z", ("below", 1), k), source, landing, up)
        send(deep > 0, ("z", ("above", 1), k), source, landing, down)
        send(None, ("x", own, k), source, landing, beside)
        send(None, ("core", "z", own, k), shards[k], mine, sibling)

    def onward(k, flow, kind, x):
        part = plane if k in halved else None
        block = view(k, level(kind), x, core, part)
        ok = valid(kind)
        if flow == "z":
            way, far = kind
            if far < 3:
                if way == "below":
                    send(ok & (deep < 3), ("z", (way, far + 1), k), block, block, up)
                else:
                    send(ok & (deep > 0), ("z", (way, far + 1), k), block, block, down)
            send(ok, ("x", kind, k), block, block, beside)
        send(ok, ("core", flow, kind, k), block, block, sibling)
        if k in halved:
            send(ok, ("y", flow, kind, k), block, block, other)

    def take(flow, kind):
        x = cross if flow == "z" else 1 - cross
        for k in range(count):
            part = plane if k in halved else None

            @pl.when(valid(kind))
            def _():
                arrived((flow, kind, k), view(k, level(kind), x, core, part))

            onward(k, flow, kind, x)

    for far in range(1, 4):
        take("z", ("below", far))
        take("z", ("above", far))
        for kind in kinds:
            if kind[1] == far - 1:
                take("x", kind)
    for kind in kinds:
        if kind[1] == 3:
            take("x", kind)
    crossing = [(flow, kind, k) for flow in ("z", "x") for kind in kinds for k in halved]
    crossing = [c for c in crossing if c[:2] != ("z", own)]
    for flow, kind, k in crossing:
        x = cross if flow == "z" else 1 - cross
        block = lambda c: view(k, level(kind), x, c, 1 - plane)

        @pl.when(valid(kind))
        def _():
            arrived(("y", flow, kind, k), block(core))

        send(valid(kind), ("core", "y", flow, kind, k), block(core), block(core), sibling)
    for flow in ("z", "x"):
        x = cross if flow == "z" else 1 - cross
        for kind in kinds:
            for k in range(count):
                part = plane if k in halved and (flow, kind) != ("z", own) else None

                @pl.when(valid(kind))
                def _():
                    arrived(("core", flow, kind, k), view(k, level(kind), x, 1 - core, part))

    for flow, kind, k in crossing:
        x = cross if flow == "z" else 1 - cross

        @pl.when(valid(kind))
        def _():
            arrived(("core", "y", flow, kind, k), view(k, level(kind), x, 1 - core, 1 - plane))

    for when, end in sends:
        if when is None:
            end()
        else:
            pl.when(when)(end)
    for held in locals_:
        held.wait()


def gather_weights(shards, halved):
    kinds = [("own", 0)] + [(way, far) for far in (1, 2, 3) for way in ("below", "above")]
    count = len(shards)
    rows = shards[0].shape[0] * 16
    copies = 6 * count + 7 * count + 13 * len(halved) + 14 * count + 13 * len(halved)
    any_space = pl.BlockSpec(memory_space=pl.ANY)
    return pl.pallas_call(
        functools.partial(gather_kernel, halved, count, kinds),
        in_specs=[any_space] * count,
        out_specs=[any_space] * count,
        out_shape=[jax.ShapeDtypeStruct((rows, s.shape[1]), BF16) for s in shards],
        scratch_shapes=[
            pltpu.SemaphoreType.DMA((copies,)),
            pltpu.SemaphoreType.DMA((copies,)),
            pltpu.SemaphoreType.DMA((count,)),
        ],
        compiler_params=pltpu.CompilerParams(
            collective_id=0, has_side_effects=True, vmem_limit_bytes=4 * 2**20
        ),
        cost_estimate=pl.CostEstimate(
            flops=8 * 10**10, bytes_accessed=4 * rows * sum(s.shape[1] for s in shards), transcendentals=0
        ),
        name="gather_weights",
    )(*shards)


def dp_pairs(flip):
    return [(i, i ^ flip) for i in range(16)]


def behind(value, *earlier):
    return lax.optimization_barrier((value, earlier))[0]


def pick(parts, at, axis):
    return lax.dynamic_index_in_dim(parts, at, axis, keepdims=False)


def add_low(a, b):
    return (a.astype(F32) + b.astype(F32)).astype(BF16)


def reduce_kernel(planes, cuts, swaps, *refs):
    count = 1 + max(k for k, _, _ in cuts)
    grads, gives = refs[:count], refs[count : count + swaps]
    long_ref, short_ref = refs[count + swaps : count + swaps + 2]
    outs = refs[count + swaps + 2 : 2 * count + swaps + 2]
    gots = refs[2 * count + swaps + 2 : 2 * count + 2 * swaps + 2]
    long_out, short_out = refs[2 * count + 2 * swaps + 2 : 2 * count + 2 * swaps + 4]
    (
        mine, got_core, got_x, line, got_z, low, got_y, parts, held, total,
        load_sem, core_sem, x_sem, z_sem, y_sem, swap_sem, sum_sem,
    ) = refs[2 * count + 2 * swaps + 4 :]
    index, plane = lax.axis_index("dp"), lax.axis_index("ctx")
    deep, cross, core = index // 4, (index // 2) % 2, index % 2
    place = lambda z, x, c: (z * 2 + x) * 2 + c
    deeps = (deep + 1 - 2 * lax.rem(deep, 2), lax.rem(deep + 2, 4), 3 - deep)
    beside, sibling = {"dp": place(deep, 1 - cross, core)}, {"dp": place(deep, cross, 1 - core)}
    other = {"ctx": 1 - plane}
    chunks = len(cuts)
    peers = long_ref.shape[0]
    rows = long_ref.shape[1]
    me = index * planes + plane

    def remote(source, landing, sems, at, device):
        return pltpu.make_async_remote_copy(
            source, landing, sems.at[(0, *at)], sems.at[(1, *at)], device_id=device, device_id_type=pl.DeviceIdType.MESH
        )

    def device(j):
        return (j // planes, lax.rem(j, planes))

    def small(phase, j, sender):
        source, landing = (parts.at[j], held.at[sender]) if phase == 0 else (total.at[sender], total.at[sender])
        return pltpu.make_async_remote_copy(
            source, landing, sum_sem.at[0, phase, j], sum_sem.at[1, phase, sender],
            device_id=device(j), device_id_type=pl.DeviceIdType.MESH,
        )

    def every(work):
        def body(step, carry):
            work(lax.rem(me + step, peers))
            return carry

        lax.fori_loop(1, peers, body, 0)

    def loop(first, last, work):
        def body(c, carry):
            work(c)
            return carry

        lax.fori_loop(first, last, body, 0)

    def load(c, x):
        k, start, wide = cuts[c]
        return pltpu.make_async_copy(
            grads[k].at[:, x, core, :, pl.ds(start, wide)], mine.at[c, x], load_sem.at[c, x]
        )

    def to_core(c, x):
        k, start, wide = cuts[c]
        return remote(
            grads[k].at[:, x, 1 - core, :, pl.ds(start, wide)], got_core.at[c, x], core_sem, (c, x), sibling
        )

    def swap(k):
        return remote(gives[k].at[1 - plane], gots[k], swap_sem, (k,), other)

    def arrived(landing, sems, at):
        remote(landing, landing, sems, at, sibling).wait_recv()

    def to_x(c):
        return remote(mine.at[c, 1 - cross], got_x.at[c], x_sem, (c,), beside)

    def to_z(c, k):
        return remote(line.at[c, deeps[k]], got_z.at[c, k], z_sem, (c, k), {"dp": place(deeps[k], cross, core)})

    def to_y(c):
        return remote(low.at[c], got_y.at[c], y_sem, (c,), other)

    for c in range(chunks):
        for x in range(2):
            load(c, x).start()
    parts[:, :rows, :] = long_ref[...]
    parts[:, rows:, :] = short_ref[...]
    barrier = pltpu.get_barrier_semaphore()
    every(lambda j: pl.semaphore_signal(barrier, inc=1, device_id=device(j), device_id_type=pl.DeviceIdType.MESH))
    pl.semaphore_wait(barrier, peers - 1)
    for c in range(chunks):
        for x in range(2):
            to_core(c, x).start()
    every(lambda j: small(0, j, me).start())
    for k in range(swaps):
        swap(k).start()
    held[me] = parts[me]

    def over_core(c):
        for x in range(2):
            pltpu.make_async_copy(mine.at[c, x], mine.at[c, x], load_sem.at[c, x]).wait()
            arrived(got_core.at[c, x], core_sem, (c, x))
            for z in range(4):
                mine[c, x, z] = add_low(mine[c, x, z], got_core[c, x, z])
        to_x(c).start()

    loop(0, chunks, over_core)
    every(lambda j: small(0, j, j).wait_recv())
    total[me] = jnp.sum(held[...], axis=0)
    every(lambda j: small(1, j, me).start())

    def over_x(c):
        arrived(got_x.at[c], x_sem, (c,))
        for z in range(4):
            line[c, z] = add_low(mine[c, cross, z], got_x[c, z])
        for k in range(3):
            to_z(c, k).start()

    def over_z(c):
        value = line[c, deep].astype(F32)
        for k in range(3):
            arrived(got_z.at[c, k], z_sem, (c, k))
            value = value + got_z[c, k].astype(F32)
        low[c] = value.astype(BF16)
        to_y(c).start()

    def both(c):
        over_x(c)
        over_z(c - 1)

    over_x(0)
    loop(1, chunks, both)
    over_z(chunks - 1)
    for c, (k, start, wide) in enumerate(cuts):
        arrived(got_y.at[c], y_sem, (c,))
        outs[k][:, start : start + wide] = low[c].astype(F32) + got_y[c].astype(F32)
    every(lambda j: small(1, j, j).wait_recv())
    long_out[...] = total[:, :rows, :]
    short_out[...] = total[:, rows:, :]
    for k in range(swaps):
        swap(k).wait_recv()
    every(lambda j: small(0, j, me).wait_send())
    every(lambda j: small(1, j, me).wait_send())
    for k in range(swaps):
        swap(k).wait_send()
    for c in range(chunks):
        for x in range(2):
            to_core(c, x).wait_send()

    def finish(c):
        to_x(c).wait_send()
        for k in range(3):
            to_z(c, k).wait_send()
        to_y(c).wait_send()

    loop(0, chunks, finish)


def reduce_all(grads, gives, long, short, planes):
    wide = 768
    shard = grads[0].shape[0] // 16
    cuts = [(k, at, wide) for k, g in enumerate(grads) for at in range(0, g.shape[1], wide)]
    chunks, peers = len(cuts), long.shape[0]
    small = (peers, long.shape[1] + short.shape[1], long.shape[2])
    vmem, hbm = pl.BlockSpec(memory_space=pltpu.VMEM), pl.BlockSpec(memory_space=pl.ANY)
    shape = jax.ShapeDtypeStruct
    dma = pltpu.SemaphoreType.DMA
    low = lambda *dims: pltpu.VMEM((chunks, *dims, shard, wide), BF16)
    out = pl.pallas_call(
        functools.partial(reduce_kernel, planes, cuts, len(gives)),
        in_specs=[hbm] * (len(grads) + len(gives)) + [vmem] * 2,
        out_specs=[vmem] * len(grads) + [hbm] * len(gives) + [vmem] * 2,
        out_shape=[shape((shard, g.shape[1]), F32) for g in grads]
        + [shape(g.shape[1:], BF16) for g in gives]
        + [shape(v.shape, F32) for v in (long, short)],
        scratch_shapes=[
            low(2, 4), low(2, 4), low(4), low(4), low(3), low(), low(),
            *[pltpu.VMEM(small, F32)] * 3,
            dma((chunks, 2)), dma((2, chunks, 2)), dma((2, chunks)), dma((2, chunks, 3)), dma((2, chunks)),
            dma((2, len(gives))), dma((2, 2, peers)),
        ],
        compiler_params=pltpu.CompilerParams(
            collective_id=1, has_side_effects=True, vmem_limit_bytes=60 * 2**20
        ),
        cost_estimate=pl.CostEstimate(flops=8 * 10**10, bytes_accessed=50 * 10**6, transcendentals=0),
        name="reduce_all",
    )(*[g.reshape(4, 2, 2, shard, g.shape[1]) for g in grads], *gives, long, short)
    return out[: len(grads)], out[len(grads) : len(grads) + len(gives)], out[-2], out[-1]


def split_heads(rows):
    return rows.reshape(rows.shape[0], rows.shape[1], H, HD)


def plain_scores(query, key, allowed):
    scores = jnp.einsum("sqhd,skhd->shqk", query, key, preferred_element_type=F32) * HD**-0.5
    return scores, allowed[None, None]


def plain_fwd(qkv, kv_all, allowed):
    width = qkv.shape[2] // 3
    query = split_heads(qkv[:, :, :width])
    key, value = split_heads(kv_all[:, :, :width]), split_heads(kv_all[:, :, width:])
    scores, allowed = plain_scores(query, key, allowed)
    raw = jnp.where(allowed, jnp.exp(scores), 0.0)
    total = jnp.sum(raw, axis=-1)
    weights = (raw / total[..., None]).astype(BF16)
    mixed = jnp.einsum("shqk,skhd->sqhd", weights, value, preferred_element_type=F32)
    return mixed.reshape(qkv.shape[0], -1, width).astype(BF16), jnp.log(total)


def plain_bwd(qkv, kv_all, allowed, log_total, grad):
    segs, width = qkv.shape[0], qkv.shape[2] // 3
    query = split_heads(qkv[:, :, :width])
    key, value = split_heads(kv_all[:, :, :width]), split_heads(kv_all[:, :, width:])
    grad = split_heads(grad)
    scores, allowed = plain_scores(query, key, allowed)
    prob = jnp.where(allowed, jnp.exp(scores - log_total[..., None]), 0.0)
    grad_p = jnp.einsum("sqhd,skhd->shqk", grad, value, preferred_element_type=F32)
    inner = jnp.sum(prob * grad_p, axis=-1, keepdims=True)
    grad_s = (prob * (grad_p - inner) * HD**-0.5).astype(BF16)
    dq = jnp.einsum("shqk,skhd->sqhd", grad_s, key, preferred_element_type=F32)
    dk = jnp.einsum("shqk,sqhd->skhd", grad_s, query, preferred_element_type=F32)
    dv = jnp.einsum("shqk,sqhd->skhd", prob.astype(BF16), grad, preferred_element_type=F32)
    flat = lambda a: a.reshape(segs, -1, width)
    return flat(dq), jnp.concatenate([flat(dk), flat(dv)], axis=2)


def memory_forward(mt, p):
    mem = mt.shape[0]
    keep = {}
    width = mt.shape[1]
    unit, rstd = norm_parts(mt)
    normed = (unit * p["one_gain"] + p["one_bias"]).astype(BF16)
    qkv = (dot_dims(normed, p["qkv"], 1, 0) + p["shift"]).astype(BF16)
    at = jnp.arange(mem, dtype=jnp.int32)
    allowed = at[None, :] <= at[:, None]
    attended, log_total = plain_fwd(qkv[None], qkv[None, :, width:], allowed)
    attended = attended[0]
    after = mt + dot_dims(attended, p["out"], 1, 0) + p["out_bias"]
    unit_b, rstd_b = norm_parts(after)
    normed_b = (unit_b * p["two_gain"] + p["two_bias"]).astype(BF16)
    expanded = dot_dims(normed_b, p["expand"], 1, 0) + p["expand_bias"]
    activ = gelu_tanh(expanded).astype(BF16)
    result = after + dot_dims(activ, p["contract"], 1, 1) + p["contract_bias"]
    key_pre = exact(result, p["key"].astype(F32), 1, 0)
    value_new = exact(result, p["value"].astype(F32), 1, 0)
    read_pre = exact(mt, p["read"].astype(F32), 1, 0)
    key_feat, key_pull = jax.vjp(feature_map, key_pre)
    read_feat, read_pull = jax.vjp(feature_map, read_pre)
    mix = exact(read_feat, key_feat, 1, 1)
    numer = exact(mix, value_new, 1, 0)
    denom = 1.0 + jnp.sum(mix, axis=1, keepdims=True)
    follow = mt + numer / denom
    unit_f, rstd_f = norm_parts(follow)
    normed_f = (unit_f * p["one_gain"] + p["one_bias"]).astype(BF16)
    kv_follow = (dot_dims(normed_f, p["qkv"][:, width:], 1, 0) + p["shift"][width:]).astype(BF16)
    keep = dict(
        unit=unit, rstd=rstd, normed=normed, qkv=qkv, allowed=allowed, attended=attended,
        log_total=log_total, unit_b=unit_b, rstd_b=rstd_b, normed_b=normed_b, expanded=expanded,
        activ=activ, result=result, key_feat=key_feat, read_feat=read_feat, key_pull=key_pull,
        read_pull=read_pull, value_new=value_new, mix=mix, numer=numer, denom=denom, unit_f=unit_f,
        rstd_f=rstd_f, normed_f=normed_f,
    )
    return qkv[:, width:], kv_follow, keep


def memory_backward(mt, p, m, grad_kv_first, grad_kv_follow, mine):
    width = mt.shape[1]
    low = lambda a: a.astype(BF16)
    grad_f = low(grad_kv_follow)
    grad_follow, gain_f, bias_f = norm_back(
        dot_dims(grad_f, p["qkv"][:, width:], 1, 1), m["unit_f"], m["rstd_f"], p["one_gain"]
    )
    grad_mt = grad_follow
    grad_numer = grad_follow / m["denom"]
    grad_denom = -jnp.sum(grad_follow * m["numer"], axis=1, keepdims=True) / (m["denom"] * m["denom"])
    grad_mix = exact(grad_numer, m["value_new"], 1, 1) + grad_denom
    grad_value = exact(m["mix"], grad_numer, 0, 0)
    [grad_read_pre] = m["read_pull"](exact(grad_mix, m["key_feat"], 1, 0))
    [grad_key_pre] = m["key_pull"](exact(grad_mix, m["read_feat"], 0, 0))
    grad_mt = grad_mt + exact(grad_read_pre, p["read"].astype(F32), 1, 1)
    grad_result = exact(grad_key_pre, p["key"].astype(F32), 1, 1) + exact(
        grad_value, p["value"].astype(F32), 1, 1
    )
    grad_contract = low(grad_result)
    _, gelu_pull = jax.vjp(gelu_tanh, m["expanded"])
    grad_expanded = low(gelu_pull(dot_dims(grad_contract, p["contract"], 1, 0))[0])
    grad_after, two_gain, two_bias = norm_back(
        dot_dims(grad_expanded, p["expand"], 1, 1), m["unit_b"], m["rstd_b"], p["two_gain"]
    )
    grad_after = grad_after + grad_result
    grad_attn_out = low(grad_after)
    grad_attended = low(dot_dims(grad_attn_out, p["out"], 1, 1))
    dq, dkv = plain_bwd(
        m["qkv"][None], m["qkv"][None, :, width:], m["allowed"], m["log_total"], grad_attended[None]
    )
    grad_qkv = low(jnp.concatenate([dq[0], dkv[0] + grad_kv_first], axis=1))
    grad_first, gain_a, bias_a = norm_back(
        dot_dims(grad_qkv, p["qkv"], 1, 1), m["unit"], m["rstd"], p["one_gain"]
    )
    grad_mt = grad_mt + grad_first + grad_after
    wide = grad_qkv.astype(F32)
    kv_rows = grad_f.astype(F32)
    sums = jnp.sum(wide, axis=0)
    follow_sums = jnp.sum(kv_rows, axis=0)
    matrices = (
        dot_dims(mine(m["normed"]), grad_qkv, 0, 0)
        + jnp.concatenate(
            [
                jnp.zeros((mine(mt).shape[1], width), F32),
                dot_dims(mine(m["normed_f"]), grad_f, 0, 0),
            ],
            axis=1,
        ),
        dot_dims(mine(m["attended"]), grad_attn_out, 0, 0),
        dot_dims(mine(m["normed_b"]), grad_expanded, 0, 0),
        dot_dims(mine(grad_contract), m["activ"], 0, 0),
        exact(mine(mt), grad_read_pre, 0, 0),
        exact(mine(m["result"]), grad_key_pre, 0, 0),
        exact(mine(m["result"]), grad_value, 0, 0),
    )
    column_sum = lambda a: jnp.sum(a.astype(F32), axis=0)
    vectors = (
        gain_f + gain_a,
        bias_f + bias_a,
        jnp.stack([sums[:width], sums[2 * width :] + follow_sums[width:]]),
        column_sum(grad_attn_out),
        two_gain,
        two_bias,
        column_sum(grad_expanded),
        column_sum(grad_contract),
    )
    return grad_mt, matrices, vectors


def local(
    tokens,
    cotangent,
    placing,
    starts,
    memory_tokens,
    norm_one_gain,
    norm_one_bias,
    qkv_weight,
    qv_bias,
    out_weight,
    out_bias,
    norm_two_gain,
    norm_two_bias,
    expand_weight,
    expand_bias,
    contract_weight,
    contract_bias,
    read_weight,
    key_weight,
    value_weight,
):
    del placing
    groups, ranks = lax.axis_size("dp"), lax.axis_size("ctx")
    group, rank = lax.axis_index("dp"), lax.axis_index("ctx")
    micros, segs_local, tok_rows, width = tokens.shape
    mem = memory_tokens.shape[0]
    shard = qkv_weight.shape[0]
    quick = groups == 16 and ranks == 2 and micros == 2 and segs_local == 2 and (tok_rows * ranks) % WIDE == 0
    names = ("qkv", "out", "expand", "contract", "read", "key", "value")
    shards = (qkv_weight, out_weight, expand_weight, contract_weight, read_weight, key_weight, value_weight)
    if quick:
        give = pick(tokens, 1 - rank, 0)
        joined = (
            jnp.concatenate([qkv_weight, read_weight, key_weight], axis=1),
            expand_weight,
            contract_weight,
            jnp.concatenate([out_weight, value_weight], axis=1),
        )
        qkv_read_key, expand_full, contract_full, out_value = gather_weights(
            behind(joined, give), (2, 3)
        )
        feat = read_weight.shape[1]
        whole = (
            qkv_read_key[:, : 3 * width],
            out_value[:, :width],
            expand_full,
            contract_full,
            qkv_read_key[:, 3 * width : 3 * width + feat],
            qkv_read_key[:, 3 * width + feat :],
            out_value[:, width:],
        )
    else:
        whole = tuple(lax.all_gather(s, "dp", axis=0, tiled=True) for s in shards)
    p = dict(zip(names, whole))
    p.update(
        one_gain=norm_one_gain, one_bias=norm_one_bias, out_bias=out_bias, two_gain=norm_two_gain,
        two_bias=norm_two_bias, expand_bias=expand_bias, contract_bias=contract_bias,
        shift=jnp.concatenate([qv_bias[0], jnp.zeros((width,), F32), qv_bias[1]]),
    )
    flags = lax.dynamic_slice_in_dim(starts, group * segs_local, segs_local, 1)

    swap = [(0, 1), (1, 0)]

    def own_and_other(rows):
        halves = rows.reshape(ranks, tok_rows, width)
        return pick(halves, rank, 0), pick(halves, 1 - rank, 0)

    def swapped(given):
        return lax.ppermute(given, "ctx", swap)

    def settle(halves, flips):
        micro_rows = []
        for micro in range(2):
            pair = [jnp.where(rank == micro, kept, got) for kept, got in halves]
            flip = flips[micro]
            micro_rows.append(
                jnp.stack([jnp.where(flip, pair[1], pair[0]), jnp.where(flip, pair[0], pair[1])])
            )
        return jnp.stack(micro_rows)

    if quick:
        flips = flags[:, 1] == 1
        flip = pick(flips, rank, 0)
        told = jnp.stack([flip.astype(jnp.int32), rank.astype(jnp.int32)])
        got = swapped(give)
        give_grad = pick(behind(cotangent, got, expand_full), 1 - rank, 0)
        flags = pick(flags, rank, 0)
        flags = jnp.where(flip, flags[::-1], flags)
        segs = segs_local
        seg_rows = ranks * tok_rows
    else:
        rows_in, rows_grad = tokens.reshape(-1, width), cotangent.reshape(-1, width)
        flags = flags.reshape(-1)
        segs = micros * segs_local
        seg_rows = tok_rows

    if quick:
        norms = tuple(v[None] for v in (norm_one_gain, norm_one_bias, norm_two_gain, norm_two_bias))
        fixed = tuple(v[None] for v in (p["shift"], out_bias, expand_bias, contract_bias))
        mem_weights_in = (qkv_read_key, out_value, expand_full, contract_full)
        *kept, kv_follow = mem_forward(memory_tokens, (*norms, *fixed), mem_weights_in)
        kv_first = kept[0][:, width:]
    else:
        kv_first, kv_follow, m = memory_forward(memory_tokens, p)
    kv_mem = jnp.where((flags == 0)[:, None, None], kv_follow[None], kv_first[None])
    if quick:
        rows_in, normed_a, qkv = enter(
            told, tokens, got, norm_one_gain, norm_one_bias, qkv_read_key, p["shift"]
        )
        attended, lse_first = attn_fwd(behind(qkv, give_grad), kv_first, 0, seg_rows, None)
        got_grad = swapped(give_grad)
        attended, lse_second = attn_fwd(qkv, kv_mem[1], 1, seg_rows, attended)
        attended, got_grad = lax.optimization_barrier((attended, got_grad))
        (
            result, rows_grad, normed_b, activ, grad_expanded, grad_attn_out, grad_attended, mid_sums, expand_sums,
        ) = middle(
            told, cotangent, got_grad, rows_in, attended, p["out"], p["expand"], p["contract"], out_bias,
            norm_two_gain, norm_two_bias, expand_bias, contract_bias,
        )
        grad_after = grad_attn_out
    else:
        hidden = rows_in.astype(F32)
        unit_a, rstd_a = norm_parts(hidden)
        normed_a = (unit_a * norm_one_gain + norm_one_bias).astype(BF16)
        qkv = (dot_dims(normed_a, p["qkv"], 1, 0) + p["shift"]).astype(BF16)
        seg_qkv = qkv.reshape(segs, seg_rows, 3 * width)
        kv_all = lax.all_gather(seg_qkv[:, :, width:], "ctx", axis=1, tiled=True)
        kv_all = jnp.concatenate([kv_mem, kv_all], axis=1)
        query_at = mem + rank * seg_rows + jnp.arange(seg_rows, dtype=jnp.int32)
        key_at = jnp.arange(mem + ranks * seg_rows, dtype=jnp.int32)
        allowed = key_at[None, :] <= query_at[:, None]
        attended, lse = plain_fwd(seg_qkv, kv_all, allowed)
        attended = attended.reshape(-1, width)
        after = hidden + dot_dims(attended, p["out"], 1, 0) + out_bias
        unit_b, rstd_b = norm_parts(after)
        normed_b = (unit_b * norm_two_gain + norm_two_bias).astype(BF16)
        expanded = dot_dims(normed_b, p["expand"], 1, 0) + expand_bias
        activ = gelu_tanh(expanded).astype(BF16)
        result = (after + dot_dims(activ, p["contract"], 1, 1) + contract_bias).astype(BF16)

    def input_back(at, grads, weights):
        grad = dot_dims(grads[0], weights[0], 1, 1)
        for g, w in zip(grads[1:], weights[1:]):
            grad = grad + dot_dims(g, w, 1, 1)
        unit, rstd = norm_parts(rows_in[at].astype(F32))
        grad_hidden, gain, bias = norm_back(grad, unit, rstd, norm_one_gain)
        return (grad_hidden + grad_after[at].astype(F32)).astype(BF16), gain, bias

    def pool(dkv_mem):
        follows = (flags == 0).astype(F32)[:, None, None]
        kinds = [jnp.sum(dkv_mem * (1.0 - follows), axis=0), jnp.sum(dkv_mem * follows, axis=0)]
        return jnp.stack(kinds)

    if quick:
        lse = jnp.concatenate([lse_first, lse_second], axis=0)
        mems = (kv_first, kv_mem[1])
        spans = [slice(0, seg_rows), slice(seg_rows, 2 * seg_rows)]
        dk_mem, dv_mem, middle_sums = attn_mem(qkv, kv_mem, attended, grad_attended, lse)
        pooled = pool(jnp.concatenate([dk_mem, dv_mem], axis=2))
        grads = [
            attn_bwd(qkv, mems[seg], grad_attended, lse, middle_sums, seg, 0, H // 2) for seg in range(2)
        ]
        ends = [input_back(spans[k], [grads[k]], [p["qkv"]]) for k in range(2)]
        one_gain, one_bias = ends[0][1] + ends[1][1], ends[0][2] + ends[1][2]
        qkv_sums = sum(jnp.sum(g.astype(F32), axis=0) for g in grads).reshape(3, width)
        terms = (
            dot_dims(rows_grad, activ, 0, 0).astype(BF16),
            dot_dims(normed_b, grad_expanded, 0, 0).astype(BF16),
            sum(dot_dims(normed_a[spans[k]], grads[k], 0, 0) for k in range(2)).astype(BF16),
            dot_dims(attended, grad_attn_out, 0, 0).astype(BF16),
        )
    else:
        _, gelu_pull = jax.vjp(gelu_tanh, expanded)
        grad_expanded = gelu_pull(dot_dims(rows_grad, p["contract"], 1, 0))[0].astype(BF16)
        grad_after, two_gain, two_bias = norm_back(
            dot_dims(grad_expanded, p["expand"], 1, 1), unit_b, rstd_b, norm_two_gain
        )
        grad_after = grad_after + rows_grad.astype(F32)
        grad_attn_out = grad_after.astype(BF16)
        grad_attended = dot_dims(grad_attn_out, p["out"], 1, 1).astype(BF16)
        dq, dkv = plain_bwd(
            seg_qkv, kv_all, allowed, lse, grad_attended.reshape(segs, seg_rows, width)
        )
        pooled = pool(dkv[:, :mem])
        dkv = lax.psum_scatter(
            dkv[:, mem:].astype(BF16), "ctx", scatter_dimension=1, tiled=True
        )
        grad_qkv = jnp.concatenate([dq.astype(BF16), dkv], axis=2).reshape(-1, 3 * width)
        grad_rows, one_gain, one_bias = input_back(slice(None), [grad_qkv], [p["qkv"]])
        terms = (
            dot_dims(normed_a, grad_qkv, 0, 0).astype(BF16),
            dot_dims(attended, grad_attn_out, 0, 0).astype(BF16),
            dot_dims(normed_b, grad_expanded, 0, 0).astype(BF16),
            dot_dims(rows_grad, activ, 0, 0).astype(BF16),
        )
        qkv_sums = jnp.sum(grad_qkv.astype(F32), axis=0).reshape(3, width)
    column_sum = lambda a: jnp.sum(a.astype(F32), axis=0)
    if quick:
        mid = (mid_sums[0], mid_sums[1], mid_sums[2], expand_sums[0], mid_sums[3])
    else:
        mid = (
            column_sum(grad_attn_out), two_gain, two_bias, column_sum(grad_expanded), column_sum(rows_grad),
        )
    vectors = (one_gain, one_bias, jnp.stack([qkv_sums[0], qkv_sums[2]]), *mid)
    if not quick:
        summed = tuple(
            lax.psum(
                lax.psum_scatter(t, "dp", scatter_dimension=0, tiled=True).astype(F32), "ctx"
            )
            for t in terms
        )
        pooled, vectors = lax.psum((pooled, vectors), ("dp", "ctx"))

    if quick:
        peers = groups * ranks
        flat = jnp.concatenate([v.reshape(-1) for v in vectors])
        lines = pl.cdiv(flat.size, peers * 128)
        flat = jnp.pad(flat, (0, peers * lines * 128 - flat.size)).reshape(peers, lines, 128)
        halves = [r.reshape(ranks, tok_rows, width) for r in (result[spans[0]], result[spans[1]], ends[0][0], ends[1][0])]
        summed, gots, pooled, flat = reduce_all(
            terms, halves, pooled.reshape(peers, -1, 128), flat, ranks
        )
        summed = (summed[2], summed[3], summed[1], summed[0])
        flat = flat.reshape(-1)
        pooled = pooled.reshape(2, mem, 2 * width)
        grad_mt, mem_matrices, mem_vectors = mem_backward(
            memory_tokens, norms, pooled, shard, group, kept, mem_weights_in
        )
    else:
        mine = lambda a: lax.dynamic_slice_in_dim(a, group * shard, shard, 1)
        grad_mt, mem_matrices, mem_vectors = memory_backward(
            memory_tokens, p, m, pooled[0], pooled[1], mine
        )
    if quick:
        split, place = [], 0
        for v in vectors:
            split.append(flat[place : place + v.size].reshape(v.shape))
            place += v.size
        vectors = tuple(split)
    matrices = tuple(a + b for a, b in zip(summed, mem_matrices)) + mem_matrices[4:]
    vectors = tuple(a + b for a, b in zip(vectors, mem_vectors))
    if quick:
        own = [pick(h, rank, 0) for h in halves]
        block_out = settle(list(zip(own[:2], gots[:2])), flips)
        token_grad = settle(list(zip(own[2:], gots[2:])), flips)
    else:
        block_out, token_grad = result.reshape(tokens.shape), grad_rows.reshape(tokens.shape)
    return (
        block_out,
        token_grad,
        grad_mt,
        vectors[0],
        vectors[1],
        matrices[0],
        vectors[2],
        matrices[1],
        vectors[3],
        vectors[4],
        vectors[5],
        matrices[2],
        vectors[6],
        matrices[3],
        vectors[7],
        matrices[4],
        matrices[5],
        matrices[6],
    )


def solution(mesh):
    rows = P(None, "dp", "ctx", None)
    matrix = P("dp", None)
    full = P()
    return jax.shard_map(
        local,
        mesh=mesh,
        in_specs=(
            rows, rows, full, full, full, full, full, matrix, full, matrix, full, full, full,
            matrix, full, matrix, full, matrix, matrix, matrix,
        ),
        out_specs=(
            rows, rows, full, full, full, matrix, full, matrix, full, full, full, matrix, full,
            matrix, full, matrix, matrix, matrix,
        ),
        check_vma=False,
    )
```

```python
import functools

import jax
import jax.numpy as jnp
from jax import lax
from jax.experimental import pallas as pl
from jax.experimental.pallas import tpu as pltpu
from jax.sharding import PartitionSpec as P

H = 12
HD = 64
EPS = 1e-05
CHUNK = 256
WIDE = 512
F32 = jnp.float32
BF16 = jnp.bfloat16


def norm_parts(rows):
    centred = rows - jnp.mean(rows, axis=-1, keepdims=True)
    spread = jnp.mean(centred * centred, axis=-1, keepdims=True)
    rstd = lax.rsqrt(spread + EPS)
    return centred * rstd, rstd


def norm_back(grad, unit, rstd, gain):
    scaled = grad * gain
    first = jnp.mean(scaled, axis=-1, keepdims=True)
    second = jnp.mean(scaled * unit, axis=-1, keepdims=True)
    grad_rows = rstd * (scaled - first - unit * second)
    return grad_rows, jnp.sum(grad * unit, axis=0), jnp.sum(grad, axis=0)


def feature_map(rows):
    halves = jnp.concatenate([jax.nn.softplus(rows), jax.nn.softplus(-rows)], axis=-1)
    return jnp.concatenate([halves * jnp.roll(halves, j, axis=-1) for j in (1, 2, 3)], axis=-1)


def gelu_tanh(rows):
    return jax.nn.gelu(rows, approximate=True)


def dot_dims(a, b, ca, cb, precision=None):
    return lax.dot_general(
        a, b, (((ca,), (cb,)), ((), ())), precision=precision, preferred_element_type=F32
    )


exact = functools.partial(dot_dims, precision=lax.Precision.HIGHEST)


def head_rows(scale):
    lane = lax.broadcasted_iota(jnp.int32, (1, 2 * HD), 1)
    low = jnp.where(lane < HD, scale, 0.0).astype(BF16)
    high = jnp.where(lane < HD, 0.0, scale).astype(BF16)
    return low, high


def causal_tail(scores):
    key = lax.broadcasted_iota(jnp.int32, scores.shape, 0)
    return jnp.where(key <= lax.broadcasted_iota(jnp.int32, scores.shape, 1), scores, 0.0)


def attn_fwd_kernel(q_ref, k_ref, v_ref, km_ref, vm_ref, o_ref, lse_ref, keys, vals_t, vmem_t):
    mem = km_ref.shape[0]
    keys[0:mem, :] = km_ref[...]
    keys[mem:, :] = k_ref[...]
    vals_t[...] = v_ref[...].T
    vmem_t[...] = vm_ref[...].T
    picks = head_rows(HD**-0.5)
    steps = [(part, head) for part in range(q_ref.shape[0] // WIDE) for head in range(2)]

    def begin(part, head):
        lo, hi = part * WIDE, (part + 1) * WIDE
        return dot_dims(keys[0 : mem + hi, :], q_ref[lo:hi, :] * picks[head], 1, 1)

    ahead = begin(*steps[0])
    outs = []
    for n, (part, head) in enumerate(steps):
        lo, hi = part * WIDE, (part + 1) * WIDE
        band = slice(head * HD, (head + 1) * HD)
        raw = jnp.exp(ahead)
        if n + 1 < len(steps):
            ahead = begin(*steps[n + 1])
        raw = jnp.concatenate([raw[: mem + lo], causal_tail(raw[mem + lo :])], axis=0)
        total = jnp.sum(raw, axis=0, keepdims=True)
        lse_ref[0, head : head + 1, lo:hi] = jnp.log(total)
        weights = (raw * (1.0 / total)).astype(BF16)
        outs.append(
            dot_dims(vals_t[band, 0:hi], weights[mem:], 1, 0)
            + dot_dims(vmem_t[band, :], weights[:mem], 1, 0)
        )
        if head == 1:
            o_ref[lo:hi, :] = jnp.concatenate(outs, axis=0).T.astype(BF16)
            outs = []


def attn_fwd_after_kernel(q_ref, k_ref, v_ref, km_ref, vm_ref, held_ref, *rest):
    del held_ref
    attn_fwd_kernel(q_ref, k_ref, v_ref, km_ref, vm_ref, *rest)


def attn_fwd(qkv, kv_mem, seg, rows, held):
    width = qkv.shape[1] // 3
    mem = kv_mem.shape[0]
    pairs = H // 2
    wide = 2 * HD
    spec = lambda off: pl.BlockSpec((rows, wide), lambda p, off=off: (seg, off * pairs + p))
    mspec = lambda off: pl.BlockSpec((mem, wide), lambda p, off=off: (0, off * pairs + p))
    more = [] if held is None else [held]
    return pl.pallas_call(
        attn_fwd_kernel if held is None else attn_fwd_after_kernel,
        grid=(pairs,),
        in_specs=[spec(0), spec(1), spec(2), mspec(0), mspec(1)]
        + [pl.BlockSpec(memory_space=pl.ANY)] * len(more),
        out_specs=[
            pl.BlockSpec((rows, wide), lambda p: (seg, p)),
            pl.BlockSpec((1, 2, rows), lambda p: (p, 0, 0)),
        ],
        out_shape=[
            jax.ShapeDtypeStruct((qkv.shape[0], width), BF16),
            jax.ShapeDtypeStruct((pairs, 2, rows), F32),
        ],
        scratch_shapes=[
            pltpu.VMEM((mem + rows, wide), BF16),
            pltpu.VMEM((wide, rows), BF16),
            pltpu.VMEM((wide, mem), BF16),
        ],
        input_output_aliases={5: 0} if more else {},
        compiler_params=pltpu.CompilerParams(vmem_limit_bytes=60 * 2**20),
        cost_estimate=pl.CostEstimate(
            flops=pairs * rows * rows * 4000,
            bytes_accessed=rows * width * 8,
            transcendentals=0,
        ),
        name="attn_fwd",
    )(qkv, qkv, qkv, kv_mem, kv_mem, *more)


def attn_mem_kernel(q_ref, km_ref, vm_ref, o_ref, g_ref, lse_ref, dkm_ref, dvm_ref, mid_ref):
    scaled_picks, picks = head_rows(HD**-0.5), head_rows(1.0)
    grad, query = g_ref[...], q_ref[...]
    inner = (grad.astype(F32) * o_ref[...].astype(F32)).T
    dk, dv = 0.0, 0.0
    for head in range(2):
        band = slice(head * HD, (head + 1) * HD)
        query_h, grad_h = query * scaled_picks[head], grad * picks[head]
        centre = jnp.sum(inner[band], axis=0, keepdims=True)
        mid_ref[0, head : head + 1, :] = centre
        prob = jnp.exp(dot_dims(km_ref[0], query_h, 1, 1) - lse_ref[0, head : head + 1, :])
        grad_s = (prob * (dot_dims(vm_ref[0], grad_h, 1, 1) - centre)).astype(BF16)
        dv = dv + dot_dims(prob.astype(BF16), grad_h, 1, 0)
        dk = dk + dot_dims(grad_s, query_h, 1, 0)
    dkm_ref[0] = dk
    dvm_ref[0] = dv


def attn_mem(qkv, kv_mem, attended, grad, lse):
    segs, pairs, mem, wide = kv_mem.shape[0], H // 2, kv_mem.shape[1], 2 * HD
    rows, width = lse.shape[2], qkv.shape[1] // 3
    spec = pl.BlockSpec((rows, wide), lambda s, p: (s, p))
    mspec = lambda off: pl.BlockSpec((1, mem, wide), lambda s, p, off=off: (s, 0, off * pairs + p))
    lspec = pl.BlockSpec((1, 2, rows), lambda s, p: (s * pairs + p, 0, 0))
    return pl.pallas_call(
        attn_mem_kernel,
        grid=(segs, pairs),
        in_specs=[spec, mspec(0), mspec(1), spec, spec, lspec],
        out_specs=[mspec(0), mspec(0), lspec],
        out_shape=[
            jax.ShapeDtypeStruct((segs, mem, width), F32),
            jax.ShapeDtypeStruct((segs, mem, width), F32),
            jax.ShapeDtypeStruct((segs * pairs, 2, rows), F32),
        ],
        compiler_params=pltpu.CompilerParams(vmem_limit_bytes=60 * 2**20),
        cost_estimate=pl.CostEstimate(
            flops=segs * rows * width * 4000, bytes_accessed=segs * rows * width * 6, transcendentals=0
        ),
        name="attn_mem",
    )(qkv, kv_mem, kv_mem, attended, grad, lse)


def attn_bwd_kernel(
    q_ref, k_ref, v_ref, km_ref, vm_ref, g_ref, lse_ref, mid_ref,
    out_ref,
    keys, vals, keys_t, kmem_t, dq, dk, dv,
):
    phase = pl.program_id(1)
    mem = km_ref.shape[1]
    rows = q_ref.shape[0]

    @pl.when((phase == 2) & (pl.program_id(0) < pl.num_programs(0) - 1))
    def _():
        keys[0:mem, :] = km_ref[0]
        keys[mem:, :] = k_ref[...]
        vals[0:mem, :] = vm_ref[0]
        vals[mem:, :] = v_ref[...]
        keys_t[...] = k_ref[...].T
        kmem_t[...] = km_ref[0].T
        dk[...] = jnp.zeros_like(dk)
        dv[...] = jnp.zeros_like(dv)
        scaled_picks = head_rows(HD**-0.5)
        picks = head_rows(1.0)
        for part in range(rows // CHUNK):
            lo, hi = part * CHUNK, (part + 1) * CHUNK
            end = mem + hi
            query = q_ref[lo:hi, :]
            grad = g_ref[lo:hi, :]
            dqs = []
            for head in range(2):
                band = slice(head * HD, (head + 1) * HD)
                query_h = query * scaled_picks[head]
                grad_h = grad * picks[head]
                log_total = lse_ref[0, head : head + 1, lo:hi]
                centre = mid_ref[0, head : head + 1, lo:hi]
                prob = jnp.exp(dot_dims(keys[0:end, :], query_h, 1, 1) - log_total)
                prob = jnp.concatenate(
                    [prob[: mem + lo], causal_tail(prob[mem + lo :])], axis=0
                )
                grad_p = dot_dims(vals[0:end, :], grad_h, 1, 1)
                grad_s = (prob * (grad_p - centre)).astype(BF16)
                dv[0:end, :] += dot_dims(prob.astype(BF16), grad_h, 1, 0)
                dk[0:end, :] += dot_dims(grad_s, query_h, 1, 0)
                dqs.append(
                    dot_dims(keys_t[band, 0:hi], grad_s[mem:], 1, 0)
                    + dot_dims(kmem_t[band, :], grad_s[:mem], 1, 0)
                )
            dq[lo:hi, :] = (jnp.concatenate(dqs, axis=0) * HD**-0.5).T.astype(BF16)
        out_ref[...] = dq[...]

    @pl.when((phase == 0) & (pl.program_id(0) > 0))
    def _():
        out_ref[...] = dk[mem:, :].astype(BF16)

    @pl.when((phase == 1) & (pl.program_id(0) > 0))
    def _():
        out_ref[...] = dv[mem:, :].astype(BF16)


def choose(told, kept, got, out):
    own = pl.program_id(0) % 2 == told[1]

    @pl.when(own)
    def _():
        out[...] = kept[0, 0]

    @pl.when(jnp.logical_not(own))
    def _():
        out[...] = got[0]


def half_specs(rows, width):
    return [
        pl.BlockSpec((1, 1, rows, width), lambda i, told: (told[1], (i // 2) ^ told[0], 0, 0)),
        pl.BlockSpec((1, rows, width), lambda i, told: ((i // 2) ^ told[0], 0, 0)),
    ]


def enter_kernel(told, kept, got, gain, bias, weight, shift, rows_ref, normed_ref, qkv_ref):
    choose(told, kept, got, rows_ref)
    unit, _ = norm_parts(rows_ref[...].astype(F32))
    normed = (unit * gain[...] + bias[...]).astype(BF16)
    normed_ref[...] = normed
    wide = weight.shape[1] // 3
    for k in range(3):
        at = slice(k * wide, (k + 1) * wide)
        qkv_ref[:, at] = (dot_dims(normed, weight[:, at], 1, 0) + shift[:, at]).astype(BF16)


def enter(told, kept, got, gain, bias, weight, shift):
    _, segs, rows, width = kept.shape
    whole = lambda r, c: pl.BlockSpec((r, c), lambda i, told: (0, 0), pipeline_mode=pl.Buffered(1))
    block = lambda c: pl.BlockSpec((rows, c), lambda i, told: (i, 0))
    sizes = (width, width, 3 * width)
    return pl.pallas_call(
        enter_kernel,
        grid_spec=pltpu.PrefetchScalarGridSpec(
            num_scalar_prefetch=1,
            grid=(2 * segs,),
            in_specs=[*half_specs(rows, width), whole(1, width), whole(1, width), whole(width, 3 * width), whole(1, 3 * width)],
            out_specs=[block(c) for c in sizes],
        ),
        out_shape=[jax.ShapeDtypeStruct((2 * segs * rows, c), BF16) for c in sizes],
        compiler_params=pltpu.CompilerParams(vmem_limit_bytes=60 * 2**20),
        cost_estimate=pl.CostEstimate(
            flops=8 * segs * rows * width * width * 3, bytes_accessed=segs * rows * width * 28, transcendentals=0
        ),
        name="enter",
    )(told, kept, got, gain[None], bias[None], weight, shift[None])


def middle_kernel(
    told, kept, got, rows_ref, attended, out_w, expand_w, contract_w, out_b, gain, bias, expand_b, contract_b,
    result_ref, cot_ref, normed_ref, activ_ref, grad_exp_ref, grad_out_ref, grad_att_ref,
    sums_ref, exp_sums_ref,
):
    choose(told, kept, got, cot_ref)
    cot = cot_ref[...]
    after = rows_ref[...].astype(F32) + dot_dims(attended[...], out_w[...], 1, 0) + out_b[...]
    unit, rstd = norm_parts(after)
    normed = (unit * gain[...] + bias[...]).astype(BF16)
    normed_ref[...] = normed
    total = after + contract_b[...]
    back = 0.0

    @pl.when(pl.program_id(0) == 0)
    def _():
        sums_ref[...] = jnp.zeros_like(sums_ref)
        exp_sums_ref[...] = jnp.zeros_like(exp_sums_ref)

    parts = 4
    wide = expand_w.shape[1] // parts
    bend, cube = 0.7978845608028654, 0.044715
    for part in range(parts):
        at = slice(part * wide, (part + 1) * wide)
        value = dot_dims(normed, expand_w[:, at], 1, 0) + expand_b[:, at]
        square = value * value
        half = 0.5 + 0.5 * jnp.tanh(value * (bend + bend * cube * square))
        activ = (value * half).astype(BF16)
        activ_ref[:, at] = activ
        slope = half + (half - half * half) * (value * (2.0 * bend + 6.0 * bend * cube * square))
        grad = (dot_dims(cot, contract_w[:, at], 1, 0) * slope).astype(BF16)
        grad_exp_ref[:, at] = grad
        exp_sums_ref[:, at] += jnp.sum(grad.astype(F32), axis=0, keepdims=True)
        total = total + dot_dims(activ, contract_w[:, at], 1, 1)
        back = back + dot_dims(grad, expand_w[:, at], 1, 1)
    result_ref[...] = total.astype(BF16)
    wide_cot = cot.astype(F32)
    grad_rows, gain_sum, bias_sum = norm_back(back, unit, rstd, gain[...])
    grad_out = (grad_rows + wide_cot).astype(BF16)
    grad_out_ref[...] = grad_out
    grad_att_ref[...] = dot_dims(grad_out, out_w[...], 1, 1).astype(BF16)
    sums = (
        jnp.sum(grad_out.astype(F32), axis=0, keepdims=True),
        gain_sum[None],
        bias_sum[None],
        jnp.sum(wide_cot, axis=0, keepdims=True),
    )
    for k, value in enumerate(sums):
        sums_ref[k : k + 1, :] += value


def middle(told, kept, got, rows_in, attended, out_w, expand_w, contract_w, out_b, gain, bias, expand_b, contract_b):
    _, segs, rows, width = kept.shape
    wide = expand_w.shape[1]
    whole = lambda r, c: pl.BlockSpec((r, c), lambda i, told: (0, 0), pipeline_mode=pl.Buffered(1))
    block = lambda c: pl.BlockSpec((rows, c), lambda i, told: (i, 0))
    sizes = (width, width, width, wide, wide, width, width)
    count = 2 * segs * rows
    fixed = lambda r, c: pl.BlockSpec((r, c), lambda i, told: (0, 0))
    return pl.pallas_call(
        middle_kernel,
        grid_spec=pltpu.PrefetchScalarGridSpec(
            num_scalar_prefetch=1,
            grid=(2 * segs,),
            in_specs=[
                *half_specs(rows, width), block(width), block(width), whole(width, width), whole(width, wide),
                whole(width, wide), whole(1, width), whole(1, width), whole(1, width), whole(1, wide), whole(1, width),
            ],
            out_specs=[*[block(c) for c in sizes], fixed(8, width), fixed(1, wide)],
        ),
        out_shape=[
            *[jax.ShapeDtypeStruct((count, c), BF16) for c in sizes],
            jax.ShapeDtypeStruct((8, width), F32),
            jax.ShapeDtypeStruct((1, wide), F32),
        ],
        compiler_params=pltpu.CompilerParams(vmem_limit_bytes=60 * 2**20),
        cost_estimate=pl.CostEstimate(
            flops=count * width * (8 * wide + 4 * width) * 2, bytes_accessed=count * (14 * width + 4 * wide), transcendentals=0
        ),
        name="middle",
    )(
        told, kept, got, rows_in, attended, out_w, expand_w, contract_w, out_b[None], gain[None], bias[None],
        expand_b[None], contract_b[None],
    )


def thirds(rows):
    parts = []
    for _ in range(3):
        parts.append(rows.astype(BF16))
        rows = rows - parts[-1].astype(F32)
    return jnp.concatenate(parts, axis=0)


def exact_low(rows, weight, side):
    count = rows.shape[0]
    out = dot_dims(thirds(rows), weight, 1, side)
    return out[:count] + out[count : 2 * count] + out[2 * count :]


def softplus(rows):
    return jnp.maximum(rows, 0.0) + jnp.log1p(jnp.exp(-jnp.abs(rows)))


def feature_parts(rows):
    halves = jnp.concatenate([softplus(rows), softplus(-rows)], axis=1)
    turned = [pltpu.roll(halves, j, 1) for j in (1, 2, 3)]
    return halves, turned, jnp.concatenate([halves * t for t in turned], axis=1)


def feature_back(rows, grad):
    halves, turned, _ = feature_parts(rows)
    wide = halves.shape[1]
    total = 0.0
    for j in (1, 2, 3):
        part = grad[:, (j - 1) * wide : j * wide]
        total = total + part * turned[j - 1] + pltpu.roll(part * halves, wide - j, 1)
    first, last = total[:, : wide // 2], total[:, wide // 2 :]
    return first * jax.nn.sigmoid(rows) - last * jax.nn.sigmoid(-rows)


def per_head(rows):
    tall = jnp.concatenate([rows] * H, axis=0)
    return tall * head_mask(tall.shape, rows.shape[0]).astype(rows.dtype)


def head_mask(shape, count):
    head = lax.broadcasted_iota(jnp.int32, shape, 0) // count
    return (lax.broadcasted_iota(jnp.int32, shape, 1) // HD == head).astype(F32)


def from_heads(tall, count):
    tall = tall * head_mask(tall.shape, count)
    total = tall[:count]
    for head in range(1, H):
        total = total + tall[head * count : (head + 1) * count]
    return total


def mem_weights(query, key):
    count = key.shape[0]
    tall = per_head(query)
    scores = dot_dims(tall, key, 1, 1) * HD**-0.5
    at = lax.rem(lax.broadcasted_iota(jnp.int32, scores.shape, 0), count)
    raw = jnp.where(lax.broadcasted_iota(jnp.int32, scores.shape, 1) <= at, jnp.exp(scores), 0.0)
    return tall, raw / jnp.sum(raw, axis=1, keepdims=True)


def read_parts(read_feat, key_feat, value_new):
    mix = exact(read_feat, key_feat, 1, 1)
    return mix, exact(mix, value_new, 1, 0), 1.0 + jnp.sum(mix, axis=1, keepdims=True)


def bring(sources, targets, sem):
    copies = [pltpu.make_async_copy(a, b, sem.at[k]) for k, (a, b) in enumerate(zip(sources, targets))]
    for copy in copies:
        copy.start()
    return copies


def mem_fwd_kernel(
    mt_ref, one_gain, one_bias, two_gain, two_bias, shift, out_b, expand_b, contract_b,
    qrk_hbm, ov_hbm, expand_hbm, contract_hbm,
    qkv_ref, attended_ref, after_ref, expanded_ref, result_ref, pre_ref, value_ref, follow_ref, kv_ref,
    qrk, ov, expand_w, contract_w, sem,
):
    copies = bring((qrk_hbm, ov_hbm, expand_hbm, contract_hbm), (qrk, ov, expand_w, contract_w), sem)
    mt = mt_ref[...]
    width = mt.shape[1]
    feat = pre_ref.shape[1] // 2
    unit, _ = norm_parts(mt)
    normed = (unit * one_gain[...] + one_bias[...]).astype(BF16)
    copies[0].wait()
    qkv = (dot_dims(normed, qrk[:, : 3 * width], 1, 0) + shift[...]).astype(BF16)
    qkv_ref[...] = qkv
    read_pre = exact_low(mt, qrk[:, 3 * width : 3 * width + feat], 0)
    _, weights = mem_weights(qkv[:, :width], qkv[:, width : 2 * width])
    mixed = dot_dims(weights.astype(BF16), qkv[:, 2 * width :], 1, 0)
    attended = from_heads(mixed, mt.shape[0]).astype(BF16)
    attended_ref[...] = attended
    copies[1].wait()
    after = mt + dot_dims(attended, ov[:, :width], 1, 0) + out_b[...]
    after_ref[...] = after
    unit, _ = norm_parts(after)
    normed = (unit * two_gain[...] + two_bias[...]).astype(BF16)
    copies[2].wait()
    expanded = dot_dims(normed, expand_w[...], 1, 0) + expand_b[...]
    expanded_ref[...] = expanded
    activ = gelu_tanh(expanded).astype(BF16)
    copies[3].wait()
    result = after + dot_dims(activ, contract_w[...], 1, 1) + contract_b[...]
    result_ref[...] = result
    key_pre = exact_low(result, qrk[:, 3 * width + feat :], 0)
    value_new = exact_low(result, ov[:, width:], 0)
    value_ref[...] = value_new
    pre_ref[:, :feat] = read_pre
    pre_ref[:, feat:] = key_pre
    _, numer, denom = read_parts(feature_parts(read_pre)[2], feature_parts(key_pre)[2], value_new)
    follow = mt + numer / denom
    follow_ref[...] = follow
    unit, _ = norm_parts(follow)
    normed = (unit * one_gain[...] + one_bias[...]).astype(BF16)
    kv_ref[...] = (dot_dims(normed, qrk[:, width : 3 * width], 1, 0) + shift[:, width:]).astype(BF16)


def mem_call(kernel, name, given, weights, outs, cycles):
    vmem = pl.BlockSpec(memory_space=pltpu.VMEM)
    return pl.pallas_call(
        kernel,
        in_specs=[vmem] * len(given) + [pl.BlockSpec(memory_space=pl.ANY)] * len(weights),
        out_specs=[vmem] * len(outs),
        out_shape=outs,
        scratch_shapes=[
            *[pltpu.VMEM(w.shape, w.dtype) for w in weights],
            pltpu.SemaphoreType.DMA((len(weights),)),
        ],
        compiler_params=pltpu.CompilerParams(vmem_limit_bytes=60 * 2**20),
        cost_estimate=pl.CostEstimate(flops=cycles * 10**9, bytes_accessed=17 * 10**6, transcendentals=0),
        name=name,
    )(*given, *weights)


def mem_forward(mt, given, weights):
    mem, width = mt.shape
    wide, feat = weights[2].shape[1], (weights[0].shape[1] - 3 * width) // 2
    shape = jax.ShapeDtypeStruct
    outs = [
        shape((mem, 3 * width), BF16), shape((mem, width), BF16), shape((mem, width), F32), shape((mem, wide), F32),
        shape((mem, width), F32), shape((mem, 2 * feat), F32), shape((mem, width), F32), shape((mem, width), F32),
        shape((mem, 2 * width), BF16),
    ]
    return mem_call(mem_fwd_kernel, "mem_fwd", (mt, *given), weights, outs, 15)


def mem_bwd_kernel(
    mt_ref, one_gain, one_bias, two_gain, two_bias, pooled, chosen,
    qkv_ref, attended_ref, after_ref, expanded_ref, result_ref, pre_ref, value_ref, follow_ref,
    qrk_hbm, ov_hbm, expand_hbm, contract_hbm,
    grad_mt_ref, qkv_grad, out_grad, expand_grad, contract_grad, read_grad, key_grad, value_grad, sums_ref, exp_sums_ref,
    qrk, ov, expand_w, contract_w, sem,
):
    copies = bring((qrk_hbm, ov_hbm, expand_hbm, contract_hbm), (qrk, ov, expand_w, contract_w), sem)
    mt = mt_ref[...]
    mem, width = mt.shape
    feat = pre_ref.shape[1] // 2
    sums_ref[...] = jnp.zeros_like(sums_ref)

    def add_row(k, value):
        sums_ref[k : k + 1, :] += value[None]

    def column(value):
        return jnp.sum(value.astype(F32), axis=0)

    unit_f, rstd_f = norm_parts(follow_ref[...])
    normed_f = (unit_f * one_gain[...] + one_bias[...]).astype(BF16)
    grad_f = pooled[1].astype(BF16)
    copies[0].wait()
    grad_follow, gain, bias = norm_back(
        dot_dims(grad_f, qrk[:, width : 3 * width], 1, 1), unit_f, rstd_f, one_gain[...]
    )
    add_row(0, gain)
    add_row(1, bias)
    add_row(3, column(grad_f[:, width:]))
    read_pre, key_pre, value_new = pre_ref[:, :feat], pre_ref[:, feat:], value_ref[...]
    read_feat, key_feat = feature_parts(read_pre)[2], feature_parts(key_pre)[2]
    mix, numer, denom = read_parts(read_feat, key_feat, value_new)
    grad_numer = grad_follow / denom
    grad_denom = -jnp.sum(grad_follow * numer, axis=1, keepdims=True) / (denom * denom)
    grad_mix = exact(grad_numer, value_new, 1, 1) + grad_denom
    grad_value = exact(mix, grad_numer, 0, 0)
    grad_read_pre = feature_back(read_pre, exact(grad_mix, key_feat, 1, 0))
    grad_key_pre = feature_back(key_pre, exact(grad_mix, read_feat, 0, 0))
    grad_mt = grad_follow + exact_low(grad_read_pre, qrk[:, 3 * width : 3 * width + feat], 1)
    copies[1].wait()
    grad_result = exact_low(grad_key_pre, qrk[:, 3 * width + feat :], 1) + exact_low(
        grad_value, ov[:, width:], 1
    )
    grad_contract = grad_result.astype(BF16)
    add_row(7, column(grad_contract))
    expanded = expanded_ref[...]
    bend, cube = 0.7978845608028654, 0.044715
    square = expanded * expanded
    curve = jnp.tanh(bend * expanded * (1.0 + cube * square))
    half = 0.5 * (1.0 + curve)
    activ = (expanded * half).astype(BF16)
    slope = half + 0.5 * bend * expanded * (1.0 - curve * curve) * (1.0 + 3.0 * cube * square)
    copies[3].wait()
    grad_expanded = (dot_dims(grad_contract, contract_w[...], 1, 0) * slope).astype(BF16)
    exp_sums_ref[...] = column(grad_expanded)[None]
    unit_b, rstd_b = norm_parts(after_ref[...])
    normed_b = (unit_b * two_gain[...] + two_bias[...]).astype(BF16)
    copies[2].wait()
    grad_after, gain, bias = norm_back(
        dot_dims(grad_expanded, expand_w[...], 1, 1), unit_b, rstd_b, two_gain[...]
    )
    add_row(5, gain)
    add_row(6, bias)
    grad_after = grad_after + grad_result
    grad_attn_out = grad_after.astype(BF16)
    add_row(4, column(grad_attn_out))
    grad_attended = dot_dims(grad_attn_out, ov[:, :width], 1, 1).astype(BF16)
    query, key, value = (qkv_ref[:, k * width : (k + 1) * width] for k in range(3))
    tall, weights = mem_weights(query, key)
    grad_tall = per_head(grad_attended)
    grad_weights = dot_dims(grad_tall, value, 1, 1)
    centre = jnp.sum(weights * grad_weights, axis=1, keepdims=True)
    grad_s = (weights * (grad_weights - centre) * HD**-0.5).astype(BF16)
    grad_qkv = jnp.concatenate(
        [
            from_heads(dot_dims(grad_s, key, 1, 0), mem),
            dot_dims(grad_s, tall, 0, 0) + pooled[0, :, :width],
            dot_dims(weights.astype(BF16), grad_tall, 0, 0) + pooled[0, :, width:],
        ],
        axis=1,
    ).astype(BF16)
    add_row(2, column(grad_qkv[:, :width]))
    add_row(3, column(grad_qkv[:, 2 * width :]))
    unit, rstd = norm_parts(mt)
    normed = (unit * one_gain[...] + one_bias[...]).astype(BF16)
    grad_first, gain, bias = norm_back(
        dot_dims(grad_qkv, qrk[:, : 3 * width], 1, 1), unit, rstd, one_gain[...]
    )
    add_row(0, gain)
    add_row(1, bias)
    grad_mt_ref[...] = grad_mt + grad_first + grad_after

    pick_low = lambda a: dot_dims(a, chosen[...], 1, 0).astype(BF16)
    pick_exact = lambda a: exact_low(a, chosen[...], 0)
    qkv_grad[...] = dot_dims(pick_low(normed), grad_qkv, 0, 0)
    qkv_grad[:, width:] += dot_dims(pick_low(normed_f), grad_f, 0, 0)
    out_grad[...] = dot_dims(pick_low(attended_ref[...]), grad_attn_out, 0, 0)
    expand_grad[...] = dot_dims(pick_low(normed_b), grad_expanded, 0, 0)
    contract_grad[...] = dot_dims(pick_low(grad_contract), activ, 0, 0)
    my_result = pick_exact(result_ref[...])
    read_grad[...] = exact(pick_exact(mt), grad_read_pre, 0, 0)
    key_grad[...] = exact(my_result, grad_key_pre, 0, 0)
    value_grad[...] = exact(my_result, grad_value, 0, 0)


def mem_reduce(mt, norms, pooled, shard, group, kept, weights, terms, gives, small, planes):
    mem, width = mt.shape
    wide, feat = weights[2].shape[1], (weights[0].shape[1] - 3 * width) // 2
    at = lax.broadcasted_iota(jnp.int32, (width, shard), 0) - group * shard
    chosen = (at == lax.broadcasted_iota(jnp.int32, (width, shard), 1)).astype(BF16)
    sizes = (3 * width, width, wide, wide, feat, feat, width)
    shape = jax.ShapeDtypeStruct
    mem_outs = [
        shape((mem, width), F32), *[shape((shard, c), F32) for c in sizes], shape((8, width), F32), shape((1, wide), F32),
    ]
    given = (mt, *norms, pooled, chosen, *kept)
    cuts, inputs, in_specs, outs, out_specs, scratch = reducer_call(terms, gives, small)
    vmem = pl.BlockSpec(memory_space=pltpu.VMEM)
    out = pl.pallas_call(
        functools.partial(
            mem_reduce_kernel, planes, cuts, (len(terms), len(gives), len(given) + len(weights), len(mem_outs))
        ),
        in_specs=[*in_specs, *[vmem] * len(given), *[pl.BlockSpec(memory_space=pl.ANY)] * len(weights)],
        out_specs=[*out_specs, *[vmem] * len(mem_outs)],
        out_shape=[*outs, *mem_outs],
        scratch_shapes=[
            *[pltpu.VMEM(w.shape, w.dtype) for w in weights],
            pltpu.SemaphoreType.DMA((len(weights),)),
            *scratch,
        ],
        compiler_params=pltpu.CompilerParams(
            collective_id=2, has_side_effects=True, vmem_limit_bytes=60 * 2**20
        ),
        cost_estimate=pl.CostEstimate(flops=5 * 10**10, bytes_accessed=30 * 10**6, transcendentals=0),
        name="mem_reduce",
    )(*inputs, *given, *weights)
    n, g = len(terms), len(gives)
    grad_mt, *rest = out[n + g + 1 :]
    sums, expand_sums = rest[7:]
    vectors = (sums[0], sums[1], sums[2:4], sums[4], sums[5], sums[6], expand_sums[0], sums[7])
    return out[:n], out[n : n + g], out[n + g], grad_mt, tuple(rest[:7]), vectors


def gather_kernel(halved, count, kinds, *refs):
    shards, outs = refs[:count], refs[count : 2 * count]
    send_sem, recv_sem, local_sem = refs[2 * count :]
    index, plane = lax.axis_index("dp"), lax.axis_index("ctx")
    deep, cross, core = index // 4, (index // 2) % 2, index % 2
    place = lambda z, x, c: (z * 2 + x) * 2 + c
    up, down = {"dp": place(deep + 1, cross, core)}, {"dp": place(deep - 1, cross, core)}
    beside, sibling = {"dp": place(deep, 1 - cross, core)}, {"dp": place(deep, cross, 1 - core)}
    other = {"ctx": 1 - plane}
    rows = shards[0].shape[0]
    numbers, sends = {}, []

    def valid(kind):
        way, far = kind
        return deep >= 0 if way == "own" else deep >= far if way == "below" else deep + far <= 3

    def level(kind):
        way, far = kind
        return deep if way == "own" else deep - far if way == "below" else deep + far

    def view(k, z, x, c, part):
        at = pl.ds(pl.multiple_of(place(z, x, c) * rows, 16), rows)
        return outs[k].at[at, :] if part is None else outs[k].at[at, half(k, part)]

    def half(k, part):
        wide = outs[k].shape[1] // 2
        return pl.ds(pl.multiple_of(part * wide, 128), wide)

    def copy(key, source, landing, device):
        number = numbers.setdefault(key, len(numbers))
        return pltpu.make_async_remote_copy(
            source, landing, send_sem.at[number], recv_sem.at[number],
            device_id=device, device_id_type=pl.DeviceIdType.MESH,
        )

    def send(when, key, source, landing, device):
        def begin():
            copy(key, source, landing, device).start()

        def end():
            copy(key, source, landing, device).wait_send()

        sends.append((when, end))
        if when is None:
            begin()
        else:
            pl.when(when)(begin)

    def arrived(key, landing):
        copy(key, landing, landing, sibling).wait_recv()

    barrier = pltpu.get_barrier_semaphore()
    for device in (beside, sibling, other):
        pl.semaphore_signal(barrier, inc=1, device_id=device, device_id_type=pl.DeviceIdType.MESH)
    for when, device in ((deep < 3, up), (deep > 0, down)):

        @pl.when(when)
        def _(device=device):
            pl.semaphore_signal(barrier, inc=1, device_id=device, device_id_type=pl.DeviceIdType.MESH)

    inner = (deep > 0) & (deep < 3)
    for when, peers in ((inner, 5), (jnp.logical_not(inner), 4)):

        @pl.when(when)
        def _(peers=peers):
            pl.semaphore_wait(barrier, peers)

    own = ("own", 0)
    locals_ = []
    for k in range(count):
        part = plane if k in halved else None
        mine = view(k, deep, cross, core, None)
        locals_.append(pltpu.make_async_copy(shards[k], mine, local_sem.at[k]))
        locals_[-1].start()
        source = shards[k] if part is None else shards[k].at[:, half(k, part)]
        landing = view(k, deep, cross, core, part)
        send(deep < 3, ("z", ("below", 1), k), source, landing, up)
        send(deep > 0, ("z", ("above", 1), k), source, landing, down)
        send(None, ("x", own, k), source, landing, beside)
        send(None, ("core", "z", own, k), shards[k], mine, sibling)

    def onward(k, flow, kind, x):
        part = plane if k in halved else None
        block = view(k, level(kind), x, core, part)
        ok = valid(kind)
        if flow == "z":
            way, far = kind
            if far < 3:
                if way == "below":
                    send(ok & (deep < 3), ("z", (way, far + 1), k), block, block, up)
                else:
                    send(ok & (deep > 0), ("z", (way, far + 1), k), block, block, down)
            send(ok, ("x", kind, k), block, block, beside)
        send(ok, ("core", flow, kind, k), block, block, sibling)
        if k in halved:
            send(ok, ("y", flow, kind, k), block, block, other)

    def take(flow, kind):
        x = cross if flow == "z" else 1 - cross
        for k in range(count):
            part = plane if k in halved else None

            @pl.when(valid(kind))
            def _():
                arrived((flow, kind, k), view(k, level(kind), x, core, part))

            onward(k, flow, kind, x)

    for far in range(1, 4):
        take("z", ("below", far))
        take("z", ("above", far))
        for kind in kinds:
            if kind[1] == far - 1:
                take("x", kind)
    for kind in kinds:
        if kind[1] == 3:
            take("x", kind)
    crossing = [(flow, kind, k) for flow in ("z", "x") for kind in kinds for k in halved]
    crossing = [c for c in crossing if c[:2] != ("z", own)]
    for flow, kind, k in crossing:
        x = cross if flow == "z" else 1 - cross
        block = lambda c: view(k, level(kind), x, c, 1 - plane)

        @pl.when(valid(kind))
        def _():
            arrived(("y", flow, kind, k), block(core))

        send(valid(kind), ("core", "y", flow, kind, k), block(core), block(core), sibling)
    for flow in ("z", "x"):
        x = cross if flow == "z" else 1 - cross
        for kind in kinds:
            for k in range(count):
                part = plane if k in halved and (flow, kind) != ("z", own) else None

                @pl.when(valid(kind))
                def _():
                    arrived(("core", flow, kind, k), view(k, level(kind), x, 1 - core, part))

    for flow, kind, k in crossing:
        x = cross if flow == "z" else 1 - cross

        @pl.when(valid(kind))
        def _():
            arrived(("core", "y", flow, kind, k), view(k, level(kind), x, 1 - core, 1 - plane))

    for when, end in sends:
        if when is None:
            end()
        else:
            pl.when(when)(end)
    for held in locals_:
        held.wait()


def gather_weights(shards, halved):
    kinds = [("own", 0)] + [(way, far) for far in (1, 2, 3) for way in ("below", "above")]
    count = len(shards)
    rows = shards[0].shape[0] * 16
    copies = 6 * count + 7 * count + 13 * len(halved) + 14 * count + 13 * len(halved)
    any_space = pl.BlockSpec(memory_space=pl.ANY)
    return pl.pallas_call(
        functools.partial(gather_kernel, halved, count, kinds),
        in_specs=[any_space] * count,
        out_specs=[any_space] * count,
        out_shape=[jax.ShapeDtypeStruct((rows, s.shape[1]), BF16) for s in shards],
        scratch_shapes=[
            pltpu.SemaphoreType.DMA((copies,)),
            pltpu.SemaphoreType.DMA((copies,)),
            pltpu.SemaphoreType.DMA((count,)),
        ],
        compiler_params=pltpu.CompilerParams(
            collective_id=0, has_side_effects=True, vmem_limit_bytes=4 * 2**20
        ),
        cost_estimate=pl.CostEstimate(
            flops=8 * 10**10, bytes_accessed=4 * rows * sum(s.shape[1] for s in shards), transcendentals=0
        ),
        name="gather_weights",
    )(*shards)


def dp_pairs(flip):
    return [(i, i ^ flip) for i in range(16)]


def behind(value, *earlier):
    return lax.optimization_barrier((value, earlier))[0]


def pick(parts, at, axis):
    return lax.dynamic_index_in_dim(parts, at, axis, keepdims=False)


def add_low(a, b):
    return (a.astype(F32) + b.astype(F32)).astype(BF16)


class Reducer:
    def __init__(self, planes, cuts, grads, gives, small_ref, outs, gots, small_out, scratch):
        self.planes, self.cuts, self.grads, self.gives, self.small_ref = planes, cuts, grads, gives, small_ref
        self.outs, self.gots, self.small_out = outs, gots, small_out
        (
            self.mine, self.got_core, self.got_x, self.line, self.got_z, self.low, self.got_y, self.held, self.total,
            self.load_sem, self.core_sem, self.x_sem, self.z_sem, self.y_sem, self.swap_sem, self.sum_sem,
        ) = scratch
        self.index, self.plane = lax.axis_index("dp"), lax.axis_index("ctx")
        deep, cross, core = self.index // 4, lax.rem(self.index // 2, 2), lax.rem(self.index, 2)
        self.deep, self.cross, self.core = deep, cross, core
        self.place = lambda z, x, c: (z * 2 + x) * 2 + c
        self.deeps = (deep + 1 - 2 * lax.rem(deep, 2), lax.rem(deep + 2, 4), 3 - deep)
        self.chunks, self.peers = len(cuts), small_ref.shape[0]
        self.me = self.index * planes + self.plane

    def remote(self, source, landing, sems, at, device):
        return pltpu.make_async_remote_copy(
            source, landing, sems.at[(0, *at)], sems.at[(1, *at)], device_id=device, device_id_type=pl.DeviceIdType.MESH
        )

    def peer(self, j):
        return (j // self.planes, lax.rem(j, self.planes))

    def small(self, phase, j, sender):
        source, landing = (
            (self.small_ref.at[j], self.held.at[sender]) if phase == 0 else (self.total.at[sender], self.total.at[sender])
        )
        return pltpu.make_async_remote_copy(
            source, landing, self.sum_sem.at[0, phase, j], self.sum_sem.at[1, phase, sender],
            device_id=self.peer(j), device_id_type=pl.DeviceIdType.MESH,
        )

    def every(self, work):
        def body(step, carry):
            work(lax.rem(self.me + step, self.peers))
            return carry

        lax.fori_loop(1, self.peers, body, 0)

    def loop(self, first, last, work):
        def body(c, carry):
            work(c)
            return carry

        lax.fori_loop(first, last, body, 0)

    def to_core(self, c, x):
        k, start, wide = self.cuts[c]
        source = self.grads[k].at[:, x, 1 - self.core, :, pl.ds(start, wide)]
        sibling = {"dp": self.place(self.deep, self.cross, 1 - self.core)}
        return self.remote(source, self.got_core.at[c, x], self.core_sem, (c, x), sibling)

    def to_x(self, c):
        beside = {"dp": self.place(self.deep, 1 - self.cross, self.core)}
        return self.remote(self.mine.at[c, 1 - self.cross], self.got_x.at[c], self.x_sem, (c,), beside)

    def to_z(self, c, k):
        far = {"dp": self.place(self.deeps[k], self.cross, self.core)}
        return self.remote(self.line.at[c, self.deeps[k]], self.got_z.at[c, k], self.z_sem, (c, k), far)

    def to_y(self, c):
        return self.remote(self.low.at[c], self.got_y.at[c], self.y_sem, (c,), {"ctx": 1 - self.plane})

    def swap(self, k):
        return self.remote(
            self.gives[k].at[1 - self.plane], self.gots[k], self.swap_sem, (k,), {"ctx": 1 - self.plane}
        )

    def arrived(self, landing, sems, at):
        self.remote(landing, landing, sems, at, {"ctx": 1 - self.plane}).wait_recv()

    def begin(self):
        for c, (k, start, wide) in enumerate(self.cuts):
            for x in range(2):
                source = self.grads[k].at[:, x, self.core, :, pl.ds(start, wide)]
                pltpu.make_async_copy(source, self.mine.at[c, x], self.load_sem.at[c, x]).start()
        barrier = pltpu.get_barrier_semaphore()
        self.every(
            lambda j: pl.semaphore_signal(
                barrier, inc=1, device_id=self.peer(j), device_id_type=pl.DeviceIdType.MESH
            )
        )
        pl.semaphore_wait(barrier, self.peers - 1)
        for c in range(self.chunks):
            for x in range(2):
                self.to_core(c, x).start()
        self.every(lambda j: self.small(0, j, self.me).start())
        for k in range(len(self.gives)):
            self.swap(k).start()
        self.held[self.me] = self.small_ref[self.me]

    def over_core(self, c):
        mine, got = self.mine, self.got_core
        for x in range(2):
            pltpu.make_async_copy(mine.at[c, x], mine.at[c, x], self.load_sem.at[c, x]).wait()
            self.arrived(got.at[c, x], self.core_sem, (c, x))
            for z in range(4):
                mine[c, x, z] = add_low(mine[c, x, z], got[c, x, z])
        self.to_x(c).start()

    def add_small(self):
        self.every(lambda j: self.small(0, j, j).wait_recv())
        self.total[self.me] = jnp.sum(self.held[...], axis=0)
        self.every(lambda j: self.small(1, j, self.me).start())

    def over_x(self, c):
        self.arrived(self.got_x.at[c], self.x_sem, (c,))
        for z in range(4):
            self.line[c, z] = add_low(self.mine[c, self.cross, z], self.got_x[c, z])
        for k in range(3):
            self.to_z(c, k).start()

    def over_z(self, c):
        value = self.line[c, self.deep].astype(F32)
        for k in range(3):
            self.arrived(self.got_z.at[c, k], self.z_sem, (c, k))
            value = value + self.got_z[c, k].astype(F32)
        self.low[c] = value.astype(BF16)
        self.to_y(c).start()

    def end(self):
        for c, (k, start, wide) in enumerate(self.cuts):
            self.arrived(self.got_y.at[c], self.y_sem, (c,))
            self.outs[k][:, start : start + wide] = self.low[c].astype(F32) + self.got_y[c].astype(F32)
        self.every(lambda j: self.small(1, j, j).wait_recv())
        self.small_out[...] = self.total[...]
        for k in range(len(self.gives)):
            self.swap(k).wait_recv()
        self.every(lambda j: self.small(0, j, self.me).wait_send())
        self.every(lambda j: self.small(1, j, self.me).wait_send())
        for k in range(len(self.gives)):
            self.swap(k).wait_send()
        for c in range(self.chunks):
            for x in range(2):
                self.to_core(c, x).wait_send()

        def finish(c):
            self.to_x(c).wait_send()
            for k in range(3):
                self.to_z(c, k).wait_send()
            self.to_y(c).wait_send()

        self.loop(0, self.chunks, finish)


REDUCER_SCRATCH = 16


def reducer_call(grads, gives, small):
    wide = 768
    shard = grads[0].shape[0] // 16
    cuts = [(k, at, wide) for k, g in enumerate(grads) for at in range(0, g.shape[1], wide)]
    chunks, peers = len(cuts), small.shape[0]
    vmem, hbm = pl.BlockSpec(memory_space=pltpu.VMEM), pl.BlockSpec(memory_space=pl.ANY)
    shape, dma = jax.ShapeDtypeStruct, pltpu.SemaphoreType.DMA
    low = lambda *dims: pltpu.VMEM((chunks, *dims, shard, wide), BF16)
    inputs = (*[g.reshape(4, 2, 2, shard, g.shape[1]) for g in grads], *gives, small)
    in_specs = [hbm] * (len(grads) + len(gives)) + [vmem]
    outs = [shape((shard, g.shape[1]), F32) for g in grads]
    outs += [shape(g.shape[1:], BF16) for g in gives] + [shape(small.shape, F32)]
    out_specs = [vmem] * len(grads) + [hbm] * len(gives) + [vmem]
    scratch = [
        low(2, 4), low(2, 4), low(4), low(4), low(3), low(), low(), pltpu.VMEM(small.shape, F32), pltpu.VMEM(small.shape, F32),
        dma((chunks, 2)), dma((2, chunks, 2)), dma((2, chunks)), dma((2, chunks, 3)), dma((2, chunks)),
        dma((2, len(gives))), dma((2, 2, peers)),
    ]
    return cuts, inputs, in_specs, outs, out_specs, scratch


def back_reduce_kernel(planes, cuts, counts, *refs):
    grads, gives = counts
    given, rest = refs[:8], refs[8:]
    ins, rest = rest[: grads + gives + 1], rest[grads + gives + 1 :]
    out_ref, rest = rest[0], rest[1:]
    outs, rest = rest[: grads + gives + 1], rest[grads + gives + 1 :]
    own_scratch, scratch = rest[: len(rest) - REDUCER_SCRATCH], rest[len(rest) - REDUCER_SCRATCH :]
    reducer = Reducer(
        planes, cuts, ins[:grads], ins[grads:-1], ins[-1], outs[:grads], outs[grads:-1], outs[-1], scratch
    )
    turn, phase = pl.program_id(0), pl.program_id(1)
    chunks = len(cuts)

    @pl.when((turn == 0) & (phase == 0))
    def _():
        reducer.begin()

    at_core = lambda t: jnp.clip(3 * t, 0, chunks)
    at_x = lambda t: jnp.clip(jnp.maximum(7 * t - 12, 0) // 8, 0, chunks)
    at_z = lambda t: at_x(t - 2)

    @pl.when((turn > 0) & (phase == 0))
    def _():
        reducer.loop(at_core(turn - 1), at_core(turn), reducer.over_core)
        reducer.loop(at_x(turn - 1), at_x(turn), reducer.over_x)
        reducer.loop(at_z(turn - 1), at_z(turn), reducer.over_z)

    @pl.when((turn == 4) & (phase == 1))
    def _():
        reducer.add_small()

    attn_bwd_kernel(*given, out_ref, *own_scratch)

    @pl.when((turn == pl.num_programs(0) - 1) & (phase == 2))
    def _():
        reducer.loop(at_x(turn), chunks, reducer.over_x)
        reducer.loop(at_z(turn), chunks, reducer.over_z)
        reducer.end()


def back_reduce(qkv, kv_mem, grad, lse, middle, terms, gives, small, planes):
    pairs = H // 2
    segs, rows, width = kv_mem.shape[0], lse.shape[2], qkv.shape[1] // 3
    mem = kv_mem.shape[1]
    wide = 2 * HD
    count = segs * pairs
    cuts, inputs, in_specs, outs, out_specs, scratch = reducer_call(terms, gives, small)
    at = lambda p: jnp.minimum(p, count - 1)
    spec = lambda off: pl.BlockSpec((rows, wide), lambda p, f, off=off: (at(p) // pairs, off * pairs + lax.rem(at(p), pairs)))
    mspec = lambda off: pl.BlockSpec(
        (1, mem, wide), lambda p, f, off=off: (at(p) // pairs, 0, off * pairs + lax.rem(at(p), pairs))
    )
    lspec = pl.BlockSpec((1, 2, rows), lambda p, f: (at(p), 0, 0))

    def place(p, f):
        which = jnp.where((f == 2) & (p < count), p, jnp.maximum(p - 1, 0))
        block = jnp.where(p == count, jnp.minimum(f, 1) + 1, jnp.where((f == 2) | (p == 0), 0, f + 1))
        return (which // pairs, block * pairs + lax.rem(which, pairs))

    out = pl.pallas_call(
        functools.partial(back_reduce_kernel, planes, cuts, (len(terms), len(gives))),
        grid=(count + 1, 3),
        in_specs=[spec(0), spec(1), spec(2), mspec(0), mspec(1), spec(0), lspec, lspec, *in_specs],
        out_specs=[pl.BlockSpec((rows, wide), place), *out_specs],
        out_shape=[jax.ShapeDtypeStruct(qkv.shape, BF16), *outs],
        scratch_shapes=[
            pltpu.VMEM((mem + rows, wide), BF16),
            pltpu.VMEM((mem + rows, wide), BF16),
            pltpu.VMEM((wide, rows), BF16),
            pltpu.VMEM((wide, mem), BF16),
            pltpu.VMEM((rows, wide), BF16),
            pltpu.VMEM((mem + rows, wide), F32),
            pltpu.VMEM((mem + rows, wide), F32),
            *scratch,
        ],
        compiler_params=pltpu.CompilerParams(
            collective_id=1, has_side_effects=True, vmem_limit_bytes=60 * 2**20
        ),
        cost_estimate=pl.CostEstimate(
            flops=count * rows * rows * 6500, bytes_accessed=rows * count * wide * 18, transcendentals=0
        ),
        name="back_reduce",
    )(qkv, qkv, qkv, kv_mem, kv_mem, grad, lse, middle, *inputs)
    return out[0], out[1 : 1 + len(terms)], out[1 + len(terms) : -1], out[-1]


def mem_reduce_kernel(planes, cuts, counts, *refs):
    grads, gives, given, made = counts
    ins, rest = refs[: grads + gives + 1], refs[grads + gives + 1 :]
    mem_ins, rest = rest[:given], rest[given:]
    outs, rest = rest[: grads + gives + 1], rest[grads + gives + 1 :]
    mem_outs, rest = rest[:made], rest[made:]
    mem_scratch, scratch = rest[: len(rest) - REDUCER_SCRATCH], rest[len(rest) - REDUCER_SCRATCH :]
    reducer = Reducer(
        planes, cuts, ins[:grads], ins[grads:-1], ins[-1], outs[:grads], outs[grads:-1], outs[-1], scratch
    )
    chunks = len(cuts)
    reducer.begin()
    reducer.loop(0, chunks, reducer.over_core)
    mem_bwd_kernel(*mem_ins, *mem_outs, *mem_scratch)
    reducer.add_small()
    reducer.over_x(0)

    def both(c):
        reducer.over_x(c)
        reducer.over_z(c - 1)

    reducer.loop(1, chunks, both)
    reducer.over_z(chunks - 1)
    reducer.end()


def split_heads(rows):
    return rows.reshape(rows.shape[0], rows.shape[1], H, HD)


def plain_scores(query, key, allowed):
    scores = jnp.einsum("sqhd,skhd->shqk", query, key, preferred_element_type=F32) * HD**-0.5
    return scores, allowed[None, None]


def plain_fwd(qkv, kv_all, allowed):
    width = qkv.shape[2] // 3
    query = split_heads(qkv[:, :, :width])
    key, value = split_heads(kv_all[:, :, :width]), split_heads(kv_all[:, :, width:])
    scores, allowed = plain_scores(query, key, allowed)
    raw = jnp.where(allowed, jnp.exp(scores), 0.0)
    total = jnp.sum(raw, axis=-1)
    weights = (raw / total[..., None]).astype(BF16)
    mixed = jnp.einsum("shqk,skhd->sqhd", weights, value, preferred_element_type=F32)
    return mixed.reshape(qkv.shape[0], -1, width).astype(BF16), jnp.log(total)


def plain_bwd(qkv, kv_all, allowed, log_total, grad):
    segs, width = qkv.shape[0], qkv.shape[2] // 3
    query = split_heads(qkv[:, :, :width])
    key, value = split_heads(kv_all[:, :, :width]), split_heads(kv_all[:, :, width:])
    grad = split_heads(grad)
    scores, allowed = plain_scores(query, key, allowed)
    prob = jnp.where(allowed, jnp.exp(scores - log_total[..., None]), 0.0)
    grad_p = jnp.einsum("sqhd,skhd->shqk", grad, value, preferred_element_type=F32)
    inner = jnp.sum(prob * grad_p, axis=-1, keepdims=True)
    grad_s = (prob * (grad_p - inner) * HD**-0.5).astype(BF16)
    dq = jnp.einsum("shqk,skhd->sqhd", grad_s, key, preferred_element_type=F32)
    dk = jnp.einsum("shqk,sqhd->skhd", grad_s, query, preferred_element_type=F32)
    dv = jnp.einsum("shqk,sqhd->skhd", prob.astype(BF16), grad, preferred_element_type=F32)
    flat = lambda a: a.reshape(segs, -1, width)
    return flat(dq), jnp.concatenate([flat(dk), flat(dv)], axis=2)


def memory_forward(mt, p):
    mem = mt.shape[0]
    keep = {}
    width = mt.shape[1]
    unit, rstd = norm_parts(mt)
    normed = (unit * p["one_gain"] + p["one_bias"]).astype(BF16)
    qkv = (dot_dims(normed, p["qkv"], 1, 0) + p["shift"]).astype(BF16)
    at = jnp.arange(mem, dtype=jnp.int32)
    allowed = at[None, :] <= at[:, None]
    attended, log_total = plain_fwd(qkv[None], qkv[None, :, width:], allowed)
    attended = attended[0]
    after = mt + dot_dims(attended, p["out"], 1, 0) + p["out_bias"]
    unit_b, rstd_b = norm_parts(after)
    normed_b = (unit_b * p["two_gain"] + p["two_bias"]).astype(BF16)
    expanded = dot_dims(normed_b, p["expand"], 1, 0) + p["expand_bias"]
    activ = gelu_tanh(expanded).astype(BF16)
    result = after + dot_dims(activ, p["contract"], 1, 1) + p["contract_bias"]
    key_pre = exact(result, p["key"].astype(F32), 1, 0)
    value_new = exact(result, p["value"].astype(F32), 1, 0)
    read_pre = exact(mt, p["read"].astype(F32), 1, 0)
    key_feat, key_pull = jax.vjp(feature_map, key_pre)
    read_feat, read_pull = jax.vjp(feature_map, read_pre)
    mix = exact(read_feat, key_feat, 1, 1)
    numer = exact(mix, value_new, 1, 0)
    denom = 1.0 + jnp.sum(mix, axis=1, keepdims=True)
    follow = mt + numer / denom
    unit_f, rstd_f = norm_parts(follow)
    normed_f = (unit_f * p["one_gain"] + p["one_bias"]).astype(BF16)
    kv_follow = (dot_dims(normed_f, p["qkv"][:, width:], 1, 0) + p["shift"][width:]).astype(BF16)
    keep = dict(
        unit=unit, rstd=rstd, normed=normed, qkv=qkv, allowed=allowed, attended=attended,
        log_total=log_total, unit_b=unit_b, rstd_b=rstd_b, normed_b=normed_b, expanded=expanded,
        activ=activ, result=result, key_feat=key_feat, read_feat=read_feat, key_pull=key_pull,
        read_pull=read_pull, value_new=value_new, mix=mix, numer=numer, denom=denom, unit_f=unit_f,
        rstd_f=rstd_f, normed_f=normed_f,
    )
    return qkv[:, width:], kv_follow, keep


def memory_backward(mt, p, m, grad_kv_first, grad_kv_follow, mine):
    width = mt.shape[1]
    low = lambda a: a.astype(BF16)
    grad_f = low(grad_kv_follow)
    grad_follow, gain_f, bias_f = norm_back(
        dot_dims(grad_f, p["qkv"][:, width:], 1, 1), m["unit_f"], m["rstd_f"], p["one_gain"]
    )
    grad_mt = grad_follow
    grad_numer = grad_follow / m["denom"]
    grad_denom = -jnp.sum(grad_follow * m["numer"], axis=1, keepdims=True) / (m["denom"] * m["denom"])
    grad_mix = exact(grad_numer, m["value_new"], 1, 1) + grad_denom
    grad_value = exact(m["mix"], grad_numer, 0, 0)
    [grad_read_pre] = m["read_pull"](exact(grad_mix, m["key_feat"], 1, 0))
    [grad_key_pre] = m["key_pull"](exact(grad_mix, m["read_feat"], 0, 0))
    grad_mt = grad_mt + exact(grad_read_pre, p["read"].astype(F32), 1, 1)
    grad_result = exact(grad_key_pre, p["key"].astype(F32), 1, 1) + exact(
        grad_value, p["value"].astype(F32), 1, 1
    )
    grad_contract = low(grad_result)
    _, gelu_pull = jax.vjp(gelu_tanh, m["expanded"])
    grad_expanded = low(gelu_pull(dot_dims(grad_contract, p["contract"], 1, 0))[0])
    grad_after, two_gain, two_bias = norm_back(
        dot_dims(grad_expanded, p["expand"], 1, 1), m["unit_b"], m["rstd_b"], p["two_gain"]
    )
    grad_after = grad_after + grad_result
    grad_attn_out = low(grad_after)
    grad_attended = low(dot_dims(grad_attn_out, p["out"], 1, 1))
    dq, dkv = plain_bwd(
        m["qkv"][None], m["qkv"][None, :, width:], m["allowed"], m["log_total"], grad_attended[None]
    )
    grad_qkv = low(jnp.concatenate([dq[0], dkv[0] + grad_kv_first], axis=1))
    grad_first, gain_a, bias_a = norm_back(
        dot_dims(grad_qkv, p["qkv"], 1, 1), m["unit"], m["rstd"], p["one_gain"]
    )
    grad_mt = grad_mt + grad_first + grad_after
    wide = grad_qkv.astype(F32)
    kv_rows = grad_f.astype(F32)
    sums = jnp.sum(wide, axis=0)
    follow_sums = jnp.sum(kv_rows, axis=0)
    matrices = (
        dot_dims(mine(m["normed"]), grad_qkv, 0, 0)
        + jnp.concatenate(
            [
                jnp.zeros((mine(mt).shape[1], width), F32),
                dot_dims(mine(m["normed_f"]), grad_f, 0, 0),
            ],
            axis=1,
        ),
        dot_dims(mine(m["attended"]), grad_attn_out, 0, 0),
        dot_dims(mine(m["normed_b"]), grad_expanded, 0, 0),
        dot_dims(mine(grad_contract), m["activ"], 0, 0),
        exact(mine(mt), grad_read_pre, 0, 0),
        exact(mine(m["result"]), grad_key_pre, 0, 0),
        exact(mine(m["result"]), grad_value, 0, 0),
    )
    column_sum = lambda a: jnp.sum(a.astype(F32), axis=0)
    vectors = (
        gain_f + gain_a,
        bias_f + bias_a,
        jnp.stack([sums[:width], sums[2 * width :] + follow_sums[width:]]),
        column_sum(grad_attn_out),
        two_gain,
        two_bias,
        column_sum(grad_expanded),
        column_sum(grad_contract),
    )
    return grad_mt, matrices, vectors


def local(
    tokens,
    cotangent,
    placing,
    starts,
    memory_tokens,
    norm_one_gain,
    norm_one_bias,
    qkv_weight,
    qv_bias,
    out_weight,
    out_bias,
    norm_two_gain,
    norm_two_bias,
    expand_weight,
    expand_bias,
    contract_weight,
    contract_bias,
    read_weight,
    key_weight,
    value_weight,
):
    del placing
    groups, ranks = lax.axis_size("dp"), lax.axis_size("ctx")
    group, rank = lax.axis_index("dp"), lax.axis_index("ctx")
    micros, segs_local, tok_rows, width = tokens.shape
    mem = memory_tokens.shape[0]
    shard = qkv_weight.shape[0]
    quick = groups == 16 and ranks == 2 and micros == 2 and segs_local == 2 and (tok_rows * ranks) % WIDE == 0
    names = ("qkv", "out", "expand", "contract", "read", "key", "value")
    shards = (qkv_weight, out_weight, expand_weight, contract_weight, read_weight, key_weight, value_weight)
    if quick:
        give = pick(tokens, 1 - rank, 0)
        joined = (
            jnp.concatenate([qkv_weight, read_weight, key_weight], axis=1),
            expand_weight,
            contract_weight,
            jnp.concatenate([out_weight, value_weight], axis=1),
        )
        qkv_read_key, expand_full, contract_full, out_value = gather_weights(
            behind(joined, give), (2, 3)
        )
        feat = read_weight.shape[1]
        whole = (
            qkv_read_key[:, : 3 * width],
            out_value[:, :width],
            expand_full,
            contract_full,
            qkv_read_key[:, 3 * width : 3 * width + feat],
            qkv_read_key[:, 3 * width + feat :],
            out_value[:, width:],
        )
    else:
        whole = tuple(lax.all_gather(s, "dp", axis=0, tiled=True) for s in shards)
    p = dict(zip(names, whole))
    p.update(
        one_gain=norm_one_gain, one_bias=norm_one_bias, out_bias=out_bias, two_gain=norm_two_gain,
        two_bias=norm_two_bias, expand_bias=expand_bias, contract_bias=contract_bias,
        shift=jnp.concatenate([qv_bias[0], jnp.zeros((width,), F32), qv_bias[1]]),
    )
    flags = lax.dynamic_slice_in_dim(starts, group * segs_local, segs_local, 1)

    swap = [(0, 1), (1, 0)]

    def own_and_other(rows):
        halves = rows.reshape(ranks, tok_rows, width)
        return pick(halves, rank, 0), pick(halves, 1 - rank, 0)

    def swapped(given):
        return lax.ppermute(given, "ctx", swap)

    def settle(halves, flips):
        micro_rows = []
        for micro in range(2):
            pair = [jnp.where(rank == micro, kept, got) for kept, got in halves]
            flip = flips[micro]
            micro_rows.append(
                jnp.stack([jnp.where(flip, pair[1], pair[0]), jnp.where(flip, pair[0], pair[1])])
            )
        return jnp.stack(micro_rows)

    if quick:
        flips = flags[:, 1] == 1
        flip = pick(flips, rank, 0)
        told = jnp.stack([flip.astype(jnp.int32), rank.astype(jnp.int32)])
        got = swapped(give)
        give_grad = pick(behind(cotangent, got, expand_full), 1 - rank, 0)
        flags = pick(flags, rank, 0)
        flags = jnp.where(flip, flags[::-1], flags)
        segs = segs_local
        seg_rows = ranks * tok_rows
    else:
        rows_in, rows_grad = tokens.reshape(-1, width), cotangent.reshape(-1, width)
        flags = flags.reshape(-1)
        segs = micros * segs_local
        seg_rows = tok_rows

    if quick:
        norms = tuple(v[None] for v in (norm_one_gain, norm_one_bias, norm_two_gain, norm_two_bias))
        fixed = tuple(v[None] for v in (p["shift"], out_bias, expand_bias, contract_bias))
        mem_weights_in = (qkv_read_key, out_value, expand_full, contract_full)
        *kept, kv_follow = mem_forward(memory_tokens, (*norms, *fixed), mem_weights_in)
        kv_first = kept[0][:, width:]
    else:
        kv_first, kv_follow, m = memory_forward(memory_tokens, p)
    kv_mem = jnp.where((flags == 0)[:, None, None], kv_follow[None], kv_first[None])
    if quick:
        rows_in, normed_a, qkv = enter(
            told, tokens, got, norm_one_gain, norm_one_bias, qkv_read_key, p["shift"]
        )
        attended, lse_first = attn_fwd(behind(qkv, give_grad), kv_first, 0, seg_rows, None)
        got_grad = swapped(give_grad)
        attended, lse_second = attn_fwd(qkv, kv_mem[1], 1, seg_rows, attended)
        attended, got_grad = lax.optimization_barrier((attended, got_grad))
        (
            result, rows_grad, normed_b, activ, grad_expanded, grad_attn_out, grad_attended, mid_sums, expand_sums,
        ) = middle(
            told, cotangent, got_grad, rows_in, attended, p["out"], p["expand"], p["contract"], out_bias,
            norm_two_gain, norm_two_bias, expand_bias, contract_bias,
        )
        grad_after = grad_attn_out
    else:
        hidden = rows_in.astype(F32)
        unit_a, rstd_a = norm_parts(hidden)
        normed_a = (unit_a * norm_one_gain + norm_one_bias).astype(BF16)
        qkv = (dot_dims(normed_a, p["qkv"], 1, 0) + p["shift"]).astype(BF16)
        seg_qkv = qkv.reshape(segs, seg_rows, 3 * width)
        kv_all = lax.all_gather(seg_qkv[:, :, width:], "ctx", axis=1, tiled=True)
        kv_all = jnp.concatenate([kv_mem, kv_all], axis=1)
        query_at = mem + rank * seg_rows + jnp.arange(seg_rows, dtype=jnp.int32)
        key_at = jnp.arange(mem + ranks * seg_rows, dtype=jnp.int32)
        allowed = key_at[None, :] <= query_at[:, None]
        attended, lse = plain_fwd(seg_qkv, kv_all, allowed)
        attended = attended.reshape(-1, width)
        after = hidden + dot_dims(attended, p["out"], 1, 0) + out_bias
        unit_b, rstd_b = norm_parts(after)
        normed_b = (unit_b * norm_two_gain + norm_two_bias).astype(BF16)
        expanded = dot_dims(normed_b, p["expand"], 1, 0) + expand_bias
        activ = gelu_tanh(expanded).astype(BF16)
        result = (after + dot_dims(activ, p["contract"], 1, 1) + contract_bias).astype(BF16)

    def input_back(at, grads, weights):
        grad = dot_dims(grads[0], weights[0], 1, 1)
        for g, w in zip(grads[1:], weights[1:]):
            grad = grad + dot_dims(g, w, 1, 1)
        unit, rstd = norm_parts(rows_in[at].astype(F32))
        grad_hidden, gain, bias = norm_back(grad, unit, rstd, norm_one_gain)
        return (grad_hidden + grad_after[at].astype(F32)).astype(BF16), gain, bias

    def pool(dkv_mem):
        follows = (flags == 0).astype(F32)[:, None, None]
        kinds = [jnp.sum(dkv_mem * (1.0 - follows), axis=0), jnp.sum(dkv_mem * follows, axis=0)]
        return jnp.stack(kinds)

    if quick:
        lse = jnp.concatenate([lse_first, lse_second], axis=0)
        spans = [slice(0, seg_rows), slice(seg_rows, 2 * seg_rows)]
        by_rank = lambda r: r.reshape(ranks, tok_rows, width)
        peers = groups * ranks
        dk_mem, dv_mem, middle_sums = attn_mem(qkv, kv_mem, attended, grad_attended, lse)
        pooled = pool(jnp.concatenate([dk_mem, dv_mem], axis=2))
        wide_terms = (
            dot_dims(rows_grad, activ, 0, 0).astype(BF16),
            dot_dims(normed_b, grad_expanded, 0, 0).astype(BF16),
        )
        result_halves = [by_rank(result[a]) for a in spans]
        grad_qkv, wide_sums, got_result, pooled = back_reduce(
            qkv, kv_mem, grad_attended, lse, middle_sums, wide_terms, result_halves, pooled.reshape(peers, -1, 128), ranks
        )
        pooled = pooled.reshape(2, mem, 2 * width)
        ends = [input_back(a, [grad_qkv[a]], [p["qkv"]]) for a in spans]
        one_gain, one_bias = ends[0][1] + ends[1][1], ends[0][2] + ends[1][2]
        qkv_sums = jnp.sum(grad_qkv.astype(F32), axis=0).reshape(3, width)
        late_terms = (
            dot_dims(normed_a, grad_qkv, 0, 0).astype(BF16),
            dot_dims(attended, grad_attn_out, 0, 0).astype(BF16),
        )
    else:
        _, gelu_pull = jax.vjp(gelu_tanh, expanded)
        grad_expanded = gelu_pull(dot_dims(rows_grad, p["contract"], 1, 0))[0].astype(BF16)
        grad_after, two_gain, two_bias = norm_back(
            dot_dims(grad_expanded, p["expand"], 1, 1), unit_b, rstd_b, norm_two_gain
        )
        grad_after = grad_after + rows_grad.astype(F32)
        grad_attn_out = grad_after.astype(BF16)
        grad_attended = dot_dims(grad_attn_out, p["out"], 1, 1).astype(BF16)
        dq, dkv = plain_bwd(
            seg_qkv, kv_all, allowed, lse, grad_attended.reshape(segs, seg_rows, width)
        )
        pooled = pool(dkv[:, :mem])
        dkv = lax.psum_scatter(
            dkv[:, mem:].astype(BF16), "ctx", scatter_dimension=1, tiled=True
        )
        grad_qkv = jnp.concatenate([dq.astype(BF16), dkv], axis=2).reshape(-1, 3 * width)
        grad_rows, one_gain, one_bias = input_back(slice(None), [grad_qkv], [p["qkv"]])
        terms = (
            dot_dims(normed_a, grad_qkv, 0, 0).astype(BF16),
            dot_dims(attended, grad_attn_out, 0, 0).astype(BF16),
            dot_dims(normed_b, grad_expanded, 0, 0).astype(BF16),
            dot_dims(rows_grad, activ, 0, 0).astype(BF16),
        )
        qkv_sums = jnp.sum(grad_qkv.astype(F32), axis=0).reshape(3, width)
    column_sum = lambda a: jnp.sum(a.astype(F32), axis=0)
    if quick:
        mid = (mid_sums[0], mid_sums[1], mid_sums[2], expand_sums[0], mid_sums[3])
    else:
        mid = (
            column_sum(grad_attn_out), two_gain, two_bias, column_sum(grad_expanded), column_sum(rows_grad),
        )
    vectors = (one_gain, one_bias, jnp.stack([qkv_sums[0], qkv_sums[2]]), *mid)
    if not quick:
        summed = tuple(
            lax.psum(
                lax.psum_scatter(t, "dp", scatter_dimension=0, tiled=True).astype(F32), "ctx"
            )
            for t in terms
        )
        pooled, vectors = lax.psum((pooled, vectors), ("dp", "ctx"))

    if quick:
        flat = jnp.concatenate([v.reshape(-1) for v in vectors])
        lines = pl.cdiv(flat.size, peers * 128)
        flat = jnp.pad(flat, (0, peers * lines * 128 - flat.size)).reshape(peers, lines, 128)
        grad_halves = [by_rank(ends[k][0]) for k in range(2)]
        late_sums, got_grad_rows, flat, grad_mt, mem_matrices, mem_vectors = mem_reduce(
            memory_tokens, norms, pooled, shard, group, kept, mem_weights_in, late_terms, grad_halves, flat, ranks
        )
        flat = flat.reshape(-1)
        summed = (late_sums[0], late_sums[1], wide_sums[1], wide_sums[0])
    else:
        mine = lambda a: lax.dynamic_slice_in_dim(a, group * shard, shard, 1)
        grad_mt, mem_matrices, mem_vectors = memory_backward(
            memory_tokens, p, m, pooled[0], pooled[1], mine
        )
    if quick:
        split, place = [], 0
        for v in vectors:
            split.append(flat[place : place + v.size].reshape(v.shape))
            place += v.size
        vectors = tuple(split)
    matrices = tuple(a + b for a, b in zip(summed, mem_matrices)) + mem_matrices[4:]
    vectors = tuple(a + b for a, b in zip(vectors, mem_vectors))
    if quick:
        own = lambda halves: [pick(h, rank, 0) for h in halves]
        block_out = settle(list(zip(own(result_halves), got_result)), flips)
        token_grad = settle(list(zip(own(grad_halves), got_grad_rows)), flips)
    else:
        block_out, token_grad = result.reshape(tokens.shape), grad_rows.reshape(tokens.shape)
    return (
        block_out,
        token_grad,
        grad_mt,
        vectors[0],
        vectors[1],
        matrices[0],
        vectors[2],
        matrices[1],
        vectors[3],
        vectors[4],
        vectors[5],
        matrices[2],
        vectors[6],
        matrices[3],
        vectors[7],
        matrices[4],
        matrices[5],
        matrices[6],
    )


def solution(mesh):
    rows = P(None, "dp", "ctx", None)
    matrix = P("dp", None)
    full = P()
    return jax.shard_map(
        local,
        mesh=mesh,
        in_specs=(
            rows, rows, full, full, full, full, full, matrix, full, matrix, full, full, full,
            matrix, full, matrix, full, matrix, matrix, matrix,
        ),
        out_specs=(
            rows, rows, full, full, full, matrix, full, matrix, full, full, full, matrix, full,
            matrix, full, matrix, matrix, matrix,
        ),
        check_vma=False,
    )
```

```python
import functools

import jax
import jax.numpy as jnp
from jax import lax
from jax.experimental import pallas as pl
from jax.experimental.pallas import tpu as pltpu
from jax.sharding import PartitionSpec as P

H = 12
HD = 64
EPS = 1e-05
CHUNK = 256
WIDE = 512
F32 = jnp.float32
BF16 = jnp.bfloat16


def norm_parts(rows):
    centred = rows - jnp.mean(rows, axis=-1, keepdims=True)
    spread = jnp.mean(centred * centred, axis=-1, keepdims=True)
    rstd = lax.rsqrt(spread + EPS)
    return centred * rstd, rstd


def norm_back(grad, unit, rstd, gain):
    scaled = grad * gain
    first = jnp.mean(scaled, axis=-1, keepdims=True)
    second = jnp.mean(scaled * unit, axis=-1, keepdims=True)
    grad_rows = rstd * (scaled - first - unit * second)
    return grad_rows, jnp.sum(grad * unit, axis=0), jnp.sum(grad, axis=0)


def feature_map(rows):
    halves = jnp.concatenate([jax.nn.softplus(rows), jax.nn.softplus(-rows)], axis=-1)
    return jnp.concatenate([halves * jnp.roll(halves, j, axis=-1) for j in (1, 2, 3)], axis=-1)


def gelu_tanh(rows):
    return jax.nn.gelu(rows, approximate=True)


def dot_dims(a, b, ca, cb, precision=None):
    return lax.dot_general(
        a, b, (((ca,), (cb,)), ((), ())), precision=precision, preferred_element_type=F32
    )


exact = functools.partial(dot_dims, precision=lax.Precision.HIGHEST)


def head_rows(scale):
    lane = lax.broadcasted_iota(jnp.int32, (1, 2 * HD), 1)
    low = jnp.where(lane < HD, scale, 0.0).astype(BF16)
    high = jnp.where(lane < HD, 0.0, scale).astype(BF16)
    return low, high


def causal_tail(scores):
    key = lax.broadcasted_iota(jnp.int32, scores.shape, 0)
    return jnp.where(key <= lax.broadcasted_iota(jnp.int32, scores.shape, 1), scores, 0.0)


def attn_fwd_kernel(q_ref, k_ref, v_ref, km_ref, vm_ref, o_ref, lse_ref, keys, vals_t, vmem_t):
    mem = km_ref.shape[0]
    keys[0:mem, :] = km_ref[...]
    keys[mem:, :] = k_ref[...]
    vals_t[...] = v_ref[...].T
    vmem_t[...] = vm_ref[...].T
    picks = head_rows(HD**-0.5)
    steps = [(part, head) for part in range(q_ref.shape[0] // WIDE) for head in range(2)]

    def begin(part, head):
        lo, hi = part * WIDE, (part + 1) * WIDE
        return dot_dims(keys[0 : mem + hi, :], q_ref[lo:hi, :] * picks[head], 1, 1)

    ahead = begin(*steps[0])
    outs = []
    for n, (part, head) in enumerate(steps):
        lo, hi = part * WIDE, (part + 1) * WIDE
        band = slice(head * HD, (head + 1) * HD)
        raw = jnp.exp(ahead)
        if n + 1 < len(steps):
            ahead = begin(*steps[n + 1])
        raw = jnp.concatenate([raw[: mem + lo], causal_tail(raw[mem + lo :])], axis=0)
        total = jnp.sum(raw, axis=0, keepdims=True)
        lse_ref[0, head : head + 1, lo:hi] = jnp.log(total)
        weights = (raw * (1.0 / total)).astype(BF16)
        outs.append(
            dot_dims(vals_t[band, 0:hi], weights[mem:], 1, 0)
            + dot_dims(vmem_t[band, :], weights[:mem], 1, 0)
        )
        if head == 1:
            o_ref[lo:hi, :] = jnp.concatenate(outs, axis=0).T.astype(BF16)
            outs = []


def attn_fwd_after_kernel(q_ref, k_ref, v_ref, km_ref, vm_ref, held_ref, *rest):
    del held_ref
    attn_fwd_kernel(q_ref, k_ref, v_ref, km_ref, vm_ref, *rest)


def attn_fwd(qkv, kv_mem, seg, rows, held):
    width = qkv.shape[1] // 3
    mem = kv_mem.shape[0]
    pairs = H // 2
    wide = 2 * HD
    spec = lambda off: pl.BlockSpec((rows, wide), lambda p, off=off: (seg, off * pairs + p))
    mspec = lambda off: pl.BlockSpec((mem, wide), lambda p, off=off: (0, off * pairs + p))
    more = [] if held is None else [held]
    return pl.pallas_call(
        attn_fwd_kernel if held is None else attn_fwd_after_kernel,
        grid=(pairs,),
        in_specs=[spec(0), spec(1), spec(2), mspec(0), mspec(1)]
        + [pl.BlockSpec(memory_space=pl.ANY)] * len(more),
        out_specs=[
            pl.BlockSpec((rows, wide), lambda p: (seg, p)),
            pl.BlockSpec((1, 2, rows), lambda p: (p, 0, 0)),
        ],
        out_shape=[
            jax.ShapeDtypeStruct((qkv.shape[0], width), BF16),
            jax.ShapeDtypeStruct((pairs, 2, rows), F32),
        ],
        scratch_shapes=[
            pltpu.VMEM((mem + rows, wide), BF16),
            pltpu.VMEM((wide, rows), BF16),
            pltpu.VMEM((wide, mem), BF16),
        ],
        input_output_aliases={5: 0} if more else {},
        compiler_params=pltpu.CompilerParams(vmem_limit_bytes=60 * 2**20),
        cost_estimate=pl.CostEstimate(
            flops=pairs * rows * rows * 4000,
            bytes_accessed=rows * width * 8,
            transcendentals=0,
        ),
        name="attn_fwd",
    )(qkv, qkv, qkv, kv_mem, kv_mem, *more)


def attn_bwd_kernel(
    q_ref, k_ref, v_ref, km_ref, vm_ref, g_ref, lse_ref, o_ref,
    out_ref, dkm_ref, dvm_ref,
    keys, vals, keys_t, kmem_t, dq, dk, dv,
):
    phase = pl.program_id(1)
    mem = km_ref.shape[1]
    rows = q_ref.shape[0]

    @pl.when((phase == 2) & (pl.program_id(0) < pl.num_programs(0) - 1))
    def _():
        keys[0:mem, :] = km_ref[0]
        keys[mem:, :] = k_ref[...]
        vals[0:mem, :] = vm_ref[0]
        vals[mem:, :] = v_ref[...]
        keys_t[...] = k_ref[...].T
        kmem_t[...] = km_ref[0].T
        dk[...] = jnp.zeros_like(dk)
        dv[...] = jnp.zeros_like(dv)
        scaled_picks = head_rows(HD**-0.5)
        picks = head_rows(1.0)
        for part in range(rows // CHUNK):
            lo, hi = part * CHUNK, (part + 1) * CHUNK
            end = mem + hi
            query = q_ref[lo:hi, :]
            grad = g_ref[lo:hi, :]
            inner = (grad.astype(F32) * o_ref[lo:hi, :].astype(F32)).T
            dqs = []
            for head in range(2):
                band = slice(head * HD, (head + 1) * HD)
                query_h = query * scaled_picks[head]
                grad_h = grad * picks[head]
                log_total = lse_ref[0, head : head + 1, lo:hi]
                centre = jnp.sum(inner[band], axis=0, keepdims=True)
                prob = jnp.exp(dot_dims(keys[0:end, :], query_h, 1, 1) - log_total)
                prob = jnp.concatenate(
                    [prob[: mem + lo], causal_tail(prob[mem + lo :])], axis=0
                )
                grad_p = dot_dims(vals[0:end, :], grad_h, 1, 1)
                grad_s = (prob * (grad_p - centre)).astype(BF16)
                dv[0:end, :] += dot_dims(prob.astype(BF16), grad_h, 1, 0)
                dk[0:end, :] += dot_dims(grad_s, query_h, 1, 0)
                dqs.append(
                    dot_dims(keys_t[band, 0:hi], grad_s[mem:], 1, 0)
                    + dot_dims(kmem_t[band, :], grad_s[:mem], 1, 0)
                )
            dq[lo:hi, :] = (jnp.concatenate(dqs, axis=0) * HD**-0.5).T.astype(BF16)
        out_ref[...] = dq[...]
        dkm_ref[0] = dk[0:mem, :]
        dvm_ref[0] = dv[0:mem, :]

    @pl.when((phase == 0) & (pl.program_id(0) > 0))
    def _():
        out_ref[...] = dk[mem:, :].astype(BF16)

    @pl.when((phase == 1) & (pl.program_id(0) > 0))
    def _():
        out_ref[...] = dv[mem:, :].astype(BF16)


def choose(told, kept, got, out):
    own = pl.program_id(0) % 2 == told[0]

    @pl.when(own)
    def _():
        out[...] = kept[0, 0]

    @pl.when(jnp.logical_not(own))
    def _():
        out[...] = got[0]


def half_specs(rows, width):
    return [
        pl.BlockSpec((1, 1, rows, width), lambda i, told: (told[0], i // 2, 0, 0)),
        pl.BlockSpec((1, rows, width), lambda i, told: (i // 2, 0, 0)),
    ]


def enter_kernel(told, kept, got, gain, bias, weight, shift, rows_ref, normed_ref, qkv_ref):
    choose(told, kept, got, rows_ref)
    unit, _ = norm_parts(rows_ref[...].astype(F32))
    normed = (unit * gain[...] + bias[...]).astype(BF16)
    normed_ref[...] = normed
    wide = weight.shape[1] // 3
    for k in range(3):
        at = slice(k * wide, (k + 1) * wide)
        qkv_ref[:, at] = (dot_dims(normed, weight[:, at], 1, 0) + shift[:, at]).astype(BF16)


def enter(told, kept, got, gain, bias, weight, shift):
    _, segs, rows, width = kept.shape
    whole = lambda r, c: pl.BlockSpec((r, c), lambda i, told: (0, 0), pipeline_mode=pl.Buffered(1))
    block = lambda c: pl.BlockSpec((rows, c), lambda i, told: (i, 0))
    sizes = (width, width, 3 * width)
    return pl.pallas_call(
        enter_kernel,
        grid_spec=pltpu.PrefetchScalarGridSpec(
            num_scalar_prefetch=1,
            grid=(2 * segs,),
            in_specs=[*half_specs(rows, width), whole(1, width), whole(1, width), whole(width, 3 * width), whole(1, 3 * width)],
            out_specs=[block(c) for c in sizes],
        ),
        out_shape=[jax.ShapeDtypeStruct((2 * segs * rows, c), BF16) for c in sizes],
        compiler_params=pltpu.CompilerParams(vmem_limit_bytes=60 * 2**20),
        cost_estimate=pl.CostEstimate(
            flops=8 * segs * rows * width * width * 3, bytes_accessed=segs * rows * width * 28, transcendentals=0
        ),
        name="enter",
    )(told, kept, got, gain[None], bias[None], weight, shift[None])


def middle_kernel(
    told, kept, got, rows_ref, attended, out_w, expand_w, contract_w, out_b, gain, bias, expand_b, contract_b,
    result_ref, cot_ref, normed_ref, activ_ref, grad_exp_ref, grad_out_ref, grad_att_ref,
    sums_ref, exp_sums_ref,
):
    choose(told, kept, got, cot_ref)
    cot = cot_ref[...]
    after = rows_ref[...].astype(F32) + dot_dims(attended[...], out_w[...], 1, 0) + out_b[...]
    unit, rstd = norm_parts(after)
    normed = (unit * gain[...] + bias[...]).astype(BF16)
    normed_ref[...] = normed
    total = after + contract_b[...]
    back = 0.0

    @pl.when(pl.program_id(0) == 0)
    def _():
        sums_ref[...] = jnp.zeros_like(sums_ref)
        exp_sums_ref[...] = jnp.zeros_like(exp_sums_ref)

    parts = 4
    wide = expand_w.shape[1] // parts
    bend, cube = 0.7978845608028654, 0.044715
    for part in range(parts):
        at = slice(part * wide, (part + 1) * wide)
        value = dot_dims(normed, expand_w[:, at], 1, 0) + expand_b[:, at]
        square = value * value
        half = 0.5 + 0.5 * jnp.tanh(value * (bend + bend * cube * square))
        activ = (value * half).astype(BF16)
        activ_ref[:, at] = activ
        slope = half + (half - half * half) * (value * (2.0 * bend + 6.0 * bend * cube * square))
        grad = (dot_dims(cot, contract_w[:, at], 1, 0) * slope).astype(BF16)
        grad_exp_ref[:, at] = grad
        exp_sums_ref[:, at] += jnp.sum(grad.astype(F32), axis=0, keepdims=True)
        total = total + dot_dims(activ, contract_w[:, at], 1, 1)
        back = back + dot_dims(grad, expand_w[:, at], 1, 1)
    result_ref[...] = total.astype(BF16)
    wide_cot = cot.astype(F32)
    grad_rows, gain_sum, bias_sum = norm_back(back, unit, rstd, gain[...])
    grad_out = (grad_rows + wide_cot).astype(BF16)
    grad_out_ref[...] = grad_out
    grad_att_ref[...] = dot_dims(grad_out, out_w[...], 1, 1).astype(BF16)
    sums = (
        jnp.sum(grad_out.astype(F32), axis=0, keepdims=True),
        gain_sum[None],
        bias_sum[None],
        jnp.sum(wide_cot, axis=0, keepdims=True),
    )
    for k, value in enumerate(sums):
        sums_ref[k : k + 1, :] += value


def middle(told, kept, got, rows_in, attended, out_w, expand_w, contract_w, out_b, gain, bias, expand_b, contract_b):
    _, segs, rows, width = kept.shape
    wide = expand_w.shape[1]
    whole = lambda r, c: pl.BlockSpec((r, c), lambda i, told: (0, 0), pipeline_mode=pl.Buffered(1))
    block = lambda c: pl.BlockSpec((rows, c), lambda i, told: (i, 0))
    sizes = (width, width, width, wide, wide, width, width)
    count = 2 * segs * rows
    fixed = lambda r, c: pl.BlockSpec((r, c), lambda i, told: (0, 0))
    return pl.pallas_call(
        middle_kernel,
        grid_spec=pltpu.PrefetchScalarGridSpec(
            num_scalar_prefetch=1,
            grid=(2 * segs,),
            in_specs=[
                *half_specs(rows, width), block(width), block(width), whole(width, width), whole(width, wide),
                whole(width, wide), whole(1, width), whole(1, width), whole(1, width), whole(1, wide), whole(1, width),
            ],
            out_specs=[*[block(c) for c in sizes], fixed(8, width), fixed(1, wide)],
        ),
        out_shape=[
            *[jax.ShapeDtypeStruct((count, c), BF16) for c in sizes],
            jax.ShapeDtypeStruct((8, width), F32),
            jax.ShapeDtypeStruct((1, wide), F32),
        ],
        compiler_params=pltpu.CompilerParams(vmem_limit_bytes=60 * 2**20),
        cost_estimate=pl.CostEstimate(
            flops=count * width * (8 * wide + 4 * width) * 2, bytes_accessed=count * (14 * width + 4 * wide), transcendentals=0
        ),
        name="middle",
    )(
        told, kept, got, rows_in, attended, out_w, expand_w, contract_w, out_b[None], gain[None], bias[None],
        expand_b[None], contract_b[None],
    )


def leave_kernel(grad_ref, weight, rows_ref, after_ref, gain, rows_out, sums_ref, col_ref):
    @pl.when(pl.program_id(0) == 0)
    def _():
        sums_ref[...] = jnp.zeros_like(sums_ref)
        col_ref[...] = jnp.zeros_like(col_ref)

    grad = grad_ref[...]
    unit, rstd = norm_parts(rows_ref[...].astype(F32))
    grad_rows, gain_sum, bias_sum = norm_back(dot_dims(grad, weight[...], 1, 1), unit, rstd, gain[...])
    rows_out[...] = (grad_rows + after_ref[...].astype(F32)).astype(BF16)
    sums_ref[0:1, :] += gain_sum[None]
    sums_ref[1:2, :] += bias_sum[None]
    col_ref[...] += jnp.sum(grad.astype(F32), axis=0, keepdims=True)


def leave(grad_qkv, weight, rows_in, grad_after, gain, rows):
    count, width = rows_in.shape
    block = lambda c: pl.BlockSpec((rows, c), lambda i: (i, 0))
    fixed = lambda r, c: pl.BlockSpec((r, c), lambda i: (0, 0))
    whole = lambda r, c: pl.BlockSpec((r, c), lambda i: (0, 0), pipeline_mode=pl.Buffered(1))
    return pl.pallas_call(
        leave_kernel,
        grid=(count // rows,),
        in_specs=[block(3 * width), whole(width, 3 * width), block(width), block(width), whole(1, width)],
        out_specs=[block(width), fixed(8, width), fixed(1, 3 * width)],
        out_shape=[
            jax.ShapeDtypeStruct((count, width), BF16),
            jax.ShapeDtypeStruct((8, width), F32),
            jax.ShapeDtypeStruct((1, 3 * width), F32),
        ],
        compiler_params=pltpu.CompilerParams(vmem_limit_bytes=60 * 2**20),
        cost_estimate=pl.CostEstimate(
            flops=6 * count * width * width, bytes_accessed=count * width * 12, transcendentals=0
        ),
        name="leave",
    )(grad_qkv, weight, rows_in, grad_after, gain[None])


def thirds(rows):
    parts = []
    for _ in range(3):
        parts.append(rows.astype(BF16))
        rows = rows - parts[-1].astype(F32)
    return jnp.concatenate(parts, axis=0)


def exact_low(rows, weight, side):
    count = rows.shape[0]
    out = dot_dims(thirds(rows), weight, 1, side)
    return out[:count] + out[count : 2 * count] + out[2 * count :]


def softplus(rows):
    return jnp.maximum(rows, 0.0) + jnp.log1p(jnp.exp(-jnp.abs(rows)))


def feature_parts(rows):
    halves = jnp.concatenate([softplus(rows), softplus(-rows)], axis=1)
    turned = [pltpu.roll(halves, j, 1) for j in (1, 2, 3)]
    return halves, turned, jnp.concatenate([halves * t for t in turned], axis=1)


def feature_back(rows, grad):
    halves, turned, _ = feature_parts(rows)
    wide = halves.shape[1]
    total = 0.0
    for j in (1, 2, 3):
        part = grad[:, (j - 1) * wide : j * wide]
        total = total + part * turned[j - 1] + pltpu.roll(part * halves, wide - j, 1)
    first, last = total[:, : wide // 2], total[:, wide // 2 :]
    return first * jax.nn.sigmoid(rows) - last * jax.nn.sigmoid(-rows)


def per_head(rows):
    tall = jnp.concatenate([rows] * H, axis=0)
    return tall * head_mask(tall.shape, rows.shape[0]).astype(rows.dtype)


def head_mask(shape, count):
    head = lax.broadcasted_iota(jnp.int32, shape, 0) // count
    return (lax.broadcasted_iota(jnp.int32, shape, 1) // HD == head).astype(F32)


def from_heads(tall, count):
    tall = tall * head_mask(tall.shape, count)
    total = tall[:count]
    for head in range(1, H):
        total = total + tall[head * count : (head + 1) * count]
    return total


def mem_weights(query, key):
    count = key.shape[0]
    tall = per_head(query)
    scores = dot_dims(tall, key, 1, 1) * HD**-0.5
    at = lax.rem(lax.broadcasted_iota(jnp.int32, scores.shape, 0), count)
    raw = jnp.where(lax.broadcasted_iota(jnp.int32, scores.shape, 1) <= at, jnp.exp(scores), 0.0)
    return tall, raw / jnp.sum(raw, axis=1, keepdims=True)


def read_parts(read_feat, key_feat, value_new):
    mix = exact(read_feat, key_feat, 1, 1)
    return mix, exact(mix, value_new, 1, 0), 1.0 + jnp.sum(mix, axis=1, keepdims=True)


def bring(sources, targets, sem):
    copies = [pltpu.make_async_copy(a, b, sem.at[k]) for k, (a, b) in enumerate(zip(sources, targets))]
    for copy in copies:
        copy.start()
    return copies


def mem_fwd_kernel(
    mt_ref, one_gain, one_bias, two_gain, two_bias, shift, out_b, expand_b, contract_b,
    qrk_hbm, ov_hbm, expand_hbm, contract_hbm,
    qkv_ref, attended_ref, after_ref, expanded_ref, result_ref, pre_ref, value_ref, follow_ref, kv_ref,
    qrk, ov, expand_w, contract_w, sem,
):
    copies = bring((qrk_hbm, ov_hbm, expand_hbm, contract_hbm), (qrk, ov, expand_w, contract_w), sem)
    mt = mt_ref[...]
    width = mt.shape[1]
    feat = pre_ref.shape[1] // 2
    unit, _ = norm_parts(mt)
    normed = (unit * one_gain[...] + one_bias[...]).astype(BF16)
    copies[0].wait()
    qkv = (dot_dims(normed, qrk[:, : 3 * width], 1, 0) + shift[...]).astype(BF16)
    qkv_ref[...] = qkv
    read_pre = exact_low(mt, qrk[:, 3 * width : 3 * width + feat], 0)
    _, weights = mem_weights(qkv[:, :width], qkv[:, width : 2 * width])
    mixed = dot_dims(weights.astype(BF16), qkv[:, 2 * width :], 1, 0)
    attended = from_heads(mixed, mt.shape[0]).astype(BF16)
    attended_ref[...] = attended
    copies[1].wait()
    after = mt + dot_dims(attended, ov[:, :width], 1, 0) + out_b[...]
    after_ref[...] = after
    unit, _ = norm_parts(after)
    normed = (unit * two_gain[...] + two_bias[...]).astype(BF16)
    copies[2].wait()
    expanded = dot_dims(normed, expand_w[...], 1, 0) + expand_b[...]
    expanded_ref[...] = expanded
    activ = gelu_tanh(expanded).astype(BF16)
    copies[3].wait()
    result = after + dot_dims(activ, contract_w[...], 1, 1) + contract_b[...]
    result_ref[...] = result
    key_pre = exact_low(result, qrk[:, 3 * width + feat :], 0)
    value_new = exact_low(result, ov[:, width:], 0)
    value_ref[...] = value_new
    pre_ref[:, :feat] = read_pre
    pre_ref[:, feat:] = key_pre
    _, numer, denom = read_parts(feature_parts(read_pre)[2], feature_parts(key_pre)[2], value_new)
    follow = mt + numer / denom
    follow_ref[...] = follow
    unit, _ = norm_parts(follow)
    normed = (unit * one_gain[...] + one_bias[...]).astype(BF16)
    kv_ref[...] = (dot_dims(normed, qrk[:, width : 3 * width], 1, 0) + shift[:, width:]).astype(BF16)


def mem_call(kernel, name, given, weights, outs, cycles):
    vmem = pl.BlockSpec(memory_space=pltpu.VMEM)
    return pl.pallas_call(
        kernel,
        in_specs=[vmem] * len(given) + [pl.BlockSpec(memory_space=pl.ANY)] * len(weights),
        out_specs=[vmem] * len(outs),
        out_shape=outs,
        scratch_shapes=[
            *[pltpu.VMEM(w.shape, w.dtype) for w in weights],
            pltpu.SemaphoreType.DMA((len(weights),)),
        ],
        compiler_params=pltpu.CompilerParams(vmem_limit_bytes=60 * 2**20),
        cost_estimate=pl.CostEstimate(flops=cycles * 10**9, bytes_accessed=17 * 10**6, transcendentals=0),
        name=name,
    )(*given, *weights)


def mem_forward(mt, given, weights):
    mem, width = mt.shape
    wide, feat = weights[2].shape[1], (weights[0].shape[1] - 3 * width) // 2
    shape = jax.ShapeDtypeStruct
    outs = [
        shape((mem, 3 * width), BF16), shape((mem, width), BF16), shape((mem, width), F32), shape((mem, wide), F32),
        shape((mem, width), F32), shape((mem, 2 * feat), F32), shape((mem, width), F32), shape((mem, width), F32),
        shape((mem, 2 * width), BF16),
    ]
    return mem_call(mem_fwd_kernel, "mem_fwd", (mt, *given), weights, outs, 15)


def mem_bwd_kernel(
    mt_ref, one_gain, one_bias, two_gain, two_bias, pooled, chosen,
    qkv_ref, attended_ref, after_ref, expanded_ref, result_ref, pre_ref, value_ref, follow_ref,
    qrk_hbm, ov_hbm, expand_hbm, contract_hbm,
    grad_mt_ref, qkv_grad, out_grad, expand_grad, contract_grad, read_grad, key_grad, value_grad, sums_ref, exp_sums_ref,
    qrk, ov, expand_w, contract_w, sem,
):
    copies = bring((qrk_hbm, ov_hbm, expand_hbm, contract_hbm), (qrk, ov, expand_w, contract_w), sem)
    mt = mt_ref[...]
    mem, width = mt.shape
    feat = pre_ref.shape[1] // 2
    sums_ref[...] = jnp.zeros_like(sums_ref)

    def add_row(k, value):
        sums_ref[k : k + 1, :] += value[None]

    def column(value):
        return jnp.sum(value.astype(F32), axis=0)

    unit_f, rstd_f = norm_parts(follow_ref[...])
    normed_f = (unit_f * one_gain[...] + one_bias[...]).astype(BF16)
    grad_f = pooled[1].astype(BF16)
    copies[0].wait()
    grad_follow, gain, bias = norm_back(
        dot_dims(grad_f, qrk[:, width : 3 * width], 1, 1), unit_f, rstd_f, one_gain[...]
    )
    add_row(0, gain)
    add_row(1, bias)
    add_row(3, column(grad_f[:, width:]))
    read_pre, key_pre, value_new = pre_ref[:, :feat], pre_ref[:, feat:], value_ref[...]
    read_feat, key_feat = feature_parts(read_pre)[2], feature_parts(key_pre)[2]
    mix, numer, denom = read_parts(read_feat, key_feat, value_new)
    grad_numer = grad_follow / denom
    grad_denom = -jnp.sum(grad_follow * numer, axis=1, keepdims=True) / (denom * denom)
    grad_mix = exact(grad_numer, value_new, 1, 1) + grad_denom
    grad_value = exact(mix, grad_numer, 0, 0)
    grad_read_pre = feature_back(read_pre, exact(grad_mix, key_feat, 1, 0))
    grad_key_pre = feature_back(key_pre, exact(grad_mix, read_feat, 0, 0))
    grad_mt = grad_follow + exact_low(grad_read_pre, qrk[:, 3 * width : 3 * width + feat], 1)
    copies[1].wait()
    grad_result = exact_low(grad_key_pre, qrk[:, 3 * width + feat :], 1) + exact_low(
        grad_value, ov[:, width:], 1
    )
    grad_contract = grad_result.astype(BF16)
    add_row(7, column(grad_contract))
    expanded = expanded_ref[...]
    bend, cube = 0.7978845608028654, 0.044715
    square = expanded * expanded
    curve = jnp.tanh(bend * expanded * (1.0 + cube * square))
    half = 0.5 * (1.0 + curve)
    activ = (expanded * half).astype(BF16)
    slope = half + 0.5 * bend * expanded * (1.0 - curve * curve) * (1.0 + 3.0 * cube * square)
    copies[3].wait()
    grad_expanded = (dot_dims(grad_contract, contract_w[...], 1, 0) * slope).astype(BF16)
    exp_sums_ref[...] = column(grad_expanded)[None]
    unit_b, rstd_b = norm_parts(after_ref[...])
    normed_b = (unit_b * two_gain[...] + two_bias[...]).astype(BF16)
    copies[2].wait()
    grad_after, gain, bias = norm_back(
        dot_dims(grad_expanded, expand_w[...], 1, 1), unit_b, rstd_b, two_gain[...]
    )
    add_row(5, gain)
    add_row(6, bias)
    grad_after = grad_after + grad_result
    grad_attn_out = grad_after.astype(BF16)
    add_row(4, column(grad_attn_out))
    grad_attended = dot_dims(grad_attn_out, ov[:, :width], 1, 1).astype(BF16)
    query, key, value = (qkv_ref[:, k * width : (k + 1) * width] for k in range(3))
    tall, weights = mem_weights(query, key)
    grad_tall = per_head(grad_attended)
    grad_weights = dot_dims(grad_tall, value, 1, 1)
    centre = jnp.sum(weights * grad_weights, axis=1, keepdims=True)
    grad_s = (weights * (grad_weights - centre) * HD**-0.5).astype(BF16)
    grad_qkv = jnp.concatenate(
        [
            from_heads(dot_dims(grad_s, key, 1, 0), mem),
            dot_dims(grad_s, tall, 0, 0) + pooled[0][:, :width],
            dot_dims(weights.astype(BF16), grad_tall, 0, 0) + pooled[0][:, width:],
        ],
        axis=1,
    ).astype(BF16)
    add_row(2, column(grad_qkv[:, :width]))
    add_row(3, column(grad_qkv[:, 2 * width :]))
    unit, rstd = norm_parts(mt)
    normed = (unit * one_gain[...] + one_bias[...]).astype(BF16)
    grad_first, gain, bias = norm_back(
        dot_dims(grad_qkv, qrk[:, : 3 * width], 1, 1), unit, rstd, one_gain[...]
    )
    add_row(0, gain)
    add_row(1, bias)
    grad_mt_ref[...] = grad_mt + grad_first + grad_after

    pick_low = lambda a: dot_dims(a, chosen[...], 1, 0).astype(BF16)
    pick_exact = lambda a: exact_low(a, chosen[...], 0)
    qkv_grad[...] = dot_dims(pick_low(normed), grad_qkv, 0, 0)
    qkv_grad[:, width:] += dot_dims(pick_low(normed_f), grad_f, 0, 0)
    out_grad[...] = dot_dims(pick_low(attended_ref[...]), grad_attn_out, 0, 0)
    expand_grad[...] = dot_dims(pick_low(normed_b), grad_expanded, 0, 0)
    contract_grad[...] = dot_dims(pick_low(grad_contract), activ, 0, 0)
    my_result = pick_exact(result_ref[...])
    read_grad[...] = exact(pick_exact(mt), grad_read_pre, 0, 0)
    key_grad[...] = exact(my_result, grad_key_pre, 0, 0)
    value_grad[...] = exact(my_result, grad_value, 0, 0)


def mem_reduce(mt, norms, lines, shard, group, kept, weights, terms, early, gives, small, planes):
    mem, width = mt.shape
    wide, feat = weights[2].shape[1], (weights[0].shape[1] - 3 * width) // 2
    at = lax.broadcasted_iota(jnp.int32, (width, shard), 0) - group * shard
    chosen = (at == lax.broadcasted_iota(jnp.int32, (width, shard), 1)).astype(BF16)
    sizes = (3 * width, width, wide, wide, feat, feat, width)
    shape = jax.ShapeDtypeStruct
    mem_outs = [
        shape((mem, width), F32), *[shape((shard, c), F32) for c in sizes], shape((8, width), F32), shape((1, wide), F32),
    ]
    given = (mt, *norms, chosen, *kept)
    cuts, inputs, in_specs, outs, out_specs, scratch = reducer_call(terms, gives, small)
    vmem = pl.BlockSpec(memory_space=pltpu.VMEM)
    out = pl.pallas_call(
        functools.partial(
            mem_reduce_kernel, planes, cuts, (len(terms), len(gives), len(given) + len(weights), len(mem_outs)), lines
        ),
        in_specs=[*in_specs, *[vmem] * (2 + len(given)), *[pl.BlockSpec(memory_space=pl.ANY)] * len(weights)],
        out_specs=[*out_specs[len(terms) :], *[vmem] * len(mem_outs)],
        out_shape=[*outs[len(terms) :], *mem_outs],
        scratch_shapes=[
            *[pltpu.VMEM(o.shape, F32) for o in outs[: len(terms)]],
            *[pltpu.VMEM(w.shape, w.dtype) for w in weights],
            pltpu.SemaphoreType.DMA((len(weights),)),
            *scratch,
        ],
        compiler_params=pltpu.CompilerParams(
            collective_id=2, has_side_effects=True, vmem_limit_bytes=60 * 2**20
        ),
        cost_estimate=pl.CostEstimate(flops=5 * 10**10, bytes_accessed=30 * 10**6, transcendentals=0),
        name="mem_reduce",
    )(*inputs, *early, *given, *weights)
    swapped, summed, grad_mt, *rest = out
    sums, expand_sums = rest[7:]
    vectors = (sums[0], sums[1], sums[2:4], sums[4], sums[5], sums[6], expand_sums[0], sums[7])
    return swapped, summed, grad_mt, tuple(rest[:7]), vectors


def gather_kernel(halved, count, kinds, *refs):
    shards, rows_ref = refs[:count], refs[count]
    outs, got_rows = refs[count + 1 : 2 * count + 1], refs[2 * count + 1]
    send_sem, recv_sem, local_sem = refs[2 * count + 2 :]
    index, plane = lax.axis_index("dp"), lax.axis_index("ctx")
    deep, cross, core = index // 4, (index // 2) % 2, index % 2
    place = lambda z, x, c: (z * 2 + x) * 2 + c
    up, down = {"dp": place(deep + 1, cross, core)}, {"dp": place(deep - 1, cross, core)}
    beside, sibling = {"dp": place(deep, 1 - cross, core)}, {"dp": place(deep, cross, 1 - core)}
    other = {"ctx": 1 - plane}
    rows = shards[0].shape[0]
    numbers, sends = {}, []

    def valid(kind):
        way, far = kind
        return deep >= 0 if way == "own" else deep >= far if way == "below" else deep + far <= 3

    def level(kind):
        way, far = kind
        return deep if way == "own" else deep - far if way == "below" else deep + far

    def view(k, z, x, c, part):
        at = pl.ds(pl.multiple_of(place(z, x, c) * rows, 16), rows)
        return outs[k].at[at, :] if part is None else outs[k].at[at, half(k, part)]

    def half(k, part):
        wide = outs[k].shape[1] // 2
        return pl.ds(pl.multiple_of(part * wide, 128), wide)

    def copy(key, source, landing, device):
        number = numbers.setdefault(key, len(numbers))
        return pltpu.make_async_remote_copy(
            source, landing, send_sem.at[number], recv_sem.at[number],
            device_id=device, device_id_type=pl.DeviceIdType.MESH,
        )

    def send(when, key, source, landing, device):
        def begin():
            copy(key, source, landing, device).start()

        def end():
            copy(key, source, landing, device).wait_send()

        sends.append((when, end))
        if when is None:
            begin()
        else:
            pl.when(when)(begin)

    def arrived(key, landing):
        copy(key, landing, landing, sibling).wait_recv()

    barrier = pltpu.get_barrier_semaphore()
    for device in (beside, sibling, other):
        pl.semaphore_signal(barrier, inc=1, device_id=device, device_id_type=pl.DeviceIdType.MESH)
    for when, device in ((deep < 3, up), (deep > 0, down)):

        @pl.when(when)
        def _(device=device):
            pl.semaphore_signal(barrier, inc=1, device_id=device, device_id_type=pl.DeviceIdType.MESH)

    inner = (deep > 0) & (deep < 3)
    for when, peers in ((inner, 5), (jnp.logical_not(inner), 4)):

        @pl.when(when)
        def _(peers=peers):
            pl.semaphore_wait(barrier, peers)

    own = ("own", 0)
    rows_key = ("rows",)
    send(None, rows_key, rows_ref.at[1 - plane], got_rows, other)
    locals_ = []
    for k in range(count):
        part = plane if k in halved else None
        mine = view(k, deep, cross, core, None)
        locals_.append(pltpu.make_async_copy(shards[k], mine, local_sem.at[k]))
        locals_[-1].start()
        source = shards[k] if part is None else shards[k].at[:, half(k, part)]
        landing = view(k, deep, cross, core, part)
        send(deep < 3, ("z", ("below", 1), k), source, landing, up)
        send(deep > 0, ("z", ("above", 1), k), source, landing, down)
        send(None, ("x", own, k), source, landing, beside)
        send(None, ("core", "z", own, k), shards[k], mine, sibling)

    def onward(k, flow, kind, x):
        part = plane if k in halved else None
        block = view(k, level(kind), x, core, part)
        ok = valid(kind)
        if flow == "z":
            way, far = kind
            if far < 3:
                if way == "below":
                    send(ok & (deep < 3), ("z", (way, far + 1), k), block, block, up)
                else:
                    send(ok & (deep > 0), ("z", (way, far + 1), k), block, block, down)
            send(ok, ("x", kind, k), block, block, beside)
        send(ok, ("core", flow, kind, k), block, block, sibling)
        if k in halved:
            send(ok, ("y", flow, kind, k), block, block, other)

    def take(flow, kind):
        x = cross if flow == "z" else 1 - cross
        for k in range(count):
            part = plane if k in halved else None

            @pl.when(valid(kind))
            def _():
                arrived((flow, kind, k), view(k, level(kind), x, core, part))

            onward(k, flow, kind, x)

    for far in range(1, 4):
        take("z", ("below", far))
        take("z", ("above", far))
        for kind in kinds:
            if kind[1] == far - 1:
                take("x", kind)
    for kind in kinds:
        if kind[1] == 3:
            take("x", kind)
    crossing = [(flow, kind, k) for flow in ("z", "x") for kind in kinds for k in halved]
    crossing = [c for c in crossing if c[:2] != ("z", own)]
    for flow, kind, k in crossing:
        x = cross if flow == "z" else 1 - cross
        block = lambda c: view(k, level(kind), x, c, 1 - plane)

        @pl.when(valid(kind))
        def _():
            arrived(("y", flow, kind, k), block(core))

        send(valid(kind), ("core", "y", flow, kind, k), block(core), block(core), sibling)
    for flow in ("z", "x"):
        x = cross if flow == "z" else 1 - cross
        for kind in kinds:
            for k in range(count):
                part = plane if k in halved and (flow, kind) != ("z", own) else None

                @pl.when(valid(kind))
                def _():
                    arrived(("core", flow, kind, k), view(k, level(kind), x, 1 - core, part))

    for flow, kind, k in crossing:
        x = cross if flow == "z" else 1 - cross

        @pl.when(valid(kind))
        def _():
            arrived(("core", "y", flow, kind, k), view(k, level(kind), x, 1 - core, 1 - plane))

    arrived(rows_key, got_rows)
    for when, end in sends:
        if when is None:
            end()
        else:
            pl.when(when)(end)
    for held in locals_:
        held.wait()


def gather_weights(shards, halved, tokens):
    kinds = [("own", 0)] + [(way, far) for far in (1, 2, 3) for way in ("below", "above")]
    count = len(shards)
    rows = shards[0].shape[0] * 16
    copies = 6 * count + 7 * count + 13 * len(halved) + 14 * count + 13 * len(halved) + 1
    any_space = pl.BlockSpec(memory_space=pl.ANY)
    return pl.pallas_call(
        functools.partial(gather_kernel, halved, count, kinds),
        in_specs=[any_space] * (count + 1),
        out_specs=[any_space] * (count + 1),
        out_shape=[
            *[jax.ShapeDtypeStruct((rows, s.shape[1]), BF16) for s in shards],
            jax.ShapeDtypeStruct(tokens.shape[1:], BF16),
        ],
        scratch_shapes=[
            pltpu.SemaphoreType.DMA((copies,)),
            pltpu.SemaphoreType.DMA((copies,)),
            pltpu.SemaphoreType.DMA((count,)),
        ],
        compiler_params=pltpu.CompilerParams(
            collective_id=0, has_side_effects=True, vmem_limit_bytes=60 * 2**20
        ),
        cost_estimate=pl.CostEstimate(
            flops=8 * 10**10, bytes_accessed=4 * rows * sum(s.shape[1] for s in shards), transcendentals=0
        ),
        name="gather_weights",
    )(*shards, tokens)


def dp_pairs(flip):
    return [(i, i ^ flip) for i in range(16)]


def behind(value, *earlier):
    return lax.optimization_barrier((value, earlier))[0]


def pick(parts, at, axis):
    return lax.dynamic_index_in_dim(parts, at, axis, keepdims=False)


def add_low(a, b):
    return (a.astype(F32) + b.astype(F32)).astype(BF16)


class Reducer:
    def __init__(self, planes, cuts, grads, gives, small_ref, outs, gots, small_out, scratch):
        self.planes, self.cuts, self.grads, self.gives, self.small_ref = planes, cuts, grads, gives, small_ref
        self.outs, self.gots, self.small_out = outs, gots, small_out
        (
            self.mine, self.got_core, self.got_x, self.line, self.got_z, self.low, self.got_y, self.held, self.total,
            self.load_sem, self.core_sem, self.x_sem, self.z_sem, self.y_sem, self.swap_sem, self.stay_sem, self.sum_sem,
        ) = scratch
        self.index, self.plane = lax.axis_index("dp"), lax.axis_index("ctx")
        deep, cross, core = self.index // 4, lax.rem(self.index // 2, 2), lax.rem(self.index, 2)
        self.deep, self.cross, self.core = deep, cross, core
        self.place = lambda z, x, c: (z * 2 + x) * 2 + c
        self.deeps = (deep + 1 - 2 * lax.rem(deep, 2), lax.rem(deep + 2, 4), 3 - deep)
        self.chunks, self.peers = len(cuts), lax.axis_size("dp") * planes
        self.me = self.index * planes + self.plane

    def remote(self, source, landing, sems, at, device):
        return pltpu.make_async_remote_copy(
            source, landing, sems.at[(0, *at)], sems.at[(1, *at)], device_id=device, device_id_type=pl.DeviceIdType.MESH
        )

    def peer(self, j):
        return (j // self.planes, lax.rem(j, self.planes))

    def small(self, phase, j, sender):
        source, landing = (
            (self.small_ref.at[j], self.held.at[sender]) if phase == 0 else (self.total.at[sender], self.total.at[sender])
        )
        return pltpu.make_async_remote_copy(
            source, landing, self.sum_sem.at[0, phase, j], self.sum_sem.at[1, phase, sender],
            device_id=self.peer(j), device_id_type=pl.DeviceIdType.MESH,
        )

    def every(self, work):
        def body(step, carry):
            work(lax.rem(self.me + step, self.peers))
            return carry

        lax.fori_loop(1, self.peers, body, 0)

    def loop(self, first, last, work):
        def body(c, carry):
            work(c)
            return carry

        lax.fori_loop(first, last, body, 0)

    def to_core(self, c, x):
        k, start, wide = self.cuts[c]
        source = self.grads[k].at[:, x, 1 - self.core, :, pl.ds(start, wide)]
        sibling = {"dp": self.place(self.deep, self.cross, 1 - self.core)}
        return self.remote(source, self.got_core.at[c, x], self.core_sem, (c, x), sibling)

    def to_x(self, c):
        beside = {"dp": self.place(self.deep, 1 - self.cross, self.core)}
        return self.remote(self.mine.at[c, 1 - self.cross], self.got_x.at[c], self.x_sem, (c,), beside)

    def to_z(self, c, k):
        far = {"dp": self.place(self.deeps[k], self.cross, self.core)}
        return self.remote(self.line.at[c, self.deeps[k]], self.got_z.at[c, k], self.z_sem, (c, k), far)

    def to_y(self, c):
        return self.remote(self.low.at[c], self.got_y.at[c], self.y_sem, (c,), {"ctx": 1 - self.plane})

    def swap(self, k):
        source, landing = self.gives[0].at[2 * k + 1 - self.plane], self.gots[0].at[self.plane, k]
        return self.remote(source, landing, self.swap_sem, (k,), {"ctx": 1 - self.plane})

    def stay(self, k):
        source, landing = self.gives[0].at[2 * k + self.plane], self.gots[0].at[self.plane, k]
        return pltpu.make_async_copy(source, landing, self.stay_sem.at[k])

    def arrived(self, landing, sems, at):
        self.remote(landing, landing, sems, at, {"ctx": 1 - self.plane}).wait_recv()

    def begin(self):
        for c, (k, start, wide) in enumerate(self.cuts):
            for x in range(2):
                source = self.grads[k].at[:, x, self.core, :, pl.ds(start, wide)]
                pltpu.make_async_copy(source, self.mine.at[c, x], self.load_sem.at[c, x]).start()
        barrier = pltpu.get_barrier_semaphore()

        def greet(device):
            pl.semaphore_signal(barrier, inc=1, device_id=device, device_id_type=pl.DeviceIdType.MESH)

        if self.small_ref is not None:
            self.every(lambda j: greet(self.peer(j)))
            pl.semaphore_wait(barrier, self.peers - 1)
        else:
            greet({"dp": self.place(self.deep, self.cross, 1 - self.core)})
            greet({"dp": self.place(self.deep, 1 - self.cross, self.core)})
            for far in self.deeps:
                greet({"dp": self.place(far, self.cross, self.core)})
            greet({"ctx": 1 - self.plane})
            pl.semaphore_wait(barrier, 6)
        if self.small_ref is not None:
            self.every(lambda j: self.small(0, j, self.me).start())
            self.held[self.me] = self.small_ref[self.me]
        for c in range(self.chunks):
            for x in range(2):
                self.to_core(c, x).start()

    def begin_swaps(self):
        for k in range(2):
            self.swap(k).start()
            self.stay(k).start()

    def over_core(self, c):
        mine, got = self.mine, self.got_core
        for x in range(2):
            pltpu.make_async_copy(mine.at[c, x], mine.at[c, x], self.load_sem.at[c, x]).wait()
            self.arrived(got.at[c, x], self.core_sem, (c, x))
            for z in range(4):
                mine[c, x, z] = add_low(mine[c, x, z], got[c, x, z])
        self.to_x(c).start()

    def add_small(self):
        self.every(lambda j: self.small(0, j, j).wait_recv())
        self.total[self.me] = jnp.sum(self.held[...], axis=0)
        self.every(lambda j: self.small(1, j, self.me).start())

    def take_small(self):
        self.every(lambda j: self.small(1, j, j).wait_recv())
        self.small_out[...] = self.total[...]

    def over_x(self, c):
        self.arrived(self.got_x.at[c], self.x_sem, (c,))
        for z in range(4):
            self.line[c, z] = add_low(self.mine[c, self.cross, z], self.got_x[c, z])
        for k in range(3):
            self.to_z(c, k).start()

    def over_z(self, c):
        value = self.line[c, self.deep].astype(F32)
        for k in range(3):
            self.arrived(self.got_z.at[c, k], self.z_sem, (c, k))
            value = value + self.got_z[c, k].astype(F32)
        self.low[c] = value.astype(BF16)
        self.to_y(c).start()

    def end(self):
        for c, (k, start, wide) in enumerate(self.cuts):
            self.arrived(self.got_y.at[c], self.y_sem, (c,))
            self.outs[k][:, start : start + wide] = self.low[c].astype(F32) + self.got_y[c].astype(F32)
        for k in range(2):
            self.arrived(self.gots[0].at[1 - self.plane, k], self.swap_sem, (k,))
            self.stay(k).wait()
        if self.small_ref is not None:
            self.every(lambda j: self.small(0, j, self.me).wait_send())
            self.every(lambda j: self.small(1, j, self.me).wait_send())
        for k in range(2):
            self.swap(k).wait_send()
        for c in range(self.chunks):
            for x in range(2):
                self.to_core(c, x).wait_send()

        def finish(c):
            self.to_x(c).wait_send()
            for k in range(3):
                self.to_z(c, k).wait_send()
            self.to_y(c).wait_send()

        self.loop(0, self.chunks, finish)


REDUCER_SCRATCH = 17


def reducer_call(grads, gives, small):
    wide = 768
    shard = grads[0].shape[0] // 16
    cuts = [(k, at, wide) for k, g in enumerate(grads) for at in range(0, g.shape[1], wide)]
    small_arrays = [] if small is None else [small]
    chunks = len(cuts)
    peers, held = (1, (8, 128)) if small is None else (small.shape[0], small.shape)
    vmem, hbm = pl.BlockSpec(memory_space=pltpu.VMEM), pl.BlockSpec(memory_space=pl.ANY)
    shape, dma = jax.ShapeDtypeStruct, pltpu.SemaphoreType.DMA
    low = lambda *dims: pltpu.VMEM((chunks, *dims, shard, wide), BF16)
    inputs = (*[g.reshape(4, 2, 2, shard, g.shape[1]) for g in grads], *gives, *small_arrays)
    in_specs = [hbm] * (len(grads) + len(gives)) + [vmem] * len(small_arrays)
    outs = [shape((shard, g.shape[1]), F32) for g in grads]
    outs += [shape((2, 2, *g.shape[1:]), BF16) for g in gives] + [shape(v.shape, F32) for v in small_arrays]
    out_specs = [vmem] * len(grads) + [hbm] * len(gives) + [vmem] * len(small_arrays)
    scratch = [
        low(2, 4), low(2, 4), low(4), low(4), low(3), low(), low(), pltpu.VMEM(held, F32), pltpu.VMEM(held, F32),
        dma((chunks, 2)), dma((2, chunks, 2)), dma((2, chunks)), dma((2, chunks, 3)), dma((2, chunks)),
        dma((2, 2)), dma((2,)), dma((2, 2, peers)),
    ]
    return cuts, inputs, in_specs, outs, out_specs, scratch


def back_reduce_kernel(planes, cuts, counts, *refs):
    grads, gives = counts
    given, rest = refs[:8], refs[8:]
    ins, rest = rest[: grads + gives], rest[grads + gives :]
    out_refs, rest = rest[:3], rest[3:]
    outs, rest = rest[: grads + gives], rest[grads + gives :]
    own_scratch, scratch = rest[: len(rest) - REDUCER_SCRATCH], rest[len(rest) - REDUCER_SCRATCH :]
    reducer = Reducer(planes, cuts, ins[:grads], ins[grads:], None, outs[:grads], outs[grads:], None, scratch)
    turn, phase = pl.program_id(0), pl.program_id(1)
    chunks = len(cuts)

    @pl.when((turn == 0) & (phase == 0))
    def _():
        reducer.begin()
        reducer.begin_swaps()

    at_core = lambda t: jnp.clip(3 * t, 0, chunks)
    at_x = lambda t: jnp.clip(jnp.maximum(7 * t - 12, 0) // 8, 0, chunks)
    at_z = lambda t: at_x(t - 2)

    @pl.when((turn > 0) & (phase == 0))
    def _():
        reducer.loop(at_core(turn - 1), at_core(turn), reducer.over_core)
        reducer.loop(at_x(turn - 1), at_x(turn), reducer.over_x)
        reducer.loop(at_z(turn - 1), at_z(turn), reducer.over_z)

    attn_bwd_kernel(*given, *out_refs, *own_scratch)

    @pl.when((turn == pl.num_programs(0) - 1) & (phase == 2))
    def _():
        reducer.loop(at_x(turn), chunks, reducer.over_x)
        reducer.loop(at_z(turn), chunks, reducer.over_z)
        reducer.end()


def back_reduce(qkv, kv_mem, attended, grad, lse, terms, gives, planes):
    pairs = H // 2
    segs, rows, width = kv_mem.shape[0], lse.shape[2], qkv.shape[1] // 3
    mem = kv_mem.shape[1]
    wide = 2 * HD
    count = segs * pairs
    cuts, inputs, in_specs, outs, out_specs, scratch = reducer_call(terms, gives, None)
    at = lambda p: jnp.minimum(p, count - 1)
    spec = lambda off: pl.BlockSpec((rows, wide), lambda p, f, off=off: (at(p) // pairs, off * pairs + lax.rem(at(p), pairs)))
    mspec = lambda off: pl.BlockSpec(
        (1, mem, wide), lambda p, f, off=off: (at(p) // pairs, 0, off * pairs + lax.rem(at(p), pairs))
    )
    lspec = pl.BlockSpec((1, 2, rows), lambda p, f: (at(p), 0, 0))

    def place(p, f):
        which = jnp.where((f == 2) & (p < count), p, jnp.maximum(p - 1, 0))
        block = jnp.where(p == count, jnp.minimum(f, 1) + 1, jnp.where((f == 2) | (p == 0), 0, f + 1))
        return (which // pairs, block * pairs + lax.rem(which, pairs))

    out = pl.pallas_call(
        functools.partial(back_reduce_kernel, planes, cuts, (len(terms), len(gives))),
        grid=(count + 1, 3),
        in_specs=[spec(0), spec(1), spec(2), mspec(0), mspec(1), spec(0), lspec, spec(0), *in_specs],
        out_specs=[pl.BlockSpec((rows, wide), place), mspec(0), mspec(0), *out_specs],
        out_shape=[
            jax.ShapeDtypeStruct(qkv.shape, BF16),
            *[jax.ShapeDtypeStruct((segs, mem, width), F32)] * 2,
            *outs,
        ],
        scratch_shapes=[
            pltpu.VMEM((mem + rows, wide), BF16),
            pltpu.VMEM((mem + rows, wide), BF16),
            pltpu.VMEM((wide, rows), BF16),
            pltpu.VMEM((wide, mem), BF16),
            pltpu.VMEM((rows, wide), BF16),
            pltpu.VMEM((mem + rows, wide), F32),
            pltpu.VMEM((mem + rows, wide), F32),
            *scratch,
        ],
        compiler_params=pltpu.CompilerParams(
            collective_id=1, has_side_effects=True, vmem_limit_bytes=60 * 2**20
        ),
        cost_estimate=pl.CostEstimate(
            flops=count * rows * rows * 6500, bytes_accessed=rows * count * wide * 18, transcendentals=0
        ),
        name="back_reduce",
    )(qkv, qkv, qkv, kv_mem, kv_mem, grad, lse, attended, *inputs)
    return out[:3], out[3 : 3 + len(terms)], out[3 + len(terms) :]


def mem_reduce_kernel(planes, cuts, counts, lines, *refs):
    grads, gives, given, made = counts
    ins, rest = refs[: grads + gives + 1], refs[grads + gives + 1 :]
    early, rest = rest[:2], rest[2:]
    mem_ins, rest = rest[:given], rest[given:]
    outs, rest = rest[: gives + 1], rest[gives + 1 :]
    mem_outs, rest = rest[:made], rest[made:]
    sums, rest = rest[:grads], rest[grads:]
    mem_scratch, scratch = rest[: len(rest) - REDUCER_SCRATCH], rest[len(rest) - REDUCER_SCRATCH :]
    reducer = Reducer(planes, cuts, ins[:grads], ins[grads:-1], ins[-1], sums, outs[:-1], outs[-1], scratch)
    chunks = len(cuts)
    reducer.begin()
    reducer.add_small()
    reducer.loop(0, chunks, reducer.over_core)
    reducer.take_small()
    reducer.begin_swaps()
    total = outs[-1]
    mem = mem_ins[0].shape[0]
    pooled = [
        jnp.concatenate([total[k * mem : (k + 1) * mem, r, :] for r in range(lines)], axis=1) for k in range(2)
    ]
    mem_bwd_kernel(*mem_ins[:5], pooled, *mem_ins[5:], *mem_outs, *mem_scratch)
    reducer.over_x(0)

    def both(c):
        reducer.over_x(c)
        reducer.over_z(c - 1)

    reducer.loop(1, chunks, both)
    reducer.over_z(chunks - 1)
    reducer.end()
    for made_here, summed in zip(mem_outs[1:5], (*sums, *early)):
        made_here[...] += summed[...]


def split_heads(rows):
    return rows.reshape(rows.shape[0], rows.shape[1], H, HD)


def plain_scores(query, key, allowed):
    scores = jnp.einsum("sqhd,skhd->shqk", query, key, preferred_element_type=F32) * HD**-0.5
    return scores, allowed[None, None]


def plain_fwd(qkv, kv_all, allowed):
    width = qkv.shape[2] // 3
    query = split_heads(qkv[:, :, :width])
    key, value = split_heads(kv_all[:, :, :width]), split_heads(kv_all[:, :, width:])
    scores, allowed = plain_scores(query, key, allowed)
    raw = jnp.where(allowed, jnp.exp(scores), 0.0)
    total = jnp.sum(raw, axis=-1)
    weights = (raw / total[..., None]).astype(BF16)
    mixed = jnp.einsum("shqk,skhd->sqhd", weights, value, preferred_element_type=F32)
    return mixed.reshape(qkv.shape[0], -1, width).astype(BF16), jnp.log(total)


def plain_bwd(qkv, kv_all, allowed, log_total, grad):
    segs, width = qkv.shape[0], qkv.shape[2] // 3
    query = split_heads(qkv[:, :, :width])
    key, value = split_heads(kv_all[:, :, :width]), split_heads(kv_all[:, :, width:])
    grad = split_heads(grad)
    scores, allowed = plain_scores(query, key, allowed)
    prob = jnp.where(allowed, jnp.exp(scores - log_total[..., None]), 0.0)
    grad_p = jnp.einsum("sqhd,skhd->shqk", grad, value, preferred_element_type=F32)
    inner = jnp.sum(prob * grad_p, axis=-1, keepdims=True)
    grad_s = (prob * (grad_p - inner) * HD**-0.5).astype(BF16)
    dq = jnp.einsum("shqk,skhd->sqhd", grad_s, key, preferred_element_type=F32)
    dk = jnp.einsum("shqk,sqhd->skhd", grad_s, query, preferred_element_type=F32)
    dv = jnp.einsum("shqk,sqhd->skhd", prob.astype(BF16), grad, preferred_element_type=F32)
    flat = lambda a: a.reshape(segs, -1, width)
    return flat(dq), jnp.concatenate([flat(dk), flat(dv)], axis=2)


def memory_forward(mt, p):
    mem = mt.shape[0]
    keep = {}
    width = mt.shape[1]
    unit, rstd = norm_parts(mt)
    normed = (unit * p["one_gain"] + p["one_bias"]).astype(BF16)
    qkv = (dot_dims(normed, p["qkv"], 1, 0) + p["shift"]).astype(BF16)
    at = jnp.arange(mem, dtype=jnp.int32)
    allowed = at[None, :] <= at[:, None]
    attended, log_total = plain_fwd(qkv[None], qkv[None, :, width:], allowed)
    attended = attended[0]
    after = mt + dot_dims(attended, p["out"], 1, 0) + p["out_bias"]
    unit_b, rstd_b = norm_parts(after)
    normed_b = (unit_b * p["two_gain"] + p["two_bias"]).astype(BF16)
    expanded = dot_dims(normed_b, p["expand"], 1, 0) + p["expand_bias"]
    activ = gelu_tanh(expanded).astype(BF16)
    result = after + dot_dims(activ, p["contract"], 1, 1) + p["contract_bias"]
    key_pre = exact(result, p["key"].astype(F32), 1, 0)
    value_new = exact(result, p["value"].astype(F32), 1, 0)
    read_pre = exact(mt, p["read"].astype(F32), 1, 0)
    key_feat, key_pull = jax.vjp(feature_map, key_pre)
    read_feat, read_pull = jax.vjp(feature_map, read_pre)
    mix = exact(read_feat, key_feat, 1, 1)
    numer = exact(mix, value_new, 1, 0)
    denom = 1.0 + jnp.sum(mix, axis=1, keepdims=True)
    follow = mt + numer / denom
    unit_f, rstd_f = norm_parts(follow)
    normed_f = (unit_f * p["one_gain"] + p["one_bias"]).astype(BF16)
    kv_follow = (dot_dims(normed_f, p["qkv"][:, width:], 1, 0) + p["shift"][width:]).astype(BF16)
    keep = dict(
        unit=unit, rstd=rstd, normed=normed, qkv=qkv, allowed=allowed, attended=attended,
        log_total=log_total, unit_b=unit_b, rstd_b=rstd_b, normed_b=normed_b, expanded=expanded,
        activ=activ, result=result, key_feat=key_feat, read_feat=read_feat, key_pull=key_pull,
        read_pull=read_pull, value_new=value_new, mix=mix, numer=numer, denom=denom, unit_f=unit_f,
        rstd_f=rstd_f, normed_f=normed_f,
    )
    return qkv[:, width:], kv_follow, keep


def memory_backward(mt, p, m, grad_kv_first, grad_kv_follow, mine):
    width = mt.shape[1]
    low = lambda a: a.astype(BF16)
    grad_f = low(grad_kv_follow)
    grad_follow, gain_f, bias_f = norm_back(
        dot_dims(grad_f, p["qkv"][:, width:], 1, 1), m["unit_f"], m["rstd_f"], p["one_gain"]
    )
    grad_mt = grad_follow
    grad_numer = grad_follow / m["denom"]
    grad_denom = -jnp.sum(grad_follow * m["numer"], axis=1, keepdims=True) / (m["denom"] * m["denom"])
    grad_mix = exact(grad_numer, m["value_new"], 1, 1) + grad_denom
    grad_value = exact(m["mix"], grad_numer, 0, 0)
    [grad_read_pre] = m["read_pull"](exact(grad_mix, m["key_feat"], 1, 0))
    [grad_key_pre] = m["key_pull"](exact(grad_mix, m["read_feat"], 0, 0))
    grad_mt = grad_mt + exact(grad_read_pre, p["read"].astype(F32), 1, 1)
    grad_result = exact(grad_key_pre, p["key"].astype(F32), 1, 1) + exact(
        grad_value, p["value"].astype(F32), 1, 1
    )
    grad_contract = low(grad_result)
    _, gelu_pull = jax.vjp(gelu_tanh, m["expanded"])
    grad_expanded = low(gelu_pull(dot_dims(grad_contract, p["contract"], 1, 0))[0])
    grad_after, two_gain, two_bias = norm_back(
        dot_dims(grad_expanded, p["expand"], 1, 1), m["unit_b"], m["rstd_b"], p["two_gain"]
    )
    grad_after = grad_after + grad_result
    grad_attn_out = low(grad_after)
    grad_attended = low(dot_dims(grad_attn_out, p["out"], 1, 1))
    dq, dkv = plain_bwd(
        m["qkv"][None], m["qkv"][None, :, width:], m["allowed"], m["log_total"], grad_attended[None]
    )
    grad_qkv = low(jnp.concatenate([dq[0], dkv[0] + grad_kv_first], axis=1))
    grad_first, gain_a, bias_a = norm_back(
        dot_dims(grad_qkv, p["qkv"], 1, 1), m["unit"], m["rstd"], p["one_gain"]
    )
    grad_mt = grad_mt + grad_first + grad_after
    wide = grad_qkv.astype(F32)
    kv_rows = grad_f.astype(F32)
    sums = jnp.sum(wide, axis=0)
    follow_sums = jnp.sum(kv_rows, axis=0)
    matrices = (
        dot_dims(mine(m["normed"]), grad_qkv, 0, 0)
        + jnp.concatenate(
            [
                jnp.zeros((mine(mt).shape[1], width), F32),
                dot_dims(mine(m["normed_f"]), grad_f, 0, 0),
            ],
            axis=1,
        ),
        dot_dims(mine(m["attended"]), grad_attn_out, 0, 0),
        dot_dims(mine(m["normed_b"]), grad_expanded, 0, 0),
        dot_dims(mine(grad_contract), m["activ"], 0, 0),
        exact(mine(mt), grad_read_pre, 0, 0),
        exact(mine(m["result"]), grad_key_pre, 0, 0),
        exact(mine(m["result"]), grad_value, 0, 0),
    )
    column_sum = lambda a: jnp.sum(a.astype(F32), axis=0)
    vectors = (
        gain_f + gain_a,
        bias_f + bias_a,
        jnp.stack([sums[:width], sums[2 * width :] + follow_sums[width:]]),
        column_sum(grad_attn_out),
        two_gain,
        two_bias,
        column_sum(grad_expanded),
        column_sum(grad_contract),
    )
    return grad_mt, matrices, vectors


def local(
    tokens,
    cotangent,
    placing,
    starts,
    memory_tokens,
    norm_one_gain,
    norm_one_bias,
    qkv_weight,
    qv_bias,
    out_weight,
    out_bias,
    norm_two_gain,
    norm_two_bias,
    expand_weight,
    expand_bias,
    contract_weight,
    contract_bias,
    read_weight,
    key_weight,
    value_weight,
):
    del placing
    groups, ranks = lax.axis_size("dp"), lax.axis_size("ctx")
    group, rank = lax.axis_index("dp"), lax.axis_index("ctx")
    micros, segs_local, tok_rows, width = tokens.shape
    mem = memory_tokens.shape[0]
    shard = qkv_weight.shape[0]
    quick = groups == 16 and ranks == 2 and micros == 2 and segs_local == 2 and (tok_rows * ranks) % WIDE == 0
    names = ("qkv", "out", "expand", "contract", "read", "key", "value")
    shards = (qkv_weight, out_weight, expand_weight, contract_weight, read_weight, key_weight, value_weight)
    if quick:
        joined = (
            jnp.concatenate([qkv_weight, read_weight, key_weight], axis=1),
            expand_weight,
            contract_weight,
            jnp.concatenate([out_weight, value_weight], axis=1),
        )
        qkv_read_key, expand_full, contract_full, out_value, got_tokens = gather_weights(
            joined, (2, 3), tokens
        )
        feat = read_weight.shape[1]
        whole = (
            qkv_read_key[:, : 3 * width],
            out_value[:, :width],
            expand_full,
            contract_full,
            qkv_read_key[:, 3 * width : 3 * width + feat],
            qkv_read_key[:, 3 * width + feat :],
            out_value[:, width:],
        )
    else:
        whole = tuple(lax.all_gather(s, "dp", axis=0, tiled=True) for s in shards)
    p = dict(zip(names, whole))
    p.update(
        one_gain=norm_one_gain, one_bias=norm_one_bias, out_bias=out_bias, two_gain=norm_two_gain,
        two_bias=norm_two_bias, expand_bias=expand_bias, contract_bias=contract_bias,
        shift=jnp.concatenate([qv_bias[0], jnp.zeros((width,), F32), qv_bias[1]]),
    )
    flags = lax.dynamic_slice_in_dim(starts, group * segs_local, segs_local, 1)

    swap = [(0, 1), (1, 0)]

    def swapped(given):
        return lax.ppermute(given, "ctx", swap)

    if quick:
        told = rank.astype(jnp.int32)[None]
        give_grad = pick(behind(cotangent, expand_full), 1 - rank, 0)
        flags = pick(flags, rank, 0)
        segs = segs_local
        seg_rows = ranks * tok_rows
    else:
        rows_in, rows_grad = tokens.reshape(-1, width), cotangent.reshape(-1, width)
        flags = flags.reshape(-1)
        segs = micros * segs_local
        seg_rows = tok_rows

    if quick:
        norms = tuple(v[None] for v in (norm_one_gain, norm_one_bias, norm_two_gain, norm_two_bias))
        fixed = tuple(v[None] for v in (p["shift"], out_bias, expand_bias, contract_bias))
        mem_weights_in = (qkv_read_key, out_value, expand_full, contract_full)
        *kept, kv_follow = mem_forward(memory_tokens, (*norms, *fixed), mem_weights_in)
        kv_first = kept[0][:, width:]
    else:
        kv_first, kv_follow, m = memory_forward(memory_tokens, p)
    kv_mem = jnp.where((flags == 0)[:, None, None], kv_follow[None], kv_first[None])
    if quick:
        rows_in, normed_a, qkv = enter(
            told, tokens, got_tokens, norm_one_gain, norm_one_bias, qkv_read_key, p["shift"]
        )
        attended, lse_first = attn_fwd(behind(qkv, give_grad), kv_mem[0], 0, seg_rows, None)
        got_grad = swapped(give_grad)
        attended, lse_second = attn_fwd(qkv, kv_mem[1], 1, seg_rows, attended)
        attended, got_grad = lax.optimization_barrier((attended, got_grad))
        (
            result, rows_grad, normed_b, activ, grad_expanded, grad_attn_out, grad_attended, mid_sums, expand_sums,
        ) = middle(
            told, cotangent, got_grad, rows_in, attended, p["out"], p["expand"], p["contract"], out_bias,
            norm_two_gain, norm_two_bias, expand_bias, contract_bias,
        )
        grad_after = grad_attn_out
    else:
        hidden = rows_in.astype(F32)
        unit_a, rstd_a = norm_parts(hidden)
        normed_a = (unit_a * norm_one_gain + norm_one_bias).astype(BF16)
        qkv = (dot_dims(normed_a, p["qkv"], 1, 0) + p["shift"]).astype(BF16)
        seg_qkv = qkv.reshape(segs, seg_rows, 3 * width)
        kv_all = lax.all_gather(seg_qkv[:, :, width:], "ctx", axis=1, tiled=True)
        kv_all = jnp.concatenate([kv_mem, kv_all], axis=1)
        query_at = mem + rank * seg_rows + jnp.arange(seg_rows, dtype=jnp.int32)
        key_at = jnp.arange(mem + ranks * seg_rows, dtype=jnp.int32)
        allowed = key_at[None, :] <= query_at[:, None]
        attended, lse = plain_fwd(seg_qkv, kv_all, allowed)
        attended = attended.reshape(-1, width)
        after = hidden + dot_dims(attended, p["out"], 1, 0) + out_bias
        unit_b, rstd_b = norm_parts(after)
        normed_b = (unit_b * norm_two_gain + norm_two_bias).astype(BF16)
        expanded = dot_dims(normed_b, p["expand"], 1, 0) + expand_bias
        activ = gelu_tanh(expanded).astype(BF16)
        result = (after + dot_dims(activ, p["contract"], 1, 1) + contract_bias).astype(BF16)

    def input_back(at, grads, weights):
        grad = dot_dims(grads[0], weights[0], 1, 1)
        for g, w in zip(grads[1:], weights[1:]):
            grad = grad + dot_dims(g, w, 1, 1)
        unit, rstd = norm_parts(rows_in[at].astype(F32))
        grad_hidden, gain, bias = norm_back(grad, unit, rstd, norm_one_gain)
        return (grad_hidden + grad_after[at].astype(F32)).astype(BF16), gain, bias

    def pool(dkv_mem):
        follows = (flags == 0).astype(F32)[:, None, None]
        kinds = [jnp.sum(dkv_mem * (1.0 - follows), axis=0), jnp.sum(dkv_mem * follows, axis=0)]
        return jnp.stack(kinds)

    if quick:
        lse = jnp.concatenate([lse_first, lse_second], axis=0)
        by_half = lambda r: r.reshape(segs * ranks, tok_rows, width)
        peers = groups * ranks
        wide_terms = (
            dot_dims(rows_grad, activ, 0, 0).astype(BF16),
            dot_dims(normed_b, grad_expanded, 0, 0).astype(BF16),
        )
        (grad_qkv, dk_mem, dv_mem), wide_sums, [block_out] = back_reduce(
            qkv, kv_mem, attended, grad_attended, lse, wide_terms, [by_half(result)], ranks
        )
        pooled = pool(jnp.concatenate([dk_mem, dv_mem], axis=2))
        grad_rows, end_sums, qkv_sums = leave(grad_qkv, qkv_read_key, rows_in, grad_after, norm_one_gain, tok_rows)
        one_gain, one_bias = end_sums[0], end_sums[1]
        qkv_sums = qkv_sums.reshape(3, width)
        late_terms = (
            dot_dims(normed_a, grad_qkv, 0, 0).astype(BF16),
            dot_dims(attended, grad_attn_out, 0, 0).astype(BF16),
        )
    else:
        _, gelu_pull = jax.vjp(gelu_tanh, expanded)
        grad_expanded = gelu_pull(dot_dims(rows_grad, p["contract"], 1, 0))[0].astype(BF16)
        grad_after, two_gain, two_bias = norm_back(
            dot_dims(grad_expanded, p["expand"], 1, 1), unit_b, rstd_b, norm_two_gain
        )
        grad_after = grad_after + rows_grad.astype(F32)
        grad_attn_out = grad_after.astype(BF16)
        grad_attended = dot_dims(grad_attn_out, p["out"], 1, 1).astype(BF16)
        dq, dkv = plain_bwd(
            seg_qkv, kv_all, allowed, lse, grad_attended.reshape(segs, seg_rows, width)
        )
        pooled = pool(dkv[:, :mem])
        dkv = lax.psum_scatter(
            dkv[:, mem:].astype(BF16), "ctx", scatter_dimension=1, tiled=True
        )
        grad_qkv = jnp.concatenate([dq.astype(BF16), dkv], axis=2).reshape(-1, 3 * width)
        grad_rows, one_gain, one_bias = input_back(slice(None), [grad_qkv], [p["qkv"]])
        terms = (
            dot_dims(normed_a, grad_qkv, 0, 0).astype(BF16),
            dot_dims(attended, grad_attn_out, 0, 0).astype(BF16),
            dot_dims(normed_b, grad_expanded, 0, 0).astype(BF16),
            dot_dims(rows_grad, activ, 0, 0).astype(BF16),
        )
        qkv_sums = jnp.sum(grad_qkv.astype(F32), axis=0).reshape(3, width)
    column_sum = lambda a: jnp.sum(a.astype(F32), axis=0)
    if quick:
        mid = (mid_sums[0], mid_sums[1], mid_sums[2], expand_sums[0], mid_sums[3])
    else:
        mid = (
            column_sum(grad_attn_out), two_gain, two_bias, column_sum(grad_expanded), column_sum(rows_grad),
        )
    vectors = (one_gain, one_bias, jnp.stack([qkv_sums[0], qkv_sums[2]]), *mid)
    if not quick:
        summed = tuple(
            lax.psum(
                lax.psum_scatter(t, "dp", scatter_dimension=0, tiled=True).astype(F32), "ctx"
            )
            for t in terms
        )
        pooled, vectors = lax.psum((pooled, vectors), ("dp", "ctx"))

    if quick:
        flat = jnp.concatenate([v.reshape(-1) for v in vectors])
        lines = pl.cdiv(flat.size, peers * 128)
        flat = jnp.pad(flat, (0, peers * lines * 128 - flat.size)).reshape(peers, lines, 128)
        pooled = pooled.reshape(peers, -1, 128)
        token_grad, small, grad_mt, mem_matrices, mem_vectors = mem_reduce(
            memory_tokens, norms, pooled.shape[1], shard, group, kept, mem_weights_in, late_terms,
            (wide_sums[1], wide_sums[0]), [by_half(grad_rows)], jnp.concatenate([pooled, flat], axis=1), ranks,
        )
        flat = small[:, pooled.shape[1] :]
        flat = flat.reshape(-1)
    else:
        mine = lambda a: lax.dynamic_slice_in_dim(a, group * shard, shard, 1)
        grad_mt, mem_matrices, mem_vectors = memory_backward(
            memory_tokens, p, m, pooled[0], pooled[1], mine
        )
    if quick:
        split, place = [], 0
        for v in vectors:
            split.append(flat[place : place + v.size].reshape(v.shape))
            place += v.size
        vectors = tuple(split)
    if quick:
        matrices = mem_matrices
    else:
        matrices = tuple(a + b for a, b in zip(summed, mem_matrices)) + mem_matrices[4:]
    vectors = tuple(a + b for a, b in zip(vectors, mem_vectors))
    if not quick:
        block_out, token_grad = result.reshape(tokens.shape), grad_rows.reshape(tokens.shape)
    return (
        block_out,
        token_grad,
        grad_mt,
        vectors[0],
        vectors[1],
        matrices[0],
        vectors[2],
        matrices[1],
        vectors[3],
        vectors[4],
        vectors[5],
        matrices[2],
        vectors[6],
        matrices[3],
        vectors[7],
        matrices[4],
        matrices[5],
        matrices[6],
    )


def solution(mesh):
    rows = P(None, "dp", "ctx", None)
    matrix = P("dp", None)
    full = P()
    return jax.shard_map(
        local,
        mesh=mesh,
        in_specs=(
            rows, rows, full, full, full, full, full, matrix, full, matrix, full, full, full,
            matrix, full, matrix, full, matrix, matrix, matrix,
        ),
        out_specs=(
            rows, rows, full, full, full, matrix, full, matrix, full, full, full, matrix, full,
            matrix, full, matrix, matrix, matrix,
        ),
        check_vma=False,
    )
```

```python
import functools

import jax
import jax.numpy as jnp
from jax import lax
from jax.experimental import pallas as pl
from jax.experimental.pallas import tpu as pltpu
from jax.sharding import PartitionSpec as P

H = 12
HD = 64
EPS = 1e-05
CHUNK = 256
WIDE = 512
F32 = jnp.float32
BF16 = jnp.bfloat16


def norm_parts(rows):
    centred = rows - jnp.mean(rows, axis=-1, keepdims=True)
    spread = jnp.mean(centred * centred, axis=-1, keepdims=True)
    rstd = lax.rsqrt(spread + EPS)
    return centred * rstd, rstd


def norm_back(grad, unit, rstd, gain):
    scaled = grad * gain
    first = jnp.mean(scaled, axis=-1, keepdims=True)
    second = jnp.mean(scaled * unit, axis=-1, keepdims=True)
    grad_rows = rstd * (scaled - first - unit * second)
    return grad_rows, jnp.sum(grad * unit, axis=0), jnp.sum(grad, axis=0)


def feature_map(rows):
    halves = jnp.concatenate([jax.nn.softplus(rows), jax.nn.softplus(-rows)], axis=-1)
    return jnp.concatenate([halves * jnp.roll(halves, j, axis=-1) for j in (1, 2, 3)], axis=-1)


def gelu_tanh(rows):
    return jax.nn.gelu(rows, approximate=True)


def dot_dims(a, b, ca, cb, precision=None):
    return lax.dot_general(
        a, b, (((ca,), (cb,)), ((), ())), precision=precision, preferred_element_type=F32
    )


exact = functools.partial(dot_dims, precision=lax.Precision.HIGHEST)


def head_rows(scale):
    lane = lax.broadcasted_iota(jnp.int32, (1, 2 * HD), 1)
    low = jnp.where(lane < HD, scale, 0.0).astype(BF16)
    high = jnp.where(lane < HD, 0.0, scale).astype(BF16)
    return low, high


def causal_tail(scores):
    key = lax.broadcasted_iota(jnp.int32, scores.shape, 0)
    return jnp.where(key <= lax.broadcasted_iota(jnp.int32, scores.shape, 1), scores, 0.0)


def attn_fwd_kernel(q_ref, k_ref, v_ref, km_ref, vm_ref, o_ref, lse_ref, keys, vals_t, vmem_t):
    mem = km_ref.shape[0]
    keys[0:mem, :] = km_ref[...]
    keys[mem:, :] = k_ref[...]
    vals_t[...] = v_ref[...].T
    vmem_t[...] = vm_ref[...].T
    picks = head_rows(HD**-0.5)
    steps = [(part, head) for part in range(q_ref.shape[0] // WIDE) for head in range(2)]

    def begin(part, head):
        lo, hi = part * WIDE, (part + 1) * WIDE
        return dot_dims(keys[0 : mem + hi, :], q_ref[lo:hi, :] * picks[head], 1, 1)

    ahead = begin(*steps[0])
    outs = []
    for n, (part, head) in enumerate(steps):
        lo, hi = part * WIDE, (part + 1) * WIDE
        band = slice(head * HD, (head + 1) * HD)
        raw = jnp.exp(ahead)
        if n + 1 < len(steps):
            ahead = begin(*steps[n + 1])
        raw = jnp.concatenate([raw[: mem + lo], causal_tail(raw[mem + lo :])], axis=0)
        total = jnp.sum(raw, axis=0, keepdims=True)
        lse_ref[0, head : head + 1, lo:hi] = jnp.log(total)
        weights = (raw * (1.0 / total)).astype(BF16)
        outs.append(
            dot_dims(vals_t[band, 0:hi], weights[mem:], 1, 0)
            + dot_dims(vmem_t[band, :], weights[:mem], 1, 0)
        )
        if head == 1:
            o_ref[lo:hi, :] = jnp.concatenate(outs, axis=0).T.astype(BF16)
            outs = []


def attn_fwd_after_kernel(q_ref, k_ref, v_ref, km_ref, vm_ref, held_ref, *rest):
    del held_ref
    attn_fwd_kernel(q_ref, k_ref, v_ref, km_ref, vm_ref, *rest)


def attn_fwd(qkv, kv_mem, seg, rows, held):
    width = qkv.shape[1] // 3
    mem = kv_mem.shape[0]
    pairs = H // 2
    wide = 2 * HD
    spec = lambda off: pl.BlockSpec((rows, wide), lambda p, off=off: (seg, off * pairs + p))
    mspec = lambda off: pl.BlockSpec((mem, wide), lambda p, off=off: (0, off * pairs + p))
    more = [] if held is None else [held]
    return pl.pallas_call(
        attn_fwd_kernel if held is None else attn_fwd_after_kernel,
        grid=(pairs,),
        in_specs=[spec(0), spec(1), spec(2), mspec(0), mspec(1)]
        + [pl.BlockSpec(memory_space=pl.ANY)] * len(more),
        out_specs=[
            pl.BlockSpec((rows, wide), lambda p: (seg, p)),
            pl.BlockSpec((1, 2, rows), lambda p: (p, 0, 0)),
        ],
        out_shape=[
            jax.ShapeDtypeStruct((qkv.shape[0], width), BF16),
            jax.ShapeDtypeStruct((pairs, 2, rows), F32),
        ],
        scratch_shapes=[
            pltpu.VMEM((mem + rows, wide), BF16),
            pltpu.VMEM((wide, rows), BF16),
            pltpu.VMEM((wide, mem), BF16),
        ],
        input_output_aliases={5: 0} if more else {},
        compiler_params=pltpu.CompilerParams(vmem_limit_bytes=60 * 2**20),
        cost_estimate=pl.CostEstimate(
            flops=pairs * rows * rows * 4000,
            bytes_accessed=rows * width * 8,
            transcendentals=0,
        ),
        name="attn_fwd",
    )(qkv, qkv, qkv, kv_mem, kv_mem, *more)


def attn_bwd_kernel(
    q_ref, k_ref, v_ref, km_ref, vm_ref, g_ref, lse_ref, o_ref,
    out_ref, dkm_ref, dvm_ref,
    keys, vals, keys_t, kmem_t, dq, dk, dv,
):
    phase = pl.program_id(1)
    mem = km_ref.shape[1]
    rows = q_ref.shape[0]

    @pl.when((phase == 2) & (pl.program_id(0) < pl.num_programs(0) - 1))
    def _():
        keys[0:mem, :] = km_ref[0]
        keys[mem:, :] = k_ref[...]
        vals[0:mem, :] = vm_ref[0]
        vals[mem:, :] = v_ref[...]
        keys_t[...] = k_ref[...].T
        kmem_t[...] = km_ref[0].T
        dk[...] = jnp.zeros_like(dk)
        dv[...] = jnp.zeros_like(dv)
        scaled_picks = head_rows(HD**-0.5)
        picks = head_rows(1.0)
        for part in range(rows // CHUNK):
            lo, hi = part * CHUNK, (part + 1) * CHUNK
            end = mem + hi
            query = q_ref[lo:hi, :]
            grad = g_ref[lo:hi, :]
            inner = (grad.astype(F32) * o_ref[lo:hi, :].astype(F32)).T
            dqs = []
            for head in range(2):
                band = slice(head * HD, (head + 1) * HD)
                query_h = query * scaled_picks[head]
                grad_h = grad * picks[head]
                log_total = lse_ref[0, head : head + 1, lo:hi]
                centre = jnp.sum(inner[band], axis=0, keepdims=True)
                prob = jnp.exp(dot_dims(keys[0:end, :], query_h, 1, 1) - log_total)
                prob = jnp.concatenate(
                    [prob[: mem + lo], causal_tail(prob[mem + lo :])], axis=0
                )
                grad_p = dot_dims(vals[0:end, :], grad_h, 1, 1)
                grad_s = (prob * (grad_p - centre)).astype(BF16)
                dv[0:end, :] += dot_dims(prob.astype(BF16), grad_h, 1, 0)
                dk[0:end, :] += dot_dims(grad_s, query_h, 1, 0)
                dqs.append(
                    dot_dims(keys_t[band, 0:hi], grad_s[mem:], 1, 0)
                    + dot_dims(kmem_t[band, :], grad_s[:mem], 1, 0)
                )
            dq[lo:hi, :] = (jnp.concatenate(dqs, axis=0) * HD**-0.5).T.astype(BF16)
        out_ref[...] = dq[...]
        dkm_ref[0] = dk[0:mem, :]
        dvm_ref[0] = dv[0:mem, :]

    @pl.when((phase == 0) & (pl.program_id(0) > 0))
    def _():
        out_ref[...] = dk[mem:, :].astype(BF16)

    @pl.when((phase == 1) & (pl.program_id(0) > 0))
    def _():
        out_ref[...] = dv[mem:, :].astype(BF16)


def choose(told, kept, got, out):
    own = pl.program_id(0) % 2 == told[0]

    @pl.when(own)
    def _():
        out[...] = kept[0, 0]

    @pl.when(jnp.logical_not(own))
    def _():
        out[...] = got[0]


def half_specs(rows, width):
    return [
        pl.BlockSpec((1, 1, rows, width), lambda i, told: (told[0], i // 2, 0, 0)),
        pl.BlockSpec((1, rows, width), lambda i, told: (i // 2, 0, 0)),
    ]


def enter_kernel(told, kept, got, gain, bias, weight, shift, rows_ref, normed_ref, qkv_ref):
    choose(told, kept, got, rows_ref)
    unit, _ = norm_parts(rows_ref[...].astype(F32))
    normed = (unit * gain[...] + bias[...]).astype(BF16)
    normed_ref[...] = normed
    wide = weight.shape[1] // 3
    for k in range(3):
        at = slice(k * wide, (k + 1) * wide)
        qkv_ref[:, at] = (dot_dims(normed, weight[:, at], 1, 0) + shift[:, at]).astype(BF16)


def enter(told, kept, got, gain, bias, weight, shift):
    _, segs, rows, width = kept.shape
    whole = lambda r, c: pl.BlockSpec((r, c), lambda i, told: (0, 0), pipeline_mode=pl.Buffered(1))
    block = lambda c: pl.BlockSpec((rows, c), lambda i, told: (i, 0))
    sizes = (width, width, 3 * width)
    return pl.pallas_call(
        enter_kernel,
        grid_spec=pltpu.PrefetchScalarGridSpec(
            num_scalar_prefetch=1,
            grid=(2 * segs,),
            in_specs=[*half_specs(rows, width), whole(1, width), whole(1, width), whole(width, 3 * width), whole(1, 3 * width)],
            out_specs=[block(c) for c in sizes],
        ),
        out_shape=[jax.ShapeDtypeStruct((2 * segs * rows, c), BF16) for c in sizes],
        compiler_params=pltpu.CompilerParams(vmem_limit_bytes=60 * 2**20),
        cost_estimate=pl.CostEstimate(
            flops=8 * segs * rows * width * width * 3, bytes_accessed=segs * rows * width * 28, transcendentals=0
        ),
        name="enter",
    )(told, kept, got, gain[None], bias[None], weight, shift[None])


def middle_kernel(
    told, kept, got, rows_ref, attended, out_w, expand_w, contract_w, out_b, gain, bias, expand_b, contract_b,
    result_ref, cot_ref, normed_ref, activ_ref, grad_exp_ref, grad_out_ref, grad_att_ref,
    sums_ref, exp_sums_ref,
):
    choose(told, kept, got, cot_ref)
    cot = cot_ref[...]
    after = rows_ref[...].astype(F32) + dot_dims(attended[...], out_w[...], 1, 0) + out_b[...]
    unit, rstd = norm_parts(after)
    normed = (unit * gain[...] + bias[...]).astype(BF16)
    normed_ref[...] = normed
    total = after + contract_b[...]
    back = 0.0

    @pl.when(pl.program_id(0) == 0)
    def _():
        sums_ref[...] = jnp.zeros_like(sums_ref)
        exp_sums_ref[...] = jnp.zeros_like(exp_sums_ref)

    parts = 4
    wide = expand_w.shape[1] // parts
    bend, cube = 0.7978845608028654, 0.044715
    for part in range(parts):
        at = slice(part * wide, (part + 1) * wide)
        value = dot_dims(normed, expand_w[:, at], 1, 0) + expand_b[:, at]
        square = value * value
        half = 0.5 + 0.5 * jnp.tanh(value * (bend + bend * cube * square))
        activ = (value * half).astype(BF16)
        activ_ref[:, at] = activ
        slope = half + (half - half * half) * (value * (2.0 * bend + 6.0 * bend * cube * square))
        grad = (dot_dims(cot, contract_w[:, at], 1, 0) * slope).astype(BF16)
        grad_exp_ref[:, at] = grad
        exp_sums_ref[:, at] += jnp.sum(grad.astype(F32), axis=0, keepdims=True)
        total = total + dot_dims(activ, contract_w[:, at], 1, 1)
        back = back + dot_dims(grad, expand_w[:, at], 1, 1)
    result_ref[...] = total.astype(BF16)
    wide_cot = cot.astype(F32)
    grad_rows, gain_sum, bias_sum = norm_back(back, unit, rstd, gain[...])
    grad_out = (grad_rows + wide_cot).astype(BF16)
    grad_out_ref[...] = grad_out
    grad_att_ref[...] = dot_dims(grad_out, out_w[...], 1, 1).astype(BF16)
    sums = (
        jnp.sum(grad_out.astype(F32), axis=0, keepdims=True),
        gain_sum[None],
        bias_sum[None],
        jnp.sum(wide_cot, axis=0, keepdims=True),
    )
    for k, value in enumerate(sums):
        sums_ref[k : k + 1, :] += value


def middle(told, kept, got, rows_in, attended, out_w, expand_w, contract_w, out_b, gain, bias, expand_b, contract_b):
    _, segs, rows, width = kept.shape
    wide = expand_w.shape[1]
    whole = lambda r, c: pl.BlockSpec((r, c), lambda i, told: (0, 0), pipeline_mode=pl.Buffered(1))
    block = lambda c: pl.BlockSpec((rows, c), lambda i, told: (i, 0))
    sizes = (width, width, width, wide, wide, width, width)
    count = 2 * segs * rows
    fixed = lambda r, c: pl.BlockSpec((r, c), lambda i, told: (0, 0))
    return pl.pallas_call(
        middle_kernel,
        grid_spec=pltpu.PrefetchScalarGridSpec(
            num_scalar_prefetch=1,
            grid=(2 * segs,),
            in_specs=[
                *half_specs(rows, width), block(width), block(width), whole(width, width), whole(width, wide),
                whole(width, wide), whole(1, width), whole(1, width), whole(1, width), whole(1, wide), whole(1, width),
            ],
            out_specs=[*[block(c) for c in sizes], fixed(8, width), fixed(1, wide)],
        ),
        out_shape=[
            *[jax.ShapeDtypeStruct((count, c), BF16) for c in sizes],
            jax.ShapeDtypeStruct((8, width), F32),
            jax.ShapeDtypeStruct((1, wide), F32),
        ],
        compiler_params=pltpu.CompilerParams(vmem_limit_bytes=60 * 2**20),
        cost_estimate=pl.CostEstimate(
            flops=count * width * (8 * wide + 4 * width) * 2, bytes_accessed=count * (14 * width + 4 * wide), transcendentals=0
        ),
        name="middle",
    )(
        told, kept, got, rows_in, attended, out_w, expand_w, contract_w, out_b[None], gain[None], bias[None],
        expand_b[None], contract_b[None],
    )


def leave_kernel(grad_ref, weight, rows_ref, after_ref, gain, rows_out, sums_ref, col_ref):
    @pl.when(pl.program_id(0) == 0)
    def _():
        sums_ref[...] = jnp.zeros_like(sums_ref)
        col_ref[...] = jnp.zeros_like(col_ref)

    grad = grad_ref[...]
    unit, rstd = norm_parts(rows_ref[...].astype(F32))
    grad_rows, gain_sum, bias_sum = norm_back(dot_dims(grad, weight[...], 1, 1), unit, rstd, gain[...])
    rows_out[...] = (grad_rows + after_ref[...].astype(F32)).astype(BF16)
    sums_ref[0:1, :] += gain_sum[None]
    sums_ref[1:2, :] += bias_sum[None]
    col_ref[...] += jnp.sum(grad.astype(F32), axis=0, keepdims=True)


def leave(grad_qkv, weight, rows_in, grad_after, gain, rows):
    count, width = rows_in.shape
    block = lambda c: pl.BlockSpec((rows, c), lambda i: (i, 0))
    fixed = lambda r, c: pl.BlockSpec((r, c), lambda i: (0, 0))
    whole = lambda r, c: pl.BlockSpec((r, c), lambda i: (0, 0), pipeline_mode=pl.Buffered(1))
    return pl.pallas_call(
        leave_kernel,
        grid=(count // rows,),
        in_specs=[block(3 * width), whole(width, 3 * width), block(width), block(width), whole(1, width)],
        out_specs=[block(width), fixed(8, width), fixed(1, 3 * width)],
        out_shape=[
            jax.ShapeDtypeStruct((count, width), BF16),
            jax.ShapeDtypeStruct((8, width), F32),
            jax.ShapeDtypeStruct((1, 3 * width), F32),
        ],
        compiler_params=pltpu.CompilerParams(vmem_limit_bytes=60 * 2**20),
        cost_estimate=pl.CostEstimate(
            flops=6 * count * width * width, bytes_accessed=count * width * 12, transcendentals=0
        ),
        name="leave",
    )(grad_qkv, weight, rows_in, grad_after, gain[None])


def thirds(rows):
    parts = []
    for _ in range(3):
        parts.append(rows.astype(BF16))
        rows = rows - parts[-1].astype(F32)
    return jnp.concatenate(parts, axis=0)


def exact_low(rows, weight, side):
    count = rows.shape[0]
    out = dot_dims(thirds(rows), weight, 1, side)
    return out[:count] + out[count : 2 * count] + out[2 * count :]


def softplus(rows):
    return jnp.maximum(rows, 0.0) + jnp.log1p(jnp.exp(-jnp.abs(rows)))


def feature_parts(rows):
    halves = jnp.concatenate([softplus(rows), softplus(-rows)], axis=1)
    turned = [pltpu.roll(halves, j, 1) for j in (1, 2, 3)]
    return halves, turned, jnp.concatenate([halves * t for t in turned], axis=1)


def feature_back(rows, grad):
    halves, turned, _ = feature_parts(rows)
    wide = halves.shape[1]
    total = 0.0
    for j in (1, 2, 3):
        part = grad[:, (j - 1) * wide : j * wide]
        total = total + part * turned[j - 1] + pltpu.roll(part * halves, wide - j, 1)
    first, last = total[:, : wide // 2], total[:, wide // 2 :]
    return first * jax.nn.sigmoid(rows) - last * jax.nn.sigmoid(-rows)


def per_head(rows):
    tall = jnp.concatenate([rows] * H, axis=0)
    return tall * head_mask(tall.shape, rows.shape[0]).astype(rows.dtype)


def head_mask(shape, count):
    head = lax.broadcasted_iota(jnp.int32, shape, 0) // count
    return (lax.broadcasted_iota(jnp.int32, shape, 1) // HD == head).astype(F32)


def from_heads(tall, count):
    tall = tall * head_mask(tall.shape, count)
    total = tall[:count]
    for head in range(1, H):
        total = total + tall[head * count : (head + 1) * count]
    return total


def mem_weights(query, key):
    count = key.shape[0]
    tall = per_head(query)
    scores = dot_dims(tall, key, 1, 1) * HD**-0.5
    at = lax.rem(lax.broadcasted_iota(jnp.int32, scores.shape, 0), count)
    raw = jnp.where(lax.broadcasted_iota(jnp.int32, scores.shape, 1) <= at, jnp.exp(scores), 0.0)
    return tall, raw / jnp.sum(raw, axis=1, keepdims=True)


def read_parts(read_feat, key_feat, value_new):
    mix = exact(read_feat, key_feat, 1, 1)
    return mix, exact(mix, value_new, 1, 0), 1.0 + jnp.sum(mix, axis=1, keepdims=True)


def bring(sources, targets, sem):
    copies = [pltpu.make_async_copy(a, b, sem.at[k]) for k, (a, b) in enumerate(zip(sources, targets))]
    for copy in copies:
        copy.start()
    return copies


def mem_fwd_kernel(
    mt_ref, one_gain, one_bias, two_gain, two_bias, shift, out_b, expand_b, contract_b,
    qrk_hbm, ov_hbm, expand_hbm, contract_hbm,
    qkv_ref, attended_ref, after_ref, expanded_ref, result_ref, pre_ref, value_ref, follow_ref, kv_ref,
    qrk, ov, expand_w, contract_w, sem,
):
    copies = bring((qrk_hbm, ov_hbm, expand_hbm, contract_hbm), (qrk, ov, expand_w, contract_w), sem)
    mt = mt_ref[...]
    width = mt.shape[1]
    feat = pre_ref.shape[1] // 2
    unit, _ = norm_parts(mt)
    normed = (unit * one_gain[...] + one_bias[...]).astype(BF16)
    copies[0].wait()
    qkv = (dot_dims(normed, qrk[:, : 3 * width], 1, 0) + shift[...]).astype(BF16)
    qkv_ref[...] = qkv
    read_pre = exact_low(mt, qrk[:, 3 * width : 3 * width + feat], 0)
    _, weights = mem_weights(qkv[:, :width], qkv[:, width : 2 * width])
    mixed = dot_dims(weights.astype(BF16), qkv[:, 2 * width :], 1, 0)
    attended = from_heads(mixed, mt.shape[0]).astype(BF16)
    attended_ref[...] = attended
    copies[1].wait()
    after = mt + dot_dims(attended, ov[:, :width], 1, 0) + out_b[...]
    after_ref[...] = after
    unit, _ = norm_parts(after)
    normed = (unit * two_gain[...] + two_bias[...]).astype(BF16)
    copies[2].wait()
    expanded = dot_dims(normed, expand_w[...], 1, 0) + expand_b[...]
    expanded_ref[...] = expanded
    activ = gelu_tanh(expanded).astype(BF16)
    copies[3].wait()
    result = after + dot_dims(activ, contract_w[...], 1, 1) + contract_b[...]
    result_ref[...] = result
    key_pre = exact_low(result, qrk[:, 3 * width + feat :], 0)
    value_new = exact_low(result, ov[:, width:], 0)
    value_ref[...] = value_new
    pre_ref[:, :feat] = read_pre
    pre_ref[:, feat:] = key_pre
    _, numer, denom = read_parts(feature_parts(read_pre)[2], feature_parts(key_pre)[2], value_new)
    follow = mt + numer / denom
    follow_ref[...] = follow
    unit, _ = norm_parts(follow)
    normed = (unit * one_gain[...] + one_bias[...]).astype(BF16)
    kv_ref[...] = (dot_dims(normed, qrk[:, width : 3 * width], 1, 0) + shift[:, width:]).astype(BF16)


def mem_call(kernel, name, given, weights, outs, cycles):
    vmem = pl.BlockSpec(memory_space=pltpu.VMEM)
    return pl.pallas_call(
        kernel,
        in_specs=[vmem] * len(given) + [pl.BlockSpec(memory_space=pl.ANY)] * len(weights),
        out_specs=[vmem] * len(outs),
        out_shape=outs,
        scratch_shapes=[
            *[pltpu.VMEM(w.shape, w.dtype) for w in weights],
            pltpu.SemaphoreType.DMA((len(weights),)),
        ],
        compiler_params=pltpu.CompilerParams(vmem_limit_bytes=60 * 2**20),
        cost_estimate=pl.CostEstimate(flops=cycles * 10**9, bytes_accessed=17 * 10**6, transcendentals=0),
        name=name,
    )(*given, *weights)


def mem_forward(mt, given, weights):
    mem, width = mt.shape
    wide, feat = weights[2].shape[1], (weights[0].shape[1] - 3 * width) // 2
    shape = jax.ShapeDtypeStruct
    outs = [
        shape((mem, 3 * width), BF16), shape((mem, width), BF16), shape((mem, width), F32), shape((mem, wide), F32),
        shape((mem, width), F32), shape((mem, 2 * feat), F32), shape((mem, width), F32), shape((mem, width), F32),
        shape((mem, 2 * width), BF16),
    ]
    return mem_call(mem_fwd_kernel, "mem_fwd", (mt, *given), weights, outs, 15)


def mem_bwd_kernel(
    mt_ref, one_gain, one_bias, two_gain, two_bias, pooled, chosen,
    qkv_ref, attended_ref, after_ref, expanded_ref, result_ref, pre_ref, value_ref, follow_ref,
    qrk_hbm, ov_hbm, expand_hbm, contract_hbm,
    grad_mt_ref, qkv_grad, out_grad, expand_grad, contract_grad, read_grad, key_grad, value_grad, sums_ref, exp_sums_ref,
    qrk, ov, expand_w, contract_w, copies,
):
    del qrk_hbm, ov_hbm, expand_hbm, contract_hbm
    mt = mt_ref[...]
    mem, width = mt.shape
    feat = pre_ref.shape[1] // 2
    sums_ref[...] = jnp.zeros_like(sums_ref)

    def add_row(k, value):
        sums_ref[k : k + 1, :] += value[None]

    def column(value):
        return jnp.sum(value.astype(F32), axis=0)

    unit_f, rstd_f = norm_parts(follow_ref[...])
    normed_f = (unit_f * one_gain[...] + one_bias[...]).astype(BF16)
    grad_f = pooled[1].astype(BF16)
    copies[0].wait()
    grad_follow, gain, bias = norm_back(
        dot_dims(grad_f, qrk[:, width : 3 * width], 1, 1), unit_f, rstd_f, one_gain[...]
    )
    add_row(0, gain)
    add_row(1, bias)
    add_row(3, column(grad_f[:, width:]))
    read_pre, key_pre, value_new = pre_ref[:, :feat], pre_ref[:, feat:], value_ref[...]
    read_feat, key_feat = feature_parts(read_pre)[2], feature_parts(key_pre)[2]
    mix, numer, denom = read_parts(read_feat, key_feat, value_new)
    grad_numer = grad_follow / denom
    grad_denom = -jnp.sum(grad_follow * numer, axis=1, keepdims=True) / (denom * denom)
    grad_mix = exact(grad_numer, value_new, 1, 1) + grad_denom
    grad_value = exact(mix, grad_numer, 0, 0)
    grad_read_pre = feature_back(read_pre, exact(grad_mix, key_feat, 1, 0))
    grad_key_pre = feature_back(key_pre, exact(grad_mix, read_feat, 0, 0))
    grad_mt = grad_follow + exact_low(grad_read_pre, qrk[:, 3 * width : 3 * width + feat], 1)
    copies[1].wait()
    grad_result = exact_low(grad_key_pre, qrk[:, 3 * width + feat :], 1) + exact_low(
        grad_value, ov[:, width:], 1
    )
    grad_contract = grad_result.astype(BF16)
    add_row(7, column(grad_contract))
    expanded = expanded_ref[...]
    bend, cube = 0.7978845608028654, 0.044715
    square = expanded * expanded
    curve = jnp.tanh(bend * expanded * (1.0 + cube * square))
    half = 0.5 * (1.0 + curve)
    activ = (expanded * half).astype(BF16)
    slope = half + 0.5 * bend * expanded * (1.0 - curve * curve) * (1.0 + 3.0 * cube * square)
    copies[3].wait()
    grad_expanded = (dot_dims(grad_contract, contract_w[...], 1, 0) * slope).astype(BF16)
    exp_sums_ref[...] = column(grad_expanded)[None]
    unit_b, rstd_b = norm_parts(after_ref[...])
    normed_b = (unit_b * two_gain[...] + two_bias[...]).astype(BF16)
    copies[2].wait()
    grad_after, gain, bias = norm_back(
        dot_dims(grad_expanded, expand_w[...], 1, 1), unit_b, rstd_b, two_gain[...]
    )
    add_row(5, gain)
    add_row(6, bias)
    grad_after = grad_after + grad_result
    grad_attn_out = grad_after.astype(BF16)
    add_row(4, column(grad_attn_out))
    grad_attended = dot_dims(grad_attn_out, ov[:, :width], 1, 1).astype(BF16)
    query, key, value = (qkv_ref[:, k * width : (k + 1) * width] for k in range(3))
    tall, weights = mem_weights(query, key)
    grad_tall = per_head(grad_attended)
    grad_weights = dot_dims(grad_tall, value, 1, 1)
    centre = jnp.sum(weights * grad_weights, axis=1, keepdims=True)
    grad_s = (weights * (grad_weights - centre) * HD**-0.5).astype(BF16)
    grad_qkv = jnp.concatenate(
        [
            from_heads(dot_dims(grad_s, key, 1, 0), mem),
            dot_dims(grad_s, tall, 0, 0) + pooled[0][:, :width],
            dot_dims(weights.astype(BF16), grad_tall, 0, 0) + pooled[0][:, width:],
        ],
        axis=1,
    ).astype(BF16)
    add_row(2, column(grad_qkv[:, :width]))
    add_row(3, column(grad_qkv[:, 2 * width :]))
    unit, rstd = norm_parts(mt)
    normed = (unit * one_gain[...] + one_bias[...]).astype(BF16)
    grad_first, gain, bias = norm_back(
        dot_dims(grad_qkv, qrk[:, : 3 * width], 1, 1), unit, rstd, one_gain[...]
    )
    add_row(0, gain)
    add_row(1, bias)
    grad_mt_ref[...] = grad_mt + grad_first + grad_after

    pick_low = lambda a: dot_dims(a, chosen[...], 1, 0).astype(BF16)
    pick_exact = lambda a: exact_low(a, chosen[...], 0)
    qkv_grad[...] = dot_dims(pick_low(normed), grad_qkv, 0, 0)
    qkv_grad[:, width:] += dot_dims(pick_low(normed_f), grad_f, 0, 0)
    out_grad[...] = dot_dims(pick_low(attended_ref[...]), grad_attn_out, 0, 0)
    expand_grad[...] = dot_dims(pick_low(normed_b), grad_expanded, 0, 0)
    contract_grad[...] = dot_dims(pick_low(grad_contract), activ, 0, 0)
    my_result = pick_exact(result_ref[...])
    read_grad[...] = exact(pick_exact(mt), grad_read_pre, 0, 0)
    key_grad[...] = exact(my_result, grad_key_pre, 0, 0)
    value_grad[...] = exact(my_result, grad_value, 0, 0)


def mem_reduce(mt, norms, lines, shard, group, kept, weights, terms, spans, early, gives, small, planes):
    mem, width = mt.shape
    wide, feat = weights[2].shape[1], (weights[0].shape[1] - 3 * width) // 2
    at = lax.broadcasted_iota(jnp.int32, (width, shard), 0) - group * shard
    chosen = (at == lax.broadcasted_iota(jnp.int32, (width, shard), 1)).astype(BF16)
    sizes = (3 * width, width, wide, wide, feat, feat, width)
    shape = jax.ShapeDtypeStruct
    mem_outs = [
        shape((mem, width), F32), *[shape((shard, c), F32) for c in sizes], shape((8, width), F32), shape((1, wide), F32),
    ]
    given = (mt, *norms, chosen, *kept)
    cuts, inputs, in_specs, outs, out_specs, scratch = reducer_call(terms, gives, small, spans)
    vmem = pl.BlockSpec(memory_space=pltpu.VMEM)
    out = pl.pallas_call(
        functools.partial(
            mem_reduce_kernel, planes, cuts, (len(terms), len(gives), len(given) + len(weights), len(mem_outs)), lines, spans
        ),
        in_specs=[*in_specs, *[vmem] * (2 + len(given)), *[pl.BlockSpec(memory_space=pl.ANY)] * len(weights)],
        out_specs=[*out_specs[len(terms) :], *[vmem] * len(mem_outs)],
        out_shape=[*outs[len(terms) :], *mem_outs],
        scratch_shapes=[
            *[pltpu.VMEM(o.shape, F32) for o in outs[: len(terms)]],
            *[pltpu.VMEM(w.shape, w.dtype) for w in weights],
            pltpu.SemaphoreType.DMA((len(weights),)),
            *scratch,
        ],
        compiler_params=pltpu.CompilerParams(
            collective_id=2, has_side_effects=True, vmem_limit_bytes=60 * 2**20
        ),
        cost_estimate=pl.CostEstimate(flops=5 * 10**10, bytes_accessed=30 * 10**6, transcendentals=0),
        name="mem_reduce",
    )(*inputs, *early, *given, *weights)
    swapped, summed, grad_mt, *rest = out
    sums, expand_sums = rest[7:]
    vectors = (sums[0], sums[1], sums[2:4], sums[4], sums[5], sums[6], expand_sums[0], sums[7])
    return swapped, summed, grad_mt, tuple(rest[:7]), vectors


def gather_kernel(halved, count, kinds, *refs):
    shards, rows_ref = refs[:count], refs[count]
    outs, got_rows = refs[count + 1 : 2 * count + 1], refs[2 * count + 1]
    send_sem, recv_sem, local_sem = refs[2 * count + 2 :]
    index, plane = lax.axis_index("dp"), lax.axis_index("ctx")
    deep, cross, core = index // 4, (index // 2) % 2, index % 2
    place = lambda z, x, c: (z * 2 + x) * 2 + c
    up, down = {"dp": place(deep + 1, cross, core)}, {"dp": place(deep - 1, cross, core)}
    beside, sibling = {"dp": place(deep, 1 - cross, core)}, {"dp": place(deep, cross, 1 - core)}
    other = {"ctx": 1 - plane}
    rows = shards[0].shape[0]
    numbers, sends = {}, []

    def valid(kind):
        way, far = kind
        return deep >= 0 if way == "own" else deep >= far if way == "below" else deep + far <= 3

    def level(kind):
        way, far = kind
        return deep if way == "own" else deep - far if way == "below" else deep + far

    def view(k, z, x, c, part):
        at = pl.ds(pl.multiple_of(place(z, x, c) * rows, 16), rows)
        return outs[k].at[at, :] if part is None else outs[k].at[at, half(k, part)]

    def half(k, part):
        wide = outs[k].shape[1] // 2
        return pl.ds(pl.multiple_of(part * wide, 128), wide)

    def copy(key, source, landing, device):
        number = numbers.setdefault(key, len(numbers))
        return pltpu.make_async_remote_copy(
            source, landing, send_sem.at[number], recv_sem.at[number],
            device_id=device, device_id_type=pl.DeviceIdType.MESH,
        )

    def send(when, key, source, landing, device):
        def begin():
            copy(key, source, landing, device).start()

        def end():
            copy(key, source, landing, device).wait_send()

        sends.append((when, end))
        if when is None:
            begin()
        else:
            pl.when(when)(begin)

    def arrived(key, landing):
        copy(key, landing, landing, sibling).wait_recv()

    barrier = pltpu.get_barrier_semaphore()
    for device in (beside, sibling, other):
        pl.semaphore_signal(barrier, inc=1, device_id=device, device_id_type=pl.DeviceIdType.MESH)
    for when, device in ((deep < 3, up), (deep > 0, down)):

        @pl.when(when)
        def _(device=device):
            pl.semaphore_signal(barrier, inc=1, device_id=device, device_id_type=pl.DeviceIdType.MESH)

    inner = (deep > 0) & (deep < 3)
    for when, peers in ((inner, 5), (jnp.logical_not(inner), 4)):

        @pl.when(when)
        def _(peers=peers):
            pl.semaphore_wait(barrier, peers)

    own = ("own", 0)
    rows_key = ("rows",)
    send(None, rows_key, rows_ref.at[1 - plane], got_rows, other)
    locals_ = []
    for k in range(count):
        part = plane if k in halved else None
        mine = view(k, deep, cross, core, None)
        locals_.append(pltpu.make_async_copy(shards[k], mine, local_sem.at[k]))
        locals_[-1].start()
        source = shards[k] if part is None else shards[k].at[:, half(k, part)]
        landing = view(k, deep, cross, core, part)
        send(deep < 3, ("z", ("below", 1), k), source, landing, up)
        send(deep > 0, ("z", ("above", 1), k), source, landing, down)
        send(None, ("x", own, k), source, landing, beside)
        send(None, ("core", "z", own, k), shards[k], mine, sibling)

    def onward(k, flow, kind, x):
        part = plane if k in halved else None
        block = view(k, level(kind), x, core, part)
        ok = valid(kind)
        if flow == "z":
            way, far = kind
            if far < 3:
                if way == "below":
                    send(ok & (deep < 3), ("z", (way, far + 1), k), block, block, up)
                else:
                    send(ok & (deep > 0), ("z", (way, far + 1), k), block, block, down)
            send(ok, ("x", kind, k), block, block, beside)
        send(ok, ("core", flow, kind, k), block, block, sibling)
        if k in halved:
            send(ok, ("y", flow, kind, k), block, block, other)

    def take(flow, kind):
        x = cross if flow == "z" else 1 - cross
        for k in range(count):
            part = plane if k in halved else None

            @pl.when(valid(kind))
            def _():
                arrived((flow, kind, k), view(k, level(kind), x, core, part))

            onward(k, flow, kind, x)

    for far in range(1, 4):
        take("z", ("below", far))
        take("z", ("above", far))
        for kind in kinds:
            if kind[1] == far - 1:
                take("x", kind)
    for kind in kinds:
        if kind[1] == 3:
            take("x", kind)
    crossing = [(flow, kind, k) for flow in ("z", "x") for kind in kinds for k in halved]
    crossing = [c for c in crossing if c[:2] != ("z", own)]
    for flow, kind, k in crossing:
        x = cross if flow == "z" else 1 - cross
        block = lambda c: view(k, level(kind), x, c, 1 - plane)

        @pl.when(valid(kind))
        def _():
            arrived(("y", flow, kind, k), block(core))

        send(valid(kind), ("core", "y", flow, kind, k), block(core), block(core), sibling)
    for flow in ("z", "x"):
        x = cross if flow == "z" else 1 - cross
        for kind in kinds:
            for k in range(count):
                part = plane if k in halved and (flow, kind) != ("z", own) else None

                @pl.when(valid(kind))
                def _():
                    arrived(("core", flow, kind, k), view(k, level(kind), x, 1 - core, part))

    for flow, kind, k in crossing:
        x = cross if flow == "z" else 1 - cross

        @pl.when(valid(kind))
        def _():
            arrived(("core", "y", flow, kind, k), view(k, level(kind), x, 1 - core, 1 - plane))

    arrived(rows_key, got_rows)
    for when, end in sends:
        if when is None:
            end()
        else:
            pl.when(when)(end)
    for held in locals_:
        held.wait()


def gather_weights(shards, halved, tokens):
    kinds = [("own", 0)] + [(way, far) for far in (1, 2, 3) for way in ("below", "above")]
    count = len(shards)
    rows = shards[0].shape[0] * 16
    copies = 6 * count + 7 * count + 13 * len(halved) + 14 * count + 13 * len(halved) + 1
    any_space = pl.BlockSpec(memory_space=pl.ANY)
    return pl.pallas_call(
        functools.partial(gather_kernel, halved, count, kinds),
        in_specs=[any_space] * (count + 1),
        out_specs=[any_space] * (count + 1),
        out_shape=[
            *[jax.ShapeDtypeStruct((rows, s.shape[1]), BF16) for s in shards],
            jax.ShapeDtypeStruct(tokens.shape[1:], BF16),
        ],
        scratch_shapes=[
            pltpu.SemaphoreType.DMA((copies,)),
            pltpu.SemaphoreType.DMA((copies,)),
            pltpu.SemaphoreType.DMA((count,)),
        ],
        compiler_params=pltpu.CompilerParams(
            collective_id=0, has_side_effects=True, vmem_limit_bytes=60 * 2**20
        ),
        cost_estimate=pl.CostEstimate(
            flops=8 * 10**10, bytes_accessed=4 * rows * sum(s.shape[1] for s in shards), transcendentals=0
        ),
        name="gather_weights",
    )(*shards, tokens)


def dp_pairs(flip):
    return [(i, i ^ flip) for i in range(16)]


def behind(value, *earlier):
    return lax.optimization_barrier((value, earlier))[0]


def pick(parts, at, axis):
    return lax.dynamic_index_in_dim(parts, at, axis, keepdims=False)


def add_low(a, b):
    return (a.astype(F32) + b.astype(F32)).astype(BF16)


class Reducer:
    def __init__(self, planes, cuts, grads, gives, small_ref, outs, gots, small_out, scratch):
        self.planes, self.cuts, self.grads, self.gives, self.small_ref = planes, cuts, grads, gives, small_ref
        self.outs, self.gots, self.small_out = outs, gots, small_out
        (
            self.mine, self.got_core, self.got_x, self.line, self.got_z, self.low, self.got_y, self.held, self.total,
            self.load_sem, self.core_sem, self.x_sem, self.z_sem, self.y_sem, self.swap_sem, self.stay_sem, self.sum_sem,
        ) = scratch
        self.index, self.plane = lax.axis_index("dp"), lax.axis_index("ctx")
        deep, cross, core = self.index // 4, lax.rem(self.index // 2, 2), lax.rem(self.index, 2)
        self.deep, self.cross, self.core = deep, cross, core
        self.place = lambda z, x, c: (z * 2 + x) * 2 + c
        self.deeps = (deep + 1 - 2 * lax.rem(deep, 2), lax.rem(deep + 2, 4), 3 - deep)
        self.chunks, self.peers = len(cuts), lax.axis_size("dp") * planes
        self.me = self.index * planes + self.plane

    def remote(self, source, landing, sems, at, device):
        return pltpu.make_async_remote_copy(
            source, landing, sems.at[(0, *at)], sems.at[(1, *at)], device_id=device, device_id_type=pl.DeviceIdType.MESH
        )

    def peer(self, j):
        return (j // self.planes, lax.rem(j, self.planes))

    def small(self, phase, j, sender):
        source, landing = (
            (self.small_ref.at[j], self.held.at[sender]) if phase == 0 else (self.total.at[sender], self.total.at[sender])
        )
        return pltpu.make_async_remote_copy(
            source, landing, self.sum_sem.at[0, phase, j], self.sum_sem.at[1, phase, sender],
            device_id=self.peer(j), device_id_type=pl.DeviceIdType.MESH,
        )

    def every(self, work):
        def body(step, carry):
            work(lax.rem(self.me + step, self.peers))
            return carry

        lax.fori_loop(1, self.peers, body, 0)

    def loop(self, first, last, work):
        def body(c, carry):
            work(c)
            return carry

        lax.fori_loop(first, last, body, 0)

    def to_core(self, c, x):
        k, start, wide = self.cuts[c]
        source = self.grads[k].at[:, x, 1 - self.core, :, pl.ds(start, wide)]
        sibling = {"dp": self.place(self.deep, self.cross, 1 - self.core)}
        return self.remote(source, self.got_core.at[c, x], self.core_sem, (c, x), sibling)

    def to_x(self, c):
        beside = {"dp": self.place(self.deep, 1 - self.cross, self.core)}
        return self.remote(self.mine.at[c, 1 - self.cross], self.got_x.at[c], self.x_sem, (c,), beside)

    def to_z(self, c, k):
        far = {"dp": self.place(self.deeps[k], self.cross, self.core)}
        return self.remote(self.line.at[c, self.deeps[k]], self.got_z.at[c, k], self.z_sem, (c, k), far)

    def to_y(self, c):
        return self.remote(self.low.at[c], self.got_y.at[c], self.y_sem, (c,), {"ctx": 1 - self.plane})

    def swap(self, k):
        source, landing = self.gives[0].at[2 * k + 1 - self.plane], self.gots[0].at[self.plane, k]
        return self.remote(source, landing, self.swap_sem, (k,), {"ctx": 1 - self.plane})

    def stay(self, k):
        source, landing = self.gives[0].at[2 * k + self.plane], self.gots[0].at[self.plane, k]
        return pltpu.make_async_copy(source, landing, self.stay_sem.at[k])

    def arrived(self, landing, sems, at):
        self.remote(landing, landing, sems, at, {"ctx": 1 - self.plane}).wait_recv()

    def begin(self):
        for c, (k, start, wide) in enumerate(self.cuts):
            for x in range(2):
                source = self.grads[k].at[:, x, self.core, :, pl.ds(start, wide)]
                pltpu.make_async_copy(source, self.mine.at[c, x], self.load_sem.at[c, x]).start()
        barrier = pltpu.get_barrier_semaphore()

        def greet(device):
            pl.semaphore_signal(barrier, inc=1, device_id=device, device_id_type=pl.DeviceIdType.MESH)

        if self.small_ref is not None:
            self.every(lambda j: greet(self.peer(j)))
            pl.semaphore_wait(barrier, self.peers - 1)
        else:
            greet({"dp": self.place(self.deep, self.cross, 1 - self.core)})
            greet({"dp": self.place(self.deep, 1 - self.cross, self.core)})
            for far in self.deeps:
                greet({"dp": self.place(far, self.cross, self.core)})
            greet({"ctx": 1 - self.plane})
            pl.semaphore_wait(barrier, 6)
        if self.small_ref is not None:
            self.every(lambda j: self.small(0, j, self.me).start())
            self.held[self.me] = self.small_ref[self.me]
        for c in range(self.chunks):
            for x in range(2):
                self.to_core(c, x).start()

    def begin_swaps(self):
        for k in range(2):
            self.swap(k).start()
            self.stay(k).start()

    def over_core(self, c):
        mine, got = self.mine, self.got_core
        for x in range(2):
            pltpu.make_async_copy(mine.at[c, x], mine.at[c, x], self.load_sem.at[c, x]).wait()
            self.arrived(got.at[c, x], self.core_sem, (c, x))
            for z in range(4):
                mine[c, x, z] = add_low(mine[c, x, z], got[c, x, z])
        self.to_x(c).start()

    def add_small(self):
        self.every(lambda j: self.small(0, j, j).wait_recv())
        self.total[self.me] = jnp.sum(self.held[...], axis=0)
        self.every(lambda j: self.small(1, j, self.me).start())

    def take_small(self):
        self.every(lambda j: self.small(1, j, j).wait_recv())
        self.small_out[...] = self.total[...]

    def over_x(self, c):
        self.arrived(self.got_x.at[c], self.x_sem, (c,))
        for z in range(4):
            self.line[c, z] = add_low(self.mine[c, self.cross, z], self.got_x[c, z])
        for k in range(3):
            self.to_z(c, k).start()

    def over_z(self, c):
        value = self.line[c, self.deep].astype(F32)
        for k in range(3):
            self.arrived(self.got_z.at[c, k], self.z_sem, (c, k))
            value = value + self.got_z[c, k].astype(F32)
        self.low[c] = value.astype(BF16)
        self.to_y(c).start()

    def end(self):
        for c, (k, start, wide) in enumerate(self.cuts):
            self.arrived(self.got_y.at[c], self.y_sem, (c,))
            self.outs[k][:, start : start + wide] = self.low[c].astype(F32) + self.got_y[c].astype(F32)
        for k in range(2):
            self.arrived(self.gots[0].at[1 - self.plane, k], self.swap_sem, (k,))
            self.stay(k).wait()
        if self.small_ref is not None:
            self.every(lambda j: self.small(0, j, self.me).wait_send())
            self.every(lambda j: self.small(1, j, self.me).wait_send())
        for k in range(2):
            self.swap(k).wait_send()
        for c in range(self.chunks):
            for x in range(2):
                self.to_core(c, x).wait_send()

        def finish(c):
            self.to_x(c).wait_send()
            for k in range(3):
                self.to_z(c, k).wait_send()
            self.to_y(c).wait_send()

        self.loop(0, self.chunks, finish)


REDUCER_SCRATCH = 17


def reducer_call(grads, gives, small, spans):
    wide = 384
    shard = grads[0].shape[0] // 16
    cuts = [(k, at, wide) for k, (first, last) in enumerate(spans) for at in range(first, last, wide)]
    small_arrays = [] if small is None else [small]
    chunks = len(cuts)
    peers, held = (1, (8, 128)) if small is None else (small.shape[0], small.shape)
    vmem, hbm = pl.BlockSpec(memory_space=pltpu.VMEM), pl.BlockSpec(memory_space=pl.ANY)
    shape, dma = jax.ShapeDtypeStruct, pltpu.SemaphoreType.DMA
    low = lambda *dims: pltpu.VMEM((chunks, *dims, shard, wide), BF16)
    inputs = (*[g.reshape(4, 2, 2, shard, g.shape[1]) for g in grads], *gives, *small_arrays)
    in_specs = [hbm] * (len(grads) + len(gives)) + [vmem] * len(small_arrays)
    outs = [shape((shard, g.shape[1]), F32) for g in grads]
    outs += [shape((2, 2, *g.shape[1:]), BF16) for g in gives] + [shape(v.shape, F32) for v in small_arrays]
    out_specs = [vmem] * len(grads) + [hbm] * len(gives) + [vmem] * len(small_arrays)
    scratch = [
        low(2, 4), low(2, 4), low(4), low(4), low(3), low(), low(), pltpu.VMEM(held, F32), pltpu.VMEM(held, F32),
        dma((chunks, 2)), dma((2, chunks, 2)), dma((2, chunks)), dma((2, chunks, 3)), dma((2, chunks)),
        dma((2, 2)), dma((2,)), dma((2, 2, peers)),
    ]
    return cuts, inputs, in_specs, outs, out_specs, scratch


def back_reduce_kernel(planes, cuts, counts, *refs):
    grads, gives = counts
    given, rest = refs[:8], refs[8:]
    ins, rest = rest[: grads + gives], rest[grads + gives :]
    out_refs, rest = rest[:3], rest[3:]
    outs, rest = rest[: grads + gives], rest[grads + gives :]
    own_scratch, scratch = rest[: len(rest) - REDUCER_SCRATCH], rest[len(rest) - REDUCER_SCRATCH :]
    reducer = Reducer(planes, cuts, ins[:grads], ins[grads:], None, outs[:grads], outs[grads:], None, scratch)
    turn, phase = pl.program_id(0), pl.program_id(1)
    chunks = len(cuts)

    @pl.when((turn == 0) & (phase == 0))
    def _():
        reducer.begin()
        reducer.begin_swaps()

    at_core = lambda t: jnp.clip(4 + 6 * t, 0, chunks)
    at_x = lambda t: jnp.clip(jnp.maximum(7 * t - 9, 0) // 4, 0, chunks)
    at_z = lambda t: at_x(t - 2)

    @pl.when((turn == 0) & (phase == 1))
    def _():
        reducer.loop(0, at_core(0), reducer.over_core)

    @pl.when((turn > 0) & (phase == 0))
    def _():
        reducer.loop(at_core(turn - 1), at_core(turn), reducer.over_core)
        reducer.loop(at_x(turn - 1), at_x(turn), reducer.over_x)
        reducer.loop(at_z(turn - 1), at_z(turn), reducer.over_z)

    attn_bwd_kernel(*given, *out_refs, *own_scratch)

    @pl.when((turn == pl.num_programs(0) - 1) & (phase == 2))
    def _():
        reducer.loop(at_x(turn), chunks, reducer.over_x)
        reducer.loop(at_z(turn), chunks, reducer.over_z)
        reducer.end()


def back_reduce(qkv, kv_mem, attended, grad, lse, terms, spans, gives, planes):
    pairs = H // 2
    segs, rows, width = kv_mem.shape[0], lse.shape[2], qkv.shape[1] // 3
    mem = kv_mem.shape[1]
    wide = 2 * HD
    count = segs * pairs
    cuts, inputs, in_specs, outs, out_specs, scratch = reducer_call(terms, gives, None, spans)
    at = lambda p: jnp.minimum(p, count - 1)
    spec = lambda off: pl.BlockSpec((rows, wide), lambda p, f, off=off: (at(p) // pairs, off * pairs + lax.rem(at(p), pairs)))
    mspec = lambda off: pl.BlockSpec(
        (1, mem, wide), lambda p, f, off=off: (at(p) // pairs, 0, off * pairs + lax.rem(at(p), pairs))
    )
    lspec = pl.BlockSpec((1, 2, rows), lambda p, f: (at(p), 0, 0))

    def place(p, f):
        which = jnp.where((f == 2) & (p < count), p, jnp.maximum(p - 1, 0))
        block = jnp.where(p == count, jnp.minimum(f, 1) + 1, jnp.where((f == 2) | (p == 0), 0, f + 1))
        return (which // pairs, block * pairs + lax.rem(which, pairs))

    out = pl.pallas_call(
        functools.partial(back_reduce_kernel, planes, cuts, (len(terms), len(gives))),
        grid=(count + 1, 3),
        in_specs=[spec(0), spec(1), spec(2), mspec(0), mspec(1), spec(0), lspec, spec(0), *in_specs],
        out_specs=[pl.BlockSpec((rows, wide), place), mspec(0), mspec(0), *out_specs],
        out_shape=[
            jax.ShapeDtypeStruct(qkv.shape, BF16),
            *[jax.ShapeDtypeStruct((segs, mem, width), F32)] * 2,
            *outs,
        ],
        scratch_shapes=[
            pltpu.VMEM((mem + rows, wide), BF16),
            pltpu.VMEM((mem + rows, wide), BF16),
            pltpu.VMEM((wide, rows), BF16),
            pltpu.VMEM((wide, mem), BF16),
            pltpu.VMEM((rows, wide), BF16),
            pltpu.VMEM((mem + rows, wide), F32),
            pltpu.VMEM((mem + rows, wide), F32),
            *scratch,
        ],
        compiler_params=pltpu.CompilerParams(
            collective_id=1, has_side_effects=True, vmem_limit_bytes=60 * 2**20
        ),
        cost_estimate=pl.CostEstimate(
            flops=count * rows * rows * 6500, bytes_accessed=rows * count * wide * 18, transcendentals=0
        ),
        name="back_reduce",
    )(qkv, qkv, qkv, kv_mem, kv_mem, grad, lse, attended, *inputs)
    return out[:3], out[3 : 3 + len(terms)], out[3 + len(terms) :]


def mem_reduce_kernel(planes, cuts, counts, lines, spans, *refs):
    grads, gives, given, made = counts
    ins, rest = refs[: grads + gives + 1], refs[grads + gives + 1 :]
    early, rest = rest[:2], rest[2:]
    mem_ins, rest = rest[:given], rest[given:]
    outs, rest = rest[: gives + 1], rest[gives + 1 :]
    mem_outs, rest = rest[:made], rest[made:]
    sums, rest = rest[:grads], rest[grads:]
    mem_scratch, scratch = rest[: len(rest) - REDUCER_SCRATCH], rest[len(rest) - REDUCER_SCRATCH :]
    reducer = Reducer(planes, cuts, ins[:grads], ins[grads:-1], ins[-1], sums, outs[:-1], outs[-1], scratch)
    chunks = len(cuts)
    copies = bring(mem_ins[-4:], mem_scratch[:4], mem_scratch[4])
    reducer.begin()
    reducer.add_small()
    reducer.begin_swaps()
    reducer.loop(0, chunks, reducer.over_core)
    reducer.take_small()
    total = outs[-1]
    mem = mem_ins[0].shape[0]
    pooled = [
        jnp.concatenate([total[k * mem : (k + 1) * mem, r, :] for r in range(lines)], axis=1) for k in range(2)
    ]
    mem_bwd_kernel(*mem_ins[:5], pooled, *mem_ins[5:], *mem_outs, *mem_scratch[:4], copies)
    reducer.over_x(0)

    def both(c):
        reducer.over_x(c)
        reducer.over_z(c - 1)

    reducer.loop(1, chunks, both)
    reducer.over_z(chunks - 1)
    reducer.end()
    qkv_made, out_made, expand_made, contract_made = mem_outs[1:5]
    qkv_made[...] += sums[0][...]
    out_made[...] += sums[1][...]
    cut = spans[2][0]
    expand_made[:, :cut] += early[0][:, :cut]
    expand_made[:, cut:] += sums[2][:, cut:]
    contract_made[...] += early[1][...]


def split_heads(rows):
    return rows.reshape(rows.shape[0], rows.shape[1], H, HD)


def plain_scores(query, key, allowed):
    scores = jnp.einsum("sqhd,skhd->shqk", query, key, preferred_element_type=F32) * HD**-0.5
    return scores, allowed[None, None]


def plain_fwd(qkv, kv_all, allowed):
    width = qkv.shape[2] // 3
    query = split_heads(qkv[:, :, :width])
    key, value = split_heads(kv_all[:, :, :width]), split_heads(kv_all[:, :, width:])
    scores, allowed = plain_scores(query, key, allowed)
    raw = jnp.where(allowed, jnp.exp(scores), 0.0)
    total = jnp.sum(raw, axis=-1)
    weights = (raw / total[..., None]).astype(BF16)
    mixed = jnp.einsum("shqk,skhd->sqhd", weights, value, preferred_element_type=F32)
    return mixed.reshape(qkv.shape[0], -1, width).astype(BF16), jnp.log(total)


def plain_bwd(qkv, kv_all, allowed, log_total, grad):
    segs, width = qkv.shape[0], qkv.shape[2] // 3
    query = split_heads(qkv[:, :, :width])
    key, value = split_heads(kv_all[:, :, :width]), split_heads(kv_all[:, :, width:])
    grad = split_heads(grad)
    scores, allowed = plain_scores(query, key, allowed)
    prob = jnp.where(allowed, jnp.exp(scores - log_total[..., None]), 0.0)
    grad_p = jnp.einsum("sqhd,skhd->shqk", grad, value, preferred_element_type=F32)
    inner = jnp.sum(prob * grad_p, axis=-1, keepdims=True)
    grad_s = (prob * (grad_p - inner) * HD**-0.5).astype(BF16)
    dq = jnp.einsum("shqk,skhd->sqhd", grad_s, key, preferred_element_type=F32)
    dk = jnp.einsum("shqk,sqhd->skhd", grad_s, query, preferred_element_type=F32)
    dv = jnp.einsum("shqk,sqhd->skhd", prob.astype(BF16), grad, preferred_element_type=F32)
    flat = lambda a: a.reshape(segs, -1, width)
    return flat(dq), jnp.concatenate([flat(dk), flat(dv)], axis=2)


def memory_forward(mt, p):
    mem = mt.shape[0]
    keep = {}
    width = mt.shape[1]
    unit, rstd = norm_parts(mt)
    normed = (unit * p["one_gain"] + p["one_bias"]).astype(BF16)
    qkv = (dot_dims(normed, p["qkv"], 1, 0) + p["shift"]).astype(BF16)
    at = jnp.arange(mem, dtype=jnp.int32)
    allowed = at[None, :] <= at[:, None]
    attended, log_total = plain_fwd(qkv[None], qkv[None, :, width:], allowed)
    attended = attended[0]
    after = mt + dot_dims(attended, p["out"], 1, 0) + p["out_bias"]
    unit_b, rstd_b = norm_parts(after)
    normed_b = (unit_b * p["two_gain"] + p["two_bias"]).astype(BF16)
    expanded = dot_dims(normed_b, p["expand"], 1, 0) + p["expand_bias"]
    activ = gelu_tanh(expanded).astype(BF16)
    result = after + dot_dims(activ, p["contract"], 1, 1) + p["contract_bias"]
    key_pre = exact(result, p["key"].astype(F32), 1, 0)
    value_new = exact(result, p["value"].astype(F32), 1, 0)
    read_pre = exact(mt, p["read"].astype(F32), 1, 0)
    key_feat, key_pull = jax.vjp(feature_map, key_pre)
    read_feat, read_pull = jax.vjp(feature_map, read_pre)
    mix = exact(read_feat, key_feat, 1, 1)
    numer = exact(mix, value_new, 1, 0)
    denom = 1.0 + jnp.sum(mix, axis=1, keepdims=True)
    follow = mt + numer / denom
    unit_f, rstd_f = norm_parts(follow)
    normed_f = (unit_f * p["one_gain"] + p["one_bias"]).astype(BF16)
    kv_follow = (dot_dims(normed_f, p["qkv"][:, width:], 1, 0) + p["shift"][width:]).astype(BF16)
    keep = dict(
        unit=unit, rstd=rstd, normed=normed, qkv=qkv, allowed=allowed, attended=attended,
        log_total=log_total, unit_b=unit_b, rstd_b=rstd_b, normed_b=normed_b, expanded=expanded,
        activ=activ, result=result, key_feat=key_feat, read_feat=read_feat, key_pull=key_pull,
        read_pull=read_pull, value_new=value_new, mix=mix, numer=numer, denom=denom, unit_f=unit_f,
        rstd_f=rstd_f, normed_f=normed_f,
    )
    return qkv[:, width:], kv_follow, keep


def memory_backward(mt, p, m, grad_kv_first, grad_kv_follow, mine):
    width = mt.shape[1]
    low = lambda a: a.astype(BF16)
    grad_f = low(grad_kv_follow)
    grad_follow, gain_f, bias_f = norm_back(
        dot_dims(grad_f, p["qkv"][:, width:], 1, 1), m["unit_f"], m["rstd_f"], p["one_gain"]
    )
    grad_mt = grad_follow
    grad_numer = grad_follow / m["denom"]
    grad_denom = -jnp.sum(grad_follow * m["numer"], axis=1, keepdims=True) / (m["denom"] * m["denom"])
    grad_mix = exact(grad_numer, m["value_new"], 1, 1) + grad_denom
    grad_value = exact(m["mix"], grad_numer, 0, 0)
    [grad_read_pre] = m["read_pull"](exact(grad_mix, m["key_feat"], 1, 0))
    [grad_key_pre] = m["key_pull"](exact(grad_mix, m["read_feat"], 0, 0))
    grad_mt = grad_mt + exact(grad_read_pre, p["read"].astype(F32), 1, 1)
    grad_result = exact(grad_key_pre, p["key"].astype(F32), 1, 1) + exact(
        grad_value, p["value"].astype(F32), 1, 1
    )
    grad_contract = low(grad_result)
    _, gelu_pull = jax.vjp(gelu_tanh, m["expanded"])
    grad_expanded = low(gelu_pull(dot_dims(grad_contract, p["contract"], 1, 0))[0])
    grad_after, two_gain, two_bias = norm_back(
        dot_dims(grad_expanded, p["expand"], 1, 1), m["unit_b"], m["rstd_b"], p["two_gain"]
    )
    grad_after = grad_after + grad_result
    grad_attn_out = low(grad_after)
    grad_attended = low(dot_dims(grad_attn_out, p["out"], 1, 1))
    dq, dkv = plain_bwd(
        m["qkv"][None], m["qkv"][None, :, width:], m["allowed"], m["log_total"], grad_attended[None]
    )
    grad_qkv = low(jnp.concatenate([dq[0], dkv[0] + grad_kv_first], axis=1))
    grad_first, gain_a, bias_a = norm_back(
        dot_dims(grad_qkv, p["qkv"], 1, 1), m["unit"], m["rstd"], p["one_gain"]
    )
    grad_mt = grad_mt + grad_first + grad_after
    wide = grad_qkv.astype(F32)
    kv_rows = grad_f.astype(F32)
    sums = jnp.sum(wide, axis=0)
    follow_sums = jnp.sum(kv_rows, axis=0)
    matrices = (
        dot_dims(mine(m["normed"]), grad_qkv, 0, 0)
        + jnp.concatenate(
            [
                jnp.zeros((mine(mt).shape[1], width), F32),
                dot_dims(mine(m["normed_f"]), grad_f, 0, 0),
            ],
            axis=1,
        ),
        dot_dims(mine(m["attended"]), grad_attn_out, 0, 0),
        dot_dims(mine(m["normed_b"]), grad_expanded, 0, 0),
        dot_dims(mine(grad_contract), m["activ"], 0, 0),
        exact(mine(mt), grad_read_pre, 0, 0),
        exact(mine(m["result"]), grad_key_pre, 0, 0),
        exact(mine(m["result"]), grad_value, 0, 0),
    )
    column_sum = lambda a: jnp.sum(a.astype(F32), axis=0)
    vectors = (
        gain_f + gain_a,
        bias_f + bias_a,
        jnp.stack([sums[:width], sums[2 * width :] + follow_sums[width:]]),
        column_sum(grad_attn_out),
        two_gain,
        two_bias,
        column_sum(grad_expanded),
        column_sum(grad_contract),
    )
    return grad_mt, matrices, vectors


def local(
    tokens,
    cotangent,
    placing,
    starts,
    memory_tokens,
    norm_one_gain,
    norm_one_bias,
    qkv_weight,
    qv_bias,
    out_weight,
    out_bias,
    norm_two_gain,
    norm_two_bias,
    expand_weight,
    expand_bias,
    contract_weight,
    contract_bias,
    read_weight,
    key_weight,
    value_weight,
):
    del placing
    groups, ranks = lax.axis_size("dp"), lax.axis_size("ctx")
    group, rank = lax.axis_index("dp"), lax.axis_index("ctx")
    micros, segs_local, tok_rows, width = tokens.shape
    mem = memory_tokens.shape[0]
    shard = qkv_weight.shape[0]
    quick = groups == 16 and ranks == 2 and micros == 2 and segs_local == 2 and (tok_rows * ranks) % WIDE == 0
    names = ("qkv", "out", "expand", "contract", "read", "key", "value")
    shards = (qkv_weight, out_weight, expand_weight, contract_weight, read_weight, key_weight, value_weight)
    if quick:
        joined = (
            jnp.concatenate([qkv_weight, read_weight, key_weight], axis=1),
            expand_weight,
            contract_weight,
            jnp.concatenate([out_weight, value_weight], axis=1),
        )
        qkv_read_key, expand_full, contract_full, out_value, got_tokens = gather_weights(
            joined, (2, 3), tokens
        )
        feat = read_weight.shape[1]
        whole = (
            qkv_read_key[:, : 3 * width],
            out_value[:, :width],
            expand_full,
            contract_full,
            qkv_read_key[:, 3 * width : 3 * width + feat],
            qkv_read_key[:, 3 * width + feat :],
            out_value[:, width:],
        )
    else:
        whole = tuple(lax.all_gather(s, "dp", axis=0, tiled=True) for s in shards)
    p = dict(zip(names, whole))
    p.update(
        one_gain=norm_one_gain, one_bias=norm_one_bias, out_bias=out_bias, two_gain=norm_two_gain,
        two_bias=norm_two_bias, expand_bias=expand_bias, contract_bias=contract_bias,
        shift=jnp.concatenate([qv_bias[0], jnp.zeros((width,), F32), qv_bias[1]]),
    )
    flags = lax.dynamic_slice_in_dim(starts, group * segs_local, segs_local, 1)

    swap = [(0, 1), (1, 0)]

    def swapped(given):
        return lax.ppermute(given, "ctx", swap)

    if quick:
        told = rank.astype(jnp.int32)[None]
        give_grad = pick(behind(cotangent, expand_full), 1 - rank, 0)
        flags = pick(flags, rank, 0)
        segs = segs_local
        seg_rows = ranks * tok_rows
    else:
        rows_in, rows_grad = tokens.reshape(-1, width), cotangent.reshape(-1, width)
        flags = flags.reshape(-1)
        segs = micros * segs_local
        seg_rows = tok_rows

    if quick:
        norms = tuple(v[None] for v in (norm_one_gain, norm_one_bias, norm_two_gain, norm_two_bias))
        fixed = tuple(v[None] for v in (p["shift"], out_bias, expand_bias, contract_bias))
        mem_weights_in = (qkv_read_key, out_value, expand_full, contract_full)
        *kept, kv_follow = mem_forward(memory_tokens, (*norms, *fixed), mem_weights_in)
        kv_first = kept[0][:, width:]
    else:
        kv_first, kv_follow, m = memory_forward(memory_tokens, p)
    kv_mem = jnp.where((flags == 0)[:, None, None], kv_follow[None], kv_first[None])
    if quick:
        rows_in, normed_a, qkv = enter(
            told, tokens, got_tokens, norm_one_gain, norm_one_bias, qkv_read_key, p["shift"]
        )
        attended, lse_first = attn_fwd(behind(qkv, give_grad), kv_mem[0], 0, seg_rows, None)
        got_grad = swapped(give_grad)
        attended, lse_second = attn_fwd(qkv, kv_mem[1], 1, seg_rows, attended)
        attended, got_grad = lax.optimization_barrier((attended, got_grad))
        (
            result, rows_grad, normed_b, activ, grad_expanded, grad_attn_out, grad_attended, mid_sums, expand_sums,
        ) = middle(
            told, cotangent, got_grad, rows_in, attended, p["out"], p["expand"], p["contract"], out_bias,
            norm_two_gain, norm_two_bias, expand_bias, contract_bias,
        )
        grad_after = grad_attn_out
    else:
        hidden = rows_in.astype(F32)
        unit_a, rstd_a = norm_parts(hidden)
        normed_a = (unit_a * norm_one_gain + norm_one_bias).astype(BF16)
        qkv = (dot_dims(normed_a, p["qkv"], 1, 0) + p["shift"]).astype(BF16)
        seg_qkv = qkv.reshape(segs, seg_rows, 3 * width)
        kv_all = lax.all_gather(seg_qkv[:, :, width:], "ctx", axis=1, tiled=True)
        kv_all = jnp.concatenate([kv_mem, kv_all], axis=1)
        query_at = mem + rank * seg_rows + jnp.arange(seg_rows, dtype=jnp.int32)
        key_at = jnp.arange(mem + ranks * seg_rows, dtype=jnp.int32)
        allowed = key_at[None, :] <= query_at[:, None]
        attended, lse = plain_fwd(seg_qkv, kv_all, allowed)
        attended = attended.reshape(-1, width)
        after = hidden + dot_dims(attended, p["out"], 1, 0) + out_bias
        unit_b, rstd_b = norm_parts(after)
        normed_b = (unit_b * norm_two_gain + norm_two_bias).astype(BF16)
        expanded = dot_dims(normed_b, p["expand"], 1, 0) + expand_bias
        activ = gelu_tanh(expanded).astype(BF16)
        result = (after + dot_dims(activ, p["contract"], 1, 1) + contract_bias).astype(BF16)

    def input_back(at, grads, weights):
        grad = dot_dims(grads[0], weights[0], 1, 1)
        for g, w in zip(grads[1:], weights[1:]):
            grad = grad + dot_dims(g, w, 1, 1)
        unit, rstd = norm_parts(rows_in[at].astype(F32))
        grad_hidden, gain, bias = norm_back(grad, unit, rstd, norm_one_gain)
        return (grad_hidden + grad_after[at].astype(F32)).astype(BF16), gain, bias

    def pool(dkv_mem):
        follows = (flags == 0).astype(F32)[:, None, None]
        kinds = [jnp.sum(dkv_mem * (1.0 - follows), axis=0), jnp.sum(dkv_mem * follows, axis=0)]
        return jnp.stack(kinds)

    if quick:
        lse = jnp.concatenate([lse_first, lse_second], axis=0)
        by_half = lambda r: r.reshape(segs * ranks, tok_rows, width)
        peers = groups * ranks
        wide_terms = (
            dot_dims(rows_grad, activ, 0, 0).astype(BF16),
            dot_dims(normed_b, grad_expanded, 0, 0).astype(BF16),
        )
        wide_ff = expand_weight.shape[1]
        cut = wide_ff - 768
        (grad_qkv, dk_mem, dv_mem), wide_sums, [block_out] = back_reduce(
            qkv, kv_mem, attended, grad_attended, lse, wide_terms, ((0, wide_ff), (0, cut)), [by_half(result)], ranks
        )
        pooled = pool(jnp.concatenate([dk_mem, dv_mem], axis=2))
        grad_rows, end_sums, qkv_sums = leave(grad_qkv, qkv_read_key, rows_in, grad_after, norm_one_gain, tok_rows)
        one_gain, one_bias = end_sums[0], end_sums[1]
        qkv_sums = qkv_sums.reshape(3, width)
        late_terms = (
            dot_dims(normed_a, grad_qkv, 0, 0).astype(BF16),
            dot_dims(attended, grad_attn_out, 0, 0).astype(BF16),
            wide_terms[1],
        )
    else:
        _, gelu_pull = jax.vjp(gelu_tanh, expanded)
        grad_expanded = gelu_pull(dot_dims(rows_grad, p["contract"], 1, 0))[0].astype(BF16)
        grad_after, two_gain, two_bias = norm_back(
            dot_dims(grad_expanded, p["expand"], 1, 1), unit_b, rstd_b, norm_two_gain
        )
        grad_after = grad_after + rows_grad.astype(F32)
        grad_attn_out = grad_after.astype(BF16)
        grad_attended = dot_dims(grad_attn_out, p["out"], 1, 1).astype(BF16)
        dq, dkv = plain_bwd(
            seg_qkv, kv_all, allowed, lse, grad_attended.reshape(segs, seg_rows, width)
        )
        pooled = pool(dkv[:, :mem])
        dkv = lax.psum_scatter(
            dkv[:, mem:].astype(BF16), "ctx", scatter_dimension=1, tiled=True
        )
        grad_qkv = jnp.concatenate([dq.astype(BF16), dkv], axis=2).reshape(-1, 3 * width)
        grad_rows, one_gain, one_bias = input_back(slice(None), [grad_qkv], [p["qkv"]])
        terms = (
            dot_dims(normed_a, grad_qkv, 0, 0).astype(BF16),
            dot_dims(attended, grad_attn_out, 0, 0).astype(BF16),
            dot_dims(normed_b, grad_expanded, 0, 0).astype(BF16),
            dot_dims(rows_grad, activ, 0, 0).astype(BF16),
        )
        qkv_sums = jnp.sum(grad_qkv.astype(F32), axis=0).reshape(3, width)
    column_sum = lambda a: jnp.sum(a.astype(F32), axis=0)
    if quick:
        mid = (mid_sums[0], mid_sums[1], mid_sums[2], expand_sums[0], mid_sums[3])
    else:
        mid = (
            column_sum(grad_attn_out), two_gain, two_bias, column_sum(grad_expanded), column_sum(rows_grad),
        )
    vectors = (one_gain, one_bias, jnp.stack([qkv_sums[0], qkv_sums[2]]), *mid)
    if not quick:
        summed = tuple(
            lax.psum(
                lax.psum_scatter(t, "dp", scatter_dimension=0, tiled=True).astype(F32), "ctx"
            )
            for t in terms
        )
        pooled, vectors = lax.psum((pooled, vectors), ("dp", "ctx"))

    if quick:
        flat = jnp.concatenate([v.reshape(-1) for v in vectors])
        lines = pl.cdiv(flat.size, peers * 128)
        flat = jnp.pad(flat, (0, peers * lines * 128 - flat.size)).reshape(peers, lines, 128)
        pooled = pooled.reshape(peers, -1, 128)
        token_grad, small, grad_mt, mem_matrices, mem_vectors = mem_reduce(
            memory_tokens, norms, pooled.shape[1], shard, group, kept, mem_weights_in, late_terms,
            ((0, 3 * width), (0, width), (cut, wide_ff)), (wide_sums[1], wide_sums[0]), [by_half(grad_rows)], jnp.concatenate([pooled, flat], axis=1), ranks,
        )
        flat = small[:, pooled.shape[1] :]
        flat = flat.reshape(-1)
    else:
        mine = lambda a: lax.dynamic_slice_in_dim(a, group * shard, shard, 1)
        grad_mt, mem_matrices, mem_vectors = memory_backward(
            memory_tokens, p, m, pooled[0], pooled[1], mine
        )
    if quick:
        split, place = [], 0
        for v in vectors:
            split.append(flat[place : place + v.size].reshape(v.shape))
            place += v.size
        vectors = tuple(split)
    if quick:
        matrices = mem_matrices
    else:
        matrices = tuple(a + b for a, b in zip(summed, mem_matrices)) + mem_matrices[4:]
    vectors = tuple(a + b for a, b in zip(vectors, mem_vectors))
    if not quick:
        block_out, token_grad = result.reshape(tokens.shape), grad_rows.reshape(tokens.shape)
    return (
        block_out,
        token_grad,
        grad_mt,
        vectors[0],
        vectors[1],
        matrices[0],
        vectors[2],
        matrices[1],
        vectors[3],
        vectors[4],
        vectors[5],
        matrices[2],
        vectors[6],
        matrices[3],
        vectors[7],
        matrices[4],
        matrices[5],
        matrices[6],
    )


def solution(mesh):
    rows = P(None, "dp", "ctx", None)
    matrix = P("dp", None)
    full = P()
    return jax.shard_map(
        local,
        mesh=mesh,
        in_specs=(
            rows, rows, full, full, full, full, full, matrix, full, matrix, full, full, full,
            matrix, full, matrix, full, matrix, matrix, matrix,
        ),
        out_specs=(
            rows, rows, full, full, full, matrix, full, matrix, full, full, full, matrix, full,
            matrix, full, matrix, matrix, matrix,
        ),
        check_vma=False,
    )
```

```python
import functools

import jax
import jax.numpy as jnp
from jax import lax
from jax.experimental import pallas as pl
from jax.experimental.pallas import tpu as pltpu
from jax.sharding import PartitionSpec as P

H = 12
HD = 64
EPS = 1e-05
CHUNK = 256
WIDE = 512
F32 = jnp.float32
BF16 = jnp.bfloat16


def norm_parts(rows):
    centred = rows - jnp.mean(rows, axis=-1, keepdims=True)
    spread = jnp.mean(centred * centred, axis=-1, keepdims=True)
    rstd = lax.rsqrt(spread + EPS)
    return centred * rstd, rstd


def norm_back(grad, unit, rstd, gain):
    scaled = grad * gain
    first = jnp.mean(scaled, axis=-1, keepdims=True)
    second = jnp.mean(scaled * unit, axis=-1, keepdims=True)
    grad_rows = rstd * (scaled - first - unit * second)
    return grad_rows, jnp.sum(grad * unit, axis=0), jnp.sum(grad, axis=0)


def feature_map(rows):
    halves = jnp.concatenate([jax.nn.softplus(rows), jax.nn.softplus(-rows)], axis=-1)
    return jnp.concatenate([halves * jnp.roll(halves, j, axis=-1) for j in (1, 2, 3)], axis=-1)


def gelu_tanh(rows):
    return jax.nn.gelu(rows, approximate=True)


def dot_dims(a, b, ca, cb, precision=None):
    return lax.dot_general(
        a, b, (((ca,), (cb,)), ((), ())), precision=precision, preferred_element_type=F32
    )


exact = functools.partial(dot_dims, precision=lax.Precision.HIGHEST)


def head_rows(scale):
    lane = lax.broadcasted_iota(jnp.int32, (1, 2 * HD), 1)
    low = jnp.where(lane < HD, scale, 0.0).astype(BF16)
    high = jnp.where(lane < HD, 0.0, scale).astype(BF16)
    return low, high


def causal_tail(scores):
    key = lax.broadcasted_iota(jnp.int32, scores.shape, 0)
    return jnp.where(key <= lax.broadcasted_iota(jnp.int32, scores.shape, 1), scores, 0.0)


def attn_fwd_kernel(q_ref, k_ref, v_ref, km_ref, vm_ref, o_ref, lse_ref, keys, vals_t, vmem_t):
    mem = km_ref.shape[0]
    keys[0:mem, :] = km_ref[...]
    keys[mem:, :] = k_ref[...]
    vals_t[...] = v_ref[...].T
    vmem_t[...] = vm_ref[...].T
    picks = head_rows(HD**-0.5)
    steps = [(part, head) for part in range(q_ref.shape[0] // WIDE) for head in range(2)]

    def begin(part, head):
        lo, hi = part * WIDE, (part + 1) * WIDE
        return dot_dims(keys[0 : mem + hi, :], q_ref[lo:hi, :] * picks[head], 1, 1)

    ahead = begin(*steps[0])
    outs = []
    for n, (part, head) in enumerate(steps):
        lo, hi = part * WIDE, (part + 1) * WIDE
        band = slice(head * HD, (head + 1) * HD)
        raw = jnp.exp(ahead)
        if n + 1 < len(steps):
            ahead = begin(*steps[n + 1])
        raw = jnp.concatenate([raw[: mem + lo], causal_tail(raw[mem + lo :])], axis=0)
        total = jnp.sum(raw, axis=0, keepdims=True)
        lse_ref[0, head : head + 1, lo:hi] = jnp.log(total)
        weights = (raw * (1.0 / total)).astype(BF16)
        outs.append(
            dot_dims(vals_t[band, 0:hi], weights[mem:], 1, 0)
            + dot_dims(vmem_t[band, :], weights[:mem], 1, 0)
        )
        if head == 1:
            o_ref[lo:hi, :] = jnp.concatenate(outs, axis=0).T.astype(BF16)
            outs = []


def attn_fwd_after_kernel(q_ref, k_ref, v_ref, km_ref, vm_ref, held_ref, *rest):
    del held_ref
    attn_fwd_kernel(q_ref, k_ref, v_ref, km_ref, vm_ref, *rest)


def attn_fwd(qkv, kv_mem, seg, rows, held):
    width = qkv.shape[1] // 3
    mem = kv_mem.shape[0]
    pairs = H // 2
    wide = 2 * HD
    spec = lambda off: pl.BlockSpec((rows, wide), lambda p, off=off: (seg, off * pairs + p))
    mspec = lambda off: pl.BlockSpec((mem, wide), lambda p, off=off: (0, off * pairs + p))
    more = [] if held is None else [held]
    return pl.pallas_call(
        attn_fwd_kernel if held is None else attn_fwd_after_kernel,
        grid=(pairs,),
        in_specs=[spec(0), spec(1), spec(2), mspec(0), mspec(1)]
        + [pl.BlockSpec(memory_space=pl.ANY)] * len(more),
        out_specs=[
            pl.BlockSpec((rows, wide), lambda p: (seg, p)),
            pl.BlockSpec((1, 2, rows), lambda p: (p, 0, 0)),
        ],
        out_shape=[
            jax.ShapeDtypeStruct((qkv.shape[0], width), BF16),
            jax.ShapeDtypeStruct((pairs, 2, rows), F32),
        ],
        scratch_shapes=[
            pltpu.VMEM((mem + rows, wide), BF16),
            pltpu.VMEM((wide, rows), BF16),
            pltpu.VMEM((wide, mem), BF16),
        ],
        input_output_aliases={5: 0} if more else {},
        compiler_params=pltpu.CompilerParams(vmem_limit_bytes=60 * 2**20),
        cost_estimate=pl.CostEstimate(
            flops=pairs * rows * rows * 4000,
            bytes_accessed=rows * width * 8,
            transcendentals=0,
        ),
        name="attn_fwd",
    )(qkv, qkv, qkv, kv_mem, kv_mem, *more)


def attn_bwd_kernel(
    q_ref, k_ref, v_ref, km_ref, vm_ref, g_ref, lse_ref, o_ref,
    out_ref, dkm_ref, dvm_ref,
    keys, vals, keys_t, kmem_t, dq, dk, dv,
):
    phase = pl.program_id(1)
    mem = km_ref.shape[1]
    rows = q_ref.shape[0]

    @pl.when((phase == 2) & (pl.program_id(0) < pl.num_programs(0) - 1))
    def _():
        keys[0:mem, :] = km_ref[0]
        keys[mem:, :] = k_ref[...]
        vals[0:mem, :] = vm_ref[0]
        vals[mem:, :] = v_ref[...]
        keys_t[...] = k_ref[...].T
        kmem_t[...] = km_ref[0].T
        dk[...] = jnp.zeros_like(dk)
        dv[...] = jnp.zeros_like(dv)
        scaled_picks = head_rows(HD**-0.5)
        picks = head_rows(1.0)
        for part in range(rows // CHUNK):
            lo, hi = part * CHUNK, (part + 1) * CHUNK
            end = mem + hi
            query = q_ref[lo:hi, :]
            grad = g_ref[lo:hi, :]
            inner = (grad.astype(F32) * o_ref[lo:hi, :].astype(F32)).T
            dqs = []
            for head in range(2):
                band = slice(head * HD, (head + 1) * HD)
                query_h = query * scaled_picks[head]
                grad_h = grad * picks[head]
                log_total = lse_ref[0, head : head + 1, lo:hi]
                centre = jnp.sum(inner[band], axis=0, keepdims=True)
                prob = jnp.exp(dot_dims(keys[0:end, :], query_h, 1, 1) - log_total)
                prob = jnp.concatenate(
                    [prob[: mem + lo], causal_tail(prob[mem + lo :])], axis=0
                )
                grad_p = dot_dims(vals[0:end, :], grad_h, 1, 1)
                grad_s = (prob * (grad_p - centre)).astype(BF16)
                dv[0:end, :] += dot_dims(prob.astype(BF16), grad_h, 1, 0)
                dk[0:end, :] += dot_dims(grad_s, query_h, 1, 0)
                dqs.append(
                    dot_dims(keys_t[band, 0:hi], grad_s[mem:], 1, 0)
                    + dot_dims(kmem_t[band, :], grad_s[:mem], 1, 0)
                )
            dq[lo:hi, :] = (jnp.concatenate(dqs, axis=0) * HD**-0.5).T.astype(BF16)
        out_ref[...] = dq[...]
        dkm_ref[0] = dk[0:mem, :]
        dvm_ref[0] = dv[0:mem, :]

    @pl.when((phase == 0) & (pl.program_id(0) > 0))
    def _():
        out_ref[...] = dk[mem:, :].astype(BF16)

    @pl.when((phase == 1) & (pl.program_id(0) > 0))
    def _():
        out_ref[...] = dv[mem:, :].astype(BF16)


def choose(told, kept, got, out):
    own = pl.program_id(0) % 2 == told[0]

    @pl.when(own)
    def _():
        out[...] = kept[0, 0]

    @pl.when(jnp.logical_not(own))
    def _():
        out[...] = got[0]


def half_specs(rows, width):
    return [
        pl.BlockSpec((1, 1, rows, width), lambda i, told: (told[0], i // 2, 0, 0)),
        pl.BlockSpec((1, rows, width), lambda i, told: (i // 2, 0, 0)),
    ]


def enter_kernel(told, kept, got, gain, bias, weight, shift, rows_ref, normed_ref, qkv_ref):
    choose(told, kept, got, rows_ref)
    unit, _ = norm_parts(rows_ref[...].astype(F32))
    normed = (unit * gain[...] + bias[...]).astype(BF16)
    normed_ref[...] = normed
    wide = weight.shape[1] // 3
    for k in range(3):
        at = slice(k * wide, (k + 1) * wide)
        qkv_ref[:, at] = (dot_dims(normed, weight[:, at], 1, 0) + shift[:, at]).astype(BF16)


def enter(told, kept, got, gain, bias, weight, shift):
    _, segs, rows, width = kept.shape
    whole = lambda r, c: pl.BlockSpec((r, c), lambda i, told: (0, 0), pipeline_mode=pl.Buffered(1))
    block = lambda c: pl.BlockSpec((rows, c), lambda i, told: (i, 0))
    sizes = (width, width, 3 * width)
    return pl.pallas_call(
        enter_kernel,
        grid_spec=pltpu.PrefetchScalarGridSpec(
            num_scalar_prefetch=1,
            grid=(2 * segs,),
            in_specs=[*half_specs(rows, width), whole(1, width), whole(1, width), whole(width, 3 * width), whole(1, 3 * width)],
            out_specs=[block(c) for c in sizes],
        ),
        out_shape=[jax.ShapeDtypeStruct((2 * segs * rows, c), BF16) for c in sizes],
        compiler_params=pltpu.CompilerParams(vmem_limit_bytes=60 * 2**20),
        cost_estimate=pl.CostEstimate(
            flops=8 * segs * rows * width * width * 3, bytes_accessed=segs * rows * width * 28, transcendentals=0
        ),
        name="enter",
    )(told, kept, got, gain[None], bias[None], weight, shift[None])


def middle_kernel(
    told, kept, got, rows_ref, attended, out_w, expand_w, contract_w, out_b, gain, bias, expand_b, contract_b,
    result_ref, cot_ref, normed_ref, activ_ref, grad_exp_ref, grad_out_ref, grad_att_ref,
    sums_ref, exp_sums_ref,
):
    choose(told, kept, got, cot_ref)
    cot = cot_ref[...]
    after = rows_ref[...].astype(F32) + dot_dims(attended[...], out_w[...], 1, 0) + out_b[...]
    unit, rstd = norm_parts(after)
    normed = (unit * gain[...] + bias[...]).astype(BF16)
    normed_ref[...] = normed
    total = after + contract_b[...]
    back = 0.0

    @pl.when(pl.program_id(0) == 0)
    def _():
        sums_ref[...] = jnp.zeros_like(sums_ref)
        exp_sums_ref[...] = jnp.zeros_like(exp_sums_ref)

    parts = 4
    wide = expand_w.shape[1] // parts
    bend, cube = 0.7978845608028654, 0.044715
    for part in range(parts):
        at = slice(part * wide, (part + 1) * wide)
        value = dot_dims(normed, expand_w[:, at], 1, 0) + expand_b[:, at]
        square = value * value
        half = 0.5 + 0.5 * jnp.tanh(value * (bend + bend * cube * square))
        activ = (value * half).astype(BF16)
        activ_ref[:, at] = activ
        slope = half + (half - half * half) * (value * (2.0 * bend + 6.0 * bend * cube * square))
        grad = (dot_dims(cot, contract_w[:, at], 1, 0) * slope).astype(BF16)
        grad_exp_ref[:, at] = grad
        exp_sums_ref[:, at] += jnp.sum(grad.astype(F32), axis=0, keepdims=True)
        total = total + dot_dims(activ, contract_w[:, at], 1, 1)
        back = back + dot_dims(grad, expand_w[:, at], 1, 1)
    result_ref[...] = total.astype(BF16)
    wide_cot = cot.astype(F32)
    grad_rows, gain_sum, bias_sum = norm_back(back, unit, rstd, gain[...])
    grad_out = (grad_rows + wide_cot).astype(BF16)
    grad_out_ref[...] = grad_out
    grad_att_ref[...] = dot_dims(grad_out, out_w[...], 1, 1).astype(BF16)
    sums = (
        jnp.sum(grad_out.astype(F32), axis=0, keepdims=True),
        gain_sum[None],
        bias_sum[None],
        jnp.sum(wide_cot, axis=0, keepdims=True),
    )
    for k, value in enumerate(sums):
        sums_ref[k : k + 1, :] += value


def middle(told, kept, got, rows_in, attended, out_w, expand_w, contract_w, out_b, gain, bias, expand_b, contract_b):
    _, segs, rows, width = kept.shape
    wide = expand_w.shape[1]
    whole = lambda r, c: pl.BlockSpec((r, c), lambda i, told: (0, 0), pipeline_mode=pl.Buffered(1))
    block = lambda c: pl.BlockSpec((rows, c), lambda i, told: (i, 0))
    sizes = (width, width, width, wide, wide, width, width)
    count = 2 * segs * rows
    fixed = lambda r, c: pl.BlockSpec((r, c), lambda i, told: (0, 0))
    return pl.pallas_call(
        middle_kernel,
        grid_spec=pltpu.PrefetchScalarGridSpec(
            num_scalar_prefetch=1,
            grid=(2 * segs,),
            in_specs=[
                *half_specs(rows, width), block(width), block(width), whole(width, width), whole(width, wide),
                whole(width, wide), whole(1, width), whole(1, width), whole(1, width), whole(1, wide), whole(1, width),
            ],
            out_specs=[*[block(c) for c in sizes], fixed(8, width), fixed(1, wide)],
        ),
        out_shape=[
            *[jax.ShapeDtypeStruct((count, c), BF16) for c in sizes],
            jax.ShapeDtypeStruct((8, width), F32),
            jax.ShapeDtypeStruct((1, wide), F32),
        ],
        compiler_params=pltpu.CompilerParams(vmem_limit_bytes=60 * 2**20),
        cost_estimate=pl.CostEstimate(
            flops=count * width * (8 * wide + 4 * width) * 2, bytes_accessed=count * (14 * width + 4 * wide), transcendentals=0
        ),
        name="middle",
    )(
        told, kept, got, rows_in, attended, out_w, expand_w, contract_w, out_b[None], gain[None], bias[None],
        expand_b[None], contract_b[None],
    )


def leave_kernel(grad_ref, weight, rows_ref, after_ref, gain, rows_out, sums_ref, col_ref):
    @pl.when(pl.program_id(0) == 0)
    def _():
        sums_ref[...] = jnp.zeros_like(sums_ref)
        col_ref[...] = jnp.zeros_like(col_ref)

    grad = grad_ref[...]
    unit, rstd = norm_parts(rows_ref[...].astype(F32))
    grad_rows, gain_sum, bias_sum = norm_back(dot_dims(grad, weight[...], 1, 1), unit, rstd, gain[...])
    rows_out[...] = (grad_rows + after_ref[...].astype(F32)).astype(BF16)
    sums_ref[0:1, :] += gain_sum[None]
    sums_ref[1:2, :] += bias_sum[None]
    col_ref[...] += jnp.sum(grad.astype(F32), axis=0, keepdims=True)


def leave(grad_qkv, weight, rows_in, grad_after, gain, rows):
    count, width = rows_in.shape
    block = lambda c: pl.BlockSpec((rows, c), lambda i: (i, 0))
    fixed = lambda r, c: pl.BlockSpec((r, c), lambda i: (0, 0))
    whole = lambda r, c: pl.BlockSpec((r, c), lambda i: (0, 0), pipeline_mode=pl.Buffered(1))
    return pl.pallas_call(
        leave_kernel,
        grid=(count // rows,),
        in_specs=[block(3 * width), whole(width, 3 * width), block(width), block(width), whole(1, width)],
        out_specs=[block(width), fixed(8, width), fixed(1, 3 * width)],
        out_shape=[
            jax.ShapeDtypeStruct((count, width), BF16),
            jax.ShapeDtypeStruct((8, width), F32),
            jax.ShapeDtypeStruct((1, 3 * width), F32),
        ],
        compiler_params=pltpu.CompilerParams(vmem_limit_bytes=60 * 2**20),
        cost_estimate=pl.CostEstimate(
            flops=6 * count * width * width, bytes_accessed=count * width * 12, transcendentals=0
        ),
        name="leave",
    )(grad_qkv, weight, rows_in, grad_after, gain[None])


def thirds(rows):
    parts = []
    for _ in range(3):
        parts.append(rows.astype(BF16))
        rows = rows - parts[-1].astype(F32)
    return jnp.concatenate(parts, axis=0)


def exact_low(rows, weight, side):
    count = rows.shape[0]
    out = dot_dims(thirds(rows), weight, 1, side)
    return out[:count] + out[count : 2 * count] + out[2 * count :]


def softplus(rows):
    return jnp.maximum(rows, 0.0) + jnp.log1p(jnp.exp(-jnp.abs(rows)))


def feature_parts(rows):
    halves = jnp.concatenate([softplus(rows), softplus(-rows)], axis=1)
    turned = [pltpu.roll(halves, j, 1) for j in (1, 2, 3)]
    return halves, turned, jnp.concatenate([halves * t for t in turned], axis=1)


def feature_back(rows, grad):
    halves, turned, _ = feature_parts(rows)
    wide = halves.shape[1]
    total = 0.0
    for j in (1, 2, 3):
        part = grad[:, (j - 1) * wide : j * wide]
        total = total + part * turned[j - 1] + pltpu.roll(part * halves, wide - j, 1)
    first, last = total[:, : wide // 2], total[:, wide // 2 :]
    return first * jax.nn.sigmoid(rows) - last * jax.nn.sigmoid(-rows)


def per_head(rows):
    tall = jnp.concatenate([rows] * H, axis=0)
    return tall * head_mask(tall.shape, rows.shape[0]).astype(rows.dtype)


def head_mask(shape, count):
    head = lax.broadcasted_iota(jnp.int32, shape, 0) // count
    return (lax.broadcasted_iota(jnp.int32, shape, 1) // HD == head).astype(F32)


def from_heads(tall, count):
    tall = tall * head_mask(tall.shape, count)
    total = tall[:count]
    for head in range(1, H):
        total = total + tall[head * count : (head + 1) * count]
    return total


def mem_weights(query, key):
    count = key.shape[0]
    tall = per_head(query)
    scores = dot_dims(tall, key, 1, 1) * HD**-0.5
    at = lax.rem(lax.broadcasted_iota(jnp.int32, scores.shape, 0), count)
    raw = jnp.where(lax.broadcasted_iota(jnp.int32, scores.shape, 1) <= at, jnp.exp(scores), 0.0)
    return tall, raw / jnp.sum(raw, axis=1, keepdims=True)


def read_parts(read_feat, key_feat, value_new):
    mix = exact(read_feat, key_feat, 1, 1)
    return mix, exact(mix, value_new, 1, 0), 1.0 + jnp.sum(mix, axis=1, keepdims=True)


def bring(sources, targets, sem):
    copies = [pltpu.make_async_copy(a, b, sem.at[k]) for k, (a, b) in enumerate(zip(sources, targets))]
    for copy in copies:
        copy.start()
    return copies


def mem_fwd_kernel(
    mt_ref, one_gain, one_bias, two_gain, two_bias, shift, out_b, expand_b, contract_b,
    qrk_hbm, ov_hbm, expand_hbm, contract_hbm,
    qkv_ref, attended_ref, after_ref, expanded_ref, result_ref, pre_ref, value_ref, follow_ref, kv_ref,
    qrk, ov, expand_w, contract_w, sem,
):
    copies = bring((qrk_hbm, ov_hbm, expand_hbm, contract_hbm), (qrk, ov, expand_w, contract_w), sem)
    mt = mt_ref[...]
    width = mt.shape[1]
    feat = pre_ref.shape[1] // 2
    unit, _ = norm_parts(mt)
    normed = (unit * one_gain[...] + one_bias[...]).astype(BF16)
    copies[0].wait()
    qkv = (dot_dims(normed, qrk[:, : 3 * width], 1, 0) + shift[...]).astype(BF16)
    qkv_ref[...] = qkv
    read_pre = exact_low(mt, qrk[:, 3 * width : 3 * width + feat], 0)
    _, weights = mem_weights(qkv[:, :width], qkv[:, width : 2 * width])
    mixed = dot_dims(weights.astype(BF16), qkv[:, 2 * width :], 1, 0)
    attended = from_heads(mixed, mt.shape[0]).astype(BF16)
    attended_ref[...] = attended
    copies[1].wait()
    after = mt + dot_dims(attended, ov[:, :width], 1, 0) + out_b[...]
    after_ref[...] = after
    unit, _ = norm_parts(after)
    normed = (unit * two_gain[...] + two_bias[...]).astype(BF16)
    copies[2].wait()
    expanded = dot_dims(normed, expand_w[...], 1, 0) + expand_b[...]
    expanded_ref[...] = expanded
    activ = gelu_tanh(expanded).astype(BF16)
    copies[3].wait()
    result = after + dot_dims(activ, contract_w[...], 1, 1) + contract_b[...]
    result_ref[...] = result
    key_pre = exact_low(result, qrk[:, 3 * width + feat :], 0)
    value_new = exact_low(result, ov[:, width:], 0)
    value_ref[...] = value_new
    pre_ref[:, :feat] = read_pre
    pre_ref[:, feat:] = key_pre
    _, numer, denom = read_parts(feature_parts(read_pre)[2], feature_parts(key_pre)[2], value_new)
    follow = mt + numer / denom
    follow_ref[...] = follow
    unit, _ = norm_parts(follow)
    normed = (unit * one_gain[...] + one_bias[...]).astype(BF16)
    kv_ref[...] = (dot_dims(normed, qrk[:, width : 3 * width], 1, 0) + shift[:, width:]).astype(BF16)


def mem_call(kernel, name, given, weights, outs, cycles):
    vmem = pl.BlockSpec(memory_space=pltpu.VMEM)
    return pl.pallas_call(
        kernel,
        in_specs=[vmem] * len(given) + [pl.BlockSpec(memory_space=pl.ANY)] * len(weights),
        out_specs=[vmem] * len(outs),
        out_shape=outs,
        scratch_shapes=[
            *[pltpu.VMEM(w.shape, w.dtype) for w in weights],
            pltpu.SemaphoreType.DMA((len(weights),)),
        ],
        compiler_params=pltpu.CompilerParams(vmem_limit_bytes=60 * 2**20),
        cost_estimate=pl.CostEstimate(flops=cycles * 10**9, bytes_accessed=17 * 10**6, transcendentals=0),
        name=name,
    )(*given, *weights)


def mem_forward(mt, given, weights):
    mem, width = mt.shape
    wide, feat = weights[2].shape[1], (weights[0].shape[1] - 3 * width) // 2
    shape = jax.ShapeDtypeStruct
    outs = [
        shape((mem, 3 * width), BF16), shape((mem, width), BF16), shape((mem, width), F32), shape((mem, wide), F32),
        shape((mem, width), F32), shape((mem, 2 * feat), F32), shape((mem, width), F32), shape((mem, width), F32),
        shape((mem, 2 * width), BF16),
    ]
    return mem_call(mem_fwd_kernel, "mem_fwd", (mt, *given), weights, outs, 15)


def mem_bwd_kernel(
    mt_ref, one_gain, one_bias, two_gain, two_bias, pooled, chosen,
    qkv_ref, attended_ref, after_ref, expanded_ref, result_ref, pre_ref, value_ref, follow_ref,
    qrk_hbm, ov_hbm, expand_hbm, contract_hbm,
    grad_mt_ref, qkv_grad, out_grad, expand_grad, contract_grad, read_grad, key_grad, value_grad, sums_ref, exp_sums_ref,
    qrk, ov, expand_w, contract_w, copies,
):
    del qrk_hbm, ov_hbm, expand_hbm, contract_hbm
    mt = mt_ref[...]
    mem, width = mt.shape
    feat = pre_ref.shape[1] // 2
    sums_ref[...] = jnp.zeros_like(sums_ref)

    def add_row(k, value):
        sums_ref[k : k + 1, :] += value[None]

    def column(value):
        return jnp.sum(value.astype(F32), axis=0)

    unit_f, rstd_f = norm_parts(follow_ref[...])
    normed_f = (unit_f * one_gain[...] + one_bias[...]).astype(BF16)
    grad_f = pooled[1].astype(BF16)
    copies[0].wait()
    grad_follow, gain, bias = norm_back(
        dot_dims(grad_f, qrk[:, width : 3 * width], 1, 1), unit_f, rstd_f, one_gain[...]
    )
    add_row(0, gain)
    add_row(1, bias)
    add_row(3, column(grad_f[:, width:]))
    read_pre, key_pre, value_new = pre_ref[:, :feat], pre_ref[:, feat:], value_ref[...]
    read_feat, key_feat = feature_parts(read_pre)[2], feature_parts(key_pre)[2]
    mix, numer, denom = read_parts(read_feat, key_feat, value_new)
    grad_numer = grad_follow / denom
    grad_denom = -jnp.sum(grad_follow * numer, axis=1, keepdims=True) / (denom * denom)
    grad_mix = exact(grad_numer, value_new, 1, 1) + grad_denom
    grad_value = exact(mix, grad_numer, 0, 0)
    grad_read_pre = feature_back(read_pre, exact(grad_mix, key_feat, 1, 0))
    grad_key_pre = feature_back(key_pre, exact(grad_mix, read_feat, 0, 0))
    grad_mt = grad_follow + exact_low(grad_read_pre, qrk[:, 3 * width : 3 * width + feat], 1)
    copies[1].wait()
    grad_result = exact_low(grad_key_pre, qrk[:, 3 * width + feat :], 1) + exact_low(
        grad_value, ov[:, width:], 1
    )
    grad_contract = grad_result.astype(BF16)
    add_row(7, column(grad_contract))
    expanded = expanded_ref[...]
    bend, cube = 0.7978845608028654, 0.044715
    square = expanded * expanded
    curve = jnp.tanh(bend * expanded * (1.0 + cube * square))
    half = 0.5 * (1.0 + curve)
    activ = (expanded * half).astype(BF16)
    slope = half + 0.5 * bend * expanded * (1.0 - curve * curve) * (1.0 + 3.0 * cube * square)
    copies[3].wait()
    grad_expanded = (dot_dims(grad_contract, contract_w[...], 1, 0) * slope).astype(BF16)
    exp_sums_ref[...] = column(grad_expanded)[None]
    unit_b, rstd_b = norm_parts(after_ref[...])
    normed_b = (unit_b * two_gain[...] + two_bias[...]).astype(BF16)
    copies[2].wait()
    grad_after, gain, bias = norm_back(
        dot_dims(grad_expanded, expand_w[...], 1, 1), unit_b, rstd_b, two_gain[...]
    )
    add_row(5, gain)
    add_row(6, bias)
    grad_after = grad_after + grad_result
    grad_attn_out = grad_after.astype(BF16)
    add_row(4, column(grad_attn_out))
    grad_attended = dot_dims(grad_attn_out, ov[:, :width], 1, 1).astype(BF16)
    query, key, value = (qkv_ref[:, k * width : (k + 1) * width] for k in range(3))
    tall, weights = mem_weights(query, key)
    grad_tall = per_head(grad_attended)
    grad_weights = dot_dims(grad_tall, value, 1, 1)
    centre = jnp.sum(weights * grad_weights, axis=1, keepdims=True)
    grad_s = (weights * (grad_weights - centre) * HD**-0.5).astype(BF16)
    grad_qkv = jnp.concatenate(
        [
            from_heads(dot_dims(grad_s, key, 1, 0), mem),
            dot_dims(grad_s, tall, 0, 0) + pooled[0][:, :width],
            dot_dims(weights.astype(BF16), grad_tall, 0, 0) + pooled[0][:, width:],
        ],
        axis=1,
    ).astype(BF16)
    add_row(2, column(grad_qkv[:, :width]))
    add_row(3, column(grad_qkv[:, 2 * width :]))
    unit, rstd = norm_parts(mt)
    normed = (unit * one_gain[...] + one_bias[...]).astype(BF16)
    grad_first, gain, bias = norm_back(
        dot_dims(grad_qkv, qrk[:, : 3 * width], 1, 1), unit, rstd, one_gain[...]
    )
    add_row(0, gain)
    add_row(1, bias)
    grad_mt_ref[...] = grad_mt + grad_first + grad_after

    pick_low = lambda a: dot_dims(a, chosen[...], 1, 0).astype(BF16)
    pick_exact = lambda a: exact_low(a, chosen[...], 0)
    qkv_grad[...] = dot_dims(pick_low(normed), grad_qkv, 0, 0)
    qkv_grad[:, width:] += dot_dims(pick_low(normed_f), grad_f, 0, 0)
    out_grad[...] = dot_dims(pick_low(attended_ref[...]), grad_attn_out, 0, 0)
    expand_grad[...] = dot_dims(pick_low(normed_b), grad_expanded, 0, 0)
    contract_grad[...] = dot_dims(pick_low(grad_contract), activ, 0, 0)
    my_result = pick_exact(result_ref[...])
    read_grad[...] = exact(pick_exact(mt), grad_read_pre, 0, 0)
    key_grad[...] = exact(my_result, grad_key_pre, 0, 0)
    value_grad[...] = exact(my_result, grad_value, 0, 0)


def mem_reduce(mt, norms, lines, shard, group, kept, weights, terms, spans, early, gives, small, planes):
    mem, width = mt.shape
    wide, feat = weights[2].shape[1], (weights[0].shape[1] - 3 * width) // 2
    at = lax.broadcasted_iota(jnp.int32, (width, shard), 0) - group * shard
    chosen = (at == lax.broadcasted_iota(jnp.int32, (width, shard), 1)).astype(BF16)
    sizes = (3 * width, width, wide, wide, feat, feat, width)
    shape = jax.ShapeDtypeStruct
    mem_outs = [
        shape((mem, width), F32), *[shape((shard, c), F32) for c in sizes], shape((8, width), F32), shape((1, wide), F32),
    ]
    given = (mt, *norms, chosen, *kept)
    cuts, inputs, in_specs, outs, out_specs, scratch = reducer_call(terms, gives, small, spans)
    vmem = pl.BlockSpec(memory_space=pltpu.VMEM)
    out = pl.pallas_call(
        functools.partial(
            mem_reduce_kernel, planes, cuts, (len(terms), len(gives), len(given) + len(weights), len(mem_outs)), lines, spans
        ),
        in_specs=[*in_specs, *[vmem] * (2 + len(given)), *[pl.BlockSpec(memory_space=pl.ANY)] * len(weights)],
        out_specs=[*out_specs[len(terms) :], *[vmem] * len(mem_outs)],
        out_shape=[*outs[len(terms) :], *mem_outs],
        scratch_shapes=[
            *[pltpu.VMEM(o.shape, F32) for o in outs[: len(terms)]],
            *[pltpu.VMEM(w.shape, w.dtype) for w in weights],
            pltpu.SemaphoreType.DMA((len(weights),)),
            *scratch,
        ],
        compiler_params=pltpu.CompilerParams(
            collective_id=2, has_side_effects=True, vmem_limit_bytes=60 * 2**20
        ),
        cost_estimate=pl.CostEstimate(flops=5 * 10**10, bytes_accessed=30 * 10**6, transcendentals=0),
        name="mem_reduce",
    )(*inputs, *early, *given, *weights)
    swapped, summed, grad_mt, *rest = out
    sums, expand_sums = rest[7:]
    vectors = (sums[0], sums[1], sums[2:4], sums[4], sums[5], sums[6], expand_sums[0], sums[7])
    return swapped, summed, grad_mt, tuple(rest[:7]), vectors


def gather_kernel(halved, count, kinds, *refs):
    shards, rows_ref = refs[:count], refs[count]
    outs, got_rows = refs[count + 1 : 2 * count + 1], refs[2 * count + 1]
    send_sem, recv_sem, local_sem = refs[2 * count + 2 :]
    index, plane = lax.axis_index("dp"), lax.axis_index("ctx")
    deep, cross, core = index // 4, (index // 2) % 2, index % 2
    place = lambda z, x, c: (z * 2 + x) * 2 + c
    up, down = {"dp": place(deep + 1, cross, core)}, {"dp": place(deep - 1, cross, core)}
    beside, sibling = {"dp": place(deep, 1 - cross, core)}, {"dp": place(deep, cross, 1 - core)}
    other = {"ctx": 1 - plane}
    rows = shards[0].shape[0]
    numbers, sends = {}, []

    def valid(kind):
        way, far = kind
        return deep >= 0 if way == "own" else deep >= far if way == "below" else deep + far <= 3

    def level(kind):
        way, far = kind
        return deep if way == "own" else deep - far if way == "below" else deep + far

    def view(k, z, x, c, part):
        at = pl.ds(pl.multiple_of(place(z, x, c) * rows, 16), rows)
        return outs[k].at[at, :] if part is None else outs[k].at[at, half(k, part)]

    def half(k, part):
        wide = outs[k].shape[1] // 2
        return pl.ds(pl.multiple_of(part * wide, 128), wide)

    def copy(key, source, landing, device):
        number = numbers.setdefault(key, len(numbers))
        return pltpu.make_async_remote_copy(
            source, landing, send_sem.at[number], recv_sem.at[number],
            device_id=device, device_id_type=pl.DeviceIdType.MESH,
        )

    def send(when, key, source, landing, device):
        def begin():
            copy(key, source, landing, device).start()

        def end():
            copy(key, source, landing, device).wait_send()

        sends.append((when, end))
        if when is None:
            begin()
        else:
            pl.when(when)(begin)

    def arrived(key, landing):
        copy(key, landing, landing, sibling).wait_recv()

    barrier = pltpu.get_barrier_semaphore()
    for device in (beside, sibling, other):
        pl.semaphore_signal(barrier, inc=1, device_id=device, device_id_type=pl.DeviceIdType.MESH)
    for when, device in ((deep < 3, up), (deep > 0, down)):

        @pl.when(when)
        def _(device=device):
            pl.semaphore_signal(barrier, inc=1, device_id=device, device_id_type=pl.DeviceIdType.MESH)

    inner = (deep > 0) & (deep < 3)
    for when, peers in ((inner, 5), (jnp.logical_not(inner), 4)):

        @pl.when(when)
        def _(peers=peers):
            pl.semaphore_wait(barrier, peers)

    own = ("own", 0)
    rows_key = ("rows",)
    send(None, rows_key, rows_ref.at[1 - plane], got_rows, other)
    locals_ = []
    for k in range(count):
        part = plane if k in halved else None
        mine = view(k, deep, cross, core, None)
        locals_.append(pltpu.make_async_copy(shards[k], mine, local_sem.at[k]))
        locals_[-1].start()
        source = shards[k] if part is None else shards[k].at[:, half(k, part)]
        landing = view(k, deep, cross, core, part)
        send(deep < 3, ("z", ("below", 1), k), source, landing, up)
        send(deep > 0, ("z", ("above", 1), k), source, landing, down)
        send(None, ("x", own, k), source, landing, beside)
        send(None, ("core", "z", own, k), shards[k], mine, sibling)

    def onward(k, flow, kind, x):
        part = plane if k in halved else None
        block = view(k, level(kind), x, core, part)
        ok = valid(kind)
        if flow == "z":
            way, far = kind
            if far < 3:
                if way == "below":
                    send(ok & (deep < 3), ("z", (way, far + 1), k), block, block, up)
                else:
                    send(ok & (deep > 0), ("z", (way, far + 1), k), block, block, down)
            send(ok, ("x", kind, k), block, block, beside)
        send(ok, ("core", flow, kind, k), block, block, sibling)
        if k in halved:
            send(ok, ("y", flow, kind, k), block, block, other)

    def take(flow, kind):
        x = cross if flow == "z" else 1 - cross
        for k in range(count):
            part = plane if k in halved else None

            @pl.when(valid(kind))
            def _():
                arrived((flow, kind, k), view(k, level(kind), x, core, part))

            onward(k, flow, kind, x)

    for far in range(1, 4):
        take("z", ("below", far))
        take("z", ("above", far))
        for kind in kinds:
            if kind[1] == far - 1:
                take("x", kind)
    for kind in kinds:
        if kind[1] == 3:
            take("x", kind)
    crossing = [(flow, kind, k) for flow in ("z", "x") for kind in kinds for k in halved]
    crossing = [c for c in crossing if c[:2] != ("z", own)]
    for flow, kind, k in crossing:
        x = cross if flow == "z" else 1 - cross
        block = lambda c: view(k, level(kind), x, c, 1 - plane)

        @pl.when(valid(kind))
        def _():
            arrived(("y", flow, kind, k), block(core))

        send(valid(kind), ("core", "y", flow, kind, k), block(core), block(core), sibling)
    for flow in ("z", "x"):
        x = cross if flow == "z" else 1 - cross
        for kind in kinds:
            for k in range(count):
                part = plane if k in halved and (flow, kind) != ("z", own) else None

                @pl.when(valid(kind))
                def _():
                    arrived(("core", flow, kind, k), view(k, level(kind), x, 1 - core, part))

    for flow, kind, k in crossing:
        x = cross if flow == "z" else 1 - cross

        @pl.when(valid(kind))
        def _():
            arrived(("core", "y", flow, kind, k), view(k, level(kind), x, 1 - core, 1 - plane))

    arrived(rows_key, got_rows)
    for when, end in sends:
        if when is None:
            end()
        else:
            pl.when(when)(end)
    for held in locals_:
        held.wait()


def gather_weights(shards, halved, tokens):
    kinds = [("own", 0)] + [(way, far) for far in (1, 2, 3) for way in ("below", "above")]
    count = len(shards)
    rows = shards[0].shape[0] * 16
    copies = 6 * count + 7 * count + 13 * len(halved) + 14 * count + 13 * len(halved) + 1
    any_space = pl.BlockSpec(memory_space=pl.ANY)
    return pl.pallas_call(
        functools.partial(gather_kernel, halved, count, kinds),
        in_specs=[any_space] * (count + 1),
        out_specs=[any_space] * (count + 1),
        out_shape=[
            *[jax.ShapeDtypeStruct((rows, s.shape[1]), BF16) for s in shards],
            jax.ShapeDtypeStruct(tokens.shape[1:], BF16),
        ],
        scratch_shapes=[
            pltpu.SemaphoreType.DMA((copies,)),
            pltpu.SemaphoreType.DMA((copies,)),
            pltpu.SemaphoreType.DMA((count,)),
        ],
        compiler_params=pltpu.CompilerParams(
            collective_id=0, has_side_effects=True, vmem_limit_bytes=60 * 2**20
        ),
        cost_estimate=pl.CostEstimate(
            flops=8 * 10**10, bytes_accessed=4 * rows * sum(s.shape[1] for s in shards), transcendentals=0
        ),
        name="gather_weights",
    )(*shards, tokens)


def dp_pairs(flip):
    return [(i, i ^ flip) for i in range(16)]


def behind(value, *earlier):
    return lax.optimization_barrier((value, earlier))[0]


def pick(parts, at, axis):
    return lax.dynamic_index_in_dim(parts, at, axis, keepdims=False)


def add_low(a, b):
    return (a.astype(F32) + b.astype(F32)).astype(BF16)


class Reducer:
    def __init__(self, planes, cuts, grads, gives, small_ref, outs, gots, small_out, scratch):
        self.planes, self.cuts, self.grads, self.gives, self.small_ref = planes, cuts, grads, gives, small_ref
        self.outs, self.gots, self.small_out = outs, gots, small_out
        (
            self.mine, self.got_core, self.got_x, self.line, self.got_z, self.low, self.got_y, self.held, self.total,
            self.load_sem, self.core_sem, self.x_sem, self.z_sem, self.y_sem, self.swap_sem, self.stay_sem, self.sum_sem,
        ) = scratch
        self.index, self.plane = lax.axis_index("dp"), lax.axis_index("ctx")
        deep, cross, core = self.index // 4, lax.rem(self.index // 2, 2), lax.rem(self.index, 2)
        self.deep, self.cross, self.core = deep, cross, core
        self.place = lambda z, x, c: (z * 2 + x) * 2 + c
        self.deeps = (deep + 1 - 2 * lax.rem(deep, 2), lax.rem(deep + 2, 4), 3 - deep)
        self.chunks, self.peers = len(cuts), lax.axis_size("dp") * planes
        self.me = self.index * planes + self.plane

    def remote(self, source, landing, sems, at, device):
        return pltpu.make_async_remote_copy(
            source, landing, sems.at[(0, *at)], sems.at[(1, *at)], device_id=device, device_id_type=pl.DeviceIdType.MESH
        )

    def peer(self, j):
        return (j // self.planes, lax.rem(j, self.planes))

    def small(self, phase, j, sender):
        source, landing = (
            (self.small_ref.at[j], self.held.at[sender]) if phase == 0 else (self.total.at[sender], self.total.at[sender])
        )
        return pltpu.make_async_remote_copy(
            source, landing, self.sum_sem.at[0, phase, j], self.sum_sem.at[1, phase, sender],
            device_id=self.peer(j), device_id_type=pl.DeviceIdType.MESH,
        )

    def every(self, work):
        def body(step, carry):
            work(lax.rem(self.me + step, self.peers))
            return carry

        lax.fori_loop(1, self.peers, body, 0)

    def loop(self, first, last, work):
        def body(c, carry):
            work(c)
            return carry

        lax.fori_loop(first, last, body, 0)

    def to_core(self, c, x):
        k, start, wide = self.cuts[c]
        source = self.grads[k].at[:, x, 1 - self.core, :, pl.ds(start, wide)]
        sibling = {"dp": self.place(self.deep, self.cross, 1 - self.core)}
        return self.remote(source, self.got_core.at[c, x], self.core_sem, (c, x), sibling)

    def to_x(self, c):
        beside = {"dp": self.place(self.deep, 1 - self.cross, self.core)}
        return self.remote(self.mine.at[c, 1 - self.cross], self.got_x.at[c], self.x_sem, (c,), beside)

    def to_z(self, c, k):
        far = {"dp": self.place(self.deeps[k], self.cross, self.core)}
        return self.remote(self.line.at[c, self.deeps[k]], self.got_z.at[c, k], self.z_sem, (c, k), far)

    def to_y(self, c):
        return self.remote(self.low.at[c], self.got_y.at[c], self.y_sem, (c,), {"ctx": 1 - self.plane})

    def swap(self, k):
        source, landing = self.gives[0].at[2 * k + 1 - self.plane], self.gots[0].at[self.plane, k]
        return self.remote(source, landing, self.swap_sem, (k,), {"ctx": 1 - self.plane})

    def stay(self, k):
        source, landing = self.gives[0].at[2 * k + self.plane], self.gots[0].at[self.plane, k]
        return pltpu.make_async_copy(source, landing, self.stay_sem.at[k])

    def arrived(self, landing, sems, at):
        self.remote(landing, landing, sems, at, {"ctx": 1 - self.plane}).wait_recv()

    def begin(self):
        for c, (k, start, wide) in enumerate(self.cuts):
            for x in range(2):
                source = self.grads[k].at[:, x, self.core, :, pl.ds(start, wide)]
                pltpu.make_async_copy(source, self.mine.at[c, x], self.load_sem.at[c, x]).start()
        barrier = pltpu.get_barrier_semaphore()

        def greet(device):
            pl.semaphore_signal(barrier, inc=1, device_id=device, device_id_type=pl.DeviceIdType.MESH)

        if self.small_ref is not None:
            self.every(lambda j: greet(self.peer(j)))
            pl.semaphore_wait(barrier, self.peers - 1)
        else:
            greet({"dp": self.place(self.deep, self.cross, 1 - self.core)})
            greet({"dp": self.place(self.deep, 1 - self.cross, self.core)})
            for far in self.deeps:
                greet({"dp": self.place(far, self.cross, self.core)})
            greet({"ctx": 1 - self.plane})
            pl.semaphore_wait(barrier, 6)
        if self.small_ref is not None:
            self.every(lambda j: self.small(0, j, self.me).start())
            self.held[self.me] = self.small_ref[self.me]
        for c in range(self.chunks):
            for x in range(2):
                self.to_core(c, x).start()

    def begin_swaps(self):
        for k in range(2):
            self.swap(k).start()
            self.stay(k).start()

    def over_core(self, c):
        mine, got = self.mine, self.got_core
        for x in range(2):
            pltpu.make_async_copy(mine.at[c, x], mine.at[c, x], self.load_sem.at[c, x]).wait()
            self.arrived(got.at[c, x], self.core_sem, (c, x))
            for z in range(4):
                mine[c, x, z] = add_low(mine[c, x, z], got[c, x, z])
        self.to_x(c).start()

    def add_small(self):
        self.every(lambda j: self.small(0, j, j).wait_recv())
        self.total[self.me] = jnp.sum(self.held[...], axis=0)
        self.every(lambda j: self.small(1, j, self.me).start())

    def take_small(self):
        self.every(lambda j: self.small(1, j, j).wait_recv())
        self.small_out[...] = self.total[...]

    def over_x(self, c):
        self.arrived(self.got_x.at[c], self.x_sem, (c,))
        for z in range(4):
            self.line[c, z] = add_low(self.mine[c, self.cross, z], self.got_x[c, z])
        for k in range(3):
            self.to_z(c, k).start()

    def over_z(self, c):
        value = self.line[c, self.deep].astype(F32)
        for k in range(3):
            self.arrived(self.got_z.at[c, k], self.z_sem, (c, k))
            value = value + self.got_z[c, k].astype(F32)
        self.low[c] = value.astype(BF16)
        self.to_y(c).start()

    def end(self):
        for c, (k, start, wide) in enumerate(self.cuts):
            self.arrived(self.got_y.at[c], self.y_sem, (c,))
            self.outs[k][:, start : start + wide] = self.low[c].astype(F32) + self.got_y[c].astype(F32)
        for k in range(2):
            self.arrived(self.gots[0].at[1 - self.plane, k], self.swap_sem, (k,))
            self.stay(k).wait()
        if self.small_ref is not None:
            self.every(lambda j: self.small(0, j, self.me).wait_send())
            self.every(lambda j: self.small(1, j, self.me).wait_send())
        for k in range(2):
            self.swap(k).wait_send()
        for c in range(self.chunks):
            for x in range(2):
                self.to_core(c, x).wait_send()

        def finish(c):
            self.to_x(c).wait_send()
            for k in range(3):
                self.to_z(c, k).wait_send()
            self.to_y(c).wait_send()

        self.loop(0, self.chunks, finish)


REDUCER_SCRATCH = 17


def reducer_call(grads, gives, small, spans):
    wide = 384
    shard = grads[0].shape[0] // 16
    cuts = [(k, at, wide) for k, (first, last) in enumerate(spans) for at in range(first, last, wide)]
    small_arrays = [] if small is None else [small]
    chunks = len(cuts)
    peers, held = (1, (8, 128)) if small is None else (small.shape[0], small.shape)
    vmem, hbm = pl.BlockSpec(memory_space=pltpu.VMEM), pl.BlockSpec(memory_space=pl.ANY)
    shape, dma = jax.ShapeDtypeStruct, pltpu.SemaphoreType.DMA
    low = lambda *dims: pltpu.VMEM((chunks, *dims, shard, wide), BF16)
    inputs = (*[g.reshape(4, 2, 2, shard, g.shape[1]) for g in grads], *gives, *small_arrays)
    in_specs = [hbm] * (len(grads) + len(gives)) + [vmem] * len(small_arrays)
    outs = [shape((shard, g.shape[1]), F32) for g in grads]
    outs += [shape((2, 2, *g.shape[1:]), BF16) for g in gives] + [shape(v.shape, F32) for v in small_arrays]
    out_specs = [vmem] * len(grads) + [hbm] * len(gives) + [vmem] * len(small_arrays)
    scratch = [
        low(2, 4), low(2, 4), low(4), low(4), low(3), low(), low(), pltpu.VMEM(held, F32), pltpu.VMEM(held, F32),
        dma((chunks, 2)), dma((2, chunks, 2)), dma((2, chunks)), dma((2, chunks, 3)), dma((2, chunks)),
        dma((2, 2)), dma((2,)), dma((2, 2, peers)),
    ]
    return cuts, inputs, in_specs, outs, out_specs, scratch


def back_reduce_kernel(planes, cuts, counts, *refs):
    grads, gives = counts
    given, rest = refs[:8], refs[8:]
    ins, rest = rest[: grads + gives], rest[grads + gives :]
    out_refs, rest = rest[:3], rest[3:]
    outs, rest = rest[: grads + gives], rest[grads + gives :]
    own_scratch, scratch = rest[: len(rest) - REDUCER_SCRATCH], rest[len(rest) - REDUCER_SCRATCH :]
    reducer = Reducer(planes, cuts, ins[:grads], ins[grads:], None, outs[:grads], outs[grads:], None, scratch)
    turn, phase = pl.program_id(0), pl.program_id(1)
    chunks = len(cuts)

    @pl.when((turn == 0) & (phase == 0))
    def _():
        reducer.begin()
        reducer.begin_swaps()

    at_core = lambda t: jnp.clip(4 + 6 * t, 0, chunks)
    at_x = lambda t: jnp.clip(jnp.maximum(7 * t - 9, 0) // 4, 0, chunks)
    at_z = lambda t: at_x(t - 2)

    @pl.when((turn == 0) & (phase == 1))
    def _():
        reducer.loop(0, at_core(0), reducer.over_core)

    @pl.when((turn > 0) & (phase == 0))
    def _():
        reducer.loop(at_core(turn - 1), at_core(turn), reducer.over_core)
        reducer.loop(at_x(turn - 1), at_x(turn), reducer.over_x)
        reducer.loop(at_z(turn - 1), at_z(turn), reducer.over_z)

    attn_bwd_kernel(*given, *out_refs, *own_scratch)

    @pl.when((turn == pl.num_programs(0) - 1) & (phase == 2))
    def _():
        reducer.loop(at_x(turn), chunks, reducer.over_x)
        reducer.loop(at_z(turn), chunks, reducer.over_z)
        reducer.end()


def back_reduce(qkv, kv_mem, attended, grad, lse, terms, spans, gives, planes):
    pairs = H // 2
    segs, rows, width = kv_mem.shape[0], lse.shape[2], qkv.shape[1] // 3
    mem = kv_mem.shape[1]
    wide = 2 * HD
    count = segs * pairs
    cuts, inputs, in_specs, outs, out_specs, scratch = reducer_call(terms, gives, None, spans)
    at = lambda p: jnp.minimum(p, count - 1)
    spec = lambda off: pl.BlockSpec((rows, wide), lambda p, f, off=off: (at(p) // pairs, off * pairs + lax.rem(at(p), pairs)))
    mspec = lambda off: pl.BlockSpec(
        (1, mem, wide), lambda p, f, off=off: (at(p) // pairs, 0, off * pairs + lax.rem(at(p), pairs))
    )
    lspec = pl.BlockSpec((1, 2, rows), lambda p, f: (at(p), 0, 0))

    def place(p, f):
        which = jnp.where((f == 2) & (p < count), p, jnp.maximum(p - 1, 0))
        block = jnp.where(p == count, jnp.minimum(f, 1) + 1, jnp.where((f == 2) | (p == 0), 0, f + 1))
        return (which // pairs, block * pairs + lax.rem(which, pairs))

    out = pl.pallas_call(
        functools.partial(back_reduce_kernel, planes, cuts, (len(terms), len(gives))),
        grid=(count + 1, 3),
        in_specs=[spec(0), spec(1), spec(2), mspec(0), mspec(1), spec(0), lspec, spec(0), *in_specs],
        out_specs=[pl.BlockSpec((rows, wide), place), mspec(0), mspec(0), *out_specs],
        out_shape=[
            jax.ShapeDtypeStruct(qkv.shape, BF16),
            *[jax.ShapeDtypeStruct((segs, mem, width), F32)] * 2,
            *outs,
        ],
        scratch_shapes=[
            pltpu.VMEM((mem + rows, wide), BF16),
            pltpu.VMEM((mem + rows, wide), BF16),
            pltpu.VMEM((wide, rows), BF16),
            pltpu.VMEM((wide, mem), BF16),
            pltpu.VMEM((rows, wide), BF16),
            pltpu.VMEM((mem + rows, wide), F32),
            pltpu.VMEM((mem + rows, wide), F32),
            *scratch,
        ],
        compiler_params=pltpu.CompilerParams(
            collective_id=1, has_side_effects=True, vmem_limit_bytes=60 * 2**20
        ),
        cost_estimate=pl.CostEstimate(
            flops=count * rows * rows * 6500, bytes_accessed=rows * count * wide * 18, transcendentals=0
        ),
        name="back_reduce",
    )(qkv, qkv, qkv, kv_mem, kv_mem, grad, lse, attended, *inputs)
    return out[:3], out[3 : 3 + len(terms)], out[3 + len(terms) :]


def mem_reduce_kernel(planes, cuts, counts, lines, spans, *refs):
    grads, gives, given, made = counts
    ins, rest = refs[: grads + gives + 1], refs[grads + gives + 1 :]
    early, rest = rest[:2], rest[2:]
    mem_ins, rest = rest[:given], rest[given:]
    outs, rest = rest[: gives + 1], rest[gives + 1 :]
    mem_outs, rest = rest[:made], rest[made:]
    sums, rest = rest[:grads], rest[grads:]
    mem_scratch, scratch = rest[: len(rest) - REDUCER_SCRATCH], rest[len(rest) - REDUCER_SCRATCH :]
    reducer = Reducer(planes, cuts, ins[:grads], ins[grads:-1], ins[-1], sums, outs[:-1], outs[-1], scratch)
    chunks = len(cuts)
    copies = bring(mem_ins[-4:], mem_scratch[:4], mem_scratch[4])
    reducer.begin()
    reducer.loop(0, 3, reducer.over_core)
    reducer.add_small()
    reducer.begin_swaps()
    reducer.loop(3, chunks, reducer.over_core)
    reducer.take_small()
    reducer.loop(0, 2, reducer.over_x)
    total = outs[-1]
    mem = mem_ins[0].shape[0]
    pooled = [
        jnp.concatenate([total[k * mem : (k + 1) * mem, r, :] for r in range(lines)], axis=1) for k in range(2)
    ]
    mem_bwd_kernel(*mem_ins[:5], pooled, *mem_ins[5:], *mem_outs, *mem_scratch[:4], copies)
    def both(c):
        reducer.over_x(c)
        reducer.over_z(c - 1)

    reducer.over_z(0)
    reducer.loop(2, chunks, both)
    reducer.over_z(chunks - 1)
    reducer.end()
    qkv_made, out_made, expand_made, contract_made = mem_outs[1:5]
    qkv_made[...] += sums[0][...]
    out_made[...] += sums[1][...]
    cut = spans[2][0]
    expand_made[:, :cut] += early[0][:, :cut]
    expand_made[:, cut:] += sums[2][:, cut:]
    contract_made[...] += early[1][...]


def split_heads(rows):
    return rows.reshape(rows.shape[0], rows.shape[1], H, HD)


def plain_scores(query, key, allowed):
    scores = jnp.einsum("sqhd,skhd->shqk", query, key, preferred_element_type=F32) * HD**-0.5
    return scores, allowed[None, None]


def plain_fwd(qkv, kv_all, allowed):
    width = qkv.shape[2] // 3
    query = split_heads(qkv[:, :, :width])
    key, value = split_heads(kv_all[:, :, :width]), split_heads(kv_all[:, :, width:])
    scores, allowed = plain_scores(query, key, allowed)
    raw = jnp.where(allowed, jnp.exp(scores), 0.0)
    total = jnp.sum(raw, axis=-1)
    weights = (raw / total[..., None]).astype(BF16)
    mixed = jnp.einsum("shqk,skhd->sqhd", weights, value, preferred_element_type=F32)
    return mixed.reshape(qkv.shape[0], -1, width).astype(BF16), jnp.log(total)


def plain_bwd(qkv, kv_all, allowed, log_total, grad):
    segs, width = qkv.shape[0], qkv.shape[2] // 3
    query = split_heads(qkv[:, :, :width])
    key, value = split_heads(kv_all[:, :, :width]), split_heads(kv_all[:, :, width:])
    grad = split_heads(grad)
    scores, allowed = plain_scores(query, key, allowed)
    prob = jnp.where(allowed, jnp.exp(scores - log_total[..., None]), 0.0)
    grad_p = jnp.einsum("sqhd,skhd->shqk", grad, value, preferred_element_type=F32)
    inner = jnp.sum(prob * grad_p, axis=-1, keepdims=True)
    grad_s = (prob * (grad_p - inner) * HD**-0.5).astype(BF16)
    dq = jnp.einsum("shqk,skhd->sqhd", grad_s, key, preferred_element_type=F32)
    dk = jnp.einsum("shqk,sqhd->skhd", grad_s, query, preferred_element_type=F32)
    dv = jnp.einsum("shqk,sqhd->skhd", prob.astype(BF16), grad, preferred_element_type=F32)
    flat = lambda a: a.reshape(segs, -1, width)
    return flat(dq), jnp.concatenate([flat(dk), flat(dv)], axis=2)


def memory_forward(mt, p):
    mem = mt.shape[0]
    keep = {}
    width = mt.shape[1]
    unit, rstd = norm_parts(mt)
    normed = (unit * p["one_gain"] + p["one_bias"]).astype(BF16)
    qkv = (dot_dims(normed, p["qkv"], 1, 0) + p["shift"]).astype(BF16)
    at = jnp.arange(mem, dtype=jnp.int32)
    allowed = at[None, :] <= at[:, None]
    attended, log_total = plain_fwd(qkv[None], qkv[None, :, width:], allowed)
    attended = attended[0]
    after = mt + dot_dims(attended, p["out"], 1, 0) + p["out_bias"]
    unit_b, rstd_b = norm_parts(after)
    normed_b = (unit_b * p["two_gain"] + p["two_bias"]).astype(BF16)
    expanded = dot_dims(normed_b, p["expand"], 1, 0) + p["expand_bias"]
    activ = gelu_tanh(expanded).astype(BF16)
    result = after + dot_dims(activ, p["contract"], 1, 1) + p["contract_bias"]
    key_pre = exact(result, p["key"].astype(F32), 1, 0)
    value_new = exact(result, p["value"].astype(F32), 1, 0)
    read_pre = exact(mt, p["read"].astype(F32), 1, 0)
    key_feat, key_pull = jax.vjp(feature_map, key_pre)
    read_feat, read_pull = jax.vjp(feature_map, read_pre)
    mix = exact(read_feat, key_feat, 1, 1)
    numer = exact(mix, value_new, 1, 0)
    denom = 1.0 + jnp.sum(mix, axis=1, keepdims=True)
    follow = mt + numer / denom
    unit_f, rstd_f = norm_parts(follow)
    normed_f = (unit_f * p["one_gain"] + p["one_bias"]).astype(BF16)
    kv_follow = (dot_dims(normed_f, p["qkv"][:, width:], 1, 0) + p["shift"][width:]).astype(BF16)
    keep = dict(
        unit=unit, rstd=rstd, normed=normed, qkv=qkv, allowed=allowed, attended=attended,
        log_total=log_total, unit_b=unit_b, rstd_b=rstd_b, normed_b=normed_b, expanded=expanded,
        activ=activ, result=result, key_feat=key_feat, read_feat=read_feat, key_pull=key_pull,
        read_pull=read_pull, value_new=value_new, mix=mix, numer=numer, denom=denom, unit_f=unit_f,
        rstd_f=rstd_f, normed_f=normed_f,
    )
    return qkv[:, width:], kv_follow, keep


def memory_backward(mt, p, m, grad_kv_first, grad_kv_follow, mine):
    width = mt.shape[1]
    low = lambda a: a.astype(BF16)
    grad_f = low(grad_kv_follow)
    grad_follow, gain_f, bias_f = norm_back(
        dot_dims(grad_f, p["qkv"][:, width:], 1, 1), m["unit_f"], m["rstd_f"], p["one_gain"]
    )
    grad_mt = grad_follow
    grad_numer = grad_follow / m["denom"]
    grad_denom = -jnp.sum(grad_follow * m["numer"], axis=1, keepdims=True) / (m["denom"] * m["denom"])
    grad_mix = exact(grad_numer, m["value_new"], 1, 1) + grad_denom
    grad_value = exact(m["mix"], grad_numer, 0, 0)
    [grad_read_pre] = m["read_pull"](exact(grad_mix, m["key_feat"], 1, 0))
    [grad_key_pre] = m["key_pull"](exact(grad_mix, m["read_feat"], 0, 0))
    grad_mt = grad_mt + exact(grad_read_pre, p["read"].astype(F32), 1, 1)
    grad_result = exact(grad_key_pre, p["key"].astype(F32), 1, 1) + exact(
        grad_value, p["value"].astype(F32), 1, 1
    )
    grad_contract = low(grad_result)
    _, gelu_pull = jax.vjp(gelu_tanh, m["expanded"])
    grad_expanded = low(gelu_pull(dot_dims(grad_contract, p["contract"], 1, 0))[0])
    grad_after, two_gain, two_bias = norm_back(
        dot_dims(grad_expanded, p["expand"], 1, 1), m["unit_b"], m["rstd_b"], p["two_gain"]
    )
    grad_after = grad_after + grad_result
    grad_attn_out = low(grad_after)
    grad_attended = low(dot_dims(grad_attn_out, p["out"], 1, 1))
    dq, dkv = plain_bwd(
        m["qkv"][None], m["qkv"][None, :, width:], m["allowed"], m["log_total"], grad_attended[None]
    )
    grad_qkv = low(jnp.concatenate([dq[0], dkv[0] + grad_kv_first], axis=1))
    grad_first, gain_a, bias_a = norm_back(
        dot_dims(grad_qkv, p["qkv"], 1, 1), m["unit"], m["rstd"], p["one_gain"]
    )
    grad_mt = grad_mt + grad_first + grad_after
    wide = grad_qkv.astype(F32)
    kv_rows = grad_f.astype(F32)
    sums = jnp.sum(wide, axis=0)
    follow_sums = jnp.sum(kv_rows, axis=0)
    matrices = (
        dot_dims(mine(m["normed"]), grad_qkv, 0, 0)
        + jnp.concatenate(
            [
                jnp.zeros((mine(mt).shape[1], width), F32),
                dot_dims(mine(m["normed_f"]), grad_f, 0, 0),
            ],
            axis=1,
        ),
        dot_dims(mine(m["attended"]), grad_attn_out, 0, 0),
        dot_dims(mine(m["normed_b"]), grad_expanded, 0, 0),
        dot_dims(mine(grad_contract), m["activ"], 0, 0),
        exact(mine(mt), grad_read_pre, 0, 0),
        exact(mine(m["result"]), grad_key_pre, 0, 0),
        exact(mine(m["result"]), grad_value, 0, 0),
    )
    column_sum = lambda a: jnp.sum(a.astype(F32), axis=0)
    vectors = (
        gain_f + gain_a,
        bias_f + bias_a,
        jnp.stack([sums[:width], sums[2 * width :] + follow_sums[width:]]),
        column_sum(grad_attn_out),
        two_gain,
        two_bias,
        column_sum(grad_expanded),
        column_sum(grad_contract),
    )
    return grad_mt, matrices, vectors


def local(
    tokens,
    cotangent,
    placing,
    starts,
    memory_tokens,
    norm_one_gain,
    norm_one_bias,
    qkv_weight,
    qv_bias,
    out_weight,
    out_bias,
    norm_two_gain,
    norm_two_bias,
    expand_weight,
    expand_bias,
    contract_weight,
    contract_bias,
    read_weight,
    key_weight,
    value_weight,
):
    del placing
    groups, ranks = lax.axis_size("dp"), lax.axis_size("ctx")
    group, rank = lax.axis_index("dp"), lax.axis_index("ctx")
    micros, segs_local, tok_rows, width = tokens.shape
    mem = memory_tokens.shape[0]
    shard = qkv_weight.shape[0]
    quick = groups == 16 and ranks == 2 and micros == 2 and segs_local == 2 and (tok_rows * ranks) % WIDE == 0
    names = ("qkv", "out", "expand", "contract", "read", "key", "value")
    shards = (qkv_weight, out_weight, expand_weight, contract_weight, read_weight, key_weight, value_weight)
    if quick:
        joined = (
            jnp.concatenate([qkv_weight, read_weight, key_weight], axis=1),
            expand_weight,
            contract_weight,
            jnp.concatenate([out_weight, value_weight], axis=1),
        )
        qkv_read_key, expand_full, contract_full, out_value, got_tokens = gather_weights(
            joined, (2, 3), tokens
        )
        feat = read_weight.shape[1]
        whole = (
            qkv_read_key[:, : 3 * width],
            out_value[:, :width],
            expand_full,
            contract_full,
            qkv_read_key[:, 3 * width : 3 * width + feat],
            qkv_read_key[:, 3 * width + feat :],
            out_value[:, width:],
        )
    else:
        whole = tuple(lax.all_gather(s, "dp", axis=0, tiled=True) for s in shards)
    p = dict(zip(names, whole))
    p.update(
        one_gain=norm_one_gain, one_bias=norm_one_bias, out_bias=out_bias, two_gain=norm_two_gain,
        two_bias=norm_two_bias, expand_bias=expand_bias, contract_bias=contract_bias,
        shift=jnp.concatenate([qv_bias[0], jnp.zeros((width,), F32), qv_bias[1]]),
    )
    flags = lax.dynamic_slice_in_dim(starts, group * segs_local, segs_local, 1)

    swap = [(0, 1), (1, 0)]

    def swapped(given):
        return lax.ppermute(given, "ctx", swap)

    if quick:
        told = rank.astype(jnp.int32)[None]
        give_grad = pick(behind(cotangent, expand_full), 1 - rank, 0)
        flags = pick(flags, rank, 0)
        segs = segs_local
        seg_rows = ranks * tok_rows
    else:
        rows_in, rows_grad = tokens.reshape(-1, width), cotangent.reshape(-1, width)
        flags = flags.reshape(-1)
        segs = micros * segs_local
        seg_rows = tok_rows

    if quick:
        norms = tuple(v[None] for v in (norm_one_gain, norm_one_bias, norm_two_gain, norm_two_bias))
        fixed = tuple(v[None] for v in (p["shift"], out_bias, expand_bias, contract_bias))
        mem_weights_in = (qkv_read_key, out_value, expand_full, contract_full)
        *kept, kv_follow = mem_forward(memory_tokens, (*norms, *fixed), mem_weights_in)
        kv_first = kept[0][:, width:]
    else:
        kv_first, kv_follow, m = memory_forward(memory_tokens, p)
    kv_mem = jnp.where((flags == 0)[:, None, None], kv_follow[None], kv_first[None])
    if quick:
        rows_in, normed_a, qkv = enter(
            told, tokens, got_tokens, norm_one_gain, norm_one_bias, qkv_read_key, p["shift"]
        )
        attended, lse_first = attn_fwd(behind(qkv, give_grad), kv_mem[0], 0, seg_rows, None)
        got_grad = swapped(give_grad)
        attended, lse_second = attn_fwd(qkv, kv_mem[1], 1, seg_rows, attended)
        attended, got_grad = lax.optimization_barrier((attended, got_grad))
        (
            result, rows_grad, normed_b, activ, grad_expanded, grad_attn_out, grad_attended, mid_sums, expand_sums,
        ) = middle(
            told, cotangent, got_grad, rows_in, attended, p["out"], p["expand"], p["contract"], out_bias,
            norm_two_gain, norm_two_bias, expand_bias, contract_bias,
        )
        grad_after = grad_attn_out
    else:
        hidden = rows_in.astype(F32)
        unit_a, rstd_a = norm_parts(hidden)
        normed_a = (unit_a * norm_one_gain + norm_one_bias).astype(BF16)
        qkv = (dot_dims(normed_a, p["qkv"], 1, 0) + p["shift"]).astype(BF16)
        seg_qkv = qkv.reshape(segs, seg_rows, 3 * width)
        kv_all = lax.all_gather(seg_qkv[:, :, width:], "ctx", axis=1, tiled=True)
        kv_all = jnp.concatenate([kv_mem, kv_all], axis=1)
        query_at = mem + rank * seg_rows + jnp.arange(seg_rows, dtype=jnp.int32)
        key_at = jnp.arange(mem + ranks * seg_rows, dtype=jnp.int32)
        allowed = key_at[None, :] <= query_at[:, None]
        attended, lse = plain_fwd(seg_qkv, kv_all, allowed)
        attended = attended.reshape(-1, width)
        after = hidden + dot_dims(attended, p["out"], 1, 0) + out_bias
        unit_b, rstd_b = norm_parts(after)
        normed_b = (unit_b * norm_two_gain + norm_two_bias).astype(BF16)
        expanded = dot_dims(normed_b, p["expand"], 1, 0) + expand_bias
        activ = gelu_tanh(expanded).astype(BF16)
        result = (after + dot_dims(activ, p["contract"], 1, 1) + contract_bias).astype(BF16)

    def input_back(at, grads, weights):
        grad = dot_dims(grads[0], weights[0], 1, 1)
        for g, w in zip(grads[1:], weights[1:]):
            grad = grad + dot_dims(g, w, 1, 1)
        unit, rstd = norm_parts(rows_in[at].astype(F32))
        grad_hidden, gain, bias = norm_back(grad, unit, rstd, norm_one_gain)
        return (grad_hidden + grad_after[at].astype(F32)).astype(BF16), gain, bias

    def pool(dkv_mem):
        follows = (flags == 0).astype(F32)[:, None, None]
        kinds = [jnp.sum(dkv_mem * (1.0 - follows), axis=0), jnp.sum(dkv_mem * follows, axis=0)]
        return jnp.stack(kinds)

    if quick:
        lse = jnp.concatenate([lse_first, lse_second], axis=0)
        by_half = lambda r: r.reshape(segs * ranks, tok_rows, width)
        peers = groups * ranks
        wide_terms = (
            dot_dims(rows_grad, activ, 0, 0).astype(BF16),
            dot_dims(normed_b, grad_expanded, 0, 0).astype(BF16),
        )
        wide_ff = expand_weight.shape[1]
        cut = wide_ff - 768
        (grad_qkv, dk_mem, dv_mem), wide_sums, [block_out] = back_reduce(
            qkv, kv_mem, attended, grad_attended, lse, wide_terms, ((0, wide_ff), (0, cut)), [by_half(result)], ranks
        )
        pooled = pool(jnp.concatenate([dk_mem, dv_mem], axis=2))
        grad_rows, end_sums, qkv_sums = leave(grad_qkv, qkv_read_key, rows_in, grad_after, norm_one_gain, tok_rows)
        one_gain, one_bias = end_sums[0], end_sums[1]
        qkv_sums = qkv_sums.reshape(3, width)
        late_terms = (
            dot_dims(normed_a, grad_qkv, 0, 0).astype(BF16),
            dot_dims(attended, grad_attn_out, 0, 0).astype(BF16),
            wide_terms[1],
        )
    else:
        _, gelu_pull = jax.vjp(gelu_tanh, expanded)
        grad_expanded = gelu_pull(dot_dims(rows_grad, p["contract"], 1, 0))[0].astype(BF16)
        grad_after, two_gain, two_bias = norm_back(
            dot_dims(grad_expanded, p["expand"], 1, 1), unit_b, rstd_b, norm_two_gain
        )
        grad_after = grad_after + rows_grad.astype(F32)
        grad_attn_out = grad_after.astype(BF16)
        grad_attended = dot_dims(grad_attn_out, p["out"], 1, 1).astype(BF16)
        dq, dkv = plain_bwd(
            seg_qkv, kv_all, allowed, lse, grad_attended.reshape(segs, seg_rows, width)
        )
        pooled = pool(dkv[:, :mem])
        dkv = lax.psum_scatter(
            dkv[:, mem:].astype(BF16), "ctx", scatter_dimension=1, tiled=True
        )
        grad_qkv = jnp.concatenate([dq.astype(BF16), dkv], axis=2).reshape(-1, 3 * width)
        grad_rows, one_gain, one_bias = input_back(slice(None), [grad_qkv], [p["qkv"]])
        terms = (
            dot_dims(normed_a, grad_qkv, 0, 0).astype(BF16),
            dot_dims(attended, grad_attn_out, 0, 0).astype(BF16),
            dot_dims(normed_b, grad_expanded, 0, 0).astype(BF16),
            dot_dims(rows_grad, activ, 0, 0).astype(BF16),
        )
        qkv_sums = jnp.sum(grad_qkv.astype(F32), axis=0).reshape(3, width)
    column_sum = lambda a: jnp.sum(a.astype(F32), axis=0)
    if quick:
        mid = (mid_sums[0], mid_sums[1], mid_sums[2], expand_sums[0], mid_sums[3])
    else:
        mid = (
            column_sum(grad_attn_out), two_gain, two_bias, column_sum(grad_expanded), column_sum(rows_grad),
        )
    vectors = (one_gain, one_bias, jnp.stack([qkv_sums[0], qkv_sums[2]]), *mid)
    if not quick:
        summed = tuple(
            lax.psum(
                lax.psum_scatter(t, "dp", scatter_dimension=0, tiled=True).astype(F32), "ctx"
            )
            for t in terms
        )
        pooled, vectors = lax.psum((pooled, vectors), ("dp", "ctx"))

    if quick:
        flat = jnp.concatenate([v.reshape(-1) for v in vectors])
        lines = pl.cdiv(flat.size, peers * 128)
        flat = jnp.pad(flat, (0, peers * lines * 128 - flat.size)).reshape(peers, lines, 128)
        pooled = pooled.reshape(peers, -1, 128)
        token_grad, small, grad_mt, mem_matrices, mem_vectors = mem_reduce(
            memory_tokens, norms, pooled.shape[1], shard, group, kept, mem_weights_in, late_terms,
            ((0, 3 * width), (0, width), (cut, wide_ff)), (wide_sums[1], wide_sums[0]), [by_half(grad_rows)], jnp.concatenate([pooled, flat], axis=1), ranks,
        )
        flat = small[:, pooled.shape[1] :]
        flat = flat.reshape(-1)
    else:
        mine = lambda a: lax.dynamic_slice_in_dim(a, group * shard, shard, 1)
        grad_mt, mem_matrices, mem_vectors = memory_backward(
            memory_tokens, p, m, pooled[0], pooled[1], mine
        )
    if quick:
        split, place = [], 0
        for v in vectors:
            split.append(flat[place : place + v.size].reshape(v.shape))
            place += v.size
        vectors = tuple(split)
    if quick:
        matrices = mem_matrices
    else:
        matrices = tuple(a + b for a, b in zip(summed, mem_matrices)) + mem_matrices[4:]
    vectors = tuple(a + b for a, b in zip(vectors, mem_vectors))
    if not quick:
        block_out, token_grad = result.reshape(tokens.shape), grad_rows.reshape(tokens.shape)
    return (
        block_out,
        token_grad,
        grad_mt,
        vectors[0],
        vectors[1],
        matrices[0],
        vectors[2],
        matrices[1],
        vectors[3],
        vectors[4],
        vectors[5],
        matrices[2],
        vectors[6],
        matrices[3],
        vectors[7],
        matrices[4],
        matrices[5],
        matrices[6],
    )


def solution(mesh):
    rows = P(None, "dp", "ctx", None)
    matrix = P("dp", None)
    full = P()
    return jax.shard_map(
        local,
        mesh=mesh,
        in_specs=(
            rows, rows, full, full, full, full, full, matrix, full, matrix, full, full, full,
            matrix, full, matrix, full, matrix, matrix, matrix,
        ),
        out_specs=(
            rows, rows, full, full, full, matrix, full, matrix, full, full, full, matrix, full,
            matrix, full, matrix, matrix, matrix,
        ),
        check_vma=False,
    )
```
